32 devices in a mesh: dp: 16 (over z, y, x), tensor: 2 (over core).
Axes of the slice: x: 2, y: 2, z: 4, core: 2. Of those that a mesh axis runs over, the one named last changes fastest.
Arguments:
- embeds: bfloat16 [24576, 640], P('dp'), may hold values from -6 to 6
- domain: int32 [24576, 1], P('dp'), may hold values from 0 to 3; in each aligned block of 768 rows (0 to 767, 768 to 1535, ...) at most 384 rows name the same one
- frozen: int32 [4], replicated, may hold values from 0 to 1, as said below
- labels: int32 [24576], P('dp'), may hold values from 0 to 1
- proj_w: bfloat16 [640, 512], P(None, ('dp', 'tensor')), may hold values from -0.25 to 0.25
- proj_b: bfloat16 [512], P(('dp', 'tensor')), may hold values from -0.625 to 0.625
- w_in: bfloat16 [12, 512, 1024], P(None, 'dp', 'tensor'), may hold values from -0.25 to 0.25
- in_bias: bfloat16 [12, 1024], P(None, ('dp', 'tensor')), may hold values from -0.625 to 0.625
- w_out: bfloat16 [12, 1024, 512], P(None, 'tensor', 'dp'), may hold values from -0.1875 to 0.1875
- out_bias: bfloat16 [12, 512], P(None, ('dp', 'tensor')), may hold values from -0.625 to 0.625
- ln_gain: bfloat16 [12, 512], P(None, ('dp', 'tensor')), may hold values from 0.5 to 1.5
- ln_shift: bfloat16 [12, 512], P(None, ('dp', 'tensor')), may hold values from -0.625 to 0.625
- gate_top: bfloat16 [4, 512, 2], P(None, ('dp', 'tensor')), may hold values from -0.1875 to 0.1875
- gate_shared: bfloat16 [4, 512, 4], P(None, ('dp', 'tensor')), may hold values from -0.1875 to 0.1875
- gate_domain: bfloat16 [4, 512, 2], P(None, ('dp', 'tensor')), may hold values from -0.1875 to 0.1875
- tower_w: bfloat16 [4, 512, 256], P(None, ('dp', 'tensor')), may hold values from -0.25 to 0.25
- tower_b: bfloat16 [4, 256], P(None, ('dp', 'tensor')), may hold values from -0.625 to 0.625
- tower_out: bfloat16 [4, 256], P(None, ('dp', 'tensor')), may hold values from -0.75 to 0.75
- tower_out_b: bfloat16 [4], replicated, may hold values from -3 to 3
Outputs:
- predictions: float32 [24576], P('dp')
- grad_embeds: bfloat16 [24576, 640], P('dp')
- grad_proj_w: float32 [640, 512], P(None, ('dp', 'tensor'))
- grad_proj_b: float32 [512], P(('dp', 'tensor'))
- grad_w_in: float32 [12, 512, 1024], P(None, 'dp', 'tensor')
- grad_in_bias: float32 [12, 1024], P(None, ('dp', 'tensor'))
- grad_w_out: float32 [12, 1024, 512], P(None, 'tensor', 'dp')
- grad_out_bias: float32 [12, 512], P(None, ('dp', 'tensor'))
- grad_ln_gain: float32 [12, 512], P(None, ('dp', 'tensor'))
- grad_ln_shift: float32 [12, 512], P(None, ('dp', 'tensor'))
- grad_gate_top: float32 [4, 512, 2], P(None, ('dp', 'tensor'))
- grad_gate_shared: float32 [4, 512, 4], P(None, ('dp', 'tensor'))
- grad_gate_domain: float32 [4, 512, 2], P(None, ('dp', 'tensor'))
- grad_tower_w: float32 [4, 512, 256], P(None, ('dp', 'tensor'))
- grad_tower_b: float32 [4, 256], P(None, ('dp', 'tensor'))
- grad_tower_out: float32 [4, 256], P(None, ('dp', 'tensor'))
- grad_tower_out_b: float32 [4], replicated
The draws below stay inside these ranges and needn't reach their ends.
Inputs may be any that keep to these rules, and one draw needn't show every extreme that they name: Among the 768 events of one device's micro-batch (aligned blocks of 768 rows) no domain has more than 384 events; some domain has exactly 384 in some blocks. `frozen`: exactly 2 domains are flagged.
All inputs are finite; a program needn't handle non-finite values.
Results may differ from the reference program's by a relative error of at most 0.017.
Values may be sent and summed in bfloat16 or wider, within the bound.
No kernel may reach another device: no remote copies, remote signals or barrier semaphores. Data moves between devices by JAX's collectives and lax.ppermute only.
A program may use at most 256 MiB of HBM per device.

```python
import math
import jax
import jax.numpy as jnp
import numpy as np
from jax import lax

E_IN = 640
D = 512
H = 1024
TW = 256
S = 4
DOM = 4
K = 2
EXPERTS = 12
EV_DEV = 768
CAP = 384
EVENTS = 24576


def draw_frozen(key, part):
    key = jax.random.fold_in(key, 5)
    order_draw = jax.random.permutation(key, DOM)
    return (order_draw < DOM // 2).astype(jnp.int32)


def touch_ends(values, key, low, top_value):
    shape = values.shape
    spot = [jax.random.randint(jax.random.fold_in(key, axis), (), 0, shape[axis]) for axis in range(len(shape))]
    values = values.at[tuple(spot)].set(low)
    longest = shape.index(max(shape))
    spot[longest] = (spot[longest] + 1) % shape[longest]
    return values.at[tuple(spot)].set(top_value)


def shard_levels(stream_key, extent, split, least, largest):
    def one(dim, blocks):
        steps = jax.random.uniform(jax.random.fold_in(jax.random.fold_in(stream_key, 6), dim), (blocks,), jnp.float32, least / len(split), largest / len(split))
        return jnp.repeat(jnp.exp(steps), extent[dim] // blocks).reshape((-1,) + (1,) * (len(extent) - dim - 1))

    level = one(*split[0])
    for cut in split[1:]:
        level = level * one(*cut)
    return level


def deal_out(key, own, number, rows, number_of, top, limit, slope):
    order = jax.random.permutation(key, number_of)
    crowded, common = shares(number_of, rows * top, limit, slope, True), shares(number_of, rows * top, limit, slope, False)
    places = jnp.arange(number_of)

    def named(sizes, turn):
        used = int((sizes > 0).sum())
        fixed = max(1, used // 4)
        moved = fixed + (places - fixed + turn * (used - fixed)) % max(1, number_of - fixed)
        return jnp.zeros((number_of,), jnp.int32).at[order[jnp.where(places < fixed, places, moved)]].set(jnp.asarray(sizes, jnp.int32))

    sizes = jnp.where(number % 4 == 0, named(crowded, number // 4), named(common, number - number // 4 - 1))
    mixed = jax.random.permutation(jax.random.fold_in(own, 3), number_of)
    giver, sink = mixed[0:number_of // 2 * 2:2], mixed[1:number_of // 2 * 2:2]
    slack = jnp.minimum(sizes[giver] - 1, limit - sizes[sink]) // 2
    slack = jnp.where((giver == order[0]) | (sink == order[0]) | (sizes[sink] == 0), 0, jnp.maximum(slack, 0))
    moved = jax.random.randint(jax.random.fold_in(own, 4), (number_of // 2,), 0, 1 << 20) % (slack + 1)
    sizes = sizes.at[giver].add(-moved).at[sink].add(moved)
    members = jnp.searchsorted(jnp.cumsum(sizes), jnp.arange(rows * top), side="right").astype(jnp.int32)
    listing = members.reshape(top, rows).T
    listing = listing[jax.random.permutation(jax.random.fold_in(own, 1), rows)]
    turn = jax.random.randint(jax.random.fold_in(own, 2), (rows, 1), 0, top)
    return jnp.take_along_axis(listing, (jnp.arange(top)[None, :] + turn) % top, axis=1)


def shares(count, total, limit, slope, full):
    portions = [(1 << 20) // math.isqrt(grade ** slope) + 1 for grade in range(1, count + 1)]
    largest = limit if full else min(limit, max(-(-total // count), total * portions[0] // sum(portions)))
    least = 1 if total - largest >= count - 1 else 0
    counts, surplus = [largest] + [least] * (count - 1), total - largest - least * (count - 1)
    while surplus > 0:
        movable = [i for i in range(1, count) if counts[i] < largest] or [i for i in range(1, count) if counts[i] < limit]
        whole, left = sum([portions[i] for i in movable]), surplus
        for i in movable:
            more = min(limit - counts[i], max(1, left * portions[i] // whole), surplus)
            counts[i] = counts[i] + more
            surplus = surplus - more
    return np.array(counts)


def gaussian(rng, dims, scale, most, cuts=(), kind=jnp.bfloat16):
    drawn = jax.random.normal(rng, dims, jnp.float32) * scale
    if len(cuts) > 0:
        drawn = shard_levels(rng, dims, cuts, -0.22, 0.18) * drawn
    return jnp.clip(drawn, min=-most, max=most).astype(kind)


def setup_inputs(seed: int = 0) -> dict:
    splits = jax.random.split(jax.random.key(seed), 20)
    embeds = gaussian(splits[0], (EVENTS, E_IN), 1, 6.0, ((0, 16),))
    domain_keys = jax.random.split(jax.random.fold_in(splits[1], 1), EVENTS // EV_DEV)
    domain_turns = jax.random.permutation(jax.random.fold_in(splits[1], 3), EVENTS // EV_DEV)
    domain = jax.vmap(lambda own, number: deal_out(jax.random.fold_in(splits[1], 2), own, number, EV_DEV, DOM, 1, CAP, 2))(domain_keys, domain_turns).reshape((EVENTS, 1))
    frozen = draw_frozen(jax.random.fold_in(splits[19], 71), 0)
    labels = touch_ends(jax.random.randint(splits[3], (EVENTS,), 0, 2), jax.random.fold_in(splits[3], 1), 0, 1).astype(jnp.int32)
    proj_w = gaussian(splits[4], (E_IN, D), E_IN ** -0.5, 0.25, ((1, 32),))
    proj_b = gaussian(splits[5], (D,), 0.1, 0.625, ((0, 32),))
    w_in = gaussian(splits[6], (EXPERTS, D, H), D ** -0.5, 0.25, ((1, 16), (2, 2)))
    in_bias = gaussian(splits[7], (EXPERTS, H), 0.1, 0.625, ((1, 32),))
    w_out = gaussian(splits[8], (EXPERTS, H, D), H ** -0.5, 0.1875, ((1, 2), (2, 16)))
    out_bias = gaussian(splits[9], (EXPERTS, D), 0.1, 0.625, ((1, 32),))
    ln_gain = jnp.clip(1.0 + 0.1 * jax.random.normal(splits[10], (EXPERTS, D), jnp.float32), 0.5, 1.5).astype(jnp.bfloat16)
    ln_shift = gaussian(splits[11], (EXPERTS, D), 0.1, 0.625, ((1, 32),))
    gate_top = gaussian(splits[12], (DOM, D, 2), 0.033, 0.1875, ((1, 32),))
    gate_shared = gaussian(splits[13], (DOM, D, S), 0.033, 0.1875, ((1, 32),))
    gate_domain = gaussian(splits[14], (DOM, D, K), 0.033, 0.1875, ((1, 32),))
    tower_w = gaussian(splits[15], (DOM, D, TW), D ** -0.5, 0.25, ((1, 32),))
    tower_b = gaussian(splits[16], (DOM, TW), 0.1, 0.625, ((1, 32),))
    tower_out = gaussian(splits[17], (DOM, TW), 0.125, 0.75, ((1, 32),))
    tower_out_b = gaussian(splits[18], (DOM,), 0.5, 3.0)
    return dict(embeds=embeds, domain=domain, frozen=frozen, labels=labels, proj_w=proj_w, proj_b=proj_b, w_in=w_in, in_bias=in_bias, w_out=w_out, out_bias=out_bias, ln_gain=ln_gain, ln_shift=ln_shift, gate_top=gate_top, gate_shared=gate_shared, gate_domain=gate_domain, tower_w=tower_w, tower_b=tower_b, tower_out=tower_out, tower_out_b=tower_out_b)


EPS = 1e-05
HIGHEST = lax.Precision.HIGHEST
FROZEN_SHARE = 0.25

@jax.custom_vjp
def low(v):
    return lax.optimization_barrier(v.astype(jnp.bfloat16)).astype(jnp.float32)

@jax.custom_vjp
def low_back(v):
    return v

def low_keep(v):
    return (low(v), None)

def low_pass(kept, grad):
    return (grad,)

def back_keep(v):
    return (v, None)

def back_low(kept, grad):
    return (low(grad),)
low.defvjp(low_keep, low_pass)
low_back.defvjp(back_keep, back_low)

def smooth(values):
    return jax.nn.gelu(values, approximate=True)

def layer_norm(values, scale_gain, shift_bias):
    centre = lax.optimization_barrier(jnp.mean(values, axis=-1, keepdims=True))
    centred = values - centre
    spread = lax.optimization_barrier(jnp.mean(centred * centred, axis=-1, keepdims=True))
    return centred * lax.rsqrt(spread + EPS) * scale_gain + shift_bias

def domain_pick(onehot, per_domain):
    return jnp.einsum('rd,rdc->rc', onehot, per_domain, precision=HIGHEST)

def forward(params, inputs, onehot, targets, loss_weight):
    proj_w, proj_b, w_in, in_bias, w_out, out_bias, ln_gain, ln_shift, gate_top, gate_shared, gate_domain, tower_w, tower_b, tower_out, tower_out_b = params
    linear = low_back(jnp.dot(inputs, proj_w, precision=HIGHEST))
    mixed_in = linear + proj_b
    mixed_low = low(mixed_in)
    pre_act = low_back(jnp.einsum('rf,efh->erh', mixed_low, w_in, precision=HIGHEST) + in_bias[:, None, :])
    hidden = low(smooth(pre_act))
    expert_sum = low_back(jnp.einsum('erh,ehf->erf', hidden, w_out, precision=HIGHEST)) + out_bias[:, None, :]
    experts = layer_norm(expert_sum, ln_gain[:, None, :], ln_shift[:, None, :])
    top_prob = jax.nn.softmax(domain_pick(onehot, jnp.einsum('rf,dfc->rdc', mixed_low, gate_top, precision=HIGHEST)), axis=-1)
    shared_prob = jax.nn.softmax(domain_pick(onehot, jnp.einsum('rf,dfc->rdc', mixed_low, gate_shared, precision=HIGHEST)), axis=-1)
    domain_prob = jax.nn.softmax(domain_pick(onehot, jnp.einsum('rf,dfc->rdc', mixed_low, gate_domain, precision=HIGHEST)), axis=-1)
    shared_coef = top_prob[:, 0:1] * shared_prob
    domain_coef = top_prob[:, 1:2] * domain_prob
    domain_experts = experts[S:].reshape(DOM, K, experts.shape[1], D)
    mixture = jnp.einsum('rs,srf->rf', shared_coef, experts[:S], precision=HIGHEST)
    mixture = mixture + jnp.einsum('rd,rk,dkrf->rf', onehot, domain_coef, domain_experts, precision=HIGHEST)
    block_out = mixed_in + mixture
    block_low = low(block_out)
    tower_pre = low_back(jnp.einsum('rf,dfc->rdc', block_low, tower_w, precision=HIGHEST)) + tower_b[None]
    logit_all = jnp.einsum('rdc,dc->rd', smooth(tower_pre), tower_out, precision=HIGHEST) + tower_out_b[None]
    logits = lax.optimization_barrier(jnp.sum(onehot * logit_all, axis=1))
    losses = loss_weight * (jax.nn.softplus(logits) - targets * logits)
    return (jnp.sum(losses), jax.nn.sigmoid(logits))

def reference(embeds, domain, frozen, labels, proj_w, proj_b, w_in, in_bias, w_out, out_bias, ln_gain, ln_shift, gate_top, gate_shared, gate_domain, tower_w, tower_b, tower_out, tower_out_b):
    params = tuple((member.astype(jnp.float32) for member in (proj_w, proj_b, w_in, in_bias, w_out, out_bias, ln_gain, ln_shift, gate_top, gate_shared, gate_domain, tower_w, tower_b, tower_out, tower_out_b)))
    total_rows = embeds.shape[0]
    block_rows = math.gcd(total_rows, 2048)
    block_count = total_rows // block_rows
    domain_ids = domain[:, 0]
    onehot_all = (domain_ids[:, None] == jnp.arange(DOM, dtype=jnp.int32)[None, :]).astype(jnp.float32)
    weight_all = 1.0 - (1.0 - FROZEN_SHARE) * lax.optimization_barrier(jnp.sum(onehot_all * frozen.astype(jnp.float32)[None, :], axis=1))
    targets_all = labels.astype(jnp.float32)
    inputs_all = embeds.astype(jnp.float32)

    def one_block(grad_sums, pieces):
        inputs, onehot, targets, loss_weight = pieces

        def closure(weights, values):
            return forward(weights, values, onehot, targets, loss_weight)
        loss_value, pull_back, predicted = jax.vjp(closure, params, inputs, has_aux=True)
        grad_params, grad_inputs = pull_back(jnp.ones_like(loss_value))
        grad_sums = jax.tree.map(lambda first_term, second_term: first_term + second_term, grad_sums, grad_params)
        return (grad_sums, (predicted, grad_inputs.astype(jnp.bfloat16)))
    grad_zeros = jax.tree.map(jnp.zeros_like, params)
    grad_sums, (predicted, grad_inputs) = lax.scan(one_block, grad_zeros, (inputs_all.reshape(block_count, block_rows, -1), onehot_all.reshape(block_count, block_rows, DOM), targets_all.reshape(block_count, block_rows), weight_all.reshape(block_count, block_rows)))
    return (predicted.reshape(total_rows), grad_inputs.reshape(total_rows, -1), grad_sums[0], grad_sums[1], grad_sums[2], grad_sums[3], grad_sums[4], grad_sums[5], grad_sums[6], grad_sums[7], grad_sums[8], grad_sums[9], grad_sums[10], grad_sums[11], grad_sums[12], grad_sums[13], grad_sums[14])
```

```python
import functools
import math

import jax
import jax.numpy as jnp
from jax import lax
from jax.experimental import pallas as pl
from jax.experimental.pallas import tpu as pltpu
from jax.sharding import PartitionSpec as P

D = 512
H = 1024
TW = 256
S = 4
DOM = 4
K = 2
EPS = 1e-05
FROZEN_SHARE = 0.25
TILE = 256
LOCAL = 6
CHUNKS_FORWARD = ((0,), (1, 2), (3, 4), (5,))
CHUNKS_BACKWARD = ((5,), (3, 4), (1, 2), (0,))
VMEM_LIMIT = 56 * 1024 * 1024
PACK = 1792

bf16 = jnp.bfloat16
f32 = jnp.float32


def dims_of(count):
    if count % 4 == 0:
        rest = count // 4
        root = math.isqrt(rest)
        if root * root == rest:
            return (4, root, root)
    return (count, 1, 1)


class Box:
    def __init__(self, count):
        self.count = count
        self.dims = dims_of(count)
        self.strides = (self.dims[1] * self.dims[2], self.dims[2], 1)

    def toward(self, dim, step):
        size, stride = self.dims[dim], self.strides[dim]
        pairs = []
        for chip in range(self.count):
            place = (chip // stride) % size
            pairs.append((chip, chip + ((place + step) % size - place) * stride))
        return pairs

    def send(self, values, dim, step):
        return lax.ppermute(values, "dp", self.toward(dim, step))

    def pieces(self, values, dim):
        size = self.dims[dim]
        return [values] + [self.send(values, dim, size - step) for step in range(1, size)]

    def collect(self, parts, dim):
        size = self.dims[dim]
        total = parts[0].astype(f32)
        for step in range(1, size):
            total = total + self.send(parts[step], dim, step).astype(f32)
        return total

    def others(self):
        me = lax.axis_index("dp")
        ahead, place = 0, 0
        chip = jnp.arange(self.count)
        weights = (1, self.dims[0], self.dims[0] * self.dims[1])
        for size, stride, weight in zip(self.dims, self.strides, weights):
            mine = (me // stride) % size
            ahead = ahead + ((mine + (chip // weight) % size) % size) * stride
            place = place + (((chip // stride) % size - mine) % size) * weight
        return ahead, place


def swap_cores(values):
    return lax.ppermute(values, "tensor", [(0, 1), (1, 0)])


def in_order(core, own, other, axis):
    return jnp.where(
        core == 0,
        jnp.concatenate([own, other], axis),
        jnp.concatenate([other, own], axis),
    )


def gelu_parts(v):
    inner = math.sqrt(2.0 / math.pi)
    square = v * v
    th = jnp.tanh(v * (inner + inner * 0.044715 * square))
    half = 0.5 * (1.0 + th)
    act = v * half
    slope = half + 0.5 * v * (1.0 - th * th) * (inner + 3.0 * inner * 0.044715 * square)
    return act, slope


def nt(a, b):
    return lax.dot_general(a, b, (((1,), (1,)), ((), ())), preferred_element_type=f32)


def tn(a, b):
    return lax.dot_general(a, b, (((0,), (0,)), ((), ())), preferred_element_type=f32)


def nn(a, b):
    return jnp.dot(a, b, preferred_element_type=f32)


def tile_range(expert, bounds, rows):
    if expert < 2:
        return 0, rows // TILE
    low = bounds[expert - 2]
    high = bounds[DOM + expert - 2]
    return low // TILE, jnp.where(high > low, (high + TILE - 1) // TILE, low // TILE)


def forward_kernel(experts, bounds, x_ref, wi_ref, wo_ref, bi_ref, vec_ref, coef_ref, mix_ref, norm_ref, stat_ref):
    rows = x_ref.shape[0]
    mix_ref[...] = jnp.zeros_like(mix_ref)
    for place, expert in enumerate(experts):
        bias_in = bi_ref[expert : expert + 1, :]
        bias_out = vec_ref[expert : expert + 1, :]
        gain = vec_ref[LOCAL + expert : LOCAL + expert + 1, :]
        shift = vec_ref[2 * LOCAL + expert : 2 * LOCAL + expert + 1, :]

        def tile(index, _, place=place, expert=expert, bias_in=bias_in, bias_out=bias_out, gain=gain, shift=shift):
            span = pl.ds(pl.multiple_of(index * TILE, TILE), TILE)
            pre = nn(x_ref[span, :], wi_ref[place]) + bias_in
            act, _ = gelu_parts(pre)
            out = nt(act.astype(bf16), wo_ref[place]) + bias_out
            centre = jnp.mean(out, axis=1, keepdims=True)
            centred = out - centre
            scale = lax.rsqrt(jnp.mean(centred * centred, axis=1, keepdims=True) + EPS)
            norm = centred * scale
            norm_ref[place, span, :] = norm.astype(bf16)
            stat_ref[span, place : place + 1] = scale
            mix_ref[span, :] += coef_ref[span, expert : expert + 1] * (norm * gain + shift)
            return 0

        low, high = tile_range(expert, bounds, rows)
        lax.fori_loop(low, high, tile, 0)


def backward_kernel(
    experts, bounds, x_ref, gb_ref, wi_ref, wo_ref, bi_ref, vec_ref, coef_ref, *refs
):
    count = len(experts)
    norm_refs, stat_refs = refs[:count], refs[count : 2 * count]
    dwi_ref, dwo_ref, dvec_ref, dbi_ref, dcoef_ref, back_ref, wi_sum, wo_sum = refs[2 * count :]
    places = tuple(p for _, p in experts)
    rows = x_ref.shape[0]
    back_ref[...] = jnp.zeros_like(back_ref)
    dvec_ref[...] = jnp.zeros_like(dvec_ref)
    dbi_ref[...] = jnp.zeros_like(dbi_ref)
    for place, (expert, held) in enumerate(experts):
        bias_in = bi_ref[expert : expert + 1, :]
        gain = vec_ref[LOCAL + expert : LOCAL + expert + 1, :]
        shift = vec_ref[2 * LOCAL + expert : 2 * LOCAL + expert + 1, :]
        wi_sum[...] = jnp.zeros_like(wi_sum)
        wo_sum[...] = jnp.zeros_like(wo_sum)

        def tile(index, _, place=place, expert=expert, held=held, bias_in=bias_in, gain=gain, shift=shift):
            span = pl.ds(pl.multiple_of(index * TILE, TILE), TILE)
            x = x_ref[span, :]
            norm = norm_refs[place][0, span, :].astype(f32)
            scale = stat_refs[place][span, held : held + 1]
            grad_block = gb_ref[span, :].astype(f32)
            dcoef_ref[span, place : place + 1] = jnp.sum(
                grad_block * (norm * gain + shift), axis=1, keepdims=True
            )
            grad_exp = coef_ref[span, expert : expert + 1] * grad_block
            scaled = grad_exp * norm
            dvec_ref[place, 1:2, :] += jnp.sum(scaled, axis=0, keepdims=True)
            dvec_ref[place, 2:3, :] += jnp.sum(grad_exp, axis=0, keepdims=True)
            dx = grad_exp * gain
            first = jnp.mean(dx, axis=1, keepdims=True)
            second = jnp.mean(dx * norm, axis=1, keepdims=True)
            grad_sum = scale * (dx - first - norm * second)
            dvec_ref[place, 0:1, :] += jnp.sum(grad_sum, axis=0, keepdims=True)
            grad_low = grad_sum.astype(bf16)
            pre = nn(x, wi_ref[place]) + bias_in
            act, slope = gelu_parts(pre)
            wo_sum[...] += tn(grad_low, act.astype(bf16))
            pre_low = (nn(grad_low, wo_ref[place]) * slope).astype(bf16)
            dbi_ref[place, 0:1, :] += jnp.sum(pre_low.astype(f32), axis=0, keepdims=True)
            wi_sum[...] += tn(x, pre_low)
            back_ref[span, :] += nt(pre_low, wi_ref[place])
            return 0

        low, high = tile_range(expert, bounds, rows)
        lax.fori_loop(low, high, tile, 0)
        dwi_ref[place] = wi_sum[...].astype(bf16)
        dwo_ref[place] = wo_sum[...].astype(bf16)


def tower_kernel(base_ref, mix_ref, row_ref, tw_ref, tv_ref, pred_ref, gb_ref, dw_ref, dv_ref):
    rows = base_ref.shape[0]
    dw_ref[...] = jnp.zeros_like(dw_ref)
    dv_ref[...] = jnp.zeros_like(dv_ref)
    bias = tv_ref[0:1, :]
    head = tv_ref[1:2, :]

    def tile(index, _):
        span = pl.ds(pl.multiple_of(index * TILE, TILE), TILE)
        block = (base_ref[span, :] + mix_ref[span, :].astype(f32)).astype(bf16)
        pre = nn(block, tw_ref[...]) + bias
        act, slope = gelu_parts(pre)
        group = lax.broadcasted_iota(jnp.int32, pre.shape, 1) // TW
        mine = group == row_ref[span, 0:1].astype(jnp.int32)
        act = jnp.where(mine, act, 0.0)
        logit = jnp.sum(act * head, axis=1, keepdims=True) + row_ref[span, 3:4]
        predicted = 1.0 / (1.0 + jnp.exp(-logit))
        grad_logit = row_ref[span, 2:3] * (predicted - row_ref[span, 1:2])
        pred_ref[span, 0:1] = predicted
        pred_ref[span, 1:2] = grad_logit
        dv_ref[1:2, :] += jnp.sum(grad_logit * act, axis=0, keepdims=True)
        grad_pre = jnp.where(mine, grad_logit * head * slope, 0.0)
        dv_ref[0:1, :] += jnp.sum(grad_pre, axis=0, keepdims=True)
        grad_low = grad_pre.astype(bf16)
        dw_ref[...] += tn(block, grad_low)
        gb_ref[span, :] = nt(grad_low, tw_ref[...])
        return 0

    lax.fori_loop(0, rows // TILE, tile, 0)


def params():
    return pltpu.CompilerParams(vmem_limit_bytes=VMEM_LIMIT)


def whole(count):
    return [pl.BlockSpec(memory_space=pltpu.VMEM)] * count


def call_forward(experts, bounds, x, wi, wo, bi, vec, coef):
    rows, count = x.shape[0], len(experts)
    return pl.pallas_call(
        functools.partial(forward_kernel, experts),
        out_shape=(
            jax.ShapeDtypeStruct((rows, D), f32),
            jax.ShapeDtypeStruct((count, rows, D), bf16),
            jax.ShapeDtypeStruct((rows, 128), f32),
        ),
        in_specs=[pl.BlockSpec(memory_space=pltpu.SMEM)] + whole(6),
        out_specs=tuple(whole(3)),
        compiler_params=params(),
        cost_estimate=pl.CostEstimate(
            flops=4 * count * rows * D * H // 2, bytes_accessed=10_000_000, transcendentals=count * rows * H // 2
        ),
        name="experts_forward",
    )(bounds, x, wi, wo, bi, vec, coef)


def call_backward(experts, bounds, x, gb, wi, wo, bi, vec, coef, norms, stats):
    rows, count = x.shape[0], len(experts)
    return pl.pallas_call(
        functools.partial(backward_kernel, experts),
        out_shape=(
            jax.ShapeDtypeStruct((count, D, H), bf16),
            jax.ShapeDtypeStruct((count, D, H), bf16),
            jax.ShapeDtypeStruct((count, 8, D), f32),
            jax.ShapeDtypeStruct((count, 8, H), f32),
            jax.ShapeDtypeStruct((rows, 128), f32),
            jax.ShapeDtypeStruct((rows, D), f32),
        ),
        in_specs=[pl.BlockSpec(memory_space=pltpu.SMEM)] + whole(7 + 2 * count),
        out_specs=tuple(whole(6)),
        scratch_shapes=[pltpu.VMEM((D, H), f32), pltpu.VMEM((D, H), f32)],
        compiler_params=params(),
        cost_estimate=pl.CostEstimate(
            flops=10 * count * rows * D * H // 2, bytes_accessed=20_000_000, transcendentals=count * rows * H // 2
        ),
        name="experts_backward",
    )(bounds, x, gb, wi, wo, bi, vec, coef, *norms, *stats)


def call_tower(base, mix, row_info, tower, tower_vec):
    rows = base.shape[0]
    return pl.pallas_call(
        tower_kernel,
        out_shape=(
            jax.ShapeDtypeStruct((rows, 128), f32),
            jax.ShapeDtypeStruct((rows, D), f32),
            jax.ShapeDtypeStruct((D, DOM * TW), f32),
            jax.ShapeDtypeStruct((8, DOM * TW), f32),
        ),
        in_specs=whole(5),
        out_specs=tuple(whole(4)),
        compiler_params=params(),
        cost_estimate=pl.CostEstimate(
            flops=6 * rows * D * DOM * TW, bytes_accessed=10_000_000, transcendentals=rows * DOM * TW
        ),
        name="towers",
    )(base, mix, row_info, tower, tower_vec)


def own_experts(per_expert, core):
    tail = per_expert.shape[1:]
    shared = per_expert[:S].reshape((2, 2) + tail)
    domain = per_expert[S:].reshape((DOM, K) + tail)

    def of(which):
        return jnp.concatenate(
            [
                lax.dynamic_index_in_dim(shared, which, 0, keepdims=False),
                lax.dynamic_index_in_dim(domain, which, 1, keepdims=False),
            ]
        )

    return of(core), of(1 - core)


def all_experts(own, other, core):
    first = jnp.where(core == 0, own, other)
    second = jnp.where(core == 0, other, own)
    tail = own.shape[1:]
    shared = jnp.concatenate([first[:2], second[:2]])
    domain = jnp.stack([first[2:], second[2:]], axis=1).reshape((DOM * K,) + tail)
    return jnp.concatenate([shared, domain])


def spread_experts(own, core):
    return all_experts(own, jnp.zeros_like(own), core)


def softmax_back(probability, grad_probs):
    return probability * (grad_probs - jnp.sum(probability * grad_probs, axis=0, keepdims=True))


def per_device(
    box,
    embeds,
    domain,
    frozen,
    labels,
    proj_w,
    proj_b,
    w_in,
    in_bias,
    w_out,
    out_bias,
    ln_gain,
    ln_shift,
    gate_top,
    gate_shared,
    gate_domain,
    tower_w,
    tower_b,
    tower_out,
    tower_out_b,
):
    core = lax.axis_index("tensor")
    places = box.count
    rows = embeds.shape[0]
    half_rows = rows // 2
    width = proj_w.shape[1]
    e_in = proj_w.shape[0]
    ahead, place_of = box.others()

    pack = jnp.concatenate(
        [
            proj_w.T,
            jnp.swapaxes(tower_w, 0, 1).reshape(width, DOM * TW),
            jnp.swapaxes(gate_top, 0, 1).reshape(width, 2 * DOM),
            jnp.swapaxes(gate_shared, 0, 1).reshape(width, S * DOM),
            jnp.swapaxes(gate_domain, 0, 1).reshape(width, K * DOM),
            jnp.concatenate([out_bias, ln_gain, ln_shift]).T,
            proj_b[:, None],
            in_bias.reshape(width, 24),
            jnp.concatenate([tower_b, tower_out]).reshape(width, 4),
        ],
        axis=1,
    )
    pack = jnp.pad(pack, ((0, 0), (0, PACK - pack.shape[1])))
    for dim in range(3):
        pack = jnp.concatenate(box.pieces(pack, dim), axis=0)
    pack = pack.reshape(places, 1, width, PACK)
    pack = in_order(core, pack, swap_cores(pack), 1)
    small = pack.reshape(D, PACK)
    proj_t = small[:, :e_in]
    at = e_in
    tower = small[:, at : at + DOM * TW]
    at += DOM * TW
    gates = small[:, at : at + 32]
    at += 32
    vectors = small[:, at : at + 37].astype(f32).T
    at += 37
    bias_blocks = jnp.take(pack[:, :, :, at : at + 28].astype(f32), place_of, axis=0)
    in_bias_all = (
        bias_blocks[..., :24]
        .reshape(places * 2, 12, width * 2)
        .transpose(1, 0, 2)
        .reshape(12, H)
    )
    tower_vec = (
        bias_blocks[..., 24:]
        .reshape(places * 2, 2, DOM, width // 2)
        .transpose(1, 2, 0, 3)
        .reshape(2, DOM * TW)
    )
    tower_vec = jnp.pad(tower_vec, ((0, 6), (0, 0)))
    vec_own = jnp.concatenate([own_experts(vectors[i * 12 : i * 12 + 12], core)[0] for i in range(3)])
    vec_own = jnp.pad(vec_own, ((0, 6), (0, 0)))
    proj_bias = vectors[36]
    bi_own = jnp.pad(own_experts(in_bias_all, core)[0], ((0, 2), (0, 0)))

    wi_own, wi_other = own_experts(w_in, core)
    wo_own, wo_other = own_experts(jnp.swapaxes(w_out, 1, 2), core)
    swapped = swap_cores(jnp.stack([wi_other, wo_other]))
    shards = in_order(core, jnp.stack([wi_own, wo_own]), swapped, 3)

    def gather(experts, after):
        low, high = experts[0], experts[-1] + 1
        shard = shards[:, low:high]
        if after is not None:
            shard = lax.optimization_barrier((shard, after))[0]
        count = high - low
        block = jnp.stack(box.pieces(shard, 0), axis=2)
        wi, wo = block[0], block[1]
        wi_y = jnp.stack(box.pieces(wi, 1), axis=1)
        wo_x = jnp.stack(box.pieces(wo, 2), axis=1)
        wi_full = jnp.stack(box.pieces(wi_y, 2), axis=1)
        wo_full = jnp.stack(box.pieces(wo_x, 1), axis=2)
        return wi_full.reshape(count, D, H), wo_full.reshape(count, D, H), wi_y

    gathered = []
    behind = [None, None]
    for experts in CHUNKS_FORWARD:
        wi, wo, mark = gather(experts, behind[-2])
        behind.append(mark)
        gathered.append((wi, wo))

    ids = domain[:, 0]
    onehot_t = (ids[None, :] == jnp.arange(DOM, dtype=jnp.int32)[:, None]).astype(f32)
    counts = jnp.sum(onehot_t, axis=1).astype(jnp.int32)
    ends = jnp.cumsum(counts)
    starts = ends - counts
    rank = jnp.cumsum(onehot_t, axis=1)
    position = jnp.sum(onehot_t * (rank + starts[:, None].astype(f32)), axis=0).astype(jnp.int32) - 1
    order = (position[None, :] == jnp.arange(rows, dtype=jnp.int32)[:, None])
    order_low = order.astype(bf16)
    bounds = jnp.concatenate([starts, ends])
    slots = jnp.arange(rows, dtype=jnp.int32)
    sorted_t = ((slots[None, :] >= starts[:, None]) & (slots[None, :] < ends[:, None])).astype(f32)
    events = jnp.dot(order_low, embeds, preferred_element_type=f32).astype(bf16)
    targets = jnp.sum(jnp.where(order, labels.astype(f32)[None, :], 0.0), axis=1)

    mixed_in = (
        lax.dot_general(events, proj_t, (((1,), (1,)), ((), ())), preferred_element_type=f32)
        + proj_bias[None, :]
    )
    mixed_low = mixed_in.astype(bf16)

    logits = lax.dot_general(
        gates, mixed_low, (((0,), (1,)), ((), ())), preferred_element_type=f32
    )


    top_prob = jax.nn.softmax(pick_gate(logits, sorted_t, 0, 2), axis=0)
    shared_prob = jax.nn.softmax(pick_gate(logits, sorted_t, 1, 4), axis=0)
    domain_prob = jax.nn.softmax(pick_gate(logits, sorted_t, 2, 2), axis=0)
    shared_coef = lax.dynamic_slice_in_dim(top_prob[0:1] * shared_prob, 2 * core, 2, 0)
    domain_coef = lax.dynamic_slice_in_dim(top_prob[1:2] * domain_prob, core, 1, 0) * sorted_t
    coef = jnp.pad(jnp.concatenate([shared_coef, domain_coef]).T, ((0, 0), (0, 128 - LOCAL)))

    mixes, kept = [], {}
    for experts, (wi, wo) in zip(CHUNKS_FORWARD, gathered):
        mix, norm, stat = call_forward(experts, bounds, mixed_low, wi, wo, bi_own, vec_own, coef)
        mixes.append(mix)
        for place, expert in enumerate(experts):
            kept[expert] = (norm[place : place + 1], stat, place, wi, wo)

    def half(values, which):
        return lax.dynamic_slice_in_dim(values, which * half_rows, half_rows, 0)

    mixture = functools.reduce(jnp.add, mixes)
    arrived = swap_cores(half(mixture, 1 - core).astype(bf16))
    base = half(mixed_in, core) + half(mixture, core)
    frozen_f = frozen.astype(f32)
    weight = 1.0 - (1.0 - FROZEN_SHARE) * jnp.sum(sorted_t * frozen_f[:, None], axis=0)
    row_bias = jnp.sum(sorted_t * tower_out_b.astype(f32)[:, None], axis=0)
    row_domain = jnp.sum(sorted_t * jnp.arange(DOM, dtype=f32)[:, None], axis=0)
    row_info = jnp.pad(jnp.stack([row_domain, targets, weight, row_bias]).T, ((0, 0), (0, 124)))
    row_out, grad_block, d_tower, d_tower_vec = call_tower(
        base, arrived, half(row_info, core), tower, tower_vec
    )
    grad_block_low = grad_block.astype(bf16)
    grad_all = in_order(core, grad_block_low, swap_cores(grad_block_low), 0)

    backs, d_vec, d_bias, d_coef, shard_in, shard_out = [], {}, {}, {}, {}, {}
    for experts in CHUNKS_BACKWARD:
        count = len(experts)
        wi, wo = kept[experts[0]][3:]
        dwi, dwo, dvec, dbi, dcoef, back = call_backward(
            tuple((e, kept[e][2]) for e in experts),
            bounds,
            mixed_low,
            grad_all,
            wi,
            wo,
            bi_own,
            vec_own,
            coef,
            [kept[e][0] for e in experts],
            [kept[e][1] for e in experts],
        )
        backs.append(back)
        box_shape = (count,) + box.dims[::-1] + (2 * width, H)
        dwi, dwo = dwi.reshape(box_shape), dwo.reshape(box_shape)
        nz, ny, nx = box.dims
        part_in = box.collect([dwi[:, s] for s in range(nx)], 2).astype(bf16)
        part_out = box.collect([dwo[:, :, s] for s in range(ny)], 1).astype(bf16)
        part_in = box.collect([part_in[:, s] for s in range(ny)], 1).astype(bf16)
        part_out = box.collect([part_out[:, s] for s in range(nx)], 2).astype(bf16)
        both = jnp.stack([part_in, part_out])
        done = box.collect([both[:, :, s] for s in range(nz)], 0)
        for place, expert in enumerate(experts):
            d_vec[expert], d_bias[expert] = dvec[place], dbi[place, 0]
            d_coef[expert] = dcoef[:, place]
            shard_in[expert], shard_out[expert] = done[0, place], done[1, place]

    back = functools.reduce(jnp.add, backs)
    back_arrived = swap_cores(half(back, 1 - core).astype(bf16))
    coef_own = jnp.stack(
        [d_coef[0], d_coef[1], functools.reduce(jnp.add, [jnp.where(sorted_t[d] > 0.5, d_coef[2 + d], 0.0) for d in range(DOM)])]
    )
    coef_own = jnp.pad(coef_own, ((0, 5), (0, 0)))

    def half_t(values, which):
        return lax.dynamic_slice_in_dim(values, which * half_rows, half_rows, 1)

    mine_coef = half_t(coef_own, core)
    other_coef = swap_cores(half_t(coef_own, 1 - core))
    coef_first = jnp.where(core == 0, mine_coef, other_coef)
    coef_second = jnp.where(core == 0, other_coef, mine_coef)
    d_shared = jnp.concatenate([coef_first[:2], coef_second[:2]])
    d_domain = jnp.concatenate([coef_first[2:3], coef_second[2:3]])
    top_half, shared_half, domain_half = (
        half_t(top_prob, core),
        half_t(shared_prob, core),
        half_t(domain_prob, core),
    )
    sorted_half = half_t(sorted_t, core)
    d_top = jnp.concatenate(
        [
            jnp.sum(d_shared * shared_half, axis=0, keepdims=True),
            jnp.sum(d_domain * domain_half, axis=0, keepdims=True),
        ]
    )
    logit_grads = (
        softmax_back(top_half, d_top),
        softmax_back(shared_half, d_shared * top_half[0:1]),
        softmax_back(domain_half, d_domain * top_half[1:2]),
    )
    spread = jnp.concatenate(
        [sorted_half[d : d + 1] * logit_grads[0] for d in range(DOM)]
        + [sorted_half[d : d + 1] * logit_grads[1] for d in range(DOM)]
        + [sorted_half[d : d + 1] * logit_grads[2] for d in range(DOM)]
    ).astype(bf16)
    mixed_half = half(mixed_low, core)
    d_gates = lax.dot_general(mixed_half, spread, (((0,), (1,)), ((), ())), preferred_element_type=f32)
    gate_back = lax.dot_general(spread, gates, (((0,), (1,)), ((), ())), preferred_element_type=f32)
    grad_mixed = grad_block + half(back, core) + back_arrived.astype(f32) + gate_back
    d_proj_bias = jnp.sum(grad_mixed, axis=0)
    mixed_grad_low = grad_mixed.astype(bf16)
    d_proj_t = lax.dot_general(
        mixed_grad_low, half(events, core), (((0,), (0,)), ((), ())), preferred_element_type=f32
    )
    grad_events = jnp.dot(mixed_grad_low, proj_t, preferred_element_type=f32).astype(bf16)
    grad_events = in_order(core, grad_events, swap_cores(grad_events), 0)
    grad_embeds = lax.dot_general(
        order_low, grad_events, (((0,), (0,)), ((), ())), preferred_element_type=f32
    ).astype(bf16)
    pred_half = jnp.broadcast_to(row_out[None, :, 0], (8, half_rows))
    pred_sorted = in_order(core, pred_half, swap_cores(pred_half), 1)[0]
    predictions = jnp.sum(jnp.where(order, pred_sorted[:, None], 0.0), axis=0)

    d_vectors = jnp.concatenate(
        [
            spread_experts(jnp.stack([d_vec[e][i] for e in range(LOCAL)]), core)
            for i in range(3)
        ]
    )
    d_vectors = jnp.concatenate([d_vectors, d_proj_bias[None]]).T
    d_in_bias = spread_experts(jnp.stack([d_bias[e] for e in range(LOCAL)]), core)
    d_in_blocks = d_in_bias.reshape(12, places, 2, 2 * width).transpose(1, 2, 0, 3)
    d_tower_blocks = (
        d_tower_vec[:2].reshape(2, DOM, places, 2, width // 2).transpose(2, 3, 0, 1, 4)
    )
    d_blocks = jnp.concatenate(
        [
            d_in_blocks.reshape(places, 2, width, 24),
            d_tower_blocks.reshape(places, 2, width, 4),
        ],
        axis=3,
    )
    d_blocks = jnp.take(d_blocks, ahead, axis=0).reshape(D, 28)
    d_small = jnp.concatenate([d_proj_t, d_tower, d_gates, d_vectors, d_blocks], axis=1)
    d_small = jnp.pad(d_small, ((0, 0), (0, PACK - d_small.shape[1])))
    d_small = d_small.reshape(places, 2, width, PACK)
    d_mine = lax.dynamic_index_in_dim(d_small, core, 1, keepdims=False)
    d_other = lax.dynamic_index_in_dim(d_small, 1 - core, 1, keepdims=False).astype(bf16)
    d_mine = (d_mine + swap_cores(d_other).astype(f32)).astype(bf16)
    d_mine = d_mine.reshape(box.dims[::-1] + (width, PACK))
    d_mine = box.collect([d_mine[s] for s in range(box.dims[2])], 2).astype(bf16)
    d_mine = box.collect([d_mine[s] for s in range(box.dims[1])], 1).astype(bf16)
    d_mine = box.collect([d_mine[s] for s in range(box.dims[0])], 0)

    grad_logit = row_out[:, 1]
    d_logit_bias = jnp.sum(sorted_half * grad_logit[None, :], axis=1)
    d_logit_bias = jnp.pad(d_logit_bias[None, :], ((0, 7), (0, 124)))
    d_logit_bias = (d_logit_bias + swap_cores(d_logit_bias))[None]
    for dim in range(3):
        d_logit_bias = jnp.concatenate(box.pieces(d_logit_bias, dim), axis=0)
    d_logit_bias = jnp.sum(jnp.take(d_logit_bias, place_of, axis=0), axis=0)[0, :DOM]

    done = jnp.stack(
        [
            jnp.stack([shard_in[e] for e in range(LOCAL)]),
            jnp.stack([shard_out[e] for e in range(LOCAL)]),
        ]
    )
    keep = lax.dynamic_slice_in_dim(done, core * (H // 2), H // 2, 3)
    give = lax.dynamic_slice_in_dim(done, (1 - core) * (H // 2), H // 2, 3)
    got = swap_cores(give)
    grad_w_in = all_experts(keep[0], got[0], core)
    grad_w_out = jnp.swapaxes(all_experts(keep[1], got[1], core), 1, 2)

    at = e_in
    grad_proj_w = d_mine[:, :at].T
    grad_tower_w = jnp.swapaxes(d_mine[:, at : at + DOM * TW].reshape(width, DOM, TW), 0, 1)
    at += DOM * TW
    d_gate = d_mine[:, at : at + 32]
    grad_gate_top = jnp.swapaxes(d_gate[:, :8].reshape(width, DOM, 2), 0, 1)
    grad_gate_shared = jnp.swapaxes(d_gate[:, 8:24].reshape(width, DOM, S), 0, 1)
    grad_gate_domain = jnp.swapaxes(d_gate[:, 24:].reshape(width, DOM, K), 0, 1)
    at += 32
    d_vecs = d_mine[:, at : at + 37].T
    at += 37
    grad_in_bias = d_mine[:, at : at + 24].reshape(12, 2 * width)
    d_tv = d_mine[:, at + 24 : at + 28].reshape(2, DOM, width // 2)
    return (
        predictions,
        grad_embeds,
        grad_proj_w,
        d_vecs[36],
        grad_w_in,
        grad_in_bias,
        grad_w_out,
        d_vecs[:12],
        d_vecs[12:24],
        d_vecs[24:36],
        grad_gate_top,
        grad_gate_shared,
        grad_gate_domain,
        grad_tower_w,
        d_tv[0],
        d_tv[1],
        d_logit_bias,
    )


def pick_gate(logits, sorted_t, which, size):
    low = (0, 2 * DOM, (2 + S) * DOM)[which]
    return functools.reduce(
        jnp.add,
        [sorted_t[d : d + 1] * logits[low + d * size : low + (d + 1) * size] for d in range(DOM)],
    )


def solution(mesh):
    both = ("dp", "tensor")
    in_specs = (
        P("dp", None),
        P("dp", None),
        P(),
        P("dp"),
        P(None, both),
        P(both),
        P(None, "dp", "tensor"),
        P(None, both),
        P(None, "tensor", "dp"),
        P(None, both),
        P(None, both),
        P(None, both),
        P(None, both, None),
        P(None, both, None),
        P(None, both, None),
        P(None, both, None),
        P(None, both),
        P(None, both),
        P(),
    )
    out_specs = (
        P("dp"),
        P("dp", None),
        P(None, both),
        P(both),
        P(None, "dp", "tensor"),
        P(None, both),
        P(None, "tensor", "dp"),
        P(None, both),
        P(None, both),
        P(None, both),
        P(None, both, None),
        P(None, both, None),
        P(None, both, None),
        P(None, both, None),
        P(None, both),
        P(None, both),
        P(),
    )
    return jax.shard_map(
        functools.partial(per_device, Box(mesh.shape["dp"])),
        mesh=mesh,
        in_specs=in_specs,
        out_specs=out_specs,
        check_vma=False,
    )
```

```python
import functools
import math

import jax
import jax.numpy as jnp
from jax import lax
from jax.experimental import pallas as pl
from jax.experimental.pallas import tpu as pltpu
from jax.sharding import PartitionSpec as P

D = 512
H = 1024
HALF = H // 2
TW = 256
S = 4
DOM = 4
K = 2
EPS = 1e-05
FROZEN_SHARE = 0.25
TILE = 256
LOCAL = 6
CHUNKS = ((5, 0), (4, 1), (3, 2))
VMEM_LIMIT = 48 * 1024 * 1024
PACK = 1792
SETS = (
    tuple(range(2)) + tuple(S + K * d for d in reversed(range(DOM))),
    tuple(range(2, 4)) + tuple(S + K * d + 1 for d in range(DOM)),
)
COEF, SCALE, DCOEF, DOMAIN, LABEL, WEIGHT, BIAS = 0, 6, 12, 18, 19, 20, 21
LOW, HIGH, ROLE, DOMAIN_OF, START, END, CORE = 0, 4, 8, 9, 13, 17, 21

bf16 = jnp.bfloat16
f32 = jnp.float32


def dims_of(count):
    if count % 4 == 0:
        rest = count // 4
        root = math.isqrt(rest)
        if root * root == rest:
            return (4, root, root)
    return (count, 1, 1)


class Box:
    def __init__(self, count):
        first, second, third = dims_of(count)
        self.count = count
        self.dims = (2, first // 2, second, third)
        self.strides = (second * third, 2 * second * third, third, 1)

    def role(self, chip):
        return (chip // self.strides[0]) % 2

    def partner(self, chip):
        return chip + (1 - 2 * self.role(chip)) * self.strides[0]

    def send(self, values, flip=0, z=0, y=0, x=0):
        pairs = []
        for chip in range(self.count):
            to = chip
            for step, size, stride in zip((flip, z, y, x), self.dims, self.strides):
                place = (chip // stride) % size
                to += ((place + step) % size - place) * stride
            pairs.append((chip, to))
        return lax.ppermute(values, "dp", pairs)

    def to_partner(self, values, home):
        pairs = []
        for chip in range(self.count):
            for core in range(2):
                if (core == self.role(chip)) == home:
                    pairs.append((2 * chip + core, 2 * self.partner(chip) + core))
        return lax.ppermute(values, ("dp", "tensor"), pairs)

    def pieces(self, values, dim):
        size = self.dims[("flip", "z", "y", "x").index(dim)]
        return [self.send(values, **{dim: -k}) for k in range(1, size)]

    def hand_out(self, parts, dim):
        return [self.send(part, **{dim: k}) for k, part in enumerate(parts) if k]

    def plane(self):
        _, _, ny, nx = self.dims
        return [(x, y) for x in range(nx) for y in range(ny)][1:]

    def gather_plane(self, values):
        return [values] + [self.send(values, y=-y, x=-x) for x, y in self.plane()]

    def hand_out_plane(self, parts):
        return [self.send(part, y=y, x=x) for part, (x, y) in zip(parts[1:], self.plane())]

    def same_sum(self, values, dim):
        number = ("flip", "z", "y", "x").index(dim)
        size, stride = self.dims[number], self.strides[number]
        found = jnp.stack([values] + self.pieces(values, dim))
        if size > 2:
            mine = (lax.axis_index("dp") // stride) % size
            found = jnp.take(found, (jnp.arange(size) - mine) % size, axis=0)
        return functools.reduce(jnp.add, [found[k] for k in range(size)])

    def others(self):
        me = lax.axis_index("dp")
        chip = jnp.arange(self.count)
        ahead, place, weight = 0, 0, 1
        for dim, (size, stride) in enumerate(zip(self.dims, self.strides)):
            mine = (me // stride) % size if dim else 0
            ahead = ahead + ((mine + (chip // weight) % size) % size) * stride
            place = place + (((chip // stride) % size - mine) % size) * weight
            weight *= size
        return ahead, place


def swap_cores(values):
    return lax.ppermute(values, "tensor", [(0, 1), (1, 0)])


def in_order(which, own, other, axis):
    return jnp.where(
        which == 0,
        jnp.concatenate([own, other], axis),
        jnp.concatenate([other, own], axis),
    )


def step(*values):
    return lax.optimization_barrier(values)


def total(first, arrived):
    return functools.reduce(jnp.add, [a.astype(f32) for a in arrived], first.astype(f32))


def gelu_parts(v):
    inner = math.sqrt(2.0 / math.pi)
    square = v * v
    th = jnp.tanh(v * (inner + inner * 0.044715 * square))
    half = 0.5 * (1.0 + th)
    act = v * half
    slope = half + 0.5 * v * (1.0 - th * th) * (inner + 3.0 * inner * 0.044715 * square)
    return act, slope


def nt(a, b):
    return lax.dot_general(a, b, (((1,), (1,)), ((), ())), preferred_element_type=f32)


def tn(a, b):
    return lax.dot_general(a, b, (((0,), (0,)), ((), ())), preferred_element_type=f32)


def nn(a, b):
    return jnp.dot(a, b, preferred_element_type=f32)


def softmax_rows(v):
    e = jnp.exp(v - jnp.max(v, axis=0, keepdims=True))
    return e / jnp.sum(e, axis=0, keepdims=True)


def prepare_kernel(ints, floats, rows_ref, embeds_ref, proj_ref, gates_ref, vec_ref, ev_ref, x_ref, mix_ref, cols_ref, prob_ref):
    tiles_of_half = pl.num_programs(0) // 2
    index = pl.program_id(0)
    role = ints[ROLE]
    count = rows_ref.shape[1]
    slot = index * TILE + lax.broadcasted_iota(jnp.int32, (TILE, count), 0)
    order = jnp.where(rows_ref[0:1, :].astype(jnp.int32) == slot, 1.0, 0.0).astype(bf16)
    events = nn(order, embeds_ref[...]).astype(bf16)
    ev_ref[...] = events
    mixed = nt(events, proj_ref[...]) + vec_ref[3 * LOCAL : 3 * LOCAL + 1, :]
    low = mixed.astype(bf16)
    x_ref[...] = low
    mix_ref[...] = mixed * jnp.where(index // tiles_of_half == role, 1.0, 0.0)
    logits = jnp.transpose(nn(low, gates_ref[...]))
    place = index * TILE + lax.broadcasted_iota(jnp.int32, (1, TILE), 1)
    picks = [
        jnp.where((place >= ints[START + d]) & (place < ints[END + d]), 1.0, 0.0) for d in range(DOM)
    ]

    def pick(low_row, size):
        return softmax_rows(
            functools.reduce(
                jnp.add,
                [picks[d] * logits[low_row + d * size : low_row + (d + 1) * size] for d in range(DOM)],
            )
        )

    top, shared, domain = pick(0, 2), pick(2 * DOM, S), pick((2 + S) * DOM, K)
    prob_ref[...] = jnp.concatenate([top, shared, domain], axis=0)
    first = role == 0
    own_shared = top[0:1] * jnp.where(first, shared[:2], shared[2:])
    own_domain = top[1:2] * jnp.where(first, domain[0:1], domain[1:2])
    labels = nt(rows_ref[...].astype(bf16), order)
    coef = [own_domain * jnp.where(first, picks[DOM - 1 - d], picks[d]) for d in range(DOM)]
    table = [
        own_shared,
        *coef,
        jnp.zeros((DOMAIN - SCALE, TILE), f32),
        sum(float(d) * picks[d] for d in range(DOM)),
        labels[1:2],
        sum(floats[d] * picks[d] for d in range(DOM)),
        sum(floats[DOM + d] * picks[d] for d in range(DOM)),
        jnp.zeros((128 - BIAS - 1, TILE), f32),
    ]
    cols_ref[...] = jnp.transpose(jnp.concatenate(table, axis=0))


def tile_of(expert, step, ints):
    if expert < 2:
        return step, True
    low, high = ints[LOW + expert - 2], ints[HIGH + expert - 2]
    return jnp.minimum(low + step, jnp.maximum(high - 1, 0)), low + step < high


def with_column(table, column, values):
    lane = lax.broadcasted_iota(jnp.int32, table.shape, 1)
    return jnp.where(lane == column, values, table)


def forward_kernel(
    expert, ints, x_ref, wi_a, wi_b, wo_a, wo_b, bi_ref, vec_ref, cols_in, mix_in, cols_ref, mix_ref, norm_ref
):
    step = pl.program_id(0)
    _, busy = tile_of(expert, step, ints)

    def work():
        x = x_ref[...]
        pre_a = nn(x, wi_a[0]) + bi_ref[expert : expert + 1, :HALF]
        act_a = gelu_parts(pre_a)[0].astype(bf16)
        pre_b = nn(x, wi_b[0]) + bi_ref[expert : expert + 1, HALF:]
        act_b = gelu_parts(pre_b)[0].astype(bf16)
        out = nt(act_a, wo_a[0]) + nt(act_b, wo_b[0]) + vec_ref[expert : expert + 1, :]
        centre = jnp.mean(out, axis=1, keepdims=True)
        centred = out - centre
        scale = lax.rsqrt(jnp.mean(centred * centred, axis=1, keepdims=True) + EPS)
        norm = centred * scale
        norm_ref[...] = norm.astype(bf16)
        cols = cols_in[...]
        cols_ref[...] = with_column(cols, SCALE + expert, scale)
        gain = vec_ref[LOCAL + expert : LOCAL + expert + 1, :]
        shift = vec_ref[2 * LOCAL + expert : 2 * LOCAL + expert + 1, :]
        mix_ref[...] = mix_in[...] + cols[:, COEF + expert : COEF + expert + 1] * (norm * gain + shift)

    if expert < 2:
        work()
    else:
        pl.when(busy)(work)

        @pl.when(jnp.logical_not(busy) & (step == 0))
        def _():
            cols_ref[...] = cols_in[...]
            mix_ref[...] = mix_in[...]


def backward_kernel(
    expert,
    ints,
    x_ref,
    gb_ref,
    norm_ref,
    wi_a,
    wi_b,
    wo_a,
    wo_b,
    bi_ref,
    vec_ref,
    cols_in,
    back_in,
    cols_ref,
    back_ref,
    keep_ref,
    give_ref,
    dvec_ref,
    dbi_ref,
    in_a,
    in_b,
    out_a,
    out_b,
):
    step = pl.program_id(0)
    _, busy = tile_of(expert, step, ints)

    @pl.when(step == 0)
    def _():
        for ref in (in_a, in_b, out_a, out_b, dvec_ref, dbi_ref):
            ref[...] = jnp.zeros_like(ref)
        if expert >= 2:
            cols_ref[...] = cols_in[...]
            back_ref[...] = back_in[...]

    def work():
        x = x_ref[...]
        norm = norm_ref[...].astype(f32)
        cols = cols_in[...]
        grad_block = gb_ref[...].astype(f32)
        gain = vec_ref[LOCAL + expert : LOCAL + expert + 1, :]
        shift = vec_ref[2 * LOCAL + expert : 2 * LOCAL + expert + 1, :]
        scale = cols[:, SCALE + expert : SCALE + expert + 1]
        grad_exp = cols[:, COEF + expert : COEF + expert + 1] * grad_block
        scaled = grad_exp * norm
        dx = grad_exp * gain
        first = jnp.mean(dx, axis=1, keepdims=True)
        second = jnp.mean(dx * norm, axis=1, keepdims=True)
        grad_sum = scale * (dx - first - norm * second)
        grad_low = grad_sum.astype(bf16)
        pre_a = nn(x, wi_a[0]) + bi_ref[expert : expert + 1, :HALF]
        act_a, slope_a = gelu_parts(pre_a)
        low_a = (nn(grad_low, wo_a[0]) * slope_a).astype(bf16)
        pre_b = nn(x, wi_b[0]) + bi_ref[expert : expert + 1, HALF:]
        act_b, slope_b = gelu_parts(pre_b)
        low_b = (nn(grad_low, wo_b[0]) * slope_b).astype(bf16)
        out_a[...] += tn(grad_low, act_a.astype(bf16))
        in_a[...] += tn(x, low_a)
        out_b[...] += tn(grad_low, act_b.astype(bf16))
        in_b[...] += tn(x, low_b)
        back_ref[...] = back_in[...] + (nt(low_a, wi_a[0]) + nt(low_b, wi_b[0]))
        dcoef = jnp.sum(grad_block * (norm * gain + shift), axis=1, keepdims=True)
        if expert < 2:
            cols_ref[...] = with_column(cols, DCOEF + expert, dcoef)
        else:
            mine = cols[:, DOMAIN : DOMAIN + 1] == ints[DOMAIN_OF + expert - 2].astype(f32)
            column = cols[:, DCOEF + 2 : DCOEF + 3] + jnp.where(mine, dcoef, 0.0)
            cols_ref[...] = with_column(cols, DCOEF + 2, column)
        dvec_ref[0:1, :] += jnp.sum(grad_sum, axis=0, keepdims=True)
        dvec_ref[1:2, :] += jnp.sum(scaled, axis=0, keepdims=True)
        dvec_ref[2:3, :] += jnp.sum(grad_exp, axis=0, keepdims=True)
        dbi_ref[0:1, :HALF] += jnp.sum(low_a.astype(f32), axis=0, keepdims=True)
        dbi_ref[0:1, HALF:] += jnp.sum(low_b.astype(f32), axis=0, keepdims=True)

    if expert < 2:
        work()
    else:
        pl.when(busy)(work)

    @pl.when(step == pl.num_programs(0) - 1)
    def _():
        keep_ref[0] = in_a[...].astype(bf16)
        keep_ref[1] = out_a[...].astype(bf16)
        give_ref[0] = in_b[...].astype(bf16)
        give_ref[1] = out_b[...].astype(bf16)


def tower_kernel(ints, mix_ref, other_ref, cols_ref, tw_ref, tv_ref, out_ref, gb_ref, low_ref, dw_ref, dv_ref):
    @pl.when(pl.program_id(0) == 0)
    def _():
        dw_ref[...] = jnp.zeros_like(dw_ref)
        dv_ref[...] = jnp.zeros_like(dv_ref)

    bias = tv_ref[0:1, :]
    head = tv_ref[1:2, :]
    cols = cols_ref[...]
    block = (mix_ref[...] + other_ref[...].astype(f32)).astype(bf16)
    pre = nn(block, tw_ref[...]) + bias
    act, slope = gelu_parts(pre)
    group = lax.broadcasted_iota(jnp.int32, pre.shape, 1) // TW
    mine = group == cols[:, DOMAIN : DOMAIN + 1].astype(jnp.int32)
    act = jnp.where(mine, act, 0.0)
    logit = jnp.sum(act * head, axis=1, keepdims=True) + cols[:, BIAS : BIAS + 1]
    predicted = 1.0 / (1.0 + jnp.exp(-logit))
    grad_logit = cols[:, WEIGHT : WEIGHT + 1] * (predicted - cols[:, LABEL : LABEL + 1])
    lane = lax.broadcasted_iota(jnp.int32, cols.shape, 1)
    out_ref[...] = jnp.transpose(jnp.where(lane == 0, predicted, jnp.where(lane == 1, grad_logit, 0.0)))[:8]
    dv_ref[1:2, :] += jnp.sum(grad_logit * act, axis=0, keepdims=True)
    grad_pre = jnp.where(mine, grad_logit * head * slope, 0.0)
    dv_ref[0:1, :] += jnp.sum(grad_pre, axis=0, keepdims=True)
    grad_low = grad_pre.astype(bf16)
    grad_block = nt(grad_low, tw_ref[...])
    gb_ref[...] = grad_block
    low_ref[...] = grad_block.astype(bf16)
    dw_ref[...] += tn(block, grad_low)


def lines_kernel(ints, row_ref, dv_ref, *refs):
    out_ref = refs[LOCAL]
    first_set, first_core = ints[ROLE] == 0, ints[CORE] == 0
    mine = [r[0:1, :] for r in refs[:LOCAL]]
    mine = jnp.concatenate(
        [jnp.where(first_core, m[:, :HALF], m[:, HALF:]) for m in mine]
        + [jnp.where(first_core, m[:, HALF:], m[:, :HALF]) for m in mine]
    )
    slot = lax.broadcasted_iota(jnp.int32, (1, row_ref.shape[1]), 1) + ints[ROLE] * row_ref.shape[1]
    lane = lax.broadcasted_iota(jnp.int32, (1, HALF), 1)
    bias = jnp.zeros((1, HALF), f32)
    for d in range(DOM):
        inside = (slot >= ints[START + d]) & (slot < ints[END + d])
        bias = jnp.where(
            lane == d, jnp.sum(jnp.where(inside, row_ref[1:2, :], 0.0), axis=1, keepdims=True), bias
        )
    out_ref[...] = jnp.concatenate(
        [
            jnp.where(first_set, mine, 0.0),
            jnp.where(first_set, 0.0, mine),
            dv_ref[0:2, :HALF],
            dv_ref[0:2, HALF:],
            bias,
            jnp.zeros((3, HALF), f32),
        ]
    )


def call_lines(ints, row_out, dv, bias_grads):
    return pl.pallas_call(
        lines_kernel,
        grid_spec=pltpu.PrefetchScalarGridSpec(
            num_scalar_prefetch=1,
            grid=(1,),
            in_specs=[fixed(row_out.shape), fixed(dv.shape)] + [fixed((8, H))] * LOCAL,
            out_specs=fixed((32, HALF)),
        ),
        out_shape=jax.ShapeDtypeStruct((32, HALF), f32),
        compiler_params=params(),
        name="lines",
    )(ints, row_out, dv, *bias_grads)


def softmax_back(probability, grad_probs):
    return probability * (grad_probs - jnp.sum(probability * grad_probs, axis=0, keepdims=True))


def finish_kernel(
    ints, gb_ref, back_ref, other_ref, cols_ref, coef_ref, prob_ref, x_ref, ev_ref, gates_ref, proj_ref, tower_ref, *refs
):
    vec_refs, (ge_ref, small_ref, proj_sum, gate_sum, bias_sum) = refs[:LOCAL], refs[LOCAL:]
    index = pl.program_id(0)
    last = pl.num_programs(0) - 1
    first = ints[ROLE] == 0

    @pl.when(index == 0)
    def _():
        for ref in (proj_sum, gate_sum, bias_sum):
            ref[...] = jnp.zeros_like(ref)

    mine = jnp.transpose(cols_ref[...])[DCOEF : DCOEF + 3]
    other = coef_ref[0:3, :]
    one, two = jnp.where(first, mine, other), jnp.where(first, other, mine)
    d_shared = jnp.concatenate([one[0:2], two[0:2]], axis=0)
    d_domain = jnp.concatenate([one[2:3], two[2:3]], axis=0)
    top, shared, domain = prob_ref[0:2, :], prob_ref[2:6, :], prob_ref[6:8, :]
    d_top = jnp.concatenate(
        [
            jnp.sum(d_shared * shared, axis=0, keepdims=True),
            jnp.sum(d_domain * domain, axis=0, keepdims=True),
        ],
        axis=0,
    )
    grads = (
        softmax_back(top, d_top),
        softmax_back(shared, d_shared * top[0:1]),
        softmax_back(domain, d_domain * top[1:2]),
    )
    place = (ints[ROLE] * pl.num_programs(0) + index) * TILE + lax.broadcasted_iota(
        jnp.int32, (1, TILE), 1
    )
    picks = [
        jnp.where((place >= ints[START + d]) & (place < ints[END + d]), 1.0, 0.0) for d in range(DOM)
    ]
    spread = jnp.concatenate(
        [picks[d] * grad for grad in grads for d in range(DOM)] + [jnp.zeros((96, TILE), f32)],
        axis=0,
    )
    spread = jnp.transpose(spread).astype(bf16)
    gate_sum[...] += tn(x_ref[...], spread)
    grad_mixed = (
        gb_ref[...] + back_ref[...] + other_ref[...].astype(f32) + nt(spread, gates_ref[...])
    )
    bias_sum[0:1, :] += jnp.sum(grad_mixed, axis=0, keepdims=True)
    low = grad_mixed.astype(bf16)
    proj_sum[...] += tn(low, ev_ref[...])
    ge_ref[...] = nn(low, proj_ref[...]).astype(bf16)

    @pl.when(index == last)
    def _():
        e_in = proj_sum.shape[1]
        vectors = jnp.concatenate([r[0:3, :] for r in vec_refs], axis=0)
        rows = jnp.concatenate(
            [
                jnp.zeros((32, D), f32),
                jnp.where(first, vectors, 0.0),
                jnp.where(first, 0.0, vectors),
                bias_sum[0:1, :],
                jnp.zeros((59, D), f32),
            ],
            axis=0,
        )
        small_ref[:, :e_in] = proj_sum[...].astype(bf16)
        small_ref[:, e_in : e_in + DOM * TW] = tower_ref[...].astype(bf16)
        small_ref[:, e_in + DOM * TW :] = (gate_sum[...] + jnp.transpose(rows)).astype(bf16)


def call_finish(ints, gb, back, other, cols, coef, probs, x, events, gates, proj_t, tower, vecs):
    rows, e_in = gb.shape[0], events.shape[1]
    tiles = rows // TILE

    def kept(width):
        return pl.BlockSpec((TILE, width), lambda i, ints: (ints[ROLE] * tiles + i, 0))

    def tile(width):
        return pl.BlockSpec((TILE, width), lambda i, *_: (i, 0))

    return pl.pallas_call(
        finish_kernel,
        grid_spec=pltpu.PrefetchScalarGridSpec(
            num_scalar_prefetch=1,
            grid=(tiles,),
            in_specs=[
                tile(D),
                kept(D),
                tile(D),
                kept(128),
                pl.BlockSpec((8, TILE), lambda i, *_: (0, i)),
                pl.BlockSpec((8, TILE), lambda i, ints: (0, ints[ROLE] * tiles + i)),
                kept(D),
                kept(e_in),
                fixed(gates.shape),
                fixed(proj_t.shape),
                fixed(tower.shape),
            ]
            + [fixed((8, D))] * LOCAL,
            out_specs=(tile(e_in), fixed((D, PACK))),
            scratch_shapes=[pltpu.VMEM((D, e_in), f32), pltpu.VMEM((D, 128), f32), pltpu.VMEM((8, D), f32)],
        ),
        out_shape=(jax.ShapeDtypeStruct((rows, e_in), bf16), jax.ShapeDtypeStruct((D, PACK), bf16)),
        compiler_params=params(),
        cost_estimate=pl.CostEstimate(
            flops=4 * rows * D * (e_in + 128), bytes_accessed=10_000_000, transcendentals=0
        ),
        name="finish",
    )(ints, gb, back, other, cols, coef, probs, x, events, gates, proj_t, tower, *vecs)


def small_kernel(*refs):
    *parts, proj_ref, tower_ref, lines_ref = refs
    added = functools.reduce(jnp.add, [p[...].astype(f32) for p in parts])
    e_in = proj_ref.shape[1]
    proj_ref[...] = added[:, :e_in]
    for d in range(DOM):
        tower_ref[d] = added[:, e_in + d * TW : e_in + (d + 1) * TW]
    lines_ref[...] = added[:, e_in + DOM * TW :]


def call_small(parts):
    width = parts[0].shape[0]
    e_in = PACK - DOM * TW - 128
    return pl.pallas_call(
        small_kernel,
        grid=(1,),
        in_specs=[fixed(p.shape) for p in parts],
        out_specs=(fixed((width, e_in)), fixed((DOM, width, TW)), fixed((width, 128))),
        out_shape=(
            jax.ShapeDtypeStruct((width, e_in), f32),
            jax.ShapeDtypeStruct((DOM, width, TW), f32),
            jax.ShapeDtypeStruct((width, 128), f32),
        ),
        compiler_params=params(),
        name="small",
    )(*parts)


def place_kernel(ints, *refs):
    *parts, in_ref, out_ref = refs
    half = len(parts) // 2
    first = ints[ROLE] == 0
    for chunk, (own, other) in enumerate(zip(parts[:half], parts[half:])):
        for place, expert in enumerate(CHUNKS[chunk]):
            for which, ref in enumerate((in_ref, out_ref)):
                a, b = own[which, place].astype(f32), other[which, place].astype(f32)
                ref[SETS[0][expert]] = jnp.where(first, a, b)
                ref[SETS[1][expert]] = jnp.where(first, b, a)


def call_place(ints, own, other):
    rows, width = own[0].shape[2:]
    shape = (2 * LOCAL, rows, width)
    return pl.pallas_call(
        place_kernel,
        grid_spec=pltpu.PrefetchScalarGridSpec(
            num_scalar_prefetch=1,
            grid=(1,),
            in_specs=[fixed(a.shape) for a in (*own, *other)],
            out_specs=(fixed(shape), fixed(shape)),
        ),
        out_shape=(jax.ShapeDtypeStruct(shape, f32),) * 2,
        compiler_params=params(),
        name="place",
    )(ints, *own, *other)


def params():
    return pltpu.CompilerParams(vmem_limit_bytes=VMEM_LIMIT)


def fixed(shape):
    return pl.BlockSpec(shape, lambda i, *_: (0,) * len(shape))


def choose_kernel(own_ids, other_ids, in_own, out_own, in_other, out_other, own_ref, other_ref):
    own_ref[0], own_ref[1] = in_own[...], out_own[...]
    other_ref[0], other_ref[1] = in_other[...], out_other[...]


def call_choose(own_ids, other_ids, w_in, w_out_t):
    block = (1,) + w_in.shape[1:]
    shape = jax.ShapeDtypeStruct((2, LOCAL) + w_in.shape[1:], bf16)
    own = pl.BlockSpec(block, lambda i, a, b: (a[i], 0, 0))
    other = pl.BlockSpec(block, lambda i, a, b: (b[i], 0, 0))
    out = pl.BlockSpec((2,) + block, lambda i, a, b: (0, i, 0, 0))
    return pl.pallas_call(
        choose_kernel,
        grid_spec=pltpu.PrefetchScalarGridSpec(
            num_scalar_prefetch=2, grid=(LOCAL,), in_specs=[own, own, other, other], out_specs=(out, out)
        ),
        out_shape=(shape, shape),
        compiler_params=params(),
        cost_estimate=pl.CostEstimate(flops=0, bytes_accessed=2_000_000, transcendentals=0),
        name="choose",
    )(own_ids, other_ids, w_in, w_out_t, w_in, w_out_t)


def call_prepare(ints, floats, table, embeds, proj_t, gates, vec):
    rows = embeds.shape[0]
    tiles = rows // TILE
    e_in = embeds.shape[1]

    def tile(width):
        return pl.BlockSpec((TILE, width), lambda i, *_: (i, 0))

    return pl.pallas_call(
        prepare_kernel,
        grid_spec=pltpu.PrefetchScalarGridSpec(
            num_scalar_prefetch=2,
            grid=(tiles,),
            in_specs=[fixed(table.shape), fixed(embeds.shape), fixed(proj_t.shape), fixed(gates.shape), fixed(vec.shape)],
            out_specs=(
                tile(e_in),
                tile(D),
                tile(D),
                tile(128),
                pl.BlockSpec((8, TILE), lambda i, *_: (0, i)),
            ),
        ),
        out_shape=(
            jax.ShapeDtypeStruct((rows, e_in), bf16),
            jax.ShapeDtypeStruct((rows, D), bf16),
            jax.ShapeDtypeStruct((rows, D), f32),
            jax.ShapeDtypeStruct((rows, 128), f32),
            jax.ShapeDtypeStruct((8, rows), f32),
        ),
        compiler_params=params(),
        cost_estimate=pl.CostEstimate(
            flops=2 * rows * e_in * (rows + D), bytes_accessed=12_000_000, transcendentals=rows * 8
        ),
        name="prepare",
    )(ints, floats, table, embeds, proj_t, gates, vec)


def expert_specs(expert, place, rows):
    steps = rows // TILE if expert < 2 else rows // TILE // 2 + 1

    def tile(width):
        return pl.BlockSpec((TILE, width), lambda i, ints: (tile_of(expert, i, ints)[0], 0))

    weights = [pl.BlockSpec((1, D, HALF), lambda i, *_: (place, 0, 0))] * 4
    return steps, tile, weights


def call_forward(expert, place, ints, x, weights, bi, vec, cols, mix):
    rows = x.shape[0]
    steps, tile, weight_specs = expert_specs(expert, place, rows)
    return pl.pallas_call(
        functools.partial(forward_kernel, expert),
        grid_spec=pltpu.PrefetchScalarGridSpec(
            num_scalar_prefetch=1,
            grid=(steps,),
            in_specs=[tile(D)] + weight_specs + [fixed(bi.shape), fixed(vec.shape), tile(128), tile(D)],
            out_specs=(tile(128), tile(D), tile(D)),
        ),
        out_shape=(
            jax.ShapeDtypeStruct((rows, 128), f32),
            jax.ShapeDtypeStruct((rows, D), f32),
            jax.ShapeDtypeStruct((rows, D), bf16),
        ),
        input_output_aliases={8: 0, 9: 1},
        compiler_params=params(),
        cost_estimate=pl.CostEstimate(
            flops=4 * steps * TILE * D * H, bytes_accessed=12_000_000, transcendentals=steps * TILE * H
        ),
        name="expert_forward",
    )(ints, x, *weights, bi, vec, cols, mix)


def call_backward(expert, place, ints, x, gb, norm, weights, bi, vec, cols, back):
    rows = x.shape[0]
    steps, tile, weight_specs = expert_specs(expert, place, rows)
    if gb.shape[0] == rows:
        gb_spec = tile(D)
    else:
        half_tiles = rows // TILE // 2
        gb_spec = pl.BlockSpec(
            (TILE, D),
            lambda i, ints: (
                jnp.clip(tile_of(expert, i, ints)[0] - ints[ROLE] * half_tiles, 0, half_tiles - 1),
                0,
            ),
        )
    return pl.pallas_call(
        functools.partial(backward_kernel, expert),
        grid_spec=pltpu.PrefetchScalarGridSpec(
            num_scalar_prefetch=1,
            grid=(steps,),
            in_specs=[tile(D), gb_spec, tile(D)]
            + weight_specs
            + [fixed(bi.shape), fixed(vec.shape), tile(128), tile(D)],
            out_specs=(
                tile(128),
                tile(D),
                fixed((2, D, HALF)),
                fixed((2, D, HALF)),
                fixed((8, D)),
                fixed((8, H)),
            ),
            scratch_shapes=[pltpu.VMEM((D, HALF), f32)] * 4,
        ),
        out_shape=(
            jax.ShapeDtypeStruct((rows, 128), f32),
            jax.ShapeDtypeStruct((rows, D), f32),
            jax.ShapeDtypeStruct((2, D, HALF), bf16),
            jax.ShapeDtypeStruct((2, D, HALF), bf16),
            jax.ShapeDtypeStruct((8, D), f32),
            jax.ShapeDtypeStruct((8, H), f32),
        ),
        input_output_aliases={10: 0, 11: 1},
        compiler_params=params(),
        cost_estimate=pl.CostEstimate(
            flops=10 * steps * TILE * D * H, bytes_accessed=20_000_000, transcendentals=steps * TILE * H
        ),
        name="expert_backward",
    )(ints, x, gb, norm, *weights, bi, vec, cols, back)


def call_tower(ints, mix, other, cols, tower, tower_vec):
    rows = other.shape[0]
    tiles = rows // TILE

    def kept(width):
        return pl.BlockSpec((TILE, width), lambda i, ints: (ints[ROLE] * tiles + i, 0))

    def tile(width):
        return pl.BlockSpec((TILE, width), lambda i, *_: (i, 0))

    return pl.pallas_call(
        tower_kernel,
        grid_spec=pltpu.PrefetchScalarGridSpec(
            num_scalar_prefetch=1,
            grid=(tiles,),
            in_specs=[kept(D), tile(D), kept(128), fixed(tower.shape), fixed(tower_vec.shape)],
            out_specs=(
                pl.BlockSpec((8, TILE), lambda i, *_: (0, i)),
                tile(D),
                tile(D),
                fixed((D, DOM * TW)),
                fixed((8, DOM * TW)),
            ),
        ),
        out_shape=(
            jax.ShapeDtypeStruct((8, rows), f32),
            jax.ShapeDtypeStruct((rows, D), f32),
            jax.ShapeDtypeStruct((rows, D), bf16),
            jax.ShapeDtypeStruct((D, DOM * TW), f32),
            jax.ShapeDtypeStruct((8, DOM * TW), f32),
        ),
        compiler_params=params(),
        cost_estimate=pl.CostEstimate(
            flops=6 * rows * D * DOM * TW, bytes_accessed=10_000_000, transcendentals=rows * DOM * TW
        ),
        name="towers",
    )(ints, mix, other, cols, tower, tower_vec)


def per_device(
    box,
    embeds,
    domain,
    frozen,
    labels,
    proj_w,
    proj_b,
    w_in,
    in_bias,
    w_out,
    out_bias,
    ln_gain,
    ln_shift,
    gate_top,
    gate_shared,
    gate_domain,
    tower_w,
    tower_b,
    tower_out,
    tower_out_b,
):
    core = lax.axis_index("tensor")
    role = box.role(lax.axis_index("dp"))
    at_home = core == role
    places = box.count
    rows = embeds.shape[0]
    half_rows = rows // 2
    width = proj_w.shape[1]
    e_in = proj_w.shape[0]
    ahead, place_of = box.others()
    nz, ny, nx = box.dims[1:]
    sets = jnp.array(SETS, jnp.int32)
    set_own, set_other = sets[role], sets[1 - role]

    def half(values, which, axis=0):
        return lax.dynamic_slice_in_dim(values, which * half_rows, half_rows, axis)

    own, other = call_choose(set_own, set_other, w_in, jnp.swapaxes(w_out, 1, 2))

    lines = jnp.concatenate(
        [
            jnp.swapaxes(gate_top, 1, 2).reshape(2 * DOM, width),
            jnp.swapaxes(gate_shared, 1, 2).reshape(S * DOM, width),
            jnp.swapaxes(gate_domain, 1, 2).reshape(K * DOM, width),
            out_bias,
            ln_gain,
            ln_shift,
            proj_b[None],
            in_bias[:, :width],
            in_bias[:, width:],
            jnp.concatenate([tower_b, tower_out], axis=1),
            jnp.zeros((31, width), bf16),
        ]
    )
    lines, _ = step(lines, other)
    pack = jnp.concatenate(
        [proj_w.T, jnp.swapaxes(tower_w, 0, 1).reshape(width, DOM * TW), lines.T], axis=1
    )
    event_rows = jnp.concatenate(
        [domain.astype(f32).T, labels.astype(f32)[None], jnp.zeros((6, rows), f32)]
    )

    other_in = box.send(other, flip=1)
    rows_in = box.to_partner(event_rows, True)
    pack = in_order(role, pack, box.send(pack, flip=1), 0)
    own, other_in, rows_in, pack, embeds = step(own, other_in, rows_in, pack, embeds)

    first = in_order(role, own[:, :3], other_in[:, :3], 2)
    first_z = box.pieces(first, "z")
    pack = jnp.concatenate([pack] + box.pieces(pack, "z"))
    embeds_in = [box.to_partner(embeds[:half_rows], True)]
    event_rows = jnp.where(at_home, event_rows, rows_in)
    ids = event_rows[0]
    onehot = (ids[None, :] == jnp.arange(DOM, dtype=f32)[:, None]).astype(f32)
    rank = jnp.cumsum(onehot, axis=1)
    counts = rank[:, -1]
    ends = jnp.cumsum(counts)
    starts = ends - counts
    position = jnp.sum(onehot * (rank + starts[:, None]), axis=0) - 1.0
    second = in_order(role, own[:, 3:], other_in[:, 3:], 2)
    first, first_z, pack, second, position, starts, ends, embeds_in, embeds = step(
        first, first_z, pack, second, position, starts, ends, embeds_in, embeds
    )

    def along_z(block, found):
        found = [block] + found
        return jnp.stack([b[0] for b in found], axis=1), jnp.stack([b[1] for b in found], axis=1)

    first_i, first_o = along_z(first, first_z)
    first_iy, first_ox = box.pieces(first_i, "y"), box.pieces(first_o, "x")
    second_z = box.pieces(second, "z")
    pack = jnp.concatenate(box.gather_plane(pack), axis=0).reshape(places, 1, width, PACK)
    embeds_in.append(box.to_partner(embeds[half_rows:], True))
    embeds = jnp.where(at_home, embeds, jnp.concatenate(embeds_in))
    first_i, first_o, first_iy, first_ox, second, second_z, pack, embeds = step(
        first_i, first_o, first_iy, first_ox, second, second_z, pack, embeds
    )

    small = in_order(core, pack, swap_cores(pack), 1).reshape(D, PACK)
    first_i = jnp.stack([first_i] + first_iy, axis=1)
    first_o = jnp.stack([first_o] + first_ox, axis=1)
    first_ix, first_oy = box.pieces(first_i, "x"), box.pieces(first_o, "y")
    second_i, second_o = along_z(second, second_z)
    second_iy, second_ox = box.pieces(second_i, "y"), box.pieces(second_o, "x")

    proj_t = small[:, :e_in]
    tower = small[:, e_in : e_in + DOM * TW]
    gates = small[:, e_in + DOM * TW :]
    picked = jnp.concatenate(
        [
            32 + set_own,
            44 + set_own,
            56 + set_own,
            jnp.array([68] + [128] * 5),
            69 + set_own,
            81 + set_own,
            93 + jnp.arange(4),
        ]
    )
    choose = (picked[:, None] == jnp.arange(128)[None, :]).astype(bf16)
    vec = nt(choose, gates)
    blocks = jnp.take(vec[24:].reshape(16, places, 2 * width), place_of, axis=1)
    bi = (
        blocks[:12]
        .reshape(2, LOCAL, places, 2, width)
        .transpose(1, 2, 3, 0, 4)
        .reshape(LOCAL, H)
    )
    bi = jnp.pad(bi, ((0, 2), (0, 0)))
    bi = jnp.where(core == 0, bi, jnp.concatenate([bi[:, HALF:], bi[:, :HALF]], axis=1))
    tower_vec = (
        blocks[12:]
        .reshape(DOM, places, 2, 2, width // 2)
        .transpose(3, 0, 1, 2, 4)
        .reshape(2, DOM * TW)
    )
    tower_vec = jnp.pad(tower_vec, ((0, 6), (0, 0)))

    table = jnp.concatenate([position[None], event_rows[1:]])
    start_i, end_i = starts.astype(jnp.int32), ends.astype(jnp.int32)
    empty = end_i == start_i
    low = jnp.where(empty, 0, start_i // TILE)
    high = jnp.where(empty, 0, (end_i + TILE - 1) // TILE)
    domains = jnp.arange(DOM, dtype=jnp.int32)
    ints = jnp.concatenate(
        [
            jnp.where(role == 0, low[::-1], low),
            jnp.where(role == 0, high[::-1], high),
            role[None],
            jnp.where(role == 0, DOM - 1 - domains, domains),
            start_i,
            end_i,
            core[None],
            jnp.zeros((2,), jnp.int32),
        ]
    )
    loss_weight = 1.0 - (1.0 - FROZEN_SHARE) * frozen.astype(f32)
    floats = jnp.concatenate([loss_weight, tower_out_b.astype(f32)])
    events, x, mix, cols, probs = call_prepare(ints, floats, table, embeds, proj_t, gates, vec)
    (
        first_i, first_o, first_ix, first_oy, second_i, second_o, second_iy, second_ox,
        events, x, mix, cols, probs, vec, bi, tower, tower_vec,
    ) = step(
        first_i, first_o, first_ix, first_oy, second_i, second_o, second_iy, second_ox,
        events, x, mix, cols, probs, vec, bi, tower, tower_vec,
    )

    def full(i, ix, o, oy):
        count = i.shape[0]
        wi = jnp.stack([i] + ix, axis=1).reshape(count, D, HALF)
        wo = jnp.stack([o] + oy, axis=2).reshape(count, D, HALF)
        return (wi, swap_cores(wi), wo, swap_cores(wo))

    norms = {}
    first_w = full(first_i, first_ix, first_o, first_oy)
    second_i = jnp.stack([second_i] + second_iy, axis=1)
    second_o = jnp.stack([second_o] + second_ox, axis=1)
    second_ix, second_oy = box.pieces(second_i, "x"), box.pieces(second_o, "y")
    for expert in range(3):
        cols, mix, norms[expert] = call_forward(expert, expert, ints, x, first_w, bi, vec, cols, mix)
    second_i, second_o, second_ix, second_oy, cols, mix = step(
        second_i, second_o, second_ix, second_oy, cols, mix
    )
    second_w = full(second_i, second_ix, second_o, second_oy)
    for expert in (3, 4):
        cols, mix, norms[expert] = call_forward(
            expert, expert - 3, ints, x, second_w, bi, vec, cols, mix
        )
    give_mix = half(mix, 1 - role).astype(bf16)
    give_mix, mix = step(give_mix, mix)
    other_mix = box.send(give_mix, flip=1)
    cols, mix, norms[5] = call_forward(5, 2, ints, x, second_w, bi, vec, cols, mix)
    row_out, grad_block, grad_low, d_tower, d_tower_vec = call_tower(
        ints, mix, other_mix, cols, tower, tower_vec
    )

    d_vec, d_bias, keep, give = {}, {}, {}, {}
    box_shape = (nx, ny, nz, 2, 2 * width, HALF)

    def backward(expert, grad, cols, back):
        pair, place = (first_w, expert) if expert < 3 else (second_w, expert - 3)
        cols, back, keep[expert], give[expert], d_vec[expert], d_bias[expert] = call_backward(
            expert, place, ints, x, grad, norms[expert], pair, bi, vec, cols, back
        )
        return cols, back

    def both_cores(experts):
        def one(which):
            return jnp.stack(
                [
                    total(keep[e][which], [give[e][which]]).astype(bf16).reshape(box_shape)
                    for e in experts
                ]
            )

        return one(0), one(1)

    class Scatter:
        def __init__(self, experts):
            self.experts = experts
            self.i, self.o = both_cores(experts)
            self.i = [self.i[:, k] for k in range(nx)]
            self.o = [self.o[:, :, k] for k in range(ny)]
            self.state = (
                self.i[0], self.o[0], box.hand_out(self.i, "x"), box.hand_out(self.o, "y")
            )

        def second(self):
            i, o, i_in, o_in = self.state
            i, o = total(i, i_in).astype(bf16), total(o, o_in).astype(bf16)
            i, o = [i[:, k] for k in range(ny)], [o[:, k] for k in range(nx)]
            self.state = (i[0], o[0], box.hand_out(i, "y"), box.hand_out(o, "x"))

        def third(self):
            i, o, i_in, o_in = self.state
            both = jnp.stack([total(i, i_in).astype(bf16), total(o, o_in).astype(bf16)])
            both = [both[:, :, k] for k in range(nz)]
            self.state = (both[0], box.hand_out(both, "z"))

        def fourth(self):
            both = total(*self.state)
            mine = lax.dynamic_index_in_dim(both, role, 2, keepdims=False)
            other = lax.dynamic_index_in_dim(both, 1 - role, 2, keepdims=False).astype(bf16)
            self.state = (mine, box.send(other, flip=1))

    def sync(scatters, *values):
        states, values = step([c.state for c in scatters], values)
        for c, state in zip(scatters, states):
            c.state = state
        return values

    back = jnp.zeros((rows, D), f32)
    grad_in = box.send(grad_low, flip=1)
    cols, back = backward(5, grad_low, cols, back)
    grad_in, cols, back, keep[5], give[5] = step(grad_in, cols, back, keep[5], give[5])
    grad_all = in_order(role, grad_low, grad_in, 0)
    give[5] = swap_cores(give[5])
    cols, back = backward(0, grad_all, cols, back)
    cols, back, keep[5], give[5], keep[0], give[0] = step(
        cols, back, keep[5], give[5], keep[0], give[0]
    )
    give[0] = swap_cores(give[0])
    cols, back = backward(4, grad_all, cols, back)
    cols, back, keep[0], give[0], keep[4], give[4] = step(
        cols, back, keep[0], give[0], keep[4], give[4]
    )
    c0 = Scatter(CHUNKS[0])
    give[4] = swap_cores(give[4])
    cols, back = backward(1, grad_all, cols, back)
    cols, back, keep[4], give[4], keep[1], give[1] = sync(
        [c0], cols, back, keep[4], give[4], keep[1], give[1]
    )
    c0.second()
    give[1] = swap_cores(give[1])
    cols, back = backward(3, grad_all, cols, back)
    cols, back, keep[1], give[1], keep[3], give[3] = sync(
        [c0], cols, back, keep[1], give[1], keep[3], give[3]
    )
    c0.third()
    c1 = Scatter(CHUNKS[1])
    give[3] = swap_cores(give[3])
    cols, back = backward(2, grad_all, cols, back)
    cols, back, keep[3], give[3], keep[2], give[2], d_vec, d_bias, row_out = sync(
        [c0, c1], cols, back, keep[3], give[3], keep[2], give[2], d_vec, d_bias, row_out
    )
    back_in = box.send(half(back, 1 - role).astype(bf16), flip=1)
    coef_t = half(cols, 1 - role)[:, DCOEF : DCOEF + 8].T
    coef_in = box.send(coef_t, flip=1)
    c0.fourth()
    c1.second()
    give[2] = swap_cores(give[2])
    d_lines = call_lines(ints, row_out, d_tower_vec, [d_bias[e] for e in range(LOCAL)])
    d_lines = d_lines + swap_cores(d_lines)
    back, back_in, coef_in, keep[2], give[2], d_lines = sync(
        [c0, c1], back, back_in, coef_in, keep[2], give[2], d_lines
    )
    c1.third()
    c2 = Scatter(CHUNKS[2])
    d_lines = box.same_sum(d_lines, "flip")
    grad_events, d_small = call_finish(
        ints, grad_block, back, back_in, cols, coef_in, probs, x, events, gates, proj_t, d_tower,
        [d_vec[e] for e in range(LOCAL)],
    )
    grad_events, d_small, d_lines = sync([c1, c2], grad_events, d_small, d_lines)
    c1.fourth()
    c2.second()
    d_small = d_small.reshape(places, 2, width, PACK)
    d_other = swap_cores(lax.dynamic_index_in_dim(d_small, 1 - core, 1, keepdims=False))
    events_in = box.to_partner(grad_events, False)
    rows_in = box.to_partner(row_out, False)
    d_lines = box.same_sum(d_lines, "z")
    d_small, d_other, grad_events, events_in, row_out, rows_in, d_lines = sync(
        [c1, c2], d_small, d_other, grad_events, events_in, row_out, rows_in, d_lines
    )
    c2.third()
    d_mine = total(lax.dynamic_index_in_dim(d_small, core, 1, keepdims=False), [d_other])
    d_mine = d_mine.astype(bf16).reshape(nx * ny, nz, 2, width, PACK)
    d_parts = [d_mine[k] for k in range(nx * ny)]
    d_in = box.hand_out_plane(d_parts)
    d_lines = box.same_sum(d_lines, "y")
    grad_events = in_order(role, grad_events, events_in, 0)
    order = position[None, :] == jnp.arange(rows, dtype=f32)[:, None]
    grad_embeds = lax.dot_general(
        order.astype(bf16), grad_events, (((0,), (0,)), ((), ())), preferred_element_type=f32
    ).astype(bf16)
    predicted = in_order(role, row_out, rows_in, 1)
    predictions = jnp.sum(jnp.where(order, predicted[0][:, None], 0.0), axis=0)
    predictions = jnp.broadcast_to(predictions[None], (8, rows))
    d_mine, d_in, grad_embeds, predictions, d_lines = sync(
        [c2], d_parts[0], d_in, grad_embeds, predictions, d_lines
    )
    c2.fourth()
    d_mine = total(d_mine, d_in).astype(bf16)
    same = [lax.dynamic_index_in_dim(d_mine[k], role, 0, keepdims=False) for k in range(nz)]
    flip = [lax.dynamic_index_in_dim(d_mine[k], 1 - role, 0, keepdims=False) for k in range(nz)]
    d_in = box.hand_out(same, "z") + [box.send(f, flip=1, z=k) for k, f in enumerate(flip)]
    d_lines = box.same_sum(d_lines, "x")
    grad_embeds = jnp.where(at_home, grad_embeds, swap_cores(grad_embeds))
    predictions = jnp.where(at_home, predictions, swap_cores(predictions))[0]

    scatters = (c0, c1, c2)
    grad_w_in, grad_w_out = call_place(
        ints, [c.state[0] for c in scatters], [c.state[1] for c in scatters]
    )
    proj_grad, grad_tower_w, columns = call_small([same[0]] + d_in)
    columns = columns.T
    grad_gates = [
        jnp.swapaxes(columns[low : low + DOM * size].reshape(DOM, size, width), 1, 2)
        for low, size in ((0, 2), (2 * DOM, S), ((2 + S) * DOM, K))
    ]
    found = {j: 18 * r + 3 * i for r, row in enumerate(SETS) for i, j in enumerate(row)}
    experts = range(2 * LOCAL)

    def vectors(which):
        return jnp.stack([columns[32 + found[j] + which] for j in experts])

    device = 2 * lax.axis_index("dp") + core
    d_bias_rows = {j: 12 * r + i for r, row in enumerate(SETS) for i, j in enumerate(row)}
    in_bias_grad = jnp.stack(
        [jnp.concatenate([d_lines[d_bias_rows[j]], d_lines[d_bias_rows[j] + 6]]) for j in experts]
    )
    in_bias_grad = lax.dynamic_slice_in_dim(in_bias_grad, device * 2 * width, 2 * width, 1)
    d_tv = jnp.concatenate([d_lines[24:26], d_lines[26:28]], axis=1).reshape(2, DOM, TW)
    d_tv = lax.dynamic_slice_in_dim(d_tv, device * (width // 2), width // 2, 2)
    return (
        predictions,
        grad_embeds,
        proj_grad.T,
        columns[68],
        grad_w_in,
        in_bias_grad,
        jnp.swapaxes(grad_w_out, 1, 2),
        vectors(0),
        vectors(1),
        vectors(2),
        *grad_gates,
        grad_tower_w,
        d_tv[0],
        d_tv[1],
        d_lines[28, :DOM],
    )


def solution(mesh):
    both = ("dp", "tensor")
    in_specs = (
        P("dp", None),
        P("dp", None),
        P(),
        P("dp"),
        P(None, both),
        P(both),
        P(None, "dp", "tensor"),
        P(None, both),
        P(None, "tensor", "dp"),
        P(None, both),
        P(None, both),
        P(None, both),
        P(None, both, None),
        P(None, both, None),
        P(None, both, None),
        P(None, both, None),
        P(None, both),
        P(None, both),
        P(),
    )
    out_specs = (
        P("dp"),
        P("dp", None),
        P(None, both),
        P(both),
        P(None, "dp", "tensor"),
        P(None, both),
        P(None, "tensor", "dp"),
        P(None, both),
        P(None, both),
        P(None, both),
        P(None, both, None),
        P(None, both, None),
        P(None, both, None),
        P(None, both, None),
        P(None, both),
        P(None, both),
        P(),
    )
    return jax.shard_map(
        functools.partial(per_device, Box(mesh.shape["dp"])),
        mesh=mesh,
        in_specs=in_specs,
        out_specs=out_specs,
        check_vma=False,
    )
```

```python
import functools
import math

import jax
import jax.numpy as jnp
from jax import lax
from jax.experimental import pallas as pl
from jax.experimental.pallas import tpu as pltpu
from jax.sharding import PartitionSpec as P

D = 512
H = 1024
HALF = H // 2
TW = 256
S = 4
DOM = 4
K = 2
EPS = 1e-05
FROZEN_SHARE = 0.25
TILE = 256
LOCAL = 6
CHUNKS = ((0, 1, 2), (3, 4, 5))
VMEM_LIMIT = 48 * 1024 * 1024
PACK = 1792
SETS = (
    tuple(range(2)) + tuple(S + K * d for d in reversed(range(DOM))),
    tuple(range(2, 4)) + tuple(S + K * d + 1 for d in range(DOM)),
)
COEF, SCALE, DCOEF, DOMAIN, LABEL, WEIGHT, BIAS = 0, 6, 12, 18, 19, 20, 21
LOW, HIGH, ROLE, DOMAIN_OF, START, END, CORE = 0, 4, 8, 9, 13, 17, 21

bf16 = jnp.bfloat16
f32 = jnp.float32


def dims_of(count):
    if count % 4 == 0:
        rest = count // 4
        root = math.isqrt(rest)
        if root * root == rest:
            return (4, root, root)
    return (count, 1, 1)


class Box:
    def __init__(self, count):
        first, second, third = dims_of(count)
        self.count = count
        self.dims = (2, first // 2, second, third)
        self.strides = (second * third, 2 * second * third, third, 1)

    def role(self, chip):
        return (chip // self.strides[0]) % 2

    def partner(self, chip):
        return chip + (1 - 2 * self.role(chip)) * self.strides[0]

    def send(self, values, flip=0, z=0, y=0, x=0):
        pairs = []
        for chip in range(self.count):
            to = chip
            for step, size, stride in zip((flip, z, y, x), self.dims, self.strides):
                place = (chip // stride) % size
                to += ((place + step) % size - place) * stride
            pairs.append((chip, to))
        return lax.ppermute(values, "dp", pairs)

    def to_partner(self, values, home):
        pairs = []
        for chip in range(self.count):
            for core in range(2):
                if (core == self.role(chip)) == home:
                    pairs.append((2 * chip + core, 2 * self.partner(chip) + core))
        return lax.ppermute(values, ("dp", "tensor"), pairs)

    def pieces(self, values, dim):
        size = self.dims[("flip", "z", "y", "x").index(dim)]
        return [self.send(values, **{dim: -k}) for k in range(1, size)]

    def hand_out(self, parts, dim):
        return [self.send(part, **{dim: k}) for k, part in enumerate(parts) if k]

    def line(self, shards):
        same, other = shards
        steps = range(self.dims[1])
        return [self.send(same, z=-z) for z in steps if z], [
            self.send(other, flip=1, z=-z) for z in steps
        ]

    def in_line(self, own, found, role, axis):
        same, other = found
        return [in_order(role, s, o, axis) for s, o in zip([own] + same, other)]

    def hand_out_flip(self, parts):
        return [self.send(part, flip=1, z=k) for k, part in enumerate(parts)]

    def plane(self):
        _, _, ny, nx = self.dims
        return [(x, y) for x in range(nx) for y in range(ny)][1:]

    def gather_plane(self, values):
        return [values] + [self.send(values, y=-y, x=-x) for x, y in self.plane()]

    def hand_out_plane(self, parts):
        return [self.send(part, y=y, x=x) for part, (x, y) in zip(parts[1:], self.plane())]

    def same_sum(self, values, dim):
        number = ("flip", "z", "y", "x").index(dim)
        size, stride = self.dims[number], self.strides[number]
        found = jnp.stack([values] + self.pieces(values, dim))
        if size > 2:
            mine = (lax.axis_index("dp") // stride) % size
            found = jnp.take(found, (jnp.arange(size) - mine) % size, axis=0)
        return functools.reduce(jnp.add, [found[k] for k in range(size)])

    def places(self):
        me = lax.axis_index("dp")
        chip = jnp.arange(self.count)
        place, weight = 0, 1
        for dim, (size, stride) in enumerate(zip(self.dims, self.strides)):
            mine = (me // stride) % size if dim else 0
            place = place + (((chip // stride) % size - mine) % size) * weight
            weight *= size
        return place

    def ahead(self):
        me = lax.axis_index("dp")
        place = jnp.arange(self.count)
        chip, weight = 0, 1
        for dim, (size, stride) in enumerate(zip(self.dims, self.strides)):
            mine = (me // stride) % size if dim else 0
            chip = chip + ((mine + (place // weight) % size) % size) * stride
            weight *= size
        return chip


def swap_cores(values):
    return lax.ppermute(values, "tensor", [(0, 1), (1, 0)])


def in_order(which, own, other, axis):
    return jnp.where(
        which == 0,
        jnp.concatenate([own, other], axis),
        jnp.concatenate([other, own], axis),
    )


def step(*values):
    return lax.optimization_barrier(values)


def total(first, arrived):
    return functools.reduce(jnp.add, [a.astype(f32) for a in arrived], first.astype(f32))


def gelu_parts(v):
    inner = math.sqrt(2.0 / math.pi)
    square = v * v
    th = jnp.tanh(v * (inner + inner * 0.044715 * square))
    half = 0.5 * (1.0 + th)
    act = v * half
    slope = half + 0.5 * v * (1.0 - th * th) * (inner + 3.0 * inner * 0.044715 * square)
    return act, slope


def nt(a, b):
    return lax.dot_general(a, b, (((1,), (1,)), ((), ())), preferred_element_type=f32)


def tn(a, b):
    return lax.dot_general(a, b, (((0,), (0,)), ((), ())), preferred_element_type=f32)


def nn(a, b):
    return jnp.dot(a, b, preferred_element_type=f32)


def softmax_rows(v):
    e = jnp.exp(v - jnp.max(v, axis=0, keepdims=True))
    return e / jnp.sum(e, axis=0, keepdims=True)


def prepare_kernel(ints, floats, rows_ref, embeds_ref, proj_ref, gates_ref, vec_ref, ev_ref, x_ref, mix_ref, cols_ref, prob_ref):
    tiles_of_half = pl.num_programs(0) // 2
    index = pl.program_id(0)
    role = ints[ROLE]
    count = rows_ref.shape[1]
    slot = index * TILE + lax.broadcasted_iota(jnp.int32, (TILE, count), 0)
    here = rows_ref[0:1, :].astype(jnp.int32) == slot
    order = jnp.where(here, 1.0, 0.0).astype(bf16)
    label = jnp.sum(jnp.where(here, rows_ref[1:2, :], 0.0), axis=1, keepdims=True)
    events = nn(order, embeds_ref[...]).astype(bf16)
    ev_ref[...] = events
    mixed = nt(events, proj_ref[...]) + vec_ref[3 * LOCAL : 3 * LOCAL + 1, :]
    low = mixed.astype(bf16)
    x_ref[...] = low
    mix_ref[...] = mixed * jnp.where(index // tiles_of_half == role, 1.0, 0.0)
    logits = jnp.transpose(nn(low, gates_ref[...]))
    place = index * TILE + lax.broadcasted_iota(jnp.int32, (1, TILE), 1)
    picks = [
        jnp.where((place >= ints[START + d]) & (place < ints[END + d]), 1.0, 0.0) for d in range(DOM)
    ]

    def pick(low_row, size):
        return softmax_rows(
            functools.reduce(
                jnp.add,
                [picks[d] * logits[low_row + d * size : low_row + (d + 1) * size] for d in range(DOM)],
            )
        )

    top, shared, domain = pick(0, 2), pick(2 * DOM, S), pick((2 + S) * DOM, K)
    prob_ref[...] = jnp.concatenate([top, shared, domain], axis=0)
    first = role == 0
    own_shared = top[0:1] * jnp.where(first, shared[:2], shared[2:])
    own_domain = top[1:2] * jnp.where(first, domain[0:1], domain[1:2])
    coef = [own_domain * jnp.where(first, picks[DOM - 1 - d], picks[d]) for d in range(DOM)]
    table = [
        own_shared,
        *coef,
        jnp.zeros((DOMAIN - SCALE, TILE), f32),
        sum(float(d) * picks[d] for d in range(DOM)),
        jnp.zeros((1, TILE), f32),
        sum(floats[d] * picks[d] for d in range(DOM)),
        sum(floats[DOM + d] * picks[d] for d in range(DOM)),
        jnp.zeros((128 - BIAS - 1, TILE), f32),
    ]
    cols_ref[...] = with_column(jnp.transpose(jnp.concatenate(table, axis=0)), LABEL, label)


def with_column(table, column, values):
    lane = lax.broadcasted_iota(jnp.int32, table.shape, 1)
    return jnp.where(lane == column, values, table)


def tiles_of(expert, ints, first, count):
    low = jnp.maximum(ints[LOW + expert - 2], first)
    high = jnp.minimum(ints[HIGH + expert - 2], first + count)
    return low - first, jnp.maximum(high, low) - first


def each_span(expert, ints, first, rows, work):
    if expert < 2:
        work(slice(0, rows))
    else:
        low, high = tiles_of(expert, ints, first, rows // TILE)

        def one(index, _):
            work(pl.ds(pl.multiple_of(index * TILE, TILE), TILE))
            return 0

        lax.fori_loop(low, high, one, 0)


def join(pieces, held):
    count = len(pieces) // 2
    for core in range(2):
        mine = pieces[core * count : core * count + count]
        by_x, by_y = split_pieces(mine)
        nx, ny = len(by_x), len(by_y)
        rows = by_x[0].shape[3]
        nz = by_x[0].shape[1]

        def at(x, y, z):
            return pl.ds(((x * ny + y) * nz + z) * rows, rows)

        for x in range(nx):
            for y in range(ny):
                for z in range(nz):
                    held[core][at(x, y, z), :] = by_x[x][y, z, 0]
                    held[2 + core][at(x, y, z), :] = by_y[y][x, z, 0]


def split_pieces(pieces):
    nx = pieces[-1].shape[0]
    return pieces[:nx], pieces[nx:]


def forward_kernel(experts, own, aliased, number, ints, x_ref, *refs):
    arrays = sorted({e // 3 for e in experts})
    weights = {a: refs[number * k : number * (k + 1)] for k, a in enumerate(arrays)}
    refs = refs[number * len(arrays) :]
    refs, held = refs[:-4], refs[-4:]
    wi_a, wi_b, wo_a, wo_b = held
    bi_ref, vec_ref, cols_in, mix_in = refs[:4]
    cols_ref, mix_ref, *norm_refs = refs[4 + aliased :]
    norm_refs = dict(zip(arrays, norm_refs))
    rows = x_ref.shape[0]
    half = ints[ROLE] if own else 1 - ints[ROLE]
    step = pl.program_id(0)

    @pl.when(step == 0)
    def _():
        cols_ref[...] = cols_in[...]
        mix_ref[...] = mix_in[...]

    def work(expert, span):
        x = x_ref[span, :]
        pre_a = nn(x, wi_a[...]) + bi_ref[expert : expert + 1, :HALF]
        act_a = gelu_parts(pre_a)[0].astype(bf16)
        pre_b = nn(x, wi_b[...]) + bi_ref[expert : expert + 1, HALF:]
        act_b = gelu_parts(pre_b)[0].astype(bf16)
        out = nt(act_a, wo_a[...]) + nt(act_b, wo_b[...]) + vec_ref[expert : expert + 1, :]
        centre = jnp.mean(out, axis=1, keepdims=True)
        centred = out - centre
        scale = lax.rsqrt(jnp.mean(centred * centred, axis=1, keepdims=True) + EPS)
        norm = centred * scale
        norm_refs[expert // 3][0, span, :] = norm.astype(bf16)
        cols = cols_ref[span, :]
        cols_ref[span, :] = with_column(cols, SCALE + expert, scale)
        gain = vec_ref[LOCAL + expert : LOCAL + expert + 1, :]
        shift = vec_ref[2 * LOCAL + expert : 2 * LOCAL + expert + 1, :]
        mix_ref[span, :] += cols[:, COEF + expert : COEF + expert + 1] * (norm * gain + shift)

    for place, expert in enumerate(experts):

        @pl.when(step == place)
        def _(expert=expert):
            join(weights[expert // 3], held)
            each_span(expert, ints, half * (rows // TILE), rows, functools.partial(work, expert))


def backward_kernel(experts, halves, keeps_back, adds, number, ints, x_ref, *refs):
    gb_refs, refs = refs[: len(halves)], refs[len(halves) :]
    norm_ref, pieces, refs = refs[0], refs[1 : 1 + number], refs[1 + number :]
    bi_ref, vec_ref, cols_in = refs[:3]
    refs, held = refs[3:-4], refs[-4:]
    wi_a, wi_b, wo_a, wo_b = held
    join(pieces, held)
    back_in, refs = refs[0], refs[1:]
    if adds:
        dvec_in, dbi_in = refs[:2]
        refs = refs[2:]
    cols_ref, back_ref, keep_ref, give_ref, dvec_ref, dbi_ref, in_a, in_b, out_a, out_b = refs
    rows = x_ref.shape[0]
    half_tiles = rows // TILE // len(halves)
    first = 0 if len(halves) == 2 else (ints[ROLE] if halves[0] == "own" else 1 - ints[ROLE]) * half_tiles
    step = pl.program_id(0)

    @pl.when(step == 0)
    def _():
        cols_ref[...] = cols_in[...]
        back_ref[...] = back_in[...] if keeps_back else jnp.zeros_like(back_ref)

    dvec_ref[...] = dvec_in[...] if adds else jnp.zeros_like(dvec_ref)
    dbi_ref[...] = dbi_in[...] if adds else jnp.zeros_like(dbi_ref)

    def work(expert, span):
        whole = isinstance(span, slice)

        def add(ref, values):
            ref[...] = values if whole else ref[...] + values

        x = x_ref[span, :]
        norm = norm_ref[0, span, :].astype(f32)
        cols = cols_ref[span, :]
        if len(halves) == 1:
            grad_block = gb_refs[0][span, :].astype(f32)
        else:
            half = span.start // (half_tiles * TILE)
            inner = pl.ds(pl.multiple_of(span.start - half * (half_tiles * TILE), TILE), TILE)
            grad_block = jnp.where(
                half == ints[ROLE], gb_refs[0][inner, :].astype(f32), gb_refs[1][inner, :].astype(f32)
            )
        gain = vec_ref[LOCAL + expert : LOCAL + expert + 1, :]
        shift = vec_ref[2 * LOCAL + expert : 2 * LOCAL + expert + 1, :]
        scale = cols[:, SCALE + expert : SCALE + expert + 1]
        grad_exp = cols[:, COEF + expert : COEF + expert + 1] * grad_block
        scaled = grad_exp * norm
        dx = grad_exp * gain
        first_mean = jnp.mean(dx, axis=1, keepdims=True)
        second_mean = jnp.mean(dx * norm, axis=1, keepdims=True)
        grad_sum = scale * (dx - first_mean - norm * second_mean)
        grad_low = grad_sum.astype(bf16)
        pre_a = nn(x, wi_a[...]) + bi_ref[expert : expert + 1, :HALF]
        act_a, slope_a = gelu_parts(pre_a)
        low_a = (nn(grad_low, wo_a[...]) * slope_a).astype(bf16)
        pre_b = nn(x, wi_b[...]) + bi_ref[expert : expert + 1, HALF:]
        act_b, slope_b = gelu_parts(pre_b)
        low_b = (nn(grad_low, wo_b[...]) * slope_b).astype(bf16)
        add(out_a, tn(grad_low, act_a.astype(bf16)))
        add(in_a, tn(x, low_a))
        add(out_b, tn(grad_low, act_b.astype(bf16)))
        add(in_b, tn(x, low_b))
        back_ref[span, :] += nt(low_a, wi_a[...]) + nt(low_b, wi_b[...])
        dcoef = jnp.sum(grad_block * (norm * gain + shift), axis=1, keepdims=True)
        if expert < 2:
            cols_ref[span, :] = with_column(cols, DCOEF + expert, dcoef)
        else:
            mine = cols[:, DOMAIN : DOMAIN + 1] == ints[DOMAIN_OF + expert - 2].astype(f32)
            column = cols[:, DCOEF + 2 : DCOEF + 3] + jnp.where(mine, dcoef, 0.0)
            cols_ref[span, :] = with_column(cols, DCOEF + 2, column)
        dvec_ref[0, 0:1, :] += jnp.sum(grad_sum, axis=0, keepdims=True)
        dvec_ref[0, 1:2, :] += jnp.sum(scaled, axis=0, keepdims=True)
        dvec_ref[0, 2:3, :] += jnp.sum(grad_exp, axis=0, keepdims=True)
        dbi_ref[0, 0:1, :HALF] += jnp.sum(low_a.astype(f32), axis=0, keepdims=True)
        dbi_ref[0, 0:1, HALF:] += jnp.sum(low_b.astype(f32), axis=0, keepdims=True)

    for place, expert in enumerate(experts):

        @pl.when(step == place)
        def _(expert=expert):
            if expert >= 2:
                for ref in (in_a, in_b, out_a, out_b):
                    ref[...] = jnp.zeros_like(ref)
            each_span(expert, ints, first, rows, functools.partial(work, expert))

    keep_ref[0, 0] = in_a[...].astype(bf16)
    keep_ref[0, 1] = out_a[...].astype(bf16)
    give_ref[0, 0] = in_b[...].astype(bf16)
    give_ref[0, 1] = out_b[...].astype(bf16)


def tower_kernel(
    ints, mix_ref, other_ref, cols_ref, tw_ref, tv_ref, out_ref, gb_ref, low_ref, dw_ref, dv_ref, db_ref
):
    @pl.when(pl.program_id(0) == 0)
    def _():
        db_ref[...] = jnp.zeros_like(db_ref)
        dw_ref[...] = jnp.zeros_like(dw_ref)
        dv_ref[...] = jnp.zeros_like(dv_ref)

    bias = tv_ref[0:1, :]
    head = tv_ref[1:2, :]
    cols = cols_ref[...]
    block = (mix_ref[...] + other_ref[...].astype(f32)).astype(bf16)
    pre = nn(block, tw_ref[...]) + bias
    act, slope = gelu_parts(pre)
    group = lax.broadcasted_iota(jnp.int32, pre.shape, 1) // TW
    mine = group == cols[:, DOMAIN : DOMAIN + 1].astype(jnp.int32)
    act = jnp.where(mine, act, 0.0)
    logit = jnp.sum(act * head, axis=1, keepdims=True) + cols[:, BIAS : BIAS + 1]
    predicted = 1.0 / (1.0 + jnp.exp(-logit))
    grad_logit = cols[:, WEIGHT : WEIGHT + 1] * (predicted - cols[:, LABEL : LABEL + 1])
    lane = lax.broadcasted_iota(jnp.int32, cols.shape, 1)
    out_ref[...] = jnp.transpose(jnp.where(lane == 0, predicted, jnp.where(lane == 1, grad_logit, 0.0)))[:8]
    by_domain = jnp.where(lane.astype(f32) == cols[:, DOMAIN : DOMAIN + 1], grad_logit, 0.0)
    db_ref[0:1, :] += jnp.sum(by_domain, axis=0, keepdims=True)
    dv_ref[1:2, :] += jnp.sum(grad_logit * act, axis=0, keepdims=True)
    grad_pre = jnp.where(mine, grad_logit * head * slope, 0.0)
    dv_ref[0:1, :] += jnp.sum(grad_pre, axis=0, keepdims=True)
    grad_low = grad_pre.astype(bf16)
    grad_block = nt(grad_low, tw_ref[...])
    gb_ref[...] = grad_block
    low_ref[...] = grad_block.astype(bf16)
    dw_ref[...] += tn(block, grad_low)


def softmax_back(probability, grad_probs):
    return probability * (grad_probs - jnp.sum(probability * grad_probs, axis=0, keepdims=True))


def gate_kernel(own, ints, back_ref, cols_ref, prob_ref, x_ref, gates_ref, sum_ref, low_ref, gate_ref):
    index = pl.program_id(0)
    half = ints[ROLE] if own else 1 - ints[ROLE]
    first = ints[ROLE] == 0

    @pl.when(index == 0)
    def _():
        gate_ref[...] = jnp.zeros_like(gate_ref)

    mine = jnp.transpose(cols_ref[...])[DCOEF : DCOEF + 3]
    none = jnp.zeros_like(mine)
    one, two = jnp.where(first, mine, none), jnp.where(first, none, mine)
    d_shared = jnp.concatenate([one[0:2], two[0:2]], axis=0)
    d_domain = jnp.concatenate([one[2:3], two[2:3]], axis=0)
    top, shared, domain = prob_ref[0:2, :], prob_ref[2:6, :], prob_ref[6:8, :]
    d_top = jnp.concatenate(
        [
            jnp.sum(d_shared * shared, axis=0, keepdims=True),
            jnp.sum(d_domain * domain, axis=0, keepdims=True),
        ],
        axis=0,
    )
    grads = (
        softmax_back(top, d_top),
        softmax_back(shared, d_shared * top[0:1]),
        softmax_back(domain, d_domain * top[1:2]),
    )
    rows = top.shape[1]
    place = (half * pl.num_programs(0) + index) * rows + lax.broadcasted_iota(jnp.int32, (1, rows), 1)
    picks = [
        jnp.where((place >= ints[START + d]) & (place < ints[END + d]), 1.0, 0.0) for d in range(DOM)
    ]
    spread = jnp.concatenate(
        [picks[d] * grad for grad in grads for d in range(DOM)] + [jnp.zeros((96, rows), f32)],
        axis=0,
    )
    spread = jnp.transpose(spread).astype(bf16)
    gate_ref[...] += tn(x_ref[...], spread)
    added = back_ref[...] + nt(spread, gates_ref[...])
    sum_ref[...] = added
    low_ref[...] = added.astype(bf16)


def call_gate(own, ints, back, cols, probs, x, gates):
    rows = x.shape[0]
    half = rows // 2

    def index(ints):
        return ints[ROLE] if own else 1 - ints[ROLE]

    return pl.pallas_call(
        functools.partial(gate_kernel, own),
        grid_spec=pltpu.PrefetchScalarGridSpec(
            num_scalar_prefetch=1,
            grid=(1,),
            in_specs=[
                half_spec(own, (half, D)),
                half_spec(own, (half, 128)),
                pl.BlockSpec((8, half), lambda i, ints: (0, index(ints))),
                half_spec(own, (half, D)),
                fixed(gates.shape),
            ],
            out_specs=(fixed((half, D)), fixed((half, D)), fixed((D, 128))),
        ),
        out_shape=(
            jax.ShapeDtypeStruct((half, D), f32),
            jax.ShapeDtypeStruct((half, D), bf16),
            jax.ShapeDtypeStruct((D, 128), f32),
        ),
        compiler_params=params(),
        cost_estimate=pl.CostEstimate(
            flops=4 * half * D * 128, bytes_accessed=5_000_000, transcendentals=0
        ),
        name="gates",
    )(ints, back, cols, probs, x, gates)


def hidden_lines(ints, lane_ref, tv_ref, line_refs):
    first_set, first_core = ints[ROLE] == 0, ints[CORE] == 0
    mine = [r[k, 0:1, :] for r in line_refs for k in range(r.shape[0])]
    mine = jnp.concatenate(mine, axis=0)
    mine = jnp.where(first_core, mine, pltpu.roll(mine, HALF, 1))
    mine = jnp.where(first_set, mine, 0.0), jnp.where(first_set, 0.0, mine)
    found = {j: mine[r][i : i + 1] for r, row in enumerate(SETS) for i, j in enumerate(row)}
    mine = jnp.concatenate([found[j] for j in range(2 * LOCAL)], axis=0).astype(bf16)

    def lanes(values, row):
        lane = lax.broadcasted_iota(jnp.int32, (H, D), 0)
        chosen = jnp.where(lane == lane_ref[row : row + 1, :], 1.0, 0.0).astype(bf16)
        return nn(values, chosen)

    tower = tv_ref[...].astype(bf16)
    rows = [lanes(mine, 0), lanes(mine, 1)]
    head = lane_ref[6:7, :] == 1
    for d in range(DOM):
        both = lanes(tower, 2 + d)
        rows.append(jnp.where(head, both[1:2], both[0:1]))
    return rows


def finish_kernel(
    ints, gb_ref, gb_in_ref, own_ref, other_ref, own_in_ref, other_in_ref, ev_ref, proj_ref, tower_ref, gate_a, gate_b, *refs
):
    lane_ref, tv_ref, *vec_refs, ge_ref, small_ref, proj_sum, bias_sum = refs
    vec_refs, line_refs = vec_refs[: len(vec_refs) // 2], vec_refs[len(vec_refs) // 2 :]
    index = pl.program_id(0)
    last = pl.num_programs(0) - 1
    first = ints[ROLE] == 0
    at_home = jnp.where(ints[CORE] == ints[ROLE], 1.0, 0.0)
    mine_half = index == ints[ROLE]

    @pl.when(index == 0)
    def _():
        for ref in (proj_sum, bias_sum):
            ref[...] = jnp.zeros_like(ref)

    grad_mixed = at_home * jnp.where(
        mine_half,
        gb_ref[...] + own_ref[...] + other_in_ref[...].astype(f32),
        gb_in_ref[...].astype(f32) + other_ref[...] + own_in_ref[...].astype(f32),
    )
    bias_sum[0:1, :] += jnp.sum(grad_mixed, axis=0, keepdims=True)
    low = grad_mixed.astype(bf16)
    proj_sum[...] += tn(low, ev_ref[...])
    ge_ref[...] = nn(low, proj_ref[...]).astype(bf16)

    @pl.when(index == last)
    def _():
        e_in = proj_sum.shape[1]
        vectors = jnp.concatenate(
            [r[k, 0:3, :] for r in vec_refs for k in range(r.shape[0])], axis=0
        )
        rows = jnp.concatenate(
            [
                jnp.zeros((32, D), f32),
                jnp.where(first, vectors, 0.0),
                jnp.where(first, 0.0, vectors),
                bias_sum[0:1, :],
                *hidden_lines(ints, lane_ref, tv_ref, line_refs),
                jnp.zeros((31, D), f32),
            ],
            axis=0,
        )
        small_ref[:, :e_in] = proj_sum[...].astype(bf16)
        small_ref[:, e_in : e_in + DOM * TW] = tower_ref[...].astype(bf16)
        small_ref[:, e_in + DOM * TW :] = (gate_a[...] + gate_b[...] + jnp.transpose(rows)).astype(bf16)


def call_finish(
    ints, gb, gb_in, own, other, own_in, other_in, events, proj_t, tower, gate_a, gate_b, lanes, tower_vec, sums
):
    rows, e_in = events.shape
    half = rows // 2

    def tile(width):
        return pl.BlockSpec((half, width), lambda i, *_: (i, 0))

    halves = (gb, gb_in, own, other, own_in, other_in)
    wholes = (proj_t, tower, gate_a, gate_b, lanes, tower_vec)
    vecs = [v for v, _ in sums] + [b for _, b in sums]
    return pl.pallas_call(
        finish_kernel,
        grid_spec=pltpu.PrefetchScalarGridSpec(
            num_scalar_prefetch=1,
            grid=(2,),
            in_specs=[fixed(a.shape) for a in halves]
            + [tile(e_in)]
            + [fixed(a.shape) for a in (*wholes, *vecs)],
            out_specs=(tile(e_in), fixed((D, PACK))),
            scratch_shapes=[pltpu.VMEM((D, e_in), f32), pltpu.VMEM((8, D), f32)],
        ),
        out_shape=(jax.ShapeDtypeStruct((rows, e_in), bf16), jax.ShapeDtypeStruct((D, PACK), bf16)),
        compiler_params=params(),
        cost_estimate=pl.CostEstimate(flops=4 * rows * D * e_in, bytes_accessed=14_000_000, transcendentals=0),
        name="finish",
    )(ints, *halves, events, *wholes, *vecs)


VECTOR_ROW = {j: 32 + 18 * r + 3 * i for r, row in enumerate(SETS) for i, j in enumerate(row)}


def small_kernel(*refs):
    parts, vec_refs = refs[:-12], refs[-3:]
    proj_ref, tower_ref, top_ref, shared_ref, domain_ref, bias_ref, hidden_ref, tb_ref, to_ref = refs[-12:-3]
    added = functools.reduce(jnp.add, [p[...].astype(f32) for p in parts])
    width, e_in = proj_ref.shape
    proj_ref[...] = added[:, :e_in]
    for d in range(DOM):
        tower_ref[d] = added[:, e_in + d * TW : e_in + (d + 1) * TW]
    rows = jnp.concatenate([added[:, e_in + DOM * TW :], jnp.zeros((128 - width, 128), f32)], axis=0)
    rows = jnp.transpose(rows)[:, :width]
    for ref, low, size in ((top_ref, 0, 2), (shared_ref, 2 * DOM, S), (domain_ref, (2 + S) * DOM, K)):
        for d in range(DOM):
            ref[d] = rows[low + d * size : low + (d + 1) * size]
    bias_ref[...] = rows[68:69]
    hidden_ref[:, :width] = rows[69:81]
    hidden_ref[:, width:] = rows[81:93]
    tb_ref[...] = rows[93:97, : width // 2]
    to_ref[...] = rows[93:97, width // 2 :]
    for which, ref in enumerate(vec_refs):
        for j in range(2 * LOCAL):
            ref[j : j + 1, :] = rows[VECTOR_ROW[j] + which : VECTOR_ROW[j] + which + 1]


def call_small(parts):
    width = parts[0].shape[0]
    e_in = PACK - DOM * TW - 128
    shapes = [(width, e_in), (DOM, width, TW), (DOM, 2, width), (DOM, S, width), (DOM, K, width), (1, width)]
    shapes += [(2 * LOCAL, 2 * width), (DOM, width // 2), (DOM, width // 2)]
    shapes += [(2 * LOCAL, width)] * 3
    return pl.pallas_call(
        small_kernel,
        grid=(1,),
        in_specs=[fixed(p.shape) for p in parts],
        out_specs=tuple(fixed(shape) for shape in shapes),
        out_shape=tuple(jax.ShapeDtypeStruct(shape, f32) for shape in shapes),
        compiler_params=params(),
        name="small",
    )(*parts)


def place_kernel(ints, *refs):
    *parts, in_ref, out_ref = refs
    half = len(parts) // 2
    first = ints[ROLE] == 0
    for chunk, (own, other) in enumerate(zip(parts[:half], parts[half:])):
        for place, expert in enumerate(CHUNKS[chunk]):
            for which, ref in enumerate((in_ref, out_ref)):
                a, b = own[which, place].astype(f32), other[which, place].astype(f32)
                ref[SETS[0][expert]] = jnp.where(first, a, b)
                ref[SETS[1][expert]] = jnp.where(first, b, a)


def call_place(ints, own, other):
    rows, width = own[0].shape[2:]
    shape = (2 * LOCAL, rows, width)
    return pl.pallas_call(
        place_kernel,
        grid_spec=pltpu.PrefetchScalarGridSpec(
            num_scalar_prefetch=1,
            grid=(1,),
            in_specs=[fixed(a.shape) for a in (*own, *other)],
            out_specs=(fixed(shape), fixed(shape)),
        ),
        out_shape=(jax.ShapeDtypeStruct(shape, f32),) * 2,
        compiler_params=params(),
        name="place",
    )(ints, *own, *other)


def params():
    return pltpu.CompilerParams(vmem_limit_bytes=VMEM_LIMIT)


def fixed(shape):
    return pl.BlockSpec(shape, lambda i, *_: (0,) * len(shape))


def pack_kernel(proj_ref, tower_ref, *refs):
    *row_refs, in_bias_ref, tower_b_ref, tower_out_ref, out_ref = refs
    width, e_in = proj_ref.shape
    out_ref[:, :e_in] = proj_ref[...]
    for d in range(DOM):
        out_ref[:, e_in + d * TW : e_in + (d + 1) * TW] = tower_ref[d]
    rows = [r[...].astype(f32) for r in row_refs]
    bias = in_bias_ref[...].astype(f32)
    rows += [bias[:, :width], bias[:, width:]]
    rows.append(
        jnp.concatenate([tower_b_ref[...].astype(f32), tower_out_ref[...].astype(f32)], axis=1)
    )
    rows = jnp.concatenate(rows + [jnp.zeros((31, width), f32)], axis=0)
    rows = jnp.concatenate([rows, jnp.zeros((128, 128 - width), f32)], axis=1)
    out_ref[:, e_in + DOM * TW :] = jnp.transpose(rows)[:width].astype(bf16)


def call_pack(*arrays):
    width = arrays[0].shape[0]
    return pl.pallas_call(
        pack_kernel,
        grid=(1,),
        in_specs=[fixed(a.shape) for a in arrays],
        out_specs=fixed((width, PACK)),
        out_shape=jax.ShapeDtypeStruct((width, PACK), bf16),
        compiler_params=params(),
        name="pack",
    )(*arrays)


def choose_kernel(own_ids, other_ids, in_own, out_own, in_other, out_other, own_ref, other_ref):
    own_ref[0], own_ref[1] = in_own[...], out_own[...]
    other_ref[0], other_ref[1] = in_other[...], out_other[...]


def call_choose(own_ids, other_ids, w_in, w_out_t):
    block = (1,) + w_in.shape[1:]
    shape = jax.ShapeDtypeStruct((2, own_ids.shape[0]) + w_in.shape[1:], bf16)
    own = pl.BlockSpec(block, lambda i, a, b: (a[i], 0, 0))
    other = pl.BlockSpec(block, lambda i, a, b: (b[i], 0, 0))
    out = pl.BlockSpec((2,) + block, lambda i, a, b: (0, i, 0, 0))
    return pl.pallas_call(
        choose_kernel,
        grid_spec=pltpu.PrefetchScalarGridSpec(
            num_scalar_prefetch=2, grid=(own_ids.shape[0],), in_specs=[own, own, other, other], out_specs=(out, out)
        ),
        out_shape=(shape, shape),
        compiler_params=params(),
        cost_estimate=pl.CostEstimate(flops=0, bytes_accessed=2_000_000, transcendentals=0),
        name="choose",
    )(own_ids, other_ids, w_in, w_out_t, w_in, w_out_t)


def call_prepare(ints, floats, table, embeds, proj_t, gates, vec):
    rows = embeds.shape[0]
    tiles = rows // TILE
    e_in = embeds.shape[1]

    def tile(width):
        return pl.BlockSpec((TILE, width), lambda i, *_: (i, 0))

    return pl.pallas_call(
        prepare_kernel,
        grid_spec=pltpu.PrefetchScalarGridSpec(
            num_scalar_prefetch=2,
            grid=(tiles,),
            in_specs=[fixed(table.shape), fixed(embeds.shape), fixed(proj_t.shape), fixed(gates.shape), fixed(vec.shape)],
            out_specs=(
                tile(e_in),
                tile(D),
                tile(D),
                tile(128),
                pl.BlockSpec((8, TILE), lambda i, *_: (0, i)),
            ),
        ),
        out_shape=(
            jax.ShapeDtypeStruct((rows, e_in), bf16),
            jax.ShapeDtypeStruct((rows, D), bf16),
            jax.ShapeDtypeStruct((rows, D), f32),
            jax.ShapeDtypeStruct((rows, 128), f32),
            jax.ShapeDtypeStruct((8, rows), f32),
        ),
        compiler_params=params(),
        cost_estimate=pl.CostEstimate(
            flops=2 * rows * e_in * (rows + D), bytes_accessed=12_000_000, transcendentals=rows * 8
        ),
        name="prepare",
    )(ints, floats, table, embeds, proj_t, gates, vec)


def half_spec(own, shape):
    rest = (0,) * (len(shape) - 1)
    return pl.BlockSpec(shape, lambda i, ints: ((ints[ROLE] if own else 1 - ints[ROLE]),) + rest)


def piece_spec(array, place):
    a, b, _, rows, width = array.shape
    return pl.BlockSpec((a, b, 1, rows, width), lambda i, *_: (0, 0, place(i), 0, 0))


MATRICES = [pltpu.VMEM((D, HALF), bf16)] * 4


def call_forward(experts, own, ints, x, weights, bi, vec, cols, mix, norms):
    rows = x.shape[0]
    half = rows // 2
    arrays = sorted({e // 3 for e in experts})
    first = {a: min(k for k, e in enumerate(experts) if e // 3 == a) for a in arrays}
    number = {a: sum(1 for e in experts if e // 3 == a) for a in arrays}

    def place(a):
        return lambda i: jnp.clip(i - first[a], 0, number[a] - 1)

    weight_specs = [piece_spec(w, place(a)) for a in arrays for w in weights[a]]
    norm_specs = [
        pl.BlockSpec(
            (1, half, D),
            lambda i, ints, a=a: (place(a)(i), ints[ROLE] if own else 1 - ints[ROLE], 0),
        )
        for a in arrays
    ]
    kept = [norms[a] for a in arrays if a in norms]
    inputs = [x] + [w for a in arrays for w in weights[a]] + [bi, vec, cols, mix] + kept
    at = len(inputs) - len(kept)
    aliases = {at - 1: 0, at: 1}
    aliases.update({at + 1 + k: 2 + k for k in range(len(kept))})
    shared = sum(1 for e in experts if e < 2)
    out = pl.pallas_call(
        functools.partial(forward_kernel, experts, own, len(kept), len(weights[arrays[0]])),
        grid_spec=pltpu.PrefetchScalarGridSpec(
            num_scalar_prefetch=1,
            grid=(len(experts),),
            in_specs=[half_spec(own, (half, D))]
            + weight_specs
            + [fixed(bi.shape), fixed(vec.shape), half_spec(own, (half, 128)), half_spec(own, (half, D))]
            + [pl.BlockSpec(memory_space=pl.ANY)] * len(kept),
            out_specs=(half_spec(own, (half, 128)), half_spec(own, (half, D)), *norm_specs),
            scratch_shapes=MATRICES,
        ),
        out_shape=(
            jax.ShapeDtypeStruct((rows, 128), f32),
            jax.ShapeDtypeStruct((rows, D), f32),
            *[jax.ShapeDtypeStruct((3, rows, D), bf16)] * len(arrays),
        ),
        input_output_aliases=aliases,
        compiler_params=params(),
        cost_estimate=pl.CostEstimate(
            flops=4 * (shared + 1) * half * D * H, bytes_accessed=12_000_000, transcendentals=0
        ),
        name="experts_forward",
    )(ints, *inputs)
    return out[0], out[1], {**norms, **dict(zip(arrays, out[2:]))}


def call_backward(experts, halves, ints, x, gbs, norms, weights, bi, vec, cols, back, sums=None):
    rows, count = x.shape[0], len(experts)
    part = rows // 2 * len(halves)
    array, low = experts[0] // 3, experts[0] % 3
    split = any(e // 3 != array for e in experts)

    def span(width):
        if len(halves) == 2:
            return fixed((rows, width))
        return half_spec(halves[0] == "own", (part, width))

    def norm_index(i, ints):
        if len(halves) == 2:
            return (low + i, 0, 0)
        return (low + i, ints[ROLE] if halves[0] == "own" else 1 - ints[ROLE], 0)

    assert not split
    pairs = pl.BlockSpec((1, 2, D, HALF), lambda i, *_: (i, 0, 0, 0))
    vec_spec = pl.BlockSpec((1, 8, D), lambda i, *_: (i, 0, 0))
    bi_spec = pl.BlockSpec((1, 8, H), lambda i, *_: (i, 0, 0))
    mode, back_array = back if back is not None else ("fresh", jnp.zeros((8, 128), f32))
    inputs = [x, *gbs, norms[array], *weights[array], bi, vec, cols, back_array]
    in_specs = (
        [span(D)]
        + [fixed(g.shape) for g in gbs]
        + [pl.BlockSpec((1, part, D), norm_index)]
        + [piece_spec(w, lambda i: low + i) for w in weights[array]]
        + [fixed(bi.shape), fixed(vec.shape), span(128)]
        + [span(D) if mode == "add" else pl.BlockSpec(memory_space=pl.ANY)]
    )
    aliases = {len(inputs) - 1: 0}
    if back is not None:
        aliases[len(inputs)] = 1
    if sums is not None:
        inputs += list(sums)
        in_specs += [vec_spec, bi_spec]
    return pl.pallas_call(
        functools.partial(
            backward_kernel, experts, halves, mode == "add", sums is not None, len(weights[array])
        ),
        grid_spec=pltpu.PrefetchScalarGridSpec(
            num_scalar_prefetch=1,
            grid=(count,),
            in_specs=in_specs,
            out_specs=(span(128), span(D), pairs, pairs, vec_spec, bi_spec),
            scratch_shapes=[pltpu.VMEM((D, HALF), f32)] * 4 + MATRICES,
        ),
        out_shape=(
            jax.ShapeDtypeStruct((rows, 128), f32),
            jax.ShapeDtypeStruct((rows, D), f32),
            jax.ShapeDtypeStruct((count, 2, D, HALF), bf16),
            jax.ShapeDtypeStruct((count, 2, D, HALF), bf16),
            jax.ShapeDtypeStruct((count, 8, D), f32),
            jax.ShapeDtypeStruct((count, 8, H), f32),
        ),
        input_output_aliases=aliases,
        compiler_params=params(),
        cost_estimate=pl.CostEstimate(
            flops=10 * count * (rows // 2) * D * H, bytes_accessed=20_000_000, transcendentals=0
        ),
        name="experts_backward",
    )(ints, *inputs)


def call_tower(ints, mix, other, cols, tower, tower_vec):
    rows = other.shape[0]
    tiles = rows // TILE

    def kept(width):
        return pl.BlockSpec((TILE, width), lambda i, ints: (ints[ROLE] * tiles + i, 0))

    def tile(width):
        return pl.BlockSpec((TILE, width), lambda i, *_: (i, 0))

    return pl.pallas_call(
        tower_kernel,
        grid_spec=pltpu.PrefetchScalarGridSpec(
            num_scalar_prefetch=1,
            grid=(tiles,),
            in_specs=[kept(D), tile(D), kept(128), fixed(tower.shape), fixed(tower_vec.shape)],
            out_specs=(
                pl.BlockSpec((8, TILE), lambda i, *_: (0, i)),
                tile(D),
                tile(D),
                fixed((D, DOM * TW)),
                fixed((8, DOM * TW)),
                fixed((8, 128)),
            ),
        ),
        out_shape=(
            jax.ShapeDtypeStruct((8, rows), f32),
            jax.ShapeDtypeStruct((rows, D), f32),
            jax.ShapeDtypeStruct((rows, D), bf16),
            jax.ShapeDtypeStruct((D, DOM * TW), f32),
            jax.ShapeDtypeStruct((8, DOM * TW), f32),
            jax.ShapeDtypeStruct((8, 128), f32),
        ),
        compiler_params=params(),
        cost_estimate=pl.CostEstimate(
            flops=6 * rows * D * DOM * TW, bytes_accessed=10_000_000, transcendentals=rows * DOM * TW
        ),
        name="towers",
    )(ints, mix, other, cols, tower, tower_vec)


def per_device(
    box,
    embeds,
    domain,
    frozen,
    labels,
    proj_w,
    proj_b,
    w_in,
    in_bias,
    w_out,
    out_bias,
    ln_gain,
    ln_shift,
    gate_top,
    gate_shared,
    gate_domain,
    tower_w,
    tower_b,
    tower_out,
    tower_out_b,
):
    core = lax.axis_index("tensor")
    role = box.role(lax.axis_index("dp"))
    at_home = core == role
    places = box.count
    rows = embeds.shape[0]
    half_rows = rows // 2
    width = proj_w.shape[1]
    e_in = proj_w.shape[0]
    place_of = box.places()
    nz, ny, nx = box.dims[1:]
    sets = jnp.array(SETS, jnp.int32)
    set_own, set_other = sets[role], sets[1 - role]

    def half(values, which, axis=0):
        return lax.dynamic_slice_in_dim(values, which * half_rows, half_rows, axis)

    w_out_t = jnp.swapaxes(w_out, 1, 2)
    first = call_choose(set_own[:3], set_other[:3], w_in, w_out_t)
    second = call_choose(set_own[3:], set_other[3:], w_in, w_out_t)

    arrays = (
        proj_w.T,
        tower_w,
        jnp.swapaxes(gate_top, 1, 2).reshape(2 * DOM, width),
        jnp.swapaxes(gate_shared, 1, 2).reshape(S * DOM, width),
        jnp.swapaxes(gate_domain, 1, 2).reshape(K * DOM, width),
        out_bias,
        ln_gain,
        ln_shift,
        proj_b[None],
        in_bias,
        tower_b,
        tower_out,
    )
    first_z = box.line(first)
    pack = call_pack(*step(arrays, first_z[0])[0])
    pack_z = box.line((pack, pack))
    first, first_z, second = step(first, first_z, second)

    def along_z(shard, found):
        found = box.in_line(shard[0], found, role, 2)
        return jnp.stack([b[0] for b in found]), jnp.stack([b[1] for b in found])

    first_i, first_o = along_z(first, first_z)
    first_iy, first_ox = box.pieces(first_i, "y"), box.pieces(first_o, "x")
    second_z = box.line(second)
    pack = step(jnp.concatenate(box.in_line(pack, pack_z, role, 0)), second_z[0])[0]
    pack = jnp.concatenate(box.gather_plane(pack), axis=0).reshape(places, 1, width, PACK)
    event_rows = jnp.concatenate(
        [domain.astype(f32).T, labels.astype(f32)[None], jnp.zeros((6, rows), f32)]
    )
    event_rows = jnp.where(at_home, event_rows, box.to_partner(event_rows, True))
    ids = event_rows[0]
    onehot = (ids[None, :] == jnp.arange(DOM, dtype=f32)[:, None]).astype(f32)
    rank = jnp.cumsum(onehot, axis=1)
    counts = rank[:, -1]
    ends = jnp.cumsum(counts)
    starts = ends - counts
    position = jnp.sum(onehot * (rank + starts[:, None]), axis=0) - 1.0
    embeds_in = box.to_partner(step(embeds, event_rows)[0], True)
    first_i, first_o, first_iy, first_ox, second, second_z, starts, ends, position = step(
        first_i, first_o, first_iy, first_ox, second, second_z, starts, ends, position
    )

    small = in_order(core, pack, swap_cores(pack), 1).reshape(D, PACK)
    first_i = jnp.stack([first_i] + first_iy)
    first_o = jnp.stack([first_o] + first_ox)
    first_ix, first_oy = box.pieces(first_i, "x"), box.pieces(first_o, "y")
    second_i, second_o = along_z(second, second_z)
    second_iy, second_ox = box.pieces(second_i, "y"), box.pieces(second_o, "x")

    proj_t = small[:, :e_in]
    tower = small[:, e_in : e_in + DOM * TW]
    gates = small[:, e_in + DOM * TW :]
    picked = jnp.concatenate(
        [
            32 + set_own,
            44 + set_own,
            56 + set_own,
            jnp.array([68] + [128] * 5),
            69 + set_own,
            81 + set_own,
            93 + jnp.arange(4),
        ]
    )
    choose = (picked[:, None] == jnp.arange(128)[None, :]).astype(bf16)
    vec = nt(choose, gates)
    blocks = jnp.take(vec[24:].reshape(16, places, 2 * width), place_of, axis=1)
    bi = (
        blocks[:12]
        .reshape(2, LOCAL, places, 2, width)
        .transpose(1, 2, 3, 0, 4)
        .reshape(LOCAL, H)
    )
    bi = jnp.pad(bi, ((0, 2), (0, 0)))
    bi = jnp.where(core == 0, bi, jnp.concatenate([bi[:, HALF:], bi[:, :HALF]], axis=1))
    tower_vec = (
        blocks[12:]
        .reshape(DOM, places, 2, 2, width // 2)
        .transpose(3, 0, 1, 2, 4)
        .reshape(2, DOM * TW)
    )
    tower_vec = jnp.pad(tower_vec, ((0, 6), (0, 0)))

    table = jnp.concatenate([position[None], event_rows[1:]])
    start_i, end_i = starts.astype(jnp.int32), ends.astype(jnp.int32)
    empty = end_i == start_i
    low = jnp.where(empty, 0, start_i // TILE)
    high = jnp.where(empty, 0, (end_i + TILE - 1) // TILE)
    domains = jnp.arange(DOM, dtype=jnp.int32)
    device = (2 * box.ahead()[:, None, None] + jnp.arange(2)[None, :, None]).astype(jnp.int32)
    unit = jnp.arange(width, dtype=jnp.int32)[None, None, :]
    narrow = width // 2
    lanes = [device * 2 * width + unit, device * 2 * width + width + unit]
    lanes += [d * TW + device * narrow + unit % narrow for d in range(DOM)]
    lanes += [jnp.broadcast_to(unit // narrow, (places, 2, width))] * 2
    lanes = jnp.stack([jnp.broadcast_to(v, (places, 2, width)).reshape(D) for v in lanes])

    ints = jnp.concatenate(
        [
            jnp.where(role == 0, low[::-1], low),
            jnp.where(role == 0, high[::-1], high),
            role[None],
            jnp.where(role == 0, DOM - 1 - domains, domains),
            start_i,
            end_i,
            core[None],
            jnp.zeros((2,), jnp.int32),
        ]
    )
    loss_weight = 1.0 - (1.0 - FROZEN_SHARE) * frozen.astype(f32)
    floats = jnp.concatenate([loss_weight, tower_out_b.astype(f32)])
    embeds = jnp.where(at_home, embeds, embeds_in)
    events, x, mix, cols, probs = call_prepare(ints, floats, table, embeds, proj_t, gates, vec)
    (
        first_i, first_o, first_ix, first_oy, second_i, second_o, second_iy, second_ox,
        ints, events, x, mix, cols, probs, vec, bi, tower, tower_vec, lanes,
    ) = step(
        first_i, first_o, first_ix, first_oy, second_i, second_o, second_iy, second_ox,
        ints, events, x, mix, cols, probs, vec, bi, tower, tower_vec, lanes,
    )

    def pieces(i, ix, o, oy):
        own = [i] + ix + [o] + oy
        return own + [swap_cores(w) for w in own]

    second_i = jnp.stack([second_i] + second_iy)
    second_o = jnp.stack([second_o] + second_ox)
    second_ix, second_oy = box.pieces(second_i, "x"), box.pieces(second_o, "y")
    weights = {0: pieces(first_i, first_ix, first_o, first_oy)}
    cols, mix, norms = call_forward((0, 1, 2), False, ints, x, weights, bi, vec, cols, mix, {})
    second_ix, second_oy, cols, mix = step(second_ix, second_oy, cols, mix)
    weights[1] = pieces(second_i, second_ix, second_o, second_oy)
    cols, mix, norms = call_forward((3, 4), False, ints, x, weights, bi, vec, cols, mix, norms)
    give_mix = half(mix, 1 - role).astype(bf16)
    give_mix, mix = step(give_mix, mix)
    other_mix = box.send(give_mix, flip=1)
    cols, mix, norms = call_forward(
        tuple(range(LOCAL)), True, ints, x, weights, bi, vec, cols, mix, norms
    )
    row_out, grad_block, grad_low, d_tower, d_tower_vec, d_logit_bias = call_tower(
        ints, mix, other_mix, cols, tower, tower_vec
    )

    box_shape = (nx, ny, nz, 2, 2 * width, HALF)

    def both_cores(keeps, gives):
        def one(which):
            added = total(keeps[0][:, which], [a[:, which] for a in keeps[1:] + gives])
            return added.astype(bf16).reshape((-1,) + box_shape)

        return one(0), one(1)

    class Scatter:
        def __init__(self, *parts):
            i, o = [jnp.concatenate(p) for p in zip(*parts)]
            i, o = [i[:, k] for k in range(nx)], [o[:, :, k] for k in range(ny)]
            self.state = (i[0], o[0], box.hand_out(i, "x"), box.hand_out(o, "y"))

        def second(self):
            i, o, i_in, o_in = self.state
            i, o = total(i, i_in).astype(bf16), total(o, o_in).astype(bf16)
            i, o = [i[:, k] for k in range(ny)], [o[:, k] for k in range(nx)]
            self.state = (i[0], o[0], box.hand_out(i, "y"), box.hand_out(o, "x"))

        def third(self):
            i, o, i_in, o_in = self.state
            both = jnp.stack([total(i, i_in).astype(bf16), total(o, o_in).astype(bf16)])
            both = [both[:, :, k] for k in range(nz)]
            self.state = (both[0], box.hand_out(both, "z"))

        def fourth(self):
            both = total(*self.state)
            mine = lax.dynamic_index_in_dim(both, role, 2, keepdims=False)
            other = lax.dynamic_index_in_dim(both, 1 - role, 2, keepdims=False).astype(bf16)
            self.state = (mine, box.send(other, flip=1))

    def sync(scatters, *values):
        states, values = step([c.state for c in scatters], values)
        for c, state in zip(scatters, states):
            c.state = state
        return values

    common = (ints, x)
    shared = (norms, weights, bi, vec)
    grad_in = box.send(grad_low, flip=1)
    cols, back, keep_a, give_a, *sums = call_backward(
        (0, 1), ("own",), *common, [grad_low], *shared, cols, None
    )
    d_logit_bias = d_logit_bias + swap_cores(d_logit_bias)
    d_logit_bias = box.same_sum(box.same_sum(d_logit_bias, "y"), "x")
    grad_in, cols, back, keep_a, give_a, sums, d_logit_bias = step(
        grad_in, cols, back, keep_a, give_a, sums, d_logit_bias
    )
    give_a = swap_cores(give_a)
    cols, back, keep_b, give_b, *sums_0 = call_backward(
        (0, 1), ("other",), *common, [grad_in], *shared, cols, ("fresh", back), sums
    )
    d_logit_bias = box.same_sum(box.same_sum(d_logit_bias, "flip"), "z")
    cols, back, keep_a, give_a, keep_b, give_b, d_logit_bias = step(
        cols, back, keep_a, give_a, keep_b, give_b, d_logit_bias
    )
    give_b = swap_cores(give_b)
    grads = [grad_low, grad_in]
    cols, back, keep_c, give_c, *sums_1 = call_backward(
        (2,), ("own", "other"), *common, grads, *shared, cols, ("add", back)
    )
    cols, back, keep_b, give_b, keep_c, give_c, row_out, d_logit_bias = step(
        cols, back, keep_b, give_b, keep_c, give_c, row_out, d_logit_bias
    )
    give_c = swap_cores(give_c)
    ab = both_cores([keep_a, keep_b], [give_a, give_b])
    give_c, keep_c, ab, cols = step(give_c, keep_c, ab, cols)
    c0 = Scatter(ab, both_cores([keep_c], [give_c]))
    cols, back, keep_d, give_d, *sums_2 = call_backward(
        (3, 4), ("own", "other"), *common, grads, *shared, cols, ("add", back)
    )
    rows_in = box.to_partner(row_out, False)
    cols, back, keep_d, give_d, rows_in = sync([c0], cols, back, keep_d, give_d, rows_in)
    c0.second()
    give_d = swap_cores(give_d)
    cols, back, _ = step(cols, back, c0.state[:2])
    g_other, g_other_low, d_gate_a = call_gate(False, ints, back, cols, probs, x, gates)
    back_other = box.to_partner(g_other_low, False)
    cols, back, _ = step(cols, back, g_other_low)
    cols, back, keep_e, give_e, *sums_3 = call_backward(
        (5,), ("own",), *common, [grad_low], *shared, cols, ("add", back)
    )
    cd = both_cores([keep_d], [give_d])
    cols, back, back_other, cd, keep_e, give_e = sync(
        [c0], cols, back, back_other, cd, keep_e, give_e
    )
    give_e = swap_cores(give_e)
    c0.third()
    c1 = Scatter(cd, both_cores([keep_e], [give_e]))
    g_own, g_own_low, d_gate_b = call_gate(True, ints, back, cols, probs, x, gates)
    back_own = box.to_partner(g_own_low, False)
    back_own, g_own, d_gate_b = sync([c0, c1], back_own, g_own, d_gate_b)
    c0.fourth()
    c1.second()
    back_own, _ = step(back_own, c1.state[:2])
    grad_events, d_small = call_finish(
        ints, grad_block, grad_in, g_own, g_other, back_own, back_other, events, proj_t, d_tower,
        d_gate_a, d_gate_b, lanes, d_tower_vec, [sums_0, sums_1, sums_2, sums_3],
    )
    grad_events, d_small = sync([c0, c1], grad_events, d_small)
    c1.third()
    d_small, _ = step(d_small, c1.state[0])
    d_small = d_small.reshape(places, 2, width, PACK)
    d_other = swap_cores(lax.dynamic_index_in_dim(d_small, 1 - core, 1, keepdims=False))
    d_mine = total(lax.dynamic_index_in_dim(d_small, core, 1, keepdims=False), [d_other])
    d_mine = d_mine.astype(bf16).reshape(nx * ny, nz, 2, width, PACK)
    d_parts = [d_mine[k] for k in range(nx * ny)]
    d_in = box.hand_out_plane(d_parts)
    order = position[None, :] == jnp.arange(rows, dtype=f32)[:, None]
    grad_embeds = lax.dot_general(
        order.astype(bf16), grad_events, (((0,), (0,)), ((), ())), preferred_element_type=f32
    ).astype(bf16)
    predicted = in_order(role, row_out, rows_in, 1)
    predictions = jnp.sum(jnp.where(order, predicted[0][:, None], 0.0), axis=0)
    predictions = jnp.broadcast_to(predictions[None], (8, rows))
    d_mine, d_in, grad_embeds, predictions = sync(
        [c0, c1], d_parts[0], d_in, grad_embeds, predictions
    )
    c1.fourth()
    d_mine = total(d_mine, d_in).astype(bf16)
    same = [lax.dynamic_index_in_dim(d_mine[k], role, 0, keepdims=False) for k in range(nz)]
    flip = [lax.dynamic_index_in_dim(d_mine[k], 1 - role, 0, keepdims=False) for k in range(nz)]
    d_in = box.hand_out(same, "z") + box.hand_out_flip(flip)
    grad_embeds = jnp.where(at_home, grad_embeds, swap_cores(grad_embeds))
    predictions = jnp.where(at_home, predictions, swap_cores(predictions))[0]
    d_in, grad_embeds, predictions = sync([c1], d_in, grad_embeds, predictions)
    (
        proj_grad, tower_grad, top, shared_gate, domain_gate, proj_b_grad, in_bias_grad, tower_b_grad,
        tower_out_grad, *vectors,
    ) = call_small([same[0]] + d_in)
    grad_w_in, grad_w_out = call_place(
        ints, [c0.state[0], c1.state[0]], [c0.state[1], c1.state[1]]
    )
    return (
        predictions,
        grad_embeds,
        proj_grad.T,
        proj_b_grad[0],
        grad_w_in,
        in_bias_grad,
        jnp.swapaxes(grad_w_out, 1, 2),
        *vectors,
        jnp.swapaxes(top, 1, 2),
        jnp.swapaxes(shared_gate, 1, 2),
        jnp.swapaxes(domain_gate, 1, 2),
        tower_grad,
        tower_b_grad,
        tower_out_grad,
        d_logit_bias[0, :DOM],
    )


def solution(mesh):
    both = ("dp", "tensor")
    in_specs = (
        P("dp", None),
        P("dp", None),
        P(),
        P("dp"),
        P(None, both),
        P(both),
        P(None, "dp", "tensor"),
        P(None, both),
        P(None, "tensor", "dp"),
        P(None, both),
        P(None, both),
        P(None, both),
        P(None, both, None),
        P(None, both, None),
        P(None, both, None),
        P(None, both, None),
        P(None, both),
        P(None, both),
        P(),
    )
    out_specs = (
        P("dp"),
        P("dp", None),
        P(None, both),
        P(both),
        P(None, "dp", "tensor"),
        P(None, both),
        P(None, "tensor", "dp"),
        P(None, both),
        P(None, both),
        P(None, both),
        P(None, both, None),
        P(None, both, None),
        P(None, both, None),
        P(None, both, None),
        P(None, both),
        P(None, both),
        P(),
    )
    return jax.shard_map(
        functools.partial(per_device, Box(mesh.shape["dp"])),
        mesh=mesh,
        in_specs=in_specs,
        out_specs=out_specs,
        check_vma=False,
    )
```

```python
import functools
import math

import jax
import jax.numpy as jnp
import numpy as np
from jax import lax
from jax.experimental import pallas as pl
from jax.experimental.pallas import tpu as pltpu
from jax.sharding import PartitionSpec as P

D = 512
H = 1024
HALF = H // 2
TW = 256
S = 4
DOM = 4
K = 2
EPS = 1e-05
FROZEN_SHARE = 0.25
TILE = 256
LOCAL = 6
CHUNKS = ((0, 1, 2), (3, 4, 5))
VMEM_LIMIT = 48 * 1024 * 1024
PACK = 1792
SETS = (
    tuple(range(2)) + tuple(S + K * d for d in reversed(range(DOM))),
    tuple(range(2, 4)) + tuple(S + K * d + 1 for d in range(DOM)),
)
COEF, SCALE, DCOEF, DOMAIN, LABEL, WEIGHT, BIAS = 0, 6, 12, 18, 19, 20, 21
LOW, HIGH, ROLE, DOMAIN_OF, START, END, CORE = 0, 4, 8, 9, 13, 17, 21

bf16 = jnp.bfloat16
f32 = jnp.float32


def dims_of(count):
    if count % 4 == 0:
        rest = count // 4
        root = math.isqrt(rest)
        if root * root == rest:
            return (4, root, root)
    return (count, 1, 1)


class Box:
    def __init__(self, count):
        first, second, third = dims_of(count)
        self.count = count
        self.dims = (2, first // 2, second, third)
        self.strides = (second * third, 2 * second * third, third, 1)

    def role(self, chip):
        return (chip // self.strides[0]) % 2

    def partner(self, chip):
        return chip + (1 - 2 * self.role(chip)) * self.strides[0]

    def send(self, values, flip=0, z=0, y=0, x=0):
        pairs = []
        for chip in range(self.count):
            to = chip
            for step, size, stride in zip((flip, z, y, x), self.dims, self.strides):
                place = (chip // stride) % size
                to += ((place + step) % size - place) * stride
            pairs.append((chip, to))
        return lax.ppermute(values, "dp", pairs)

    def to_partner(self, values, home):
        pairs = []
        for chip in range(self.count):
            for core in range(2):
                if (core == self.role(chip)) == home:
                    pairs.append((2 * chip + core, 2 * self.partner(chip) + core))
        return lax.ppermute(values, ("dp", "tensor"), pairs)

    def pieces(self, values, dim):
        size = self.dims[("flip", "z", "y", "x").index(dim)]
        return [self.send(values, **{dim: -k}) for k in range(1, size)]

    def hand_out(self, parts, dim):
        return [self.send(part, **{dim: k}) for k, part in enumerate(parts) if k]

    def line(self, same, other):
        steps = range(1, self.dims[1])
        return [self.send(same, z=-z) for z in steps], [self.send(other, flip=1, z=-z) for z in steps]

    def in_line(self, own, flip, found, role, axis):
        same, other = found
        return [in_order(role, s, o, axis) for s, o in zip([own] + same, [flip] + other)]

    def hand_out_flip(self, parts):
        return [self.send(part, flip=1, z=k) for k, part in enumerate(parts)]

    def plane(self):
        _, _, ny, nx = self.dims
        return [(x, y) for x in range(nx) for y in range(ny)][1:]

    def gather_plane(self, values):
        return [values] + [self.send(values, y=-y, x=-x) for x, y in self.plane()]

    def hand_out_plane(self, parts):
        return [self.send(part, y=y, x=x) for part, (x, y) in zip(parts[1:], self.plane())]

    def same_sum(self, values, found, dim):
        number = ("flip", "z", "y", "x").index(dim)
        size, stride = self.dims[number], self.strides[number]
        found = jnp.stack([values] + found)
        if size > 2:
            mine = (lax.axis_index("dp") // stride) % size
            found = jnp.take(found, (jnp.arange(size) - mine) % size, axis=0)
        return functools.reduce(jnp.add, [found[k] for k in range(size)])

    def places(self):
        me = lax.axis_index("dp")
        chip = jnp.arange(self.count)
        place, weight = 0, 1
        for dim, (size, stride) in enumerate(zip(self.dims, self.strides)):
            mine = (me // stride) % size if dim else 0
            place = place + (((chip // stride) % size - mine) % size) * weight
            weight *= size
        return place

    def ahead(self):
        me = lax.axis_index("dp")
        place = jnp.arange(self.count)
        chip, weight = 0, 1
        for dim, (size, stride) in enumerate(zip(self.dims, self.strides)):
            mine = (me // stride) % size if dim else 0
            chip = chip + ((mine + (place // weight) % size) % size) * stride
            weight *= size
        return chip


def swap_cores(values):
    return lax.ppermute(values, "tensor", [(0, 1), (1, 0)])


def in_order(which, own, other, axis):
    return jnp.where(
        which == 0,
        jnp.concatenate([own, other], axis),
        jnp.concatenate([other, own], axis),
    )


def step(*values):
    return lax.optimization_barrier(values)


def total(first, arrived):
    return functools.reduce(jnp.add, [a.astype(f32) for a in arrived], first.astype(f32))


def gelu_parts(v):
    inner = math.sqrt(2.0 / math.pi)
    square = v * v
    th = jnp.tanh(v * (inner + inner * 0.044715 * square))
    half = 0.5 * (1.0 + th)
    act = v * half
    slope = half + 0.5 * v * (1.0 - th * th) * (inner + 3.0 * inner * 0.044715 * square)
    return act, slope


def nt(a, b):
    return lax.dot_general(a, b, (((1,), (1,)), ((), ())), preferred_element_type=f32)


def tn(a, b):
    return lax.dot_general(a, b, (((0,), (0,)), ((), ())), preferred_element_type=f32)


def nn(a, b):
    return jnp.dot(a, b, preferred_element_type=f32)


def softmax_rows(v):
    e = jnp.exp(v - jnp.max(v, axis=0, keepdims=True))
    return e / jnp.sum(e, axis=0, keepdims=True)


def prepare_kernel(ints, floats, rows_ref, embeds_ref, proj_ref, gates_ref, vec_ref, ev_ref, x_ref, mix_ref, cols_ref, prob_ref):
    tiles_of_half = pl.num_programs(0) // 2
    index = pl.program_id(0)
    role = ints[ROLE]
    count = rows_ref.shape[1]
    slot = index * TILE + lax.broadcasted_iota(jnp.int32, (TILE, count), 0)
    here = rows_ref[0:1, :].astype(jnp.int32) == slot
    order = jnp.where(here, 1.0, 0.0).astype(bf16)
    label = jnp.sum(jnp.where(here, rows_ref[1:2, :], 0.0), axis=1, keepdims=True)
    events = nn(order, embeds_ref[...]).astype(bf16)
    ev_ref[...] = events
    mixed = nt(events, proj_ref[...]) + vec_ref[3 * LOCAL : 3 * LOCAL + 1, :]
    low = mixed.astype(bf16)
    x_ref[...] = low
    mix_ref[...] = mixed * jnp.where(index // tiles_of_half == role, 1.0, 0.0)
    logits = jnp.transpose(nn(low, gates_ref[...]))
    place = index * TILE + lax.broadcasted_iota(jnp.int32, (1, TILE), 1)
    picks = [
        jnp.where((place >= ints[START + d]) & (place < ints[END + d]), 1.0, 0.0) for d in range(DOM)
    ]

    def pick(low_row, size):
        return softmax_rows(
            functools.reduce(
                jnp.add,
                [picks[d] * logits[low_row + d * size : low_row + (d + 1) * size] for d in range(DOM)],
            )
        )

    top, shared, domain = pick(0, 2), pick(2 * DOM, S), pick((2 + S) * DOM, K)
    prob_ref[...] = jnp.concatenate([top, shared, domain], axis=0)
    first = role == 0
    own_shared = top[0:1] * jnp.where(first, shared[:2], shared[2:])
    own_domain = top[1:2] * jnp.where(first, domain[0:1], domain[1:2])
    coef = [own_domain * jnp.where(first, picks[DOM - 1 - d], picks[d]) for d in range(DOM)]
    table = [
        own_shared,
        *coef,
        jnp.zeros((DOMAIN - SCALE, TILE), f32),
        sum(float(d) * picks[d] for d in range(DOM)),
        jnp.zeros((1, TILE), f32),
        sum(floats[d] * picks[d] for d in range(DOM)),
        sum(floats[DOM + d] * picks[d] for d in range(DOM)),
        jnp.zeros((128 - BIAS - 1, TILE), f32),
    ]
    cols_ref[...] = with_column(jnp.transpose(jnp.concatenate(table, axis=0)), LABEL, label)


def with_column(table, column, values):
    lane = lax.broadcasted_iota(jnp.int32, table.shape, 1)
    return jnp.where(lane == column, values, table)


def tiles_of(expert, ints, first, count):
    low = jnp.maximum(ints[LOW + expert - 2], first)
    high = jnp.minimum(ints[HIGH + expert - 2], first + count)
    return low - first, jnp.maximum(high, low) - first


def each_span(expert, ints, first, rows, work):
    if expert < 2:
        work(slice(0, rows))
    else:
        low, high = tiles_of(expert, ints, first, rows // TILE)

        def one(index, _):
            work(pl.ds(pl.multiple_of(index * TILE, TILE), TILE))
            return 0

        lax.fori_loop(low, high, one, 0)


def join(pieces, held):
    count = len(pieces) // 2
    for core in range(2):
        mine = pieces[core * count : core * count + count]
        by_x, by_y = split_pieces(mine)
        nx, ny = len(by_x), len(by_y)
        rows = by_x[0].shape[3]
        nz = by_x[0].shape[1]

        def at(x, y, z):
            return pl.ds(((x * ny + y) * nz + z) * rows, rows)

        for x in range(nx):
            for y in range(ny):
                for z in range(nz):
                    held[core][at(x, y, z), :] = by_x[x][y, z, 0]
                    held[2 + core][at(x, y, z), :] = by_y[y][x, z, 0]


def split_pieces(pieces):
    nx = pieces[-1].shape[0]
    return pieces[:nx], pieces[nx:]


def forward_kernel(experts, own, aliased, number, gives, ints, x_ref, *refs):
    arrays = sorted({e // 3 for e in experts})
    weights = {a: refs[number * k : number * (k + 1)] for k, a in enumerate(arrays)}
    refs = refs[number * len(arrays) :]
    refs, held = refs[:-4], refs[-4:]
    wi_a, wi_b, wo_a, wo_b = held
    bi_ref, vec_ref, cols_in, mix_in = refs[:4]
    cols_ref, mix_ref, *norm_refs = refs[4 + aliased :]
    if gives:
        *norm_refs, give_ref = norm_refs
    norm_refs = dict(zip(arrays, norm_refs))
    rows = x_ref.shape[0]
    half = ints[ROLE] if own else 1 - ints[ROLE]
    step = pl.program_id(0)

    @pl.when(step == 0)
    def _():
        cols_ref[...] = cols_in[...]
        mix_ref[...] = mix_in[...]

    def work(expert, span):
        x = x_ref[span, :]
        pre_a = nn(x, wi_a[...]) + bi_ref[expert : expert + 1, :HALF]
        act_a = gelu_parts(pre_a)[0].astype(bf16)
        pre_b = nn(x, wi_b[...]) + bi_ref[expert : expert + 1, HALF:]
        act_b = gelu_parts(pre_b)[0].astype(bf16)
        out = nt(act_a, wo_a[...]) + nt(act_b, wo_b[...]) + vec_ref[expert : expert + 1, :]
        centre = jnp.mean(out, axis=1, keepdims=True)
        centred = out - centre
        scale = lax.rsqrt(jnp.mean(centred * centred, axis=1, keepdims=True) + EPS)
        norm = centred * scale
        norm_refs[expert // 3][0, span, :] = norm.astype(bf16)
        cols = cols_ref[span, :]
        cols_ref[span, :] = with_column(cols, SCALE + expert, scale)
        gain = vec_ref[LOCAL + expert : LOCAL + expert + 1, :]
        shift = vec_ref[2 * LOCAL + expert : 2 * LOCAL + expert + 1, :]
        mix_ref[span, :] += cols[:, COEF + expert : COEF + expert + 1] * (norm * gain + shift)

    for place, expert in enumerate(experts):

        @pl.when(step == place)
        def _(expert=expert):
            join(weights[expert // 3], held)
            each_span(expert, ints, half * (rows // TILE), rows, functools.partial(work, expert))

    if gives:

        @pl.when(step == len(experts) - 1)
        def _():
            give_ref[...] = mix_ref[...].astype(bf16)


def backward_kernel(experts, halves, keeps_back, adds, number, ints, x_ref, *refs):
    gb_refs, refs = refs[: len(halves)], refs[len(halves) :]
    norm_ref, pieces, refs = refs[0], refs[1 : 1 + number], refs[1 + number :]
    bi_ref, vec_ref, cols_in = refs[:3]
    refs, held = refs[3:-4], refs[-4:]
    wi_a, wi_b, wo_a, wo_b = held
    join(pieces, held)
    back_in, refs = refs[0], refs[1:]
    if adds:
        dvec_in, dbi_in = refs[:2]
        refs = refs[2:]
    cols_ref, back_ref, keep_ref, give_ref, dvec_ref, dbi_ref, in_a, in_b, out_a, out_b = refs
    rows = x_ref.shape[0]
    half_tiles = rows // TILE // len(halves)
    first = 0 if len(halves) == 2 else (ints[ROLE] if halves[0] == "own" else 1 - ints[ROLE]) * half_tiles
    step = pl.program_id(0)

    @pl.when(step == 0)
    def _():
        cols_ref[...] = cols_in[...]
        back_ref[...] = back_in[...] if keeps_back else jnp.zeros_like(back_ref)

    dvec_ref[...] = dvec_in[...] if adds else jnp.zeros_like(dvec_ref)
    dbi_ref[...] = dbi_in[...] if adds else jnp.zeros_like(dbi_ref)

    def work(expert, span):
        whole = isinstance(span, slice)

        def add(ref, target, which, values):
            if whole:
                target[0, which] = values.astype(bf16)
            else:
                ref[...] += values

        x = x_ref[span, :]
        norm = norm_ref[0, span, :].astype(f32)
        cols = cols_ref[span, :]
        if len(halves) == 1:
            grad_block = gb_refs[0][span, :].astype(f32)
        else:
            half = span.start // (half_tiles * TILE)
            inner = pl.ds(pl.multiple_of(span.start - half * (half_tiles * TILE), TILE), TILE)
            grad_block = jnp.where(
                half == ints[ROLE], gb_refs[0][inner, :].astype(f32), gb_refs[1][inner, :].astype(f32)
            )
        gain = vec_ref[LOCAL + expert : LOCAL + expert + 1, :]
        shift = vec_ref[2 * LOCAL + expert : 2 * LOCAL + expert + 1, :]
        scale = cols[:, SCALE + expert : SCALE + expert + 1]
        grad_exp = cols[:, COEF + expert : COEF + expert + 1] * grad_block
        scaled = grad_exp * norm
        dx = grad_exp * gain
        first_mean = jnp.mean(dx, axis=1, keepdims=True)
        second_mean = jnp.mean(dx * norm, axis=1, keepdims=True)
        grad_sum = scale * (dx - first_mean - norm * second_mean)
        grad_low = grad_sum.astype(bf16)
        pre_a = nn(x, wi_a[...]) + bi_ref[expert : expert + 1, :HALF]
        act_a, slope_a = gelu_parts(pre_a)
        low_a = (nn(grad_low, wo_a[...]) * slope_a).astype(bf16)
        pre_b = nn(x, wi_b[...]) + bi_ref[expert : expert + 1, HALF:]
        act_b, slope_b = gelu_parts(pre_b)
        low_b = (nn(grad_low, wo_b[...]) * slope_b).astype(bf16)
        add(out_a, keep_ref, 1, tn(grad_low, act_a.astype(bf16)))
        add(in_a, keep_ref, 0, tn(x, low_a))
        add(out_b, give_ref, 1, tn(grad_low, act_b.astype(bf16)))
        add(in_b, give_ref, 0, tn(x, low_b))
        back_ref[span, :] += nt(low_a, wi_a[...]) + nt(low_b, wi_b[...])
        dcoef = jnp.sum(grad_block * (norm * gain + shift), axis=1, keepdims=True)
        if expert < 2:
            cols_ref[span, :] = with_column(cols, DCOEF + expert, dcoef)
        else:
            mine = cols[:, DOMAIN : DOMAIN + 1] == ints[DOMAIN_OF + expert - 2].astype(f32)
            column = cols[:, DCOEF + 2 : DCOEF + 3] + jnp.where(mine, dcoef, 0.0)
            cols_ref[span, :] = with_column(cols, DCOEF + 2, column)
        dvec_ref[0, 0:1, :] += jnp.sum(grad_sum, axis=0, keepdims=True)
        dvec_ref[0, 1:2, :] += jnp.sum(scaled, axis=0, keepdims=True)
        dvec_ref[0, 2:3, :] += jnp.sum(grad_exp, axis=0, keepdims=True)
        dbi_ref[0, 0:1, :HALF] += jnp.sum(low_a.astype(f32), axis=0, keepdims=True)
        dbi_ref[0, 0:1, HALF:] += jnp.sum(low_b.astype(f32), axis=0, keepdims=True)

    for place, expert in enumerate(experts):

        @pl.when(step == place)
        def _(expert=expert):
            if expert >= 2:
                for ref in (in_a, in_b, out_a, out_b):
                    ref[...] = jnp.zeros_like(ref)
            each_span(expert, ints, first, rows, functools.partial(work, expert))
            if expert >= 2:
                keep_ref[0, 0] = in_a[...].astype(bf16)
                keep_ref[0, 1] = out_a[...].astype(bf16)
                give_ref[0, 0] = in_b[...].astype(bf16)
                give_ref[0, 1] = out_b[...].astype(bf16)


def tower_kernel(
    ints, mix_ref, other_ref, cols_ref, tw_ref, tv_ref, out_ref, gb_ref, low_ref, dw_ref, dv_ref, db_ref
):
    @pl.when(pl.program_id(0) == 0)
    def _():
        db_ref[...] = jnp.zeros_like(db_ref)
        dw_ref[...] = jnp.zeros_like(dw_ref)
        dv_ref[...] = jnp.zeros_like(dv_ref)

    bias = tv_ref[0:1, :]
    head = tv_ref[1:2, :]
    cols = cols_ref[...]
    block = (mix_ref[...] + other_ref[...].astype(f32)).astype(bf16)
    tower = slice(PACK - 128 - DOM * TW, PACK - 128)
    pre = nn(block, tw_ref[:, tower]) + bias
    act, slope = gelu_parts(pre)
    group = lax.broadcasted_iota(jnp.int32, pre.shape, 1) // TW
    mine = group == cols[:, DOMAIN : DOMAIN + 1].astype(jnp.int32)
    act = jnp.where(mine, act, 0.0)
    logit = jnp.sum(act * head, axis=1, keepdims=True) + cols[:, BIAS : BIAS + 1]
    predicted = 1.0 / (1.0 + jnp.exp(-logit))
    grad_logit = cols[:, WEIGHT : WEIGHT + 1] * (predicted - cols[:, LABEL : LABEL + 1])
    lane = lax.broadcasted_iota(jnp.int32, cols.shape, 1)
    out_ref[...] = jnp.transpose(jnp.where(lane == 0, predicted, jnp.where(lane == 1, grad_logit, 0.0)))[:8]
    by_domain = jnp.where(lane.astype(f32) == cols[:, DOMAIN : DOMAIN + 1], grad_logit, 0.0)
    db_ref[0:1, :] += jnp.sum(by_domain, axis=0, keepdims=True)
    dv_ref[1:2, :] += jnp.sum(grad_logit * act, axis=0, keepdims=True)
    grad_pre = jnp.where(mine, grad_logit * head * slope, 0.0)
    dv_ref[0:1, :] += jnp.sum(grad_pre, axis=0, keepdims=True)
    grad_low = grad_pre.astype(bf16)
    grad_block = nt(grad_low, tw_ref[:, tower])
    gb_ref[...] = grad_block
    low_ref[...] = grad_block.astype(bf16)
    dw_ref[...] += tn(block, grad_low)


def softmax_back(probability, grad_probs):
    return probability * (grad_probs - jnp.sum(probability * grad_probs, axis=0, keepdims=True))


def gate_kernel(ints, back_ref, cols_ref, prob_ref, x_ref, gates_ref, sum_ref, low_ref, gate_ref):
    index = pl.program_id(0)
    first = ints[ROLE] == 0

    @pl.when(index == 0)
    def _():
        gate_ref[...] = jnp.zeros_like(gate_ref)

    mine = jnp.transpose(cols_ref[...])[DCOEF : DCOEF + 3]
    none = jnp.zeros_like(mine)
    one, two = jnp.where(first, mine, none), jnp.where(first, none, mine)
    d_shared = jnp.concatenate([one[0:2], two[0:2]], axis=0)
    d_domain = jnp.concatenate([one[2:3], two[2:3]], axis=0)
    top, shared, domain = prob_ref[0:2, :], prob_ref[2:6, :], prob_ref[6:8, :]
    d_top = jnp.concatenate(
        [
            jnp.sum(d_shared * shared, axis=0, keepdims=True),
            jnp.sum(d_domain * domain, axis=0, keepdims=True),
        ],
        axis=0,
    )
    grads = (
        softmax_back(top, d_top),
        softmax_back(shared, d_shared * top[0:1]),
        softmax_back(domain, d_domain * top[1:2]),
    )
    rows = top.shape[1]
    place = index * rows + lax.broadcasted_iota(jnp.int32, (1, rows), 1)
    picks = [
        jnp.where((place >= ints[START + d]) & (place < ints[END + d]), 1.0, 0.0) for d in range(DOM)
    ]
    spread = jnp.concatenate(
        [picks[d] * grad for grad in grads for d in range(DOM)] + [jnp.zeros((96, rows), f32)],
        axis=0,
    )
    spread = jnp.transpose(spread).astype(bf16)
    gate_ref[...] += tn(x_ref[...], spread)
    added = back_ref[...] + nt(spread, gates_ref[...])
    sum_ref[...] = added
    low_ref[...] = added.astype(bf16)


def call_gate(ints, back, cols, probs, x, small):
    rows = x.shape[0]
    half = rows // 2

    def tile(width):
        return pl.BlockSpec((half, width), lambda i, *_: (i, 0))

    return pl.pallas_call(
        gate_kernel,
        grid_spec=pltpu.PrefetchScalarGridSpec(
            num_scalar_prefetch=1,
            grid=(2,),
            in_specs=[
                tile(D),
                tile(128),
                pl.BlockSpec((8, half), lambda i, *_: (0, i)),
                tile(D),
                GATES_SPEC,
            ],
            out_specs=(tile(D), tile(D), fixed((D, 128))),
        ),
        out_shape=(
            jax.ShapeDtypeStruct((rows, D), f32),
            jax.ShapeDtypeStruct((rows, D), bf16),
            jax.ShapeDtypeStruct((D, 128), f32),
        ),
        compiler_params=params(),
        cost_estimate=pl.CostEstimate(
            flops=4 * rows * D * 128, bytes_accessed=10_000_000, transcendentals=0
        ),
        name="gates",
    )(ints, back, cols, probs, x, small)


def hidden_lines(ints, lane_ref, tv_ref, line_refs):
    first_set, first_core = ints[ROLE] == 0, ints[CORE] == 0
    mine = [r[k, 0:1, :] for r in line_refs for k in range(r.shape[0])]
    mine = jnp.concatenate(mine, axis=0)
    mine = jnp.where(first_core, mine, pltpu.roll(mine, HALF, 1))
    mine = jnp.where(first_set, mine, 0.0), jnp.where(first_set, 0.0, mine)
    found = {j: mine[r][i : i + 1] for r, row in enumerate(SETS) for i, j in enumerate(row)}
    mine = jnp.concatenate([found[j] for j in range(2 * LOCAL)], axis=0).astype(bf16)

    def lanes(values, row):
        lane = lax.broadcasted_iota(jnp.int32, (H, D), 0)
        chosen = jnp.where(lane == lane_ref[row : row + 1, :], 1.0, 0.0).astype(bf16)
        return nn(values, chosen)

    tower = tv_ref[...].astype(bf16)
    rows = [lanes(mine, 0), lanes(mine, 1)]
    head = lane_ref[6:7, :] == 1
    for d in range(DOM):
        both = lanes(tower, 2 + d)
        rows.append(jnp.where(head, both[1:2], both[0:1]))
    return rows


def finish_kernel(
    ints, gb_ref, gb_in_ref, sum_ref, in_ref, ev_ref, proj_ref, tower_ref, gate_ref, *refs
):
    lane_ref, tv_ref, *vec_refs, ge_ref, small_ref, proj_sum, bias_sum = refs
    vec_refs, line_refs = vec_refs[: len(vec_refs) // 2], vec_refs[len(vec_refs) // 2 :]
    index = pl.program_id(0)
    last = pl.num_programs(0) - 1
    first = ints[ROLE] == 0
    at_home = jnp.where(ints[CORE] == ints[ROLE], 1.0, 0.0)
    mine_half = index == ints[ROLE]

    @pl.when(index == 0)
    def _():
        for ref in (proj_sum, bias_sum):
            ref[...] = jnp.zeros_like(ref)

    grad_mixed = jnp.where(mine_half, gb_ref[...], gb_in_ref[...].astype(f32))
    grad_mixed = at_home * (grad_mixed + sum_ref[...] + in_ref[...].astype(f32))
    bias_sum[0:1, :] += jnp.sum(grad_mixed, axis=0, keepdims=True)
    low = grad_mixed.astype(bf16)
    proj_sum[...] += tn(low, ev_ref[...])
    ge_ref[...] = nn(low, proj_ref[...]).astype(bf16)

    @pl.when(index == last)
    def _():
        e_in = proj_sum.shape[1]
        vectors = jnp.concatenate(
            [r[k, 0:3, :] for r in vec_refs for k in range(r.shape[0])], axis=0
        )
        rows = jnp.concatenate(
            [
                jnp.zeros((32, D), f32),
                jnp.where(first, vectors, 0.0),
                jnp.where(first, 0.0, vectors),
                bias_sum[0:1, :],
                *hidden_lines(ints, lane_ref, tv_ref, line_refs),
                jnp.zeros((31, D), f32),
            ],
            axis=0,
        )
        small_ref[:, :e_in] = proj_sum[...].astype(bf16)
        small_ref[:, e_in : e_in + DOM * TW] = tower_ref[...].astype(bf16)
        small_ref[:, e_in + DOM * TW :] = (gate_ref[...] + jnp.transpose(rows)).astype(bf16)


def call_finish(ints, gb, gb_in, added, arrived, events, small, tower, gate, lanes, tower_vec, sums):
    rows, e_in = events.shape
    half = rows // 2

    def tile(width):
        return pl.BlockSpec((half, width), lambda i, *_: (i, 0))

    halves = (gb, gb_in)
    wholes = (tower, gate, lanes, tower_vec)
    vecs = [v for v, _ in sums] + [b for _, b in sums]
    return pl.pallas_call(
        finish_kernel,
        grid_spec=pltpu.PrefetchScalarGridSpec(
            num_scalar_prefetch=1,
            grid=(2,),
            in_specs=[fixed(a.shape) for a in halves]
            + [tile(D), tile(D), tile(e_in), proj_spec(e_in)]
            + [fixed(a.shape) for a in (*wholes, *vecs)],
            out_specs=(tile(e_in), fixed((D, PACK))),
            scratch_shapes=[pltpu.VMEM((D, e_in), f32), pltpu.VMEM((8, D), f32)],
        ),
        out_shape=(jax.ShapeDtypeStruct((rows, e_in), bf16), jax.ShapeDtypeStruct((D, PACK), bf16)),
        compiler_params=params(),
        cost_estimate=pl.CostEstimate(flops=4 * rows * D * e_in, bytes_accessed=14_000_000, transcendentals=0),
        name="finish",
    )(ints, *halves, added, arrived, events, small, *wholes, *vecs)


VECTOR_ROW = {j: 32 + 18 * r + 3 * i for r, row in enumerate(SETS) for i, j in enumerate(row)}


def small_kernel(*refs):
    parts, vec_refs = refs[:-12], refs[-3:]
    proj_ref, tower_ref, top_ref, shared_ref, domain_ref, bias_ref, hidden_ref, tb_ref, to_ref = refs[-12:-3]
    added = functools.reduce(jnp.add, [p[...].astype(f32) for p in parts])
    width, e_in = proj_ref.shape
    proj_ref[...] = added[:, :e_in]
    for d in range(DOM):
        tower_ref[d] = added[:, e_in + d * TW : e_in + (d + 1) * TW]
    rows = jnp.concatenate([added[:, e_in + DOM * TW :], jnp.zeros((128 - width, 128), f32)], axis=0)
    rows = jnp.transpose(rows)[:, :width]
    for ref, low, size in ((top_ref, 0, 2), (shared_ref, 2 * DOM, S), (domain_ref, (2 + S) * DOM, K)):
        for d in range(DOM):
            ref[d] = rows[low + d * size : low + (d + 1) * size]
    bias_ref[...] = rows[68:69]
    hidden_ref[:, :width] = rows[69:81]
    hidden_ref[:, width:] = rows[81:93]
    tb_ref[...] = rows[93:97, : width // 2]
    to_ref[...] = rows[93:97, width // 2 :]
    for which, ref in enumerate(vec_refs):
        for j in range(2 * LOCAL):
            ref[j : j + 1, :] = rows[VECTOR_ROW[j] + which : VECTOR_ROW[j] + which + 1]


def call_small(parts):
    width = parts[0].shape[0]
    e_in = PACK - DOM * TW - 128
    shapes = [(width, e_in), (DOM, width, TW), (DOM, 2, width), (DOM, S, width), (DOM, K, width), (1, width)]
    shapes += [(2 * LOCAL, 2 * width), (DOM, width // 2), (DOM, width // 2)]
    shapes += [(2 * LOCAL, width)] * 3
    return pl.pallas_call(
        small_kernel,
        grid=(1,),
        in_specs=[fixed(p.shape) for p in parts],
        out_specs=tuple(fixed(shape) for shape in shapes),
        out_shape=tuple(jax.ShapeDtypeStruct(shape, f32) for shape in shapes),
        compiler_params=params(),
        name="small",
    )(*parts)


def place_kernel(ints, *refs):
    *parts, in_ref, out_ref = refs
    half = len(parts) // 2
    first = ints[ROLE] == 0
    for chunk, (own, other) in enumerate(zip(parts[:half], parts[half:])):
        for place, expert in enumerate(CHUNKS[chunk]):
            for which, ref in enumerate((in_ref, out_ref)):
                a, b = own[which, place].astype(f32), other[which, place].astype(f32)
                ref[SETS[0][expert]] = jnp.where(first, a, b)
                ref[SETS[1][expert]] = jnp.where(first, b, a)


def call_place(ints, own, other):
    rows, width = own[0].shape[2:]
    shape = (2 * LOCAL, rows, width)
    return pl.pallas_call(
        place_kernel,
        grid_spec=pltpu.PrefetchScalarGridSpec(
            num_scalar_prefetch=1,
            grid=(1,),
            in_specs=[fixed(a.shape) for a in (*own, *other)],
            out_specs=(fixed(shape), fixed(shape)),
        ),
        out_shape=(jax.ShapeDtypeStruct(shape, f32),) * 2,
        compiler_params=params(),
        name="place",
    )(ints, *own, *other)


def params():
    return pltpu.CompilerParams(vmem_limit_bytes=VMEM_LIMIT)


def fixed(shape):
    return pl.BlockSpec(shape, lambda i, *_: (0,) * len(shape))


def pack_kernel(count, *refs):
    sources, out_ref, held, arrived = refs[:count], refs[count], refs[count + 1 : -1], refs[-1]
    copies = [pltpu.make_async_copy(a, b, arrived.at[k]) for k, (a, b) in enumerate(zip(sources, held))]
    for copy in copies:
        copy.start()
    for copy in copies:
        copy.wait()
    proj_ref, tower_ref, *row_refs, in_bias_ref, tower_b_ref, tower_out_ref = held
    width, e_in = proj_ref.shape
    out_ref[:, :e_in] = proj_ref[...]
    for d in range(DOM):
        out_ref[:, e_in + d * TW : e_in + (d + 1) * TW] = tower_ref[d]
    rows = [r[...].astype(f32) for r in row_refs]
    bias = in_bias_ref[...].astype(f32)
    rows += [bias[:, :width], bias[:, width:]]
    rows.append(
        jnp.concatenate([tower_b_ref[...].astype(f32), tower_out_ref[...].astype(f32)], axis=1)
    )
    rows = jnp.concatenate(rows + [jnp.zeros((31, width), f32)], axis=0)
    rows = jnp.concatenate([rows, jnp.zeros((128, 128 - width), f32)], axis=1)
    out_ref[:, e_in + DOM * TW :] = jnp.transpose(rows)[:width].astype(bf16)


def call_pack(*arrays):
    width = arrays[0].shape[0]
    return pl.pallas_call(
        functools.partial(pack_kernel, len(arrays)),
        in_specs=[pl.BlockSpec(memory_space=pltpu.HBM)] * len(arrays),
        out_specs=pl.BlockSpec(memory_space=pltpu.VMEM),
        out_shape=jax.ShapeDtypeStruct((width, PACK), bf16),
        scratch_shapes=[pltpu.VMEM(a.shape, a.dtype) for a in arrays]
        + [pltpu.SemaphoreType.DMA((len(arrays),))],
        compiler_params=params(),
        name="pack",
    )(*arrays)


PICKED = [
    [32 + e for e in row] + [44 + e for e in row] + [56 + e for e in row] + [68] + [127] * 5
    + [69 + e for e in row] + [81 + e for e in row] + [93 + d for d in range(DOM)]
    for row in SETS
]


def unpack_kernel(ints, small_ref, choose_ref, lane_ref, vec_ref, bi_ref, tower_ref):
    vec = nt(choose_ref[0], small_ref[...])
    vec_ref[...] = vec

    def lanes(values, row):
        lane = lax.broadcasted_iota(jnp.int32, (H, D), 0)
        chosen = jnp.where(lane == lane_ref[row : row + 1, :], 1.0, 0.0).astype(bf16)
        return nt(values.astype(bf16), chosen)

    bias = lanes(jnp.concatenate([vec[24:30], jnp.zeros((2, D), f32)], axis=0), 0)
    bias += lanes(jnp.concatenate([vec[30:36], jnp.zeros((2, D), f32)], axis=0), 1)
    bi_ref[...] = jnp.where(ints[1] == 0, bias, pltpu.roll(bias, HALF, 1))
    head = lane_ref[6:7, :] == 1
    tower = jnp.zeros((8, H), f32)
    for d in range(DOM):
        row = vec[36 + d : 37 + d]
        rows = [jnp.where(head, 0.0, row), jnp.where(head, row, 0.0), jnp.zeros((6, D), f32)]
        tower += lanes(jnp.concatenate(rows, axis=0), 2 + d)
    tower_ref[...] = tower


def call_unpack(ints, small, lanes):
    choose = np.zeros((2, 40, 128), np.float32)
    for r in range(2):
        for row, column in enumerate(PICKED[r]):
            choose[r, row, column] = 1.0
    shapes = [(40, D), (8, H), (8, DOM * TW)]
    return pl.pallas_call(
        unpack_kernel,
        grid_spec=pltpu.PrefetchScalarGridSpec(
            num_scalar_prefetch=1,
            grid=(1,),
            in_specs=[
                pl.BlockSpec((D, 128), lambda i, ints: (0, PACK // 128 - 1)),
                pl.BlockSpec((1, 40, 128), lambda i, ints: (ints[0], 0, 0)),
                fixed(lanes.shape),
            ],
            out_specs=tuple(fixed(shape) for shape in shapes),
        ),
        out_shape=tuple(jax.ShapeDtypeStruct(shape, f32) for shape in shapes),
        compiler_params=params(),
        name="unpack",
    )(ints, small, jnp.asarray(choose, bf16), lanes)


def choose_kernel(own_ids, other_ids, in_own, out_own, in_other, out_other, *refs):
    own_refs, other_refs, all_ref = refs[:2], refs[2:4], refs[4]
    step = pl.program_id(0)
    for part in range(2):

        @pl.when(step // 3 == part)
        def _(part=part):
            own_refs[part][0], own_refs[part][1] = in_own[...], out_own[...]
            other_refs[part][0], other_refs[part][1] = in_other[...], out_other[...]

    all_ref[0], all_ref[1] = in_other[...], out_other[...]


def call_choose(own_ids, other_ids, w_in, w_out_t):
    tail = w_in.shape[1:]
    block = (1,) + tail

    def shape(count):
        return jax.ShapeDtypeStruct((2, count) + tail, bf16)

    own = pl.BlockSpec(block, lambda i, a, b: (a[i], 0, 0))
    other = pl.BlockSpec(block, lambda i, a, b: (b[i], 0, 0))
    low = pl.BlockSpec((2,) + block, lambda i, a, b: (0, jnp.minimum(i, 2), 0, 0))
    high = pl.BlockSpec((2,) + block, lambda i, a, b: (0, jnp.maximum(i - 3, 0), 0, 0))
    every = pl.BlockSpec((2,) + block, lambda i, a, b: (0, i, 0, 0))
    return pl.pallas_call(
        choose_kernel,
        grid_spec=pltpu.PrefetchScalarGridSpec(
            num_scalar_prefetch=2,
            grid=(LOCAL,),
            in_specs=[own, own, other, other],
            out_specs=(low, high, low, high, every),
        ),
        out_shape=(shape(3), shape(3), shape(3), shape(3), shape(6)),
        compiler_params=params(),
        cost_estimate=pl.CostEstimate(flops=0, bytes_accessed=3_000_000, transcendentals=0),
        name="choose",
    )(own_ids, other_ids, w_in, w_out_t, w_in, w_out_t)


def proj_spec(e_in):
    return pl.BlockSpec((D, e_in), lambda *_: (0, 0))


GATES_SPEC = pl.BlockSpec((D, 128), lambda *_: (0, PACK // 128 - 1))


def call_prepare(ints, floats, table, embeds, small, vec):
    rows = embeds.shape[0]
    tiles = rows // TILE
    e_in = embeds.shape[1]

    def tile(width):
        return pl.BlockSpec((TILE, width), lambda i, *_: (i, 0))

    return pl.pallas_call(
        prepare_kernel,
        grid_spec=pltpu.PrefetchScalarGridSpec(
            num_scalar_prefetch=2,
            grid=(tiles,),
            in_specs=[fixed(table.shape), fixed(embeds.shape), proj_spec(e_in), GATES_SPEC, fixed(vec.shape)],
            out_specs=(
                tile(e_in),
                tile(D),
                tile(D),
                tile(128),
                pl.BlockSpec((8, TILE), lambda i, *_: (0, i)),
            ),
        ),
        out_shape=(
            jax.ShapeDtypeStruct((rows, e_in), bf16),
            jax.ShapeDtypeStruct((rows, D), bf16),
            jax.ShapeDtypeStruct((rows, D), f32),
            jax.ShapeDtypeStruct((rows, 128), f32),
            jax.ShapeDtypeStruct((8, rows), f32),
        ),
        compiler_params=params(),
        cost_estimate=pl.CostEstimate(
            flops=2 * rows * e_in * (rows + D), bytes_accessed=12_000_000, transcendentals=rows * 8
        ),
        name="prepare",
    )(ints, floats, table, embeds, small, small, vec)


def half_spec(own, shape):
    rest = (0,) * (len(shape) - 1)
    return pl.BlockSpec(shape, lambda i, ints: ((ints[ROLE] if own else 1 - ints[ROLE]),) + rest)


def piece_spec(array, place):
    a, b, _, rows, width = array.shape
    return pl.BlockSpec((a, b, 1, rows, width), lambda i, *_: (0, 0, place(i), 0, 0))


MATRICES = [pltpu.VMEM((D, HALF), bf16)] * 4


def call_forward(experts, own, ints, x, weights, bi, vec, cols, mix, norms, gives=False):
    rows = x.shape[0]
    half = rows // 2
    arrays = sorted({e // 3 for e in experts})
    first = {a: min(k for k, e in enumerate(experts) if e // 3 == a) for a in arrays}
    number = {a: sum(1 for e in experts if e // 3 == a) for a in arrays}

    def place(a):
        return lambda i: jnp.clip(i - first[a], 0, number[a] - 1)

    weight_specs = [piece_spec(w, place(a)) for a in arrays for w in weights[a]]
    norm_specs = [
        pl.BlockSpec(
            (1, half, D),
            lambda i, ints, a=a: (place(a)(i), ints[ROLE] if own else 1 - ints[ROLE], 0),
        )
        for a in arrays
    ]
    kept = [norms[a] for a in arrays if a in norms]
    inputs = [x] + [w for a in arrays for w in weights[a]] + [bi, vec, cols, mix] + kept
    at = len(inputs) - len(kept)
    aliases = {at - 1: 0, at: 1}
    aliases.update({at + 1 + k: 2 + k for k in range(len(kept))})
    shared = sum(1 for e in experts if e < 2)
    out = pl.pallas_call(
        functools.partial(
            forward_kernel, experts, own, len(kept), len(weights[arrays[0]]), gives
        ),
        grid_spec=pltpu.PrefetchScalarGridSpec(
            num_scalar_prefetch=1,
            grid=(len(experts),),
            in_specs=[half_spec(own, (half, D))]
            + weight_specs
            + [fixed(bi.shape), fixed(vec.shape), half_spec(own, (half, 128)), half_spec(own, (half, D))]
            + [pl.BlockSpec(memory_space=pl.ANY)] * len(kept),
            out_specs=(half_spec(own, (half, 128)), half_spec(own, (half, D)), *norm_specs)
            + ((fixed((half, D)),) if gives else ()),
            scratch_shapes=MATRICES,
        ),
        out_shape=(
            jax.ShapeDtypeStruct((rows, 128), f32),
            jax.ShapeDtypeStruct((rows, D), f32),
            *[jax.ShapeDtypeStruct((3, rows, D), bf16)] * len(arrays),
        )
        + ((jax.ShapeDtypeStruct((half, D), bf16),) if gives else ()),
        input_output_aliases=aliases,
        compiler_params=params(),
        cost_estimate=pl.CostEstimate(
            flops=4 * (shared + 1) * half * D * H, bytes_accessed=12_000_000, transcendentals=0
        ),
        name="experts_forward",
    )(ints, *inputs)
    found = out[0], out[1], {**norms, **dict(zip(arrays, out[2:]))}
    return found + (out[-1],) if gives else found


def call_backward(experts, halves, ints, x, gbs, norms, weights, bi, vec, cols, back, sums=None):
    rows, count = x.shape[0], len(experts)
    part = rows // 2 * len(halves)
    array, low = experts[0] // 3, experts[0] % 3
    split = any(e // 3 != array for e in experts)

    def span(width):
        if len(halves) == 2:
            return fixed((rows, width))
        return half_spec(halves[0] == "own", (part, width))

    def norm_index(i, ints):
        if len(halves) == 2:
            return (low + i, 0, 0)
        return (low + i, ints[ROLE] if halves[0] == "own" else 1 - ints[ROLE], 0)

    assert not split
    pairs = pl.BlockSpec((1, 2, D, HALF), lambda i, *_: (i, 0, 0, 0))
    vec_spec = pl.BlockSpec((1, 8, D), lambda i, *_: (i, 0, 0))
    bi_spec = pl.BlockSpec((1, 8, H), lambda i, *_: (i, 0, 0))
    mode, back_array = back if back is not None else ("fresh", jnp.zeros((8, 128), f32))
    inputs = [x, *gbs, norms[array], *weights[array], bi, vec, cols, back_array]
    in_specs = (
        [span(D)]
        + [fixed(g.shape) for g in gbs]
        + [pl.BlockSpec((1, part, D), norm_index)]
        + [piece_spec(w, lambda i: low + i) for w in weights[array]]
        + [fixed(bi.shape), fixed(vec.shape), span(128)]
        + [span(D) if mode == "add" else pl.BlockSpec(memory_space=pl.ANY)]
    )
    aliases = {len(inputs) - 1: 0}
    if back is not None:
        aliases[len(inputs)] = 1
    if sums is not None:
        inputs += list(sums)
        in_specs += [vec_spec, bi_spec]
    return pl.pallas_call(
        functools.partial(
            backward_kernel, experts, halves, mode == "add", sums is not None, len(weights[array])
        ),
        grid_spec=pltpu.PrefetchScalarGridSpec(
            num_scalar_prefetch=1,
            grid=(count,),
            in_specs=in_specs,
            out_specs=(span(128), span(D), pairs, pairs, vec_spec, bi_spec),
            scratch_shapes=[pltpu.VMEM((D, HALF), f32)] * 4 + MATRICES,
        ),
        out_shape=(
            jax.ShapeDtypeStruct((rows, 128), f32),
            jax.ShapeDtypeStruct((rows, D), f32),
            jax.ShapeDtypeStruct((count, 2, D, HALF), bf16),
            jax.ShapeDtypeStruct((count, 2, D, HALF), bf16),
            jax.ShapeDtypeStruct((count, 8, D), f32),
            jax.ShapeDtypeStruct((count, 8, H), f32),
        ),
        input_output_aliases=aliases,
        compiler_params=params(),
        cost_estimate=pl.CostEstimate(
            flops=10 * count * (rows // 2) * D * H, bytes_accessed=20_000_000, transcendentals=0
        ),
        name="experts_backward",
    )(ints, *inputs)


def call_tower(ints, mix, other, cols, small, tower_vec):
    rows = other.shape[0]
    tiles = 2
    size = rows // tiles

    def kept(width):
        return pl.BlockSpec((size, width), lambda i, ints: (ints[ROLE] * tiles + i, 0))

    def tile(width):
        return pl.BlockSpec((size, width), lambda i, *_: (i, 0))

    return pl.pallas_call(
        tower_kernel,
        grid_spec=pltpu.PrefetchScalarGridSpec(
            num_scalar_prefetch=1,
            grid=(tiles,),
            in_specs=[kept(D), tile(D), kept(128), fixed(small.shape), fixed(tower_vec.shape)],
            out_specs=(
                pl.BlockSpec((8, size), lambda i, *_: (0, i)),
                tile(D),
                tile(D),
                fixed((D, DOM * TW)),
                fixed((8, DOM * TW)),
                fixed((8, 128)),
            ),
        ),
        out_shape=(
            jax.ShapeDtypeStruct((8, rows), f32),
            jax.ShapeDtypeStruct((rows, D), f32),
            jax.ShapeDtypeStruct((rows, D), bf16),
            jax.ShapeDtypeStruct((D, DOM * TW), f32),
            jax.ShapeDtypeStruct((8, DOM * TW), f32),
            jax.ShapeDtypeStruct((8, 128), f32),
        ),
        compiler_params=params(),
        cost_estimate=pl.CostEstimate(
            flops=6 * rows * D * DOM * TW, bytes_accessed=10_000_000, transcendentals=rows * DOM * TW
        ),
        name="towers",
    )(ints, mix, other, cols, small, tower_vec)


def per_device(
    box,
    embeds,
    domain,
    frozen,
    labels,
    proj_w,
    proj_b,
    w_in,
    in_bias,
    w_out,
    out_bias,
    ln_gain,
    ln_shift,
    gate_top,
    gate_shared,
    gate_domain,
    tower_w,
    tower_b,
    tower_out,
    tower_out_b,
):
    core = lax.axis_index("tensor")
    role = box.role(lax.axis_index("dp"))
    at_home = core == role
    places = box.count
    rows = embeds.shape[0]
    half_rows = rows // 2
    width = proj_w.shape[1]
    e_in = proj_w.shape[0]
    place_of = box.places()
    nz, ny, nx = box.dims[1:]
    sets = jnp.array(SETS, jnp.int32)
    set_own, set_other = sets[role], sets[1 - role]

    def half(values, which, axis=0):
        return lax.dynamic_slice_in_dim(values, which * half_rows, half_rows, axis)

    w_out_t = jnp.swapaxes(w_out, 1, 2)
    first, second, first_other, second_other, others = call_choose(set_own, set_other, w_in, w_out_t)

    arrays = (
        proj_w.T,
        tower_w,
        jnp.swapaxes(gate_top, 1, 2).reshape(2 * DOM, width),
        jnp.swapaxes(gate_shared, 1, 2).reshape(S * DOM, width),
        jnp.swapaxes(gate_domain, 1, 2).reshape(K * DOM, width),
        out_bias,
        ln_gain,
        ln_shift,
        proj_b[None],
        in_bias,
        tower_b,
        tower_out,
    )
    flips = box.send(others, flip=1)
    first_z = box.line(first, first_other)
    pack = call_pack(*step(arrays, flips)[0])
    pack = in_order(role, pack, box.send(pack, flip=1), 0)
    pack = jnp.concatenate([pack] + box.pieces(pack, "z"))
    flips, first, first_z, second, second_other = step(flips, first, first_z, second, second_other)

    def along_z(shard, flip, found):
        found = box.in_line(shard, flip, found, role, 2)
        return jnp.stack([b[0] for b in found]), jnp.stack([b[1] for b in found])

    first_i, first_o = along_z(first, flips[:, :3], first_z)
    first_iy, first_ox = box.pieces(first_i, "y"), box.pieces(first_o, "x")
    second_z = box.line(second, second_other)
    pack = jnp.concatenate([pack] + box.pieces(pack, "y"))
    pack = jnp.concatenate([pack] + box.pieces(pack, "x")).reshape(places, 1, width, PACK)
    domain, labels = step((domain, labels), first)[0]
    event_rows = jnp.concatenate(
        [domain.astype(f32).T, labels.astype(f32)[None], jnp.zeros((6, rows), f32)]
    )
    event_rows = jnp.where(at_home, event_rows, box.to_partner(event_rows, True))
    ids = event_rows[0]
    onehot = (ids[None, :] == jnp.arange(DOM, dtype=f32)[:, None]).astype(f32)
    rank = jnp.cumsum(onehot, axis=1)
    counts = rank[:, -1]
    ends = jnp.cumsum(counts)
    starts = ends - counts
    position = jnp.sum(onehot * (rank + starts[:, None]), axis=0) - 1.0
    embeds_in = box.to_partner(step(embeds, second_z[0])[0], True)
    first_i, first_o, first_iy, first_ox, second, second_z, flips, starts, ends, position = step(
        first_i, first_o, first_iy, first_ox, second, second_z, flips, starts, ends, position
    )

    small = in_order(core, pack, swap_cores(pack), 1).reshape(D, PACK)
    first_i = jnp.stack([first_i] + first_iy)
    first_o = jnp.stack([first_o] + first_ox)
    first_ix, first_oy = box.pieces(first_i, "x"), box.pieces(first_o, "y")
    second_i, second_o = along_z(second, flips[:, 3:], second_z)
    second_iy, second_ox = box.pieces(second_i, "y"), box.pieces(second_o, "x")

    device = (2 * box.ahead()[:, None, None] + jnp.arange(2)[None, :, None]).astype(jnp.int32)
    unit = jnp.arange(width, dtype=jnp.int32)[None, None, :]
    narrow = width // 2
    lanes = [device * 2 * width + unit, device * 2 * width + width + unit]
    lanes += [d * TW + device * narrow + unit % narrow for d in range(DOM)]
    lanes += [jnp.broadcast_to(unit // narrow, (places, 2, width))] * 2
    lanes = jnp.stack([jnp.broadcast_to(v, (places, 2, width)).reshape(D) for v in lanes])
    vec, bi, tower_vec = call_unpack(jnp.stack([role, core]), small, lanes)

    table = jnp.concatenate([position[None], event_rows[1:]])
    start_i, end_i = starts.astype(jnp.int32), ends.astype(jnp.int32)
    empty = end_i == start_i
    low = jnp.where(empty, 0, start_i // TILE)
    high = jnp.where(empty, 0, (end_i + TILE - 1) // TILE)
    domains = jnp.arange(DOM, dtype=jnp.int32)
    ints = jnp.concatenate(
        [
            jnp.where(role == 0, low[::-1], low),
            jnp.where(role == 0, high[::-1], high),
            role[None],
            jnp.where(role == 0, DOM - 1 - domains, domains),
            start_i,
            end_i,
            core[None],
            jnp.zeros((2,), jnp.int32),
        ]
    )
    loss_weight = 1.0 - (1.0 - FROZEN_SHARE) * frozen.astype(f32)
    floats = jnp.concatenate([loss_weight, tower_out_b.astype(f32)])
    embeds = jnp.where(at_home, embeds, embeds_in)
    events, x, mix, cols, probs = call_prepare(ints, floats, table, embeds, small, vec)
    (
        first_i, first_o, first_ix, first_oy, second_i, second_o, second_iy, second_ox,
        ints, events, x, mix, cols, probs, vec, bi, small, tower_vec, lanes,
    ) = step(
        first_i, first_o, first_ix, first_oy, second_i, second_o, second_iy, second_ox,
        ints, events, x, mix, cols, probs, vec, bi, small, tower_vec, lanes,
    )

    def pieces(i, ix, o, oy):
        own = [i] + ix + [o] + oy
        return own + [swap_cores(w) for w in own]

    second_i = jnp.stack([second_i] + second_iy)
    second_o = jnp.stack([second_o] + second_ox)
    second_ix, second_oy = box.pieces(second_i, "x"), box.pieces(second_o, "y")
    weights = {0: pieces(first_i, first_ix, first_o, first_oy)}
    cols, mix, norms = call_forward((0, 1, 2), False, ints, x, weights, bi, vec, cols, mix, {})
    second_ix, second_oy, cols, mix = step(second_ix, second_oy, cols, mix)
    weights[1] = pieces(second_i, second_ix, second_o, second_oy)
    cols, mix, norms, give_mix = call_forward(
        (3, 4), False, ints, x, weights, bi, vec, cols, mix, norms, True
    )
    give_mix, mix = step(give_mix, mix)
    other_mix = box.send(give_mix, flip=1)
    cols, mix, norms = call_forward(
        tuple(range(LOCAL)), True, ints, x, weights, bi, vec, cols, mix, norms
    )
    row_out, grad_block, grad_low, d_tower, d_tower_vec, d_logit_bias = call_tower(
        ints, mix, other_mix, cols, small, tower_vec
    )

    box_shape = (nx, ny, nz, 2, 2 * width, HALF)

    def both_cores(keeps, gives):
        def one(which):
            added = total(keeps[0][:, which], [a[:, which] for a in keeps[1:] + gives])
            return added.astype(bf16).reshape((-1,) + box_shape)

        return one(0), one(1)

    class Scatter:
        def __init__(self, *parts):
            i, o = [jnp.concatenate(p) for p in zip(*parts)]
            i, o = [i[:, k] for k in range(nx)], [o[:, :, k] for k in range(ny)]
            self.state = (i[0], o[0], box.hand_out(i, "x"), box.hand_out(o, "y"))

        def second(self):
            i, o, i_in, o_in = self.state
            i, o = total(i, i_in).astype(bf16), total(o, o_in).astype(bf16)
            i, o = [i[:, k] for k in range(ny)], [o[:, k] for k in range(nx)]
            self.state = (i[0], o[0], box.hand_out(i, "y"), box.hand_out(o, "x"))

        def third(self):
            i, o, i_in, o_in = self.state
            both = jnp.stack([total(i, i_in).astype(bf16), total(o, o_in).astype(bf16)])
            both = [both[:, :, k] for k in range(nz)]
            self.state = (both[0], box.hand_out(both, "z"))

        def fourth(self):
            both = total(*self.state)
            mine = lax.dynamic_index_in_dim(both, role, 2, keepdims=False)
            other = lax.dynamic_index_in_dim(both, 1 - role, 2, keepdims=False).astype(bf16)
            self.state = (mine, box.send(other, flip=1))

    def sync(scatters, *values):
        states, values = step([c.state for c in scatters], values)
        for c, state in zip(scatters, states):
            c.state = state
        return values

    common = (ints, x)
    shared = (norms, weights, bi, vec)
    grad_in = box.send(grad_low, flip=1)
    cols, back, keep_a, give_a, *sums = call_backward(
        (0, 1), ("own",), *common, [grad_low], *shared, cols, None
    )
    d_logit_bias = d_logit_bias + swap_cores(d_logit_bias)
    logit_in = box.pieces(d_logit_bias, "y")
    grad_in, cols, back, keep_a, give_a, sums, logit_in = step(
        grad_in, cols, back, keep_a, give_a, sums, logit_in
    )
    d_logit_bias = box.same_sum(d_logit_bias, logit_in, "y")
    give_a = swap_cores(give_a)
    cols, back, keep_b, give_b, *sums_0 = call_backward(
        (0, 1), ("other",), *common, [grad_in], *shared, cols, ("fresh", back), sums
    )
    logit_in = box.pieces(d_logit_bias, "x")
    cols, back, keep_a, give_a, keep_b, give_b, logit_in = step(
        cols, back, keep_a, give_a, keep_b, give_b, logit_in
    )
    d_logit_bias = box.same_sum(d_logit_bias, logit_in, "x")
    give_b = swap_cores(give_b)
    grads = [grad_low, grad_in]
    cols, back, keep_c, give_c, *sums_1 = call_backward(
        (2,), ("own", "other"), *common, grads, *shared, cols, ("add", back)
    )
    logit_in = box.pieces(d_logit_bias, "flip")
    cols, back, keep_b, give_b, keep_c, give_c, row_out, logit_in = step(
        cols, back, keep_b, give_b, keep_c, give_c, row_out, logit_in
    )
    d_logit_bias = box.same_sum(d_logit_bias, logit_in, "flip")
    give_c = swap_cores(give_c)
    ab = both_cores([keep_a, keep_b], [give_a, give_b])
    give_c, keep_c, ab, cols = step(give_c, keep_c, ab, cols)
    c0 = Scatter(ab, both_cores([keep_c], [give_c]))
    cols, back, keep_d, give_d, *sums_2 = call_backward(
        (3, 4, 5), ("own", "other"), *common, grads, *shared, cols, ("add", back)
    )
    rows_in = box.to_partner(row_out, False)
    logit_in = box.pieces(d_logit_bias, "z")
    cols, back, keep_d, give_d, rows_in, logit_in = sync(
        [c0], cols, back, keep_d, give_d, rows_in, logit_in
    )
    d_logit_bias = box.same_sum(d_logit_bias, logit_in, "z")
    c0.second()
    give_d = swap_cores(give_d)
    c1 = Scatter(both_cores([keep_d], [give_d]))
    cols, back, _ = step(cols, back, (c0.state[:2], c1.state[:2]))
    g_sum, g_low, d_gate = call_gate(ints, back, cols, probs, x, small)
    back_in = box.to_partner(g_low, False)
    (back_in,) = sync([c0, c1], back_in)
    c0.third()
    c1.second()
    back_in, _ = step(back_in, c1.state[:2])
    grad_events, d_small = call_finish(
        ints, grad_block, grad_in, g_sum, back_in, events, small, d_tower, d_gate, lanes, d_tower_vec,
        [sums_0, sums_1, sums_2],
    )
    grad_events, d_small = sync([c0, c1], grad_events, d_small)
    c0.fourth()
    c1.third()
    d_small, _ = step(d_small, c1.state[0])
    d_small = d_small.reshape(places, 2, width, PACK)
    d_other = swap_cores(lax.dynamic_index_in_dim(d_small, 1 - core, 1, keepdims=False))
    d_mine = total(lax.dynamic_index_in_dim(d_small, core, 1, keepdims=False), [d_other])
    d_mine = d_mine.astype(bf16).reshape(nx * ny, nz, 2, width, PACK)
    d_parts = [d_mine[k] for k in range(nx * ny)]
    d_in = box.hand_out_plane(d_parts)
    order = position[None, :] == jnp.arange(rows, dtype=f32)[:, None]
    grad_embeds = lax.dot_general(
        order.astype(bf16), grad_events, (((0,), (0,)), ((), ())), preferred_element_type=f32
    ).astype(bf16)
    predicted = in_order(role, row_out, rows_in, 1)
    predictions = jnp.sum(jnp.where(order, predicted[0][:, None], 0.0), axis=0)
    predictions = jnp.broadcast_to(predictions[None], (8, rows))
    d_mine, d_in, grad_embeds, predictions = sync(
        [c0, c1], d_parts[0], d_in, grad_embeds, predictions
    )
    c1.fourth()
    d_mine, _ = step(d_mine, c1.state[0])
    d_mine = total(d_mine, d_in).astype(bf16)
    same = [lax.dynamic_index_in_dim(d_mine[k], role, 0, keepdims=False) for k in range(nz)]
    flip = [lax.dynamic_index_in_dim(d_mine[k], 1 - role, 0, keepdims=False) for k in range(nz)]
    d_in = box.hand_out(same, "z") + box.hand_out_flip(flip)
    grad_embeds = jnp.where(at_home, grad_embeds, swap_cores(grad_embeds))
    predictions = jnp.where(at_home, predictions, swap_cores(predictions))[0]
    d_in, grad_embeds, predictions = sync([c1], d_in, grad_embeds, predictions)
    (
        proj_grad, tower_grad, top, shared_gate, domain_gate, proj_b_grad, in_bias_grad, tower_b_grad,
        tower_out_grad, *vectors,
    ) = call_small([same[0]] + d_in)
    grad_w_in, grad_w_out = call_place(
        ints, [c0.state[0], c1.state[0]], [c0.state[1], c1.state[1]]
    )
    return (
        predictions,
        grad_embeds,
        proj_grad.T,
        proj_b_grad[0],
        grad_w_in,
        in_bias_grad,
        jnp.swapaxes(grad_w_out, 1, 2),
        *vectors,
        jnp.swapaxes(top, 1, 2),
        jnp.swapaxes(shared_gate, 1, 2),
        jnp.swapaxes(domain_gate, 1, 2),
        tower_grad,
        tower_b_grad,
        tower_out_grad,
        d_logit_bias[0, :DOM],
    )


def solution(mesh):
    both = ("dp", "tensor")
    in_specs = (
        P("dp", None),
        P("dp", None),
        P(),
        P("dp"),
        P(None, both),
        P(both),
        P(None, "dp", "tensor"),
        P(None, both),
        P(None, "tensor", "dp"),
        P(None, both),
        P(None, both),
        P(None, both),
        P(None, both, None),
        P(None, both, None),
        P(None, both, None),
        P(None, both, None),
        P(None, both),
        P(None, both),
        P(),
    )
    out_specs = (
        P("dp"),
        P("dp", None),
        P(None, both),
        P(both),
        P(None, "dp", "tensor"),
        P(None, both),
        P(None, "tensor", "dp"),
        P(None, both),
        P(None, both),
        P(None, both),
        P(None, both, None),
        P(None, both, None),
        P(None, both, None),
        P(None, both, None),
        P(None, both),
        P(None, both),
        P(),
    )
    return jax.shard_map(
        functools.partial(per_device, Box(mesh.shape["dp"])),
        mesh=mesh,
        in_specs=in_specs,
        out_specs=out_specs,
        check_vma=False,
    )
```

```python
import functools
import math

import jax
import jax.numpy as jnp
import numpy as np
from jax import lax
from jax.experimental import pallas as pl
from jax.experimental.pallas import tpu as pltpu
from jax.sharding import PartitionSpec as P

D = 512
H = 1024
HALF = H // 2
TW = 256
S = 4
DOM = 4
K = 2
EPS = 1e-05
FROZEN_SHARE = 0.25
TILE = 256
LOCAL = 6
CHUNKS = ((0, 1, 2), (3, 4, 5))
VMEM_LIMIT = 48 * 1024 * 1024
PACK = 1792
SETS = (
    tuple(range(2)) + tuple(S + K * d for d in reversed(range(DOM))),
    tuple(range(2, 4)) + tuple(S + K * d + 1 for d in range(DOM)),
)
COEF, SCALE, DCOEF, DOMAIN, LABEL, WEIGHT, BIAS = 0, 6, 12, 18, 19, 20, 21
LOW, HIGH, ROLE, DOMAIN_OF, START, END, CORE = 0, 4, 8, 9, 13, 17, 21

bf16 = jnp.bfloat16
f32 = jnp.float32


def dims_of(count):
    if count % 4 == 0:
        rest = count // 4
        root = math.isqrt(rest)
        if root * root == rest:
            return (4, root, root)
    return (count, 1, 1)


class Box:
    def __init__(self, count):
        first, second, third = dims_of(count)
        self.count = count
        self.dims = (2, first // 2, second, third)
        self.strides = (second * third, 2 * second * third, third, 1)

    def role(self, chip):
        return (chip // self.strides[0]) % 2

    def partner(self, chip):
        return chip + (1 - 2 * self.role(chip)) * self.strides[0]

    def send(self, values, flip=0, z=0, y=0, x=0):
        pairs = []
        for chip in range(self.count):
            to = chip
            for step, size, stride in zip((flip, z, y, x), self.dims, self.strides):
                place = (chip // stride) % size
                to += ((place + step) % size - place) * stride
            pairs.append((chip, to))
        return lax.ppermute(values, "dp", pairs)

    def to_partner(self, values, home):
        pairs = []
        for chip in range(self.count):
            for core in range(2):
                if (core == self.role(chip)) == home:
                    pairs.append((2 * chip + core, 2 * self.partner(chip) + core))
        return lax.ppermute(values, ("dp", "tensor"), pairs)

    def pieces(self, values, dim):
        size = self.dims[("flip", "z", "y", "x").index(dim)]
        return [self.send(values, **{dim: -k}) for k in range(1, size)]

    def hand_out(self, parts, dim):
        return [self.send(part, **{dim: k}) for k, part in enumerate(parts) if k]

    def line(self, same, other):
        steps = range(1, self.dims[1])
        return [self.send(same, z=-z) for z in steps], [self.send(other, flip=1, z=-z) for z in steps]

    def in_line(self, own, flip, found, role, axis):
        same, other = found
        return [in_order(role, s, o, axis) for s, o in zip([own] + same, [flip] + other)]

    def hand_out_flip(self, parts):
        return [self.send(part, flip=1, z=k) for k, part in enumerate(parts)]

    def plane(self):
        _, _, ny, nx = self.dims
        return [(x, y) for x in range(nx) for y in range(ny)][1:]

    def gather_plane(self, values):
        return [values] + [self.send(values, y=-y, x=-x) for x, y in self.plane()]

    def hand_out_plane(self, parts):
        return [self.send(part, y=y, x=x) for part, (x, y) in zip(parts[1:], self.plane())]

    def same_sum(self, values, found, dim):
        number = ("flip", "z", "y", "x").index(dim)
        size, stride = self.dims[number], self.strides[number]
        found = jnp.stack([values] + found)
        if size > 2:
            mine = (lax.axis_index("dp") // stride) % size
            found = jnp.take(found, (jnp.arange(size) - mine) % size, axis=0)
        return functools.reduce(jnp.add, [found[k] for k in range(size)])

    def ahead(self, place):
        me = lax.axis_index("dp")
        chip, weight = 0, 1
        for dim, (size, stride) in enumerate(zip(self.dims, self.strides)):
            mine = (me // stride) % size if dim else 0
            chip = chip + ((mine + (place // weight) % size) % size) * stride
            weight *= size
        return chip


def swap_cores(values):
    return lax.ppermute(values, "tensor", [(0, 1), (1, 0)])


def in_order(which, own, other, axis):
    return jnp.where(
        which == 0,
        jnp.concatenate([own, other], axis),
        jnp.concatenate([other, own], axis),
    )


def step(*values):
    return lax.optimization_barrier(values)


def total(first, arrived):
    return functools.reduce(jnp.add, [a.astype(f32) for a in arrived], first.astype(f32))


def gelu_parts(v):
    inner = math.sqrt(2.0 / math.pi)
    square = v * v
    th = jnp.tanh(v * (inner + inner * 0.044715 * square))
    half = 0.5 * (1.0 + th)
    act = v * half
    slope = half + 0.5 * v * (1.0 - th * th) * (inner + 3.0 * inner * 0.044715 * square)
    return act, slope


def nt(a, b):
    return lax.dot_general(a, b, (((1,), (1,)), ((), ())), preferred_element_type=f32)


def tn(a, b):
    return lax.dot_general(a, b, (((0,), (0,)), ((), ())), preferred_element_type=f32)


def nn(a, b):
    return jnp.dot(a, b, preferred_element_type=f32)


def softmax_rows(v):
    e = jnp.exp(v - jnp.max(v, axis=0, keepdims=True))
    return e / jnp.sum(e, axis=0, keepdims=True)


def prepare_kernel(
    ints, floats, rows_ref, own_ref, in_ref, proj_ref, gates_ref, vec_ref, ev_ref, x_ref, mix_ref, cols_ref, prob_ref, embeds_ref, arrived
):
    tiles_of_half = pl.num_programs(0) // 2
    index = pl.program_id(0)
    role = ints[ROLE]
    count = rows_ref.shape[1]
    at_home = ints[CORE] == role

    @pl.when((index == 0) & at_home)
    def _():
        copy = pltpu.make_async_copy(own_ref, embeds_ref, arrived.at[0])
        copy.start()
        copy.wait()

    @pl.when((index == 0) & jnp.logical_not(at_home))
    def _():
        copy = pltpu.make_async_copy(in_ref, embeds_ref, arrived.at[0])
        copy.start()
        copy.wait()

    slot = index * TILE + lax.broadcasted_iota(jnp.int32, (TILE, count), 0)
    here = rows_ref[0:1, :].astype(jnp.int32) == slot
    order = jnp.where(here, 1.0, 0.0).astype(bf16)
    label = jnp.sum(jnp.where(here, rows_ref[1:2, :], 0.0), axis=1, keepdims=True)
    events = nn(order, embeds_ref[...]).astype(bf16)
    ev_ref[...] = events
    mixed = nt(events, proj_ref[...]) + vec_ref[3 * LOCAL : 3 * LOCAL + 1, :]
    low = mixed.astype(bf16)
    x_ref[...] = low
    mix_ref[...] = mixed * jnp.where(index // tiles_of_half == role, 1.0, 0.0)
    logits = jnp.transpose(nn(low, gates_ref[...]))
    place = index * TILE + lax.broadcasted_iota(jnp.int32, (1, TILE), 1)
    picks = [
        jnp.where((place >= ints[START + d]) & (place < ints[END + d]), 1.0, 0.0) for d in range(DOM)
    ]

    def pick(low_row, size):
        return softmax_rows(
            functools.reduce(
                jnp.add,
                [picks[d] * logits[low_row + d * size : low_row + (d + 1) * size] for d in range(DOM)],
            )
        )

    top, shared, domain = pick(0, 2), pick(2 * DOM, S), pick((2 + S) * DOM, K)
    prob_ref[...] = jnp.concatenate([top, shared, domain], axis=0)
    first = role == 0
    own_shared = top[0:1] * jnp.where(first, shared[:2], shared[2:])
    own_domain = top[1:2] * jnp.where(first, domain[0:1], domain[1:2])
    coef = [own_domain * jnp.where(first, picks[DOM - 1 - d], picks[d]) for d in range(DOM)]
    table = [
        own_shared,
        *coef,
        jnp.zeros((DOMAIN - SCALE, TILE), f32),
        sum(float(d) * picks[d] for d in range(DOM)),
        jnp.zeros((1, TILE), f32),
        sum(floats[d] * picks[d] for d in range(DOM)),
        sum(floats[DOM + d] * picks[d] for d in range(DOM)),
        jnp.zeros((128 - BIAS - 1, TILE), f32),
    ]
    cols_ref[...] = with_column(jnp.transpose(jnp.concatenate(table, axis=0)), LABEL, label)


def with_column(table, column, values):
    lane = lax.broadcasted_iota(jnp.int32, table.shape, 1)
    return jnp.where(lane == column, values, table)


def tiles_of(expert, ints, first, count):
    low = jnp.maximum(ints[LOW + expert - 2], first)
    high = jnp.minimum(ints[HIGH + expert - 2], first + count)
    return low - first, jnp.maximum(high, low) - first


def each_span(expert, ints, first, rows, work):
    if expert < 2:
        work(slice(0, rows))
    else:
        low, high = tiles_of(expert, ints, first, rows // TILE)

        def one(index, _):
            work(pl.ds(pl.multiple_of(index * TILE, TILE), TILE))
            return 0

        lax.fori_loop(low, high, one, 0)


def join(pieces, held):
    count = len(pieces) // 2
    for core in range(2):
        mine = pieces[core * count : core * count + count]
        by_x, by_y = split_pieces(mine)
        nx, ny = len(by_x), len(by_y)
        rows = by_x[0].shape[3]
        nz = by_x[0].shape[1]

        def at(x, y, z):
            return pl.ds(((x * ny + y) * nz + z) * rows, rows)

        for x in range(nx):
            for y in range(ny):
                for z in range(nz):
                    held[core][at(x, y, z), :] = by_x[x][y, z, 0]
                    held[2 + core][at(x, y, z), :] = by_y[y][x, z, 0]


def split_pieces(pieces):
    nx = pieces[-1].shape[0]
    return pieces[:nx], pieces[nx:]


def forward_kernel(experts, own, aliased, number, gives, ints, x_ref, *refs):
    arrays = sorted({e // 3 for e in experts})
    weights = {a: refs[number * k : number * (k + 1)] for k, a in enumerate(arrays)}
    refs = refs[number * len(arrays) :]
    refs, held = refs[:-4], refs[-4:]
    wi_a, wi_b, wo_a, wo_b = held
    bi_ref, vec_ref, cols_in, mix_in = refs[:4]
    cols_ref, mix_ref, *norm_refs = refs[4 + aliased :]
    if gives:
        *norm_refs, give_ref = norm_refs
    norm_refs = dict(zip(arrays, norm_refs))
    rows = x_ref.shape[0]
    half = ints[ROLE] if own else 1 - ints[ROLE]
    step = pl.program_id(0)

    @pl.when(step == 0)
    def _():
        cols_ref[...] = cols_in[...]
        mix_ref[...] = mix_in[...]

    def work(expert, span):
        x = x_ref[span, :]
        pre_a = nn(x, wi_a[...]) + bi_ref[expert : expert + 1, :HALF]
        act_a = gelu_parts(pre_a)[0].astype(bf16)
        pre_b = nn(x, wi_b[...]) + bi_ref[expert : expert + 1, HALF:]
        act_b = gelu_parts(pre_b)[0].astype(bf16)
        out = nt(act_a, wo_a[...]) + nt(act_b, wo_b[...]) + vec_ref[expert : expert + 1, :]
        centre = jnp.mean(out, axis=1, keepdims=True)
        centred = out - centre
        scale = lax.rsqrt(jnp.mean(centred * centred, axis=1, keepdims=True) + EPS)
        norm = centred * scale
        norm_refs[expert // 3][0, span, :] = norm.astype(bf16)
        cols = cols_ref[span, :]
        cols_ref[span, :] = with_column(cols, SCALE + expert, scale)
        gain = vec_ref[LOCAL + expert : LOCAL + expert + 1, :]
        shift = vec_ref[2 * LOCAL + expert : 2 * LOCAL + expert + 1, :]
        mix_ref[span, :] += cols[:, COEF + expert : COEF + expert + 1] * (norm * gain + shift)

    for place, expert in enumerate(experts):

        @pl.when(step == place)
        def _(expert=expert):
            join(weights[expert // 3], held)
            each_span(expert, ints, half * (rows // TILE), rows, functools.partial(work, expert))

    if gives:

        @pl.when(step == len(experts) - 1)
        def _():
            give_ref[...] = mix_ref[...].astype(bf16)


def backward_kernel(experts, halves, keeps_back, adds, number, ints, x_ref, *refs):
    gb_refs, refs = refs[: len(halves)], refs[len(halves) :]
    norm_ref, pieces, refs = refs[0], refs[1 : 1 + number], refs[1 + number :]
    bi_ref, vec_ref, cols_in = refs[:3]
    refs, held = refs[3:-4], refs[-4:]
    wi_a, wi_b, wo_a, wo_b = held
    join(pieces, held)
    back_in, refs = refs[0], refs[1:]
    if adds:
        dvec_in, dbi_in = refs[:2]
        refs = refs[2:]
    cols_ref, back_ref, keep_ref, give_ref, dvec_ref, dbi_ref, in_a, in_b, out_a, out_b = refs
    rows = x_ref.shape[0]
    half_tiles = rows // TILE // len(halves)
    first = 0 if len(halves) == 2 else (ints[ROLE] if halves[0] == "own" else 1 - ints[ROLE]) * half_tiles
    step = pl.program_id(0)

    @pl.when(step == 0)
    def _():
        cols_ref[...] = cols_in[...]
        back_ref[...] = back_in[...] if keeps_back else jnp.zeros_like(back_ref)

    dvec_ref[...] = dvec_in[...] if adds else jnp.zeros_like(dvec_ref)
    dbi_ref[...] = dbi_in[...] if adds else jnp.zeros_like(dbi_ref)

    def work(expert, span):
        whole = isinstance(span, slice)

        def add(ref, target, which, values):
            if whole:
                target[0, which] = values.astype(bf16)
            else:
                ref[...] += values

        x = x_ref[span, :]
        norm = norm_ref[0, span, :].astype(f32)
        cols = cols_ref[span, :]
        if len(halves) == 1:
            grad_block = gb_refs[0][span, :].astype(f32)
        else:
            half = span.start // (half_tiles * TILE)
            inner = pl.ds(pl.multiple_of(span.start - half * (half_tiles * TILE), TILE), TILE)
            grad_block = jnp.where(
                half == ints[ROLE], gb_refs[0][inner, :].astype(f32), gb_refs[1][inner, :].astype(f32)
            )
        gain = vec_ref[LOCAL + expert : LOCAL + expert + 1, :]
        shift = vec_ref[2 * LOCAL + expert : 2 * LOCAL + expert + 1, :]
        scale = cols[:, SCALE + expert : SCALE + expert + 1]
        grad_exp = cols[:, COEF + expert : COEF + expert + 1] * grad_block
        scaled = grad_exp * norm
        dx = grad_exp * gain
        first_mean = jnp.mean(dx, axis=1, keepdims=True)
        second_mean = jnp.mean(dx * norm, axis=1, keepdims=True)
        grad_sum = scale * (dx - first_mean - norm * second_mean)
        grad_low = grad_sum.astype(bf16)
        pre_a = nn(x, wi_a[...]) + bi_ref[expert : expert + 1, :HALF]
        act_a, slope_a = gelu_parts(pre_a)
        low_a = (nn(grad_low, wo_a[...]) * slope_a).astype(bf16)
        pre_b = nn(x, wi_b[...]) + bi_ref[expert : expert + 1, HALF:]
        act_b, slope_b = gelu_parts(pre_b)
        low_b = (nn(grad_low, wo_b[...]) * slope_b).astype(bf16)
        add(out_a, keep_ref, 1, tn(grad_low, act_a.astype(bf16)))
        add(in_a, keep_ref, 0, tn(x, low_a))
        add(out_b, give_ref, 1, tn(grad_low, act_b.astype(bf16)))
        add(in_b, give_ref, 0, tn(x, low_b))
        back_ref[span, :] += nt(low_a, wi_a[...]) + nt(low_b, wi_b[...])
        dcoef = jnp.sum(grad_block * (norm * gain + shift), axis=1, keepdims=True)
        if expert < 2:
            cols_ref[span, :] = with_column(cols, DCOEF + expert, dcoef)
        else:
            mine = cols[:, DOMAIN : DOMAIN + 1] == ints[DOMAIN_OF + expert - 2].astype(f32)
            column = cols[:, DCOEF + 2 : DCOEF + 3] + jnp.where(mine, dcoef, 0.0)
            cols_ref[span, :] = with_column(cols, DCOEF + 2, column)
        dvec_ref[0, 0:1, :] += jnp.sum(grad_sum, axis=0, keepdims=True)
        dvec_ref[0, 1:2, :] += jnp.sum(scaled, axis=0, keepdims=True)
        dvec_ref[0, 2:3, :] += jnp.sum(grad_exp, axis=0, keepdims=True)
        dbi_ref[0, 0:1, :HALF] += jnp.sum(low_a.astype(f32), axis=0, keepdims=True)
        dbi_ref[0, 0:1, HALF:] += jnp.sum(low_b.astype(f32), axis=0, keepdims=True)

    for place, expert in enumerate(experts):

        @pl.when(step == place)
        def _(expert=expert):
            if expert >= 2:
                for ref in (in_a, in_b, out_a, out_b):
                    ref[...] = jnp.zeros_like(ref)
            each_span(expert, ints, first, rows, functools.partial(work, expert))
            if expert >= 2:
                keep_ref[0, 0] = in_a[...].astype(bf16)
                keep_ref[0, 1] = out_a[...].astype(bf16)
                give_ref[0, 0] = in_b[...].astype(bf16)
                give_ref[0, 1] = out_b[...].astype(bf16)


def tower_kernel(
    ints, mix_ref, other_ref, cols_ref, tw_ref, tv_ref, out_ref, gb_ref, low_ref, dw_ref, dv_ref, db_ref
):
    @pl.when(pl.program_id(0) == 0)
    def _():
        db_ref[...] = jnp.zeros_like(db_ref)
        dw_ref[...] = jnp.zeros_like(dw_ref)
        dv_ref[...] = jnp.zeros_like(dv_ref)

    bias = tv_ref[0:1, :]
    head = tv_ref[1:2, :]
    cols = cols_ref[...]
    block = (mix_ref[...] + other_ref[...].astype(f32)).astype(bf16)
    tower = slice(PACK - 128 - DOM * TW, PACK - 128)
    pre = nn(block, tw_ref[:, tower]) + bias
    act, slope = gelu_parts(pre)
    group = lax.broadcasted_iota(jnp.int32, pre.shape, 1) // TW
    mine = group == cols[:, DOMAIN : DOMAIN + 1].astype(jnp.int32)
    act = jnp.where(mine, act, 0.0)
    logit = jnp.sum(act * head, axis=1, keepdims=True) + cols[:, BIAS : BIAS + 1]
    predicted = 1.0 / (1.0 + jnp.exp(-logit))
    grad_logit = cols[:, WEIGHT : WEIGHT + 1] * (predicted - cols[:, LABEL : LABEL + 1])
    lane = lax.broadcasted_iota(jnp.int32, cols.shape, 1)
    out_ref[...] = jnp.transpose(jnp.where(lane == 0, predicted, jnp.where(lane == 1, grad_logit, 0.0)))[:8]
    by_domain = jnp.where(lane.astype(f32) == cols[:, DOMAIN : DOMAIN + 1], grad_logit, 0.0)
    db_ref[0:1, :] += jnp.sum(by_domain, axis=0, keepdims=True)
    dv_ref[1:2, :] += jnp.sum(grad_logit * act, axis=0, keepdims=True)
    grad_pre = jnp.where(mine, grad_logit * head * slope, 0.0)
    dv_ref[0:1, :] += jnp.sum(grad_pre, axis=0, keepdims=True)
    grad_low = grad_pre.astype(bf16)
    grad_block = nt(grad_low, tw_ref[:, tower])
    gb_ref[...] = grad_block
    low_ref[...] = grad_block.astype(bf16)
    dw_ref[...] += tn(block, grad_low)


def softmax_back(probability, grad_probs):
    return probability * (grad_probs - jnp.sum(probability * grad_probs, axis=0, keepdims=True))


def gate_kernel(ints, back_ref, cols_ref, prob_ref, x_ref, gates_ref, sum_ref, low_ref, gate_ref):
    index = pl.program_id(0)
    first = ints[ROLE] == 0

    @pl.when(index == 0)
    def _():
        gate_ref[...] = jnp.zeros_like(gate_ref)

    mine = jnp.transpose(cols_ref[...])[DCOEF : DCOEF + 3]
    none = jnp.zeros_like(mine)
    one, two = jnp.where(first, mine, none), jnp.where(first, none, mine)
    d_shared = jnp.concatenate([one[0:2], two[0:2]], axis=0)
    d_domain = jnp.concatenate([one[2:3], two[2:3]], axis=0)
    top, shared, domain = prob_ref[0:2, :], prob_ref[2:6, :], prob_ref[6:8, :]
    d_top = jnp.concatenate(
        [
            jnp.sum(d_shared * shared, axis=0, keepdims=True),
            jnp.sum(d_domain * domain, axis=0, keepdims=True),
        ],
        axis=0,
    )
    grads = (
        softmax_back(top, d_top),
        softmax_back(shared, d_shared * top[0:1]),
        softmax_back(domain, d_domain * top[1:2]),
    )
    rows = top.shape[1]
    place = index * rows + lax.broadcasted_iota(jnp.int32, (1, rows), 1)
    picks = [
        jnp.where((place >= ints[START + d]) & (place < ints[END + d]), 1.0, 0.0) for d in range(DOM)
    ]
    spread = jnp.concatenate(
        [picks[d] * grad for grad in grads for d in range(DOM)] + [jnp.zeros((96, rows), f32)],
        axis=0,
    )
    spread = jnp.transpose(spread).astype(bf16)
    gate_ref[...] += tn(x_ref[...], spread)
    added = back_ref[...] + nt(spread, gates_ref[...])
    sum_ref[...] = added
    low_ref[...] = added.astype(bf16)


def call_gate(ints, back, cols, probs, x, small):
    rows = x.shape[0]
    half = rows // 2

    def tile(width):
        return pl.BlockSpec((half, width), lambda i, *_: (i, 0))

    return pl.pallas_call(
        gate_kernel,
        grid_spec=pltpu.PrefetchScalarGridSpec(
            num_scalar_prefetch=1,
            grid=(2,),
            in_specs=[
                tile(D),
                tile(128),
                pl.BlockSpec((8, half), lambda i, *_: (0, i)),
                tile(D),
                GATES_SPEC,
            ],
            out_specs=(tile(D), tile(D), fixed((D, 128))),
        ),
        out_shape=(
            jax.ShapeDtypeStruct((rows, D), f32),
            jax.ShapeDtypeStruct((rows, D), bf16),
            jax.ShapeDtypeStruct((D, 128), f32),
        ),
        compiler_params=params(),
        cost_estimate=pl.CostEstimate(
            flops=4 * rows * D * 128, bytes_accessed=10_000_000, transcendentals=0
        ),
        name="gates",
    )(ints, back, cols, probs, x, small)


def hidden_lines(ints, lane_ref, tv_ref, line_refs):
    first_set, first_core = ints[ROLE] == 0, ints[CORE] == 0
    mine = [r[k, 0:1, :] for r in line_refs for k in range(r.shape[0])]
    mine = jnp.concatenate(mine, axis=0)
    mine = jnp.where(first_core, mine, pltpu.roll(mine, HALF, 1))
    mine = jnp.where(first_set, mine, 0.0), jnp.where(first_set, 0.0, mine)
    found = {j: mine[r][i : i + 1] for r, row in enumerate(SETS) for i, j in enumerate(row)}
    mine = jnp.concatenate([found[j] for j in range(2 * LOCAL)], axis=0).astype(bf16)

    def lanes(values, row):
        lane = lax.broadcasted_iota(jnp.int32, (H, D), 0)
        chosen = jnp.where(lane == lane_ref[row : row + 1, :], 1.0, 0.0).astype(bf16)
        return nn(values, chosen)

    tower = tv_ref[...].astype(bf16)
    rows = [lanes(mine, 0), lanes(mine, 1)]
    head = lane_ref[6:7, :] == 1
    for d in range(DOM):
        both = lanes(tower, 2 + d)
        rows.append(jnp.where(head, both[1:2], both[0:1]))
    return rows


def finish_kernel(
    ints, gb_ref, gb_in_ref, sum_ref, in_ref, ev_ref, proj_ref, tower_ref, gate_ref, *refs
):
    lane_ref, tv_ref, *vec_refs, ge_ref, small_ref, proj_sum, bias_sum = refs
    vec_refs, line_refs = vec_refs[: len(vec_refs) // 2], vec_refs[len(vec_refs) // 2 :]
    index = pl.program_id(0)
    last = pl.num_programs(0) - 1
    first = ints[ROLE] == 0
    at_home = jnp.where(ints[CORE] == ints[ROLE], 1.0, 0.0)
    mine_half = index == ints[ROLE]

    @pl.when(index == 0)
    def _():
        for ref in (proj_sum, bias_sum):
            ref[...] = jnp.zeros_like(ref)

    grad_mixed = jnp.where(mine_half, gb_ref[...], gb_in_ref[...].astype(f32))
    grad_mixed = at_home * (grad_mixed + sum_ref[...] + in_ref[...].astype(f32))
    bias_sum[0:1, :] += jnp.sum(grad_mixed, axis=0, keepdims=True)
    low = grad_mixed.astype(bf16)
    proj_sum[...] += tn(low, ev_ref[...])
    ge_ref[...] = nn(low, proj_ref[...]).astype(bf16)

    @pl.when(index == last)
    def _():
        e_in = proj_sum.shape[1]
        vectors = jnp.concatenate(
            [r[k, 0:3, :] for r in vec_refs for k in range(r.shape[0])], axis=0
        )
        rows = jnp.concatenate(
            [
                jnp.zeros((32, D), f32),
                jnp.where(first, vectors, 0.0),
                jnp.where(first, 0.0, vectors),
                bias_sum[0:1, :],
                *hidden_lines(ints, lane_ref, tv_ref, line_refs),
                jnp.zeros((31, D), f32),
            ],
            axis=0,
        )
        small_ref[:, :e_in] = proj_sum[...].astype(bf16)
        small_ref[:, e_in : e_in + DOM * TW] = tower_ref[...].astype(bf16)
        small_ref[:, e_in + DOM * TW :] = (gate_ref[...] + jnp.transpose(rows)).astype(bf16)


def call_finish(ints, gb, gb_in, added, arrived, events, small, tower, gate, lanes, tower_vec, sums):
    rows, e_in = events.shape
    half = rows // 2

    def tile(width):
        return pl.BlockSpec((half, width), lambda i, *_: (i, 0))

    halves = (gb, gb_in)
    wholes = (tower, gate, lanes, tower_vec)
    vecs = [v for v, _ in sums] + [b for _, b in sums]
    return pl.pallas_call(
        finish_kernel,
        grid_spec=pltpu.PrefetchScalarGridSpec(
            num_scalar_prefetch=1,
            grid=(2,),
            in_specs=[fixed(a.shape) for a in halves]
            + [tile(D), tile(D), tile(e_in), proj_spec(e_in)]
            + [fixed(a.shape) for a in (*wholes, *vecs)],
            out_specs=(tile(e_in), fixed((D, PACK))),
            scratch_shapes=[pltpu.VMEM((D, e_in), f32), pltpu.VMEM((8, D), f32)],
        ),
        out_shape=(jax.ShapeDtypeStruct((rows, e_in), bf16), jax.ShapeDtypeStruct((D, PACK), bf16)),
        compiler_params=params(),
        cost_estimate=pl.CostEstimate(flops=4 * rows * D * e_in, bytes_accessed=14_000_000, transcendentals=0),
        name="finish",
    )(ints, *halves, added, arrived, events, small, *wholes, *vecs)


VECTOR_ROW = {j: 32 + 18 * r + 3 * i for r, row in enumerate(SETS) for i, j in enumerate(row)}


def small_kernel(*refs):
    parts, vec_refs = refs[:-12], refs[-3:]
    proj_ref, tower_ref, top_ref, shared_ref, domain_ref, bias_ref, hidden_ref, tb_ref, to_ref = refs[-12:-3]
    added = functools.reduce(jnp.add, [p[...].astype(f32) for p in parts])
    width, e_in = proj_ref.shape
    proj_ref[...] = added[:, :e_in]
    for d in range(DOM):
        tower_ref[d] = added[:, e_in + d * TW : e_in + (d + 1) * TW]
    rows = jnp.concatenate([added[:, e_in + DOM * TW :], jnp.zeros((128 - width, 128), f32)], axis=0)
    rows = jnp.transpose(rows)[:, :width]
    for ref, low, size in ((top_ref, 0, 2), (shared_ref, 2 * DOM, S), (domain_ref, (2 + S) * DOM, K)):
        for d in range(DOM):
            ref[d] = rows[low + d * size : low + (d + 1) * size]
    bias_ref[...] = rows[68:69]
    hidden_ref[:, :width] = rows[69:81]
    hidden_ref[:, width:] = rows[81:93]
    tb_ref[...] = rows[93:97, : width // 2]
    to_ref[...] = rows[93:97, width // 2 :]
    for which, ref in enumerate(vec_refs):
        for j in range(2 * LOCAL):
            ref[j : j + 1, :] = rows[VECTOR_ROW[j] + which : VECTOR_ROW[j] + which + 1]


def call_small(parts):
    width = parts[0].shape[0]
    e_in = PACK - DOM * TW - 128
    shapes = [(width, e_in), (DOM, width, TW), (DOM, 2, width), (DOM, S, width), (DOM, K, width), (1, width)]
    shapes += [(2 * LOCAL, 2 * width), (DOM, width // 2), (DOM, width // 2)]
    shapes += [(2 * LOCAL, width)] * 3
    return pl.pallas_call(
        small_kernel,
        grid=(1,),
        in_specs=[fixed(p.shape) for p in parts],
        out_specs=tuple(fixed(shape) for shape in shapes),
        out_shape=tuple(jax.ShapeDtypeStruct(shape, f32) for shape in shapes),
        compiler_params=params(),
        name="small",
    )(*parts)


def place_kernel(ints, *refs):
    *parts, in_ref, out_ref = refs
    half = len(parts) // 2
    first = ints[ROLE] == 0
    for chunk, (own, other) in enumerate(zip(parts[:half], parts[half:])):
        for place, expert in enumerate(CHUNKS[chunk]):
            for which, ref in enumerate((in_ref, out_ref)):
                a, b = own[which, place].astype(f32), other[which, place].astype(f32)
                ref[SETS[0][expert]] = jnp.where(first, a, b)
                ref[SETS[1][expert]] = jnp.where(first, b, a)


def call_place(ints, own, other):
    rows, width = own[0].shape[2:]
    shape = (2 * LOCAL, rows, width)
    return pl.pallas_call(
        place_kernel,
        grid_spec=pltpu.PrefetchScalarGridSpec(
            num_scalar_prefetch=1,
            grid=(1,),
            in_specs=[fixed(a.shape) for a in (*own, *other)],
            out_specs=(fixed(shape), fixed(shape)),
        ),
        out_shape=(jax.ShapeDtypeStruct(shape, f32),) * 2,
        compiler_params=params(),
        name="place",
    )(ints, *own, *other)


def params():
    return pltpu.CompilerParams(vmem_limit_bytes=VMEM_LIMIT)


def fixed(shape):
    return pl.BlockSpec(shape, lambda i, *_: (0,) * len(shape))


def pack_kernel(proj_ref, tower_ref, gate_ref, rest_ref, out_ref):
    width, e_in = proj_ref.shape
    out_ref[:, :e_in] = proj_ref[...]
    for d in range(DOM):
        out_ref[:, e_in + d * TW : e_in + (d + 1) * TW] = tower_ref[d]
    gates, rest = gate_ref[...].astype(f32), rest_ref[...].astype(f32)
    rows = []
    for low, size in ((0, 2), (2, S), (2 + S, K)):
        rows += [gates[d, low : low + size] for d in range(DOM)]
    rows += [rest[:12, k * width : (k + 1) * width] for k in range(3)] + [rest[16:17, :width]]
    rows += [rest[:12, k * width : (k + 1) * width] for k in (3, 4)] + [rest[12:16, :width]]
    rows = jnp.concatenate(rows + [jnp.zeros((31, width), f32)], axis=0)
    rows = jnp.concatenate([rows, jnp.zeros((128, 128 - width), f32)], axis=1)
    out_ref[:, e_in + DOM * TW :] = jnp.transpose(rows)[:width].astype(bf16)


def call_pack(*arrays):
    width = arrays[0].shape[0]
    return pl.pallas_call(
        pack_kernel,
        grid=(1,),
        in_specs=[fixed(a.shape) for a in arrays],
        out_specs=fixed((width, PACK)),
        out_shape=jax.ShapeDtypeStruct((width, PACK), bf16),
        compiler_params=params(),
        name="pack",
    )(*arrays)


PICKED = [
    [32 + e for e in row] + [44 + e for e in row] + [56 + e for e in row] + [68] + [127] * 5
    + [69 + e for e in row] + [81 + e for e in row] + [93 + d for d in range(DOM)]
    for row in SETS
]


def unpack_kernel(ints, small_ref, choose_ref, lane_ref, vec_ref, bi_ref, tower_ref):
    vec = nt(choose_ref[0], small_ref[...])
    vec_ref[...] = vec

    def lanes(values, row):
        lane = lax.broadcasted_iota(jnp.int32, (H, D), 0)
        chosen = jnp.where(lane == lane_ref[row : row + 1, :], 1.0, 0.0).astype(bf16)
        return nt(values.astype(bf16), chosen)

    bias = lanes(jnp.concatenate([vec[24:30], jnp.zeros((2, D), f32)], axis=0), 0)
    bias += lanes(jnp.concatenate([vec[30:36], jnp.zeros((2, D), f32)], axis=0), 1)
    bi_ref[...] = jnp.where(ints[1] == 0, bias, pltpu.roll(bias, HALF, 1))
    head = lane_ref[6:7, :] == 1
    tower = jnp.zeros((8, H), f32)
    for d in range(DOM):
        row = vec[36 + d : 37 + d]
        rows = [jnp.where(head, 0.0, row), jnp.where(head, row, 0.0), jnp.zeros((6, D), f32)]
        tower += lanes(jnp.concatenate(rows, axis=0), 2 + d)
    tower_ref[...] = tower


def call_unpack(ints, small, lanes):
    choose = np.zeros((2, 40, 128), np.float32)
    for r in range(2):
        for row, column in enumerate(PICKED[r]):
            choose[r, row, column] = 1.0
    shapes = [(40, D), (8, H), (8, DOM * TW)]
    return pl.pallas_call(
        unpack_kernel,
        grid_spec=pltpu.PrefetchScalarGridSpec(
            num_scalar_prefetch=1,
            grid=(1,),
            in_specs=[
                pl.BlockSpec((D, 128), lambda i, ints: (0, PACK // 128 - 1)),
                pl.BlockSpec((1, 40, 128), lambda i, ints: (ints[0], 0, 0)),
                fixed(lanes.shape),
            ],
            out_specs=tuple(fixed(shape) for shape in shapes),
        ),
        out_shape=tuple(jax.ShapeDtypeStruct(shape, f32) for shape in shapes),
        compiler_params=params(),
        name="unpack",
    )(ints, small, jnp.asarray(choose, bf16), lanes)


def choose_kernel(own_ids, other_ids, in_own, out_own, in_other, out_other, *refs):
    own_refs, other_refs, all_ref = refs[:2], refs[2:4], refs[4]
    step = pl.program_id(0)
    for part in range(2):

        @pl.when(step // 3 == part)
        def _(part=part):
            own_refs[part][0], own_refs[part][1] = in_own[...], out_own[...]
            other_refs[part][0], other_refs[part][1] = in_other[...], out_other[...]

    all_ref[0], all_ref[1] = in_other[...], out_other[...]


def call_choose(own_ids, other_ids, w_in, w_out_t):
    tail = w_in.shape[1:]
    block = (1,) + tail

    def shape(count):
        return jax.ShapeDtypeStruct((2, count) + tail, bf16)

    own = pl.BlockSpec(block, lambda i, a, b: (a[i], 0, 0))
    other = pl.BlockSpec(block, lambda i, a, b: (b[i], 0, 0))
    low = pl.BlockSpec((2,) + block, lambda i, a, b: (0, jnp.minimum(i, 2), 0, 0))
    high = pl.BlockSpec((2,) + block, lambda i, a, b: (0, jnp.maximum(i - 3, 0), 0, 0))
    every = pl.BlockSpec((2,) + block, lambda i, a, b: (0, i, 0, 0))
    return pl.pallas_call(
        choose_kernel,
        grid_spec=pltpu.PrefetchScalarGridSpec(
            num_scalar_prefetch=2,
            grid=(LOCAL,),
            in_specs=[own, own, other, other],
            out_specs=(low, high, low, high, every),
        ),
        out_shape=(shape(3), shape(3), shape(3), shape(3), shape(6)),
        compiler_params=params(),
        cost_estimate=pl.CostEstimate(flops=0, bytes_accessed=3_000_000, transcendentals=0),
        name="choose",
    )(own_ids, other_ids, w_in, w_out_t, w_in, w_out_t)


def proj_spec(e_in):
    return pl.BlockSpec((D, e_in), lambda *_: (0, 0))


GATES_SPEC = pl.BlockSpec((D, 128), lambda *_: (0, PACK // 128 - 1))


def call_prepare(ints, floats, table, embeds, embeds_in, small, vec):
    rows = embeds.shape[0]
    tiles = rows // TILE
    e_in = embeds.shape[1]

    def tile(width):
        return pl.BlockSpec((TILE, width), lambda i, *_: (i, 0))

    return pl.pallas_call(
        prepare_kernel,
        grid_spec=pltpu.PrefetchScalarGridSpec(
            num_scalar_prefetch=2,
            grid=(tiles,),
            in_specs=[fixed(table.shape)]
            + [pl.BlockSpec(memory_space=pl.ANY)] * 2
            + [proj_spec(e_in), GATES_SPEC, fixed(vec.shape)],
            scratch_shapes=[pltpu.VMEM(embeds.shape, bf16), pltpu.SemaphoreType.DMA((1,))],
            out_specs=(
                tile(e_in),
                tile(D),
                tile(D),
                tile(128),
                pl.BlockSpec((8, TILE), lambda i, *_: (0, i)),
            ),
        ),
        out_shape=(
            jax.ShapeDtypeStruct((rows, e_in), bf16),
            jax.ShapeDtypeStruct((rows, D), bf16),
            jax.ShapeDtypeStruct((rows, D), f32),
            jax.ShapeDtypeStruct((rows, 128), f32),
            jax.ShapeDtypeStruct((8, rows), f32),
        ),
        compiler_params=params(),
        cost_estimate=pl.CostEstimate(
            flops=2 * rows * e_in * (rows + D), bytes_accessed=12_000_000, transcendentals=rows * 8
        ),
        name="prepare",
    )(ints, floats, table, embeds, embeds_in, small, small, vec)


def half_spec(own, shape):
    rest = (0,) * (len(shape) - 1)
    return pl.BlockSpec(shape, lambda i, ints: ((ints[ROLE] if own else 1 - ints[ROLE]),) + rest)


def piece_spec(array, place):
    a, b, _, rows, width = array.shape
    return pl.BlockSpec((a, b, 1, rows, width), lambda i, *_: (0, 0, place(i), 0, 0))


MATRICES = [pltpu.VMEM((D, HALF), bf16)] * 4


def call_forward(experts, own, ints, x, weights, bi, vec, cols, mix, norms, gives=False):
    rows = x.shape[0]
    half = rows // 2
    arrays = sorted({e // 3 for e in experts})
    first = {a: min(k for k, e in enumerate(experts) if e // 3 == a) for a in arrays}
    number = {a: sum(1 for e in experts if e // 3 == a) for a in arrays}

    def place(a):
        return lambda i: jnp.clip(i - first[a], 0, number[a] - 1)

    weight_specs = [piece_spec(w, place(a)) for a in arrays for w in weights[a]]
    norm_specs = [
        pl.BlockSpec(
            (1, half, D),
            lambda i, ints, a=a: (place(a)(i), ints[ROLE] if own else 1 - ints[ROLE], 0),
        )
        for a in arrays
    ]
    kept = [norms[a] for a in arrays if a in norms]
    inputs = [x] + [w for a in arrays for w in weights[a]] + [bi, vec, cols, mix] + kept
    at = len(inputs) - len(kept)
    aliases = {at - 1: 0, at: 1}
    aliases.update({at + 1 + k: 2 + k for k in range(len(kept))})
    shared = sum(1 for e in experts if e < 2)
    out = pl.pallas_call(
        functools.partial(
            forward_kernel, experts, own, len(kept), len(weights[arrays[0]]), gives
        ),
        grid_spec=pltpu.PrefetchScalarGridSpec(
            num_scalar_prefetch=1,
            grid=(len(experts),),
            in_specs=[half_spec(own, (half, D))]
            + weight_specs
            + [fixed(bi.shape), fixed(vec.shape), half_spec(own, (half, 128)), half_spec(own, (half, D))]
            + [pl.BlockSpec(memory_space=pl.ANY)] * len(kept),
            out_specs=(half_spec(own, (half, 128)), half_spec(own, (half, D)), *norm_specs)
            + ((fixed((half, D)),) if gives else ()),
            scratch_shapes=MATRICES,
        ),
        out_shape=(
            jax.ShapeDtypeStruct((rows, 128), f32),
            jax.ShapeDtypeStruct((rows, D), f32),
            *[jax.ShapeDtypeStruct((3, rows, D), bf16)] * len(arrays),
        )
        + ((jax.ShapeDtypeStruct((half, D), bf16),) if gives else ()),
        input_output_aliases=aliases,
        compiler_params=params(),
        cost_estimate=pl.CostEstimate(
            flops=4 * (shared + 1) * half * D * H, bytes_accessed=12_000_000, transcendentals=0
        ),
        name="experts_forward",
    )(ints, *inputs)
    found = out[0], out[1], {**norms, **dict(zip(arrays, out[2:]))}
    return found + (out[-1],) if gives else found


def call_backward(experts, halves, ints, x, gbs, norms, weights, bi, vec, cols, back, sums=None):
    rows, count = x.shape[0], len(experts)
    part = rows // 2 * len(halves)
    array, low = experts[0] // 3, experts[0] % 3
    split = any(e // 3 != array for e in experts)

    def span(width):
        if len(halves) == 2:
            return fixed((rows, width))
        return half_spec(halves[0] == "own", (part, width))

    def norm_index(i, ints):
        if len(halves) == 2:
            return (low + i, 0, 0)
        return (low + i, ints[ROLE] if halves[0] == "own" else 1 - ints[ROLE], 0)

    assert not split
    pairs = pl.BlockSpec((1, 2, D, HALF), lambda i, *_: (i, 0, 0, 0))
    vec_spec = pl.BlockSpec((1, 8, D), lambda i, *_: (i, 0, 0))
    bi_spec = pl.BlockSpec((1, 8, H), lambda i, *_: (i, 0, 0))
    mode, back_array = back if back is not None else ("fresh", jnp.zeros((8, 128), f32))
    inputs = [x, *gbs, norms[array], *weights[array], bi, vec, cols, back_array]
    in_specs = (
        [span(D)]
        + [fixed(g.shape) for g in gbs]
        + [pl.BlockSpec((1, part, D), norm_index)]
        + [piece_spec(w, lambda i: low + i) for w in weights[array]]
        + [fixed(bi.shape), fixed(vec.shape), span(128)]
        + [span(D) if mode == "add" else pl.BlockSpec(memory_space=pl.ANY)]
    )
    aliases = {len(inputs) - 1: 0}
    if back is not None:
        aliases[len(inputs)] = 1
    if sums is not None:
        inputs += list(sums)
        in_specs += [vec_spec, bi_spec]
    return pl.pallas_call(
        functools.partial(
            backward_kernel, experts, halves, mode == "add", sums is not None, len(weights[array])
        ),
        grid_spec=pltpu.PrefetchScalarGridSpec(
            num_scalar_prefetch=1,
            grid=(count,),
            in_specs=in_specs,
            out_specs=(span(128), span(D), pairs, pairs, vec_spec, bi_spec),
            scratch_shapes=[pltpu.VMEM((D, HALF), f32)] * 4 + MATRICES,
        ),
        out_shape=(
            jax.ShapeDtypeStruct((rows, 128), f32),
            jax.ShapeDtypeStruct((rows, D), f32),
            jax.ShapeDtypeStruct((count, 2, D, HALF), bf16),
            jax.ShapeDtypeStruct((count, 2, D, HALF), bf16),
            jax.ShapeDtypeStruct((count, 8, D), f32),
            jax.ShapeDtypeStruct((count, 8, H), f32),
        ),
        input_output_aliases=aliases,
        compiler_params=params(),
        cost_estimate=pl.CostEstimate(
            flops=10 * count * (rows // 2) * D * H, bytes_accessed=20_000_000, transcendentals=0
        ),
        name="experts_backward",
    )(ints, *inputs)


def call_tower(ints, mix, other, cols, small, tower_vec):
    rows = other.shape[0]
    tiles = 2
    size = rows // tiles

    def kept(width):
        return pl.BlockSpec((size, width), lambda i, ints: (ints[ROLE] * tiles + i, 0))

    def tile(width):
        return pl.BlockSpec((size, width), lambda i, *_: (i, 0))

    return pl.pallas_call(
        tower_kernel,
        grid_spec=pltpu.PrefetchScalarGridSpec(
            num_scalar_prefetch=1,
            grid=(tiles,),
            in_specs=[kept(D), tile(D), kept(128), fixed(small.shape), fixed(tower_vec.shape)],
            out_specs=(
                pl.BlockSpec((8, size), lambda i, *_: (0, i)),
                tile(D),
                tile(D),
                fixed((D, DOM * TW)),
                fixed((8, DOM * TW)),
                fixed((8, 128)),
            ),
        ),
        out_shape=(
            jax.ShapeDtypeStruct((8, rows), f32),
            jax.ShapeDtypeStruct((rows, D), f32),
            jax.ShapeDtypeStruct((rows, D), bf16),
            jax.ShapeDtypeStruct((D, DOM * TW), f32),
            jax.ShapeDtypeStruct((8, DOM * TW), f32),
            jax.ShapeDtypeStruct((8, 128), f32),
        ),
        compiler_params=params(),
        cost_estimate=pl.CostEstimate(
            flops=6 * rows * D * DOM * TW, bytes_accessed=10_000_000, transcendentals=rows * DOM * TW
        ),
        name="towers",
    )(ints, mix, other, cols, small, tower_vec)


def per_device(
    box,
    embeds,
    domain,
    frozen,
    labels,
    proj_w,
    proj_b,
    w_in,
    in_bias,
    w_out,
    out_bias,
    ln_gain,
    ln_shift,
    gate_top,
    gate_shared,
    gate_domain,
    tower_w,
    tower_b,
    tower_out,
    tower_out_b,
):
    core = lax.axis_index("tensor")
    role = box.role(lax.axis_index("dp"))
    at_home = core == role
    places = box.count
    rows = embeds.shape[0]
    half_rows = rows // 2
    width = proj_w.shape[1]
    e_in = proj_w.shape[0]
    nz, ny, nx = box.dims[1:]
    sets = jnp.array(SETS, jnp.int32)
    set_own, set_other = sets[role], sets[1 - role]

    def half(values, which, axis=0):
        return lax.dynamic_slice_in_dim(values, which * half_rows, half_rows, axis)

    w_out_t = jnp.swapaxes(w_out, 1, 2)
    first, second, first_other, second_other, others = call_choose(set_own, set_other, w_in, w_out_t)

    def wide(values):
        return jnp.pad(values, ((0, 0), (0, 5 * width - values.shape[1])))

    arrays = (
        proj_w.T,
        tower_w,
        jnp.concatenate([jnp.swapaxes(g, 1, 2) for g in (gate_top, gate_shared, gate_domain)], axis=1),
        jnp.concatenate(
            [
                jnp.concatenate([out_bias, ln_gain, ln_shift, in_bias], axis=1),
                wide(jnp.concatenate([tower_b, tower_out], axis=1)),
                wide(proj_b[None]),
            ]
        ),
    )

    flips = box.send(others, flip=1)
    first_z = box.line(first, first_other)
    pack = call_pack(*step(arrays, first)[0])
    pack = in_order(role, pack, box.send(pack, flip=1), 0)
    pack = jnp.concatenate([pack] + box.pieces(pack, "z"))
    flips, first, first_z, second, second_other = step(flips, first, first_z, second, second_other)

    def along_z(shard, flip, found):
        found = box.in_line(shard, flip, found, role, 2)
        return jnp.stack([b[0] for b in found]), jnp.stack([b[1] for b in found])

    first_i, first_o = along_z(first, flips[:, :3], first_z)
    first_iy, first_ox = box.pieces(first_i, "y"), box.pieces(first_o, "x")
    second_z = box.line(second, second_other)
    pack = jnp.concatenate([pack] + box.pieces(pack, "y"))
    pack = jnp.concatenate([pack] + box.pieces(pack, "x")).reshape(places, 1, width, PACK)
    domain, labels = step((domain, labels), first)[0]
    event_rows = jnp.concatenate(
        [domain.astype(f32).T, labels.astype(f32)[None], jnp.zeros((6, rows), f32)]
    )
    event_rows = jnp.where(at_home, event_rows, box.to_partner(event_rows, True))
    ids = event_rows[0]
    onehot = (ids[None, :] == jnp.arange(DOM, dtype=f32)[:, None]).astype(f32)
    rank = jnp.cumsum(onehot, axis=1)
    counts = rank[:, -1]
    ends = jnp.cumsum(counts)
    starts = ends - counts
    position = jnp.sum(onehot * (rank + starts[:, None]), axis=0) - 1.0
    embeds_in = box.to_partner(step(embeds, second_z[0])[0], True)
    first_i, first_o, first_iy, first_ox, second, second_z, flips, starts, ends, position = step(
        first_i, first_o, first_iy, first_ox, second, second_z, flips, starts, ends, position
    )

    small = in_order(core, pack, swap_cores(pack), 1).reshape(D, PACK)
    first_i = jnp.stack([first_i] + first_iy)
    first_o = jnp.stack([first_o] + first_ox)
    first_ix, first_oy = box.pieces(first_i, "x"), box.pieces(first_o, "y")
    second_i, second_o = along_z(second, flips[:, 3:], second_z)
    second_iy, second_ox = box.pieces(second_i, "y"), box.pieces(second_o, "x")

    at = lax.broadcasted_iota(jnp.int32, (8, D), 1)
    row = lax.broadcasted_iota(jnp.int32, (8, D), 0)
    unit, narrow = at % width, width // 2
    device = 2 * box.ahead(at // (2 * width)) + (at // width) % 2
    hidden = device * (2 * width) + jnp.where(row == 1, width, 0) + unit
    lanes = (row - 2) * TW + device * narrow + unit % narrow
    lanes = jnp.where(row < 2, hidden, jnp.where(row < 2 + DOM, lanes, unit // narrow))
    vec, bi, tower_vec = call_unpack(jnp.stack([role, core]), small, lanes)

    table = jnp.concatenate([position[None], event_rows[1:]])
    start_i, end_i = starts.astype(jnp.int32), ends.astype(jnp.int32)
    empty = end_i == start_i
    low = jnp.where(empty, 0, start_i // TILE)
    high = jnp.where(empty, 0, (end_i + TILE - 1) // TILE)
    domains = jnp.arange(DOM, dtype=jnp.int32)
    ints = jnp.concatenate(
        [
            jnp.where(role == 0, low[::-1], low),
            jnp.where(role == 0, high[::-1], high),
            role[None],
            jnp.where(role == 0, DOM - 1 - domains, domains),
            start_i,
            end_i,
            core[None],
            jnp.zeros((2,), jnp.int32),
        ]
    )
    loss_weight = 1.0 - (1.0 - FROZEN_SHARE) * frozen.astype(f32)
    floats = jnp.concatenate([loss_weight, tower_out_b.astype(f32)])
    events, x, mix, cols, probs = call_prepare(ints, floats, table, embeds, embeds_in, small, vec)
    (
        first_i, first_o, first_ix, first_oy, second_i, second_o, second_iy, second_ox,
        ints, events, x, mix, cols, probs, vec, bi, small, tower_vec, lanes,
    ) = step(
        first_i, first_o, first_ix, first_oy, second_i, second_o, second_iy, second_ox,
        ints, events, x, mix, cols, probs, vec, bi, small, tower_vec, lanes,
    )

    def pieces(i, ix, o, oy):
        own = [i] + ix + [o] + oy
        return own + [swap_cores(w) for w in own]

    second_i = jnp.stack([second_i] + second_iy)
    second_o = jnp.stack([second_o] + second_ox)
    second_ix, second_oy = box.pieces(second_i, "x"), box.pieces(second_o, "y")
    weights = {0: pieces(first_i, first_ix, first_o, first_oy)}
    cols, mix, norms = call_forward((0, 1, 2), False, ints, x, weights, bi, vec, cols, mix, {})
    second_ix, second_oy, cols, mix = step(second_ix, second_oy, cols, mix)
    weights[1] = pieces(second_i, second_ix, second_o, second_oy)
    cols, mix, norms, give_mix = call_forward(
        (3, 4), False, ints, x, weights, bi, vec, cols, mix, norms, True
    )
    give_mix, mix = step(give_mix, mix)
    other_mix = box.send(give_mix, flip=1)
    cols, mix, norms = call_forward(
        tuple(range(LOCAL)), True, ints, x, weights, bi, vec, cols, mix, norms
    )
    row_out, grad_block, grad_low, d_tower, d_tower_vec, d_logit_bias = call_tower(
        ints, mix, other_mix, cols, small, tower_vec
    )

    box_shape = (nx, ny, nz, 2, 2 * width, HALF)

    def both_cores(keeps, gives):
        def one(which):
            added = total(keeps[0][:, which], [a[:, which] for a in keeps[1:] + gives])
            return added.astype(bf16).reshape((-1,) + box_shape)

        return one(0), one(1)

    class Scatter:
        def __init__(self, *parts):
            i, o = [jnp.concatenate(p) for p in zip(*parts)]
            i, o = [i[:, k] for k in range(nx)], [o[:, :, k] for k in range(ny)]
            self.state = (i[0], o[0], box.hand_out(i, "x"), box.hand_out(o, "y"))

        def second(self):
            i, o, i_in, o_in = self.state
            i, o = total(i, i_in).astype(bf16), total(o, o_in).astype(bf16)
            i, o = [i[:, k] for k in range(ny)], [o[:, k] for k in range(nx)]
            self.state = (i[0], o[0], box.hand_out(i, "y"), box.hand_out(o, "x"))

        def third(self):
            i, o, i_in, o_in = self.state
            both = jnp.stack([total(i, i_in).astype(bf16), total(o, o_in).astype(bf16)])
            both = [both[:, :, k] for k in range(nz)]
            self.state = (both[0], box.hand_out(both, "z"))

        def fourth(self):
            both = total(*self.state)
            mine = lax.dynamic_index_in_dim(both, role, 2, keepdims=False)
            other = lax.dynamic_index_in_dim(both, 1 - role, 2, keepdims=False).astype(bf16)
            self.state = (mine, box.send(other, flip=1))

    def sync(scatters, *values):
        states, values = step([c.state for c in scatters], values)
        for c, state in zip(scatters, states):
            c.state = state
        return values

    common = (ints, x)
    shared = (norms, weights, bi, vec)
    grad_in = box.send(grad_low, flip=1)
    cols, back, keep_a, give_a, *sums = call_backward(
        (0, 1), ("own",), *common, [grad_low], *shared, cols, None
    )
    d_logit_bias = d_logit_bias + swap_cores(d_logit_bias)
    logit_in = box.pieces(d_logit_bias, "y")
    grad_in, cols, back, keep_a, give_a, sums, logit_in = step(
        grad_in, cols, back, keep_a, give_a, sums, logit_in
    )
    d_logit_bias = box.same_sum(d_logit_bias, logit_in, "y")
    give_a = swap_cores(give_a)
    cols, back, keep_b, give_b, *sums_0 = call_backward(
        (0, 1), ("other",), *common, [grad_in], *shared, cols, ("fresh", back), sums
    )
    logit_in = box.pieces(d_logit_bias, "x")
    cols, back, keep_a, give_a, keep_b, give_b, logit_in = step(
        cols, back, keep_a, give_a, keep_b, give_b, logit_in
    )
    d_logit_bias = box.same_sum(d_logit_bias, logit_in, "x")
    give_b = swap_cores(give_b)
    grads = [grad_low, grad_in]
    cols, back, keep_c, give_c, *sums_1 = call_backward(
        (2,), ("own", "other"), *common, grads, *shared, cols, ("add", back)
    )
    logit_in = box.pieces(d_logit_bias, "flip")
    cols, back, keep_b, give_b, keep_c, give_c, row_out, logit_in = step(
        cols, back, keep_b, give_b, keep_c, give_c, row_out, logit_in
    )
    d_logit_bias = box.same_sum(d_logit_bias, logit_in, "flip")
    give_c = swap_cores(give_c)
    ab = both_cores([keep_a, keep_b], [give_a, give_b])
    give_c, keep_c, ab, cols = step(give_c, keep_c, ab, cols)
    c0 = Scatter(ab, both_cores([keep_c], [give_c]))
    cols, back, keep_d, give_d, *sums_2 = call_backward(
        (3, 4, 5), ("own", "other"), *common, grads, *shared, cols, ("add", back)
    )
    rows_in = box.to_partner(row_out, False)
    logit_in = box.pieces(d_logit_bias, "z")
    cols, back, keep_d, give_d, rows_in, logit_in = sync(
        [c0], cols, back, keep_d, give_d, rows_in, logit_in
    )
    d_logit_bias = box.same_sum(d_logit_bias, logit_in, "z")
    c0.second()
    give_d = swap_cores(give_d)
    g_sum, g_low, d_gate = call_gate(ints, back, cols, probs, x, small)
    cd = both_cores([keep_d], [give_d])
    g_sum, g_low, d_gate, cd = sync([c0], g_sum, g_low, d_gate, cd)
    c1 = Scatter(cd)
    back_in = box.to_partner(g_low, False)
    (back_in,) = sync([c0, c1], back_in)
    c0.third()
    c1.second()
    back_in, _ = step(back_in, c1.state[:2])
    grad_events, d_small = call_finish(
        ints, grad_block, grad_in, g_sum, back_in, events, small, d_tower, d_gate, lanes, d_tower_vec,
        [sums_0, sums_1, sums_2],
    )
    grad_events, d_small = sync([c0, c1], grad_events, d_small)
    c1.third()
    c0.fourth()
    d_small, _ = step(d_small, c1.state[0])
    d_small = d_small.reshape(places, 2, width, PACK)
    d_other = swap_cores(lax.dynamic_index_in_dim(d_small, 1 - core, 1, keepdims=False))
    d_mine = total(lax.dynamic_index_in_dim(d_small, core, 1, keepdims=False), [d_other])
    d_mine = d_mine.astype(bf16).reshape(nx * ny, nz, 2, width, PACK)
    d_parts = [d_mine[k] for k in range(nx * ny)]
    d_in = box.hand_out_plane(d_parts)
    order = position[None, :] == jnp.arange(rows, dtype=f32)[:, None]
    grad_embeds = lax.dot_general(
        order.astype(bf16), grad_events, (((0,), (0,)), ((), ())), preferred_element_type=f32
    ).astype(bf16)
    predicted = in_order(role, row_out, rows_in, 1)
    predictions = jnp.sum(jnp.where(order, predicted[0][:, None], 0.0), axis=0)
    predictions = jnp.broadcast_to(predictions[None], (8, rows))
    d_mine, d_in, grad_embeds, predictions = sync(
        [c0, c1], d_parts[0], d_in, grad_embeds, predictions
    )
    c1.fourth()
    d_mine, _ = step(d_mine, c1.state[0])
    d_mine = total(d_mine, d_in).astype(bf16)
    same = [lax.dynamic_index_in_dim(d_mine[k], role, 0, keepdims=False) for k in range(nz)]
    flip = [lax.dynamic_index_in_dim(d_mine[k], 1 - role, 0, keepdims=False) for k in range(nz)]
    d_in = box.hand_out(same, "z") + box.hand_out_flip(flip)
    grad_embeds = jnp.where(at_home, grad_embeds, swap_cores(grad_embeds))
    predictions = jnp.where(at_home, predictions, swap_cores(predictions))[0]
    d_in, grad_embeds, predictions = sync([c1], d_in, grad_embeds, predictions)
    (
        proj_grad, tower_grad, top, shared_gate, domain_gate, proj_b_grad, in_bias_grad, tower_b_grad,
        tower_out_grad, *vectors,
    ) = call_small([same[0]] + d_in)
    grad_w_in, grad_w_out = call_place(
        ints, [c0.state[0], c1.state[0]], [c0.state[1], c1.state[1]]
    )
    return (
        predictions,
        grad_embeds,
        proj_grad.T,
        proj_b_grad[0],
        grad_w_in,
        in_bias_grad,
        jnp.swapaxes(grad_w_out, 1, 2),
        *vectors,
        jnp.swapaxes(top, 1, 2),
        jnp.swapaxes(shared_gate, 1, 2),
        jnp.swapaxes(domain_gate, 1, 2),
        tower_grad,
        tower_b_grad,
        tower_out_grad,
        d_logit_bias[0, :DOM],
    )


def solution(mesh):
    both = ("dp", "tensor")
    in_specs = (
        P("dp", None),
        P("dp", None),
        P(),
        P("dp"),
        P(None, both),
        P(both),
        P(None, "dp", "tensor"),
        P(None, both),
        P(None, "tensor", "dp"),
        P(None, both),
        P(None, both),
        P(None, both),
        P(None, both, None),
        P(None, both, None),
        P(None, both, None),
        P(None, both, None),
        P(None, both),
        P(None, both),
        P(),
    )
    out_specs = (
        P("dp"),
        P("dp", None),
        P(None, both),
        P(both),
        P(None, "dp", "tensor"),
        P(None, both),
        P(None, "tensor", "dp"),
        P(None, both),
        P(None, both),
        P(None, both),
        P(None, both, None),
        P(None, both, None),
        P(None, both, None),
        P(None, both, None),
        P(None, both),
        P(None, both),
        P(),
    )
    return jax.shard_map(
        functools.partial(per_device, Box(mesh.shape["dp"])),
        mesh=mesh,
        in_specs=in_specs,
        out_specs=out_specs,
        check_vma=False,
    )
```

```python
import functools
import math

import jax
import jax.numpy as jnp
import numpy as np
from jax import lax
from jax.experimental import pallas as pl
from jax.experimental.pallas import tpu as pltpu
from jax.sharding import PartitionSpec as P

D = 512
H = 1024
HALF = H // 2
TW = 256
S = 4
DOM = 4
K = 2
EPS = 1e-05
FROZEN_SHARE = 0.25
TILE = 256
LOCAL = 6
CHUNKS = ((0, 1, 2), (3, 4, 5))
VMEM_LIMIT = 48 * 1024 * 1024
PACK = 1792
SETS = (
    tuple(range(2)) + tuple(S + K * d for d in reversed(range(DOM))),
    tuple(range(2, 4)) + tuple(S + K * d + 1 for d in range(DOM)),
)
COEF, SCALE, DCOEF, DOMAIN, LABEL, WEIGHT, BIAS = 0, 6, 12, 18, 19, 20, 21
LOW, HIGH, ROLE, DOMAIN_OF, START, END, CORE = 0, 4, 8, 9, 13, 17, 21

bf16 = jnp.bfloat16
f32 = jnp.float32


def dims_of(count):
    if count % 4 == 0:
        rest = count // 4
        root = math.isqrt(rest)
        if root * root == rest:
            return (4, root, root)
    return (count, 1, 1)


class Box:
    def __init__(self, count):
        first, second, third = dims_of(count)
        self.count = count
        self.dims = (2, first // 2, second, third)
        self.strides = (second * third, 2 * second * third, third, 1)

    def role(self, chip):
        return (chip // self.strides[0]) % 2

    def partner(self, chip):
        return chip + (1 - 2 * self.role(chip)) * self.strides[0]

    def send(self, values, flip=0, z=0, y=0, x=0):
        pairs = []
        for chip in range(self.count):
            to = chip
            for step, size, stride in zip((flip, z, y, x), self.dims, self.strides):
                place = (chip // stride) % size
                to += ((place + step) % size - place) * stride
            pairs.append((chip, to))
        return lax.ppermute(values, "dp", pairs)

    def to_partner(self, values, home):
        pairs = []
        for chip in range(self.count):
            for core in range(2):
                if (core == self.role(chip)) == home:
                    pairs.append((2 * chip + core, 2 * self.partner(chip) + core))
        return lax.ppermute(values, ("dp", "tensor"), pairs)

    def pieces(self, values, dim):
        size = self.dims[("flip", "z", "y", "x").index(dim)]
        return [self.send(values, **{dim: -k}) for k in range(1, size)]

    def hand_out(self, parts, dim):
        return [self.send(part, **{dim: k}) for k, part in enumerate(parts) if k]

    def line(self, same, other):
        steps = range(1, self.dims[1])
        return [self.send(same, z=-z) for z in steps], [self.send(other, flip=1, z=-z) for z in steps]

    def in_line(self, own, flip, found, role, axis):
        same, other = found
        return [in_order(role, s, o, axis) for s, o in zip([own] + same, [flip] + other)]

    def hand_out_flip(self, parts):
        return [self.send(part, flip=1, z=k) for k, part in enumerate(parts)]

    def plane(self):
        _, _, ny, nx = self.dims
        return [(x, y) for x in range(nx) for y in range(ny)][1:]

    def gather_plane(self, values):
        return [values] + [self.send(values, y=-y, x=-x) for x, y in self.plane()]

    def hand_out_plane(self, parts):
        return [self.send(part, y=y, x=x) for part, (x, y) in zip(parts[1:], self.plane())]

    def same_sum(self, values, found, dim):
        number = ("flip", "z", "y", "x").index(dim)
        size, stride = self.dims[number], self.strides[number]
        found = jnp.stack([values] + found)
        if size > 2:
            mine = (lax.axis_index("dp") // stride) % size
            found = jnp.take(found, (jnp.arange(size) - mine) % size, axis=0)
        return functools.reduce(jnp.add, [found[k] for k in range(size)])

    def ahead(self, place):
        me = lax.axis_index("dp")
        chip, weight = 0, 1
        for dim, (size, stride) in enumerate(zip(self.dims, self.strides)):
            mine = (me // stride) % size if dim else 0
            chip = chip + ((mine + (place // weight) % size) % size) * stride
            weight *= size
        return chip


def swap_cores(values):
    return lax.ppermute(values, "tensor", [(0, 1), (1, 0)])


def in_order(which, own, other, axis):
    return jnp.where(
        which == 0,
        jnp.concatenate([own, other], axis),
        jnp.concatenate([other, own], axis),
    )


def step(*values):
    return lax.optimization_barrier(values)


def total(first, arrived):
    return functools.reduce(jnp.add, [a.astype(f32) for a in arrived], first.astype(f32))


def gelu_parts(v):
    inner = math.sqrt(2.0 / math.pi)
    square = v * v
    th = jnp.tanh(v * (inner + inner * 0.044715 * square))
    half = 0.5 * (1.0 + th)
    act = v * half
    slope = half + 0.5 * v * (1.0 - th * th) * (inner + 3.0 * inner * 0.044715 * square)
    return act, slope


def nt(a, b):
    return lax.dot_general(a, b, (((1,), (1,)), ((), ())), preferred_element_type=f32)


def tn(a, b):
    return lax.dot_general(a, b, (((0,), (0,)), ((), ())), preferred_element_type=f32)


def nn(a, b):
    return jnp.dot(a, b, preferred_element_type=f32)


def softmax_rows(v):
    e = jnp.exp(v - jnp.max(v, axis=0, keepdims=True))
    return e / jnp.sum(e, axis=0, keepdims=True)


def prepare_kernel(
    ints, floats, rows_ref, own_ref, in_ref, proj_ref, gates_ref, vec_ref, ev_ref, x_ref, mix_ref, cols_ref, prob_ref, embeds_ref, arrived
):
    tiles_of_half = pl.num_programs(0) // 2
    index = pl.program_id(0)
    role = ints[ROLE]
    count = rows_ref.shape[1]
    at_home = ints[CORE] == role

    @pl.when((index == 0) & at_home)
    def _():
        copy = pltpu.make_async_copy(own_ref, embeds_ref, arrived.at[0])
        copy.start()
        copy.wait()

    @pl.when((index == 0) & jnp.logical_not(at_home))
    def _():
        copy = pltpu.make_async_copy(in_ref, embeds_ref, arrived.at[0])
        copy.start()
        copy.wait()

    slot = index * TILE + lax.broadcasted_iota(jnp.int32, (TILE, count), 0)
    here = rows_ref[0:1, :].astype(jnp.int32) == slot
    order = jnp.where(here, 1.0, 0.0).astype(bf16)
    label = jnp.sum(jnp.where(here, rows_ref[1:2, :], 0.0), axis=1, keepdims=True)
    events = nn(order, embeds_ref[...]).astype(bf16)
    ev_ref[...] = events
    mixed = nt(events, proj_ref[...]) + vec_ref[3 * LOCAL : 3 * LOCAL + 1, :]
    low = mixed.astype(bf16)
    x_ref[...] = low
    mix_ref[...] = mixed * jnp.where(index // tiles_of_half == role, 1.0, 0.0)
    logits = jnp.transpose(nn(low, gates_ref[...]))
    place = index * TILE + lax.broadcasted_iota(jnp.int32, (1, TILE), 1)
    picks = [
        jnp.where((place >= ints[START + d]) & (place < ints[END + d]), 1.0, 0.0) for d in range(DOM)
    ]

    def pick(low_row, size):
        return softmax_rows(
            functools.reduce(
                jnp.add,
                [picks[d] * logits[low_row + d * size : low_row + (d + 1) * size] for d in range(DOM)],
            )
        )

    top, shared, domain = pick(0, 2), pick(2 * DOM, S), pick((2 + S) * DOM, K)
    prob_ref[...] = jnp.concatenate([top, shared, domain], axis=0)
    first = role == 0
    own_shared = top[0:1] * jnp.where(first, shared[:2], shared[2:])
    own_domain = top[1:2] * jnp.where(first, domain[0:1], domain[1:2])
    coef = [own_domain * jnp.where(first, picks[DOM - 1 - d], picks[d]) for d in range(DOM)]
    table = [
        own_shared,
        *coef,
        jnp.zeros((DOMAIN - SCALE, TILE), f32),
        sum(float(d) * picks[d] for d in range(DOM)),
        jnp.zeros((1, TILE), f32),
        sum(floats[d] * picks[d] for d in range(DOM)),
        sum(floats[DOM + d] * picks[d] for d in range(DOM)),
        jnp.zeros((128 - BIAS - 1, TILE), f32),
    ]
    cols_ref[...] = with_column(jnp.transpose(jnp.concatenate(table, axis=0)), LABEL, label)


def with_column(table, column, values):
    lane = lax.broadcasted_iota(jnp.int32, table.shape, 1)
    return jnp.where(lane == column, values, table)


def tiles_of(expert, ints, first, count):
    low = jnp.maximum(ints[LOW + expert - 2], first)
    high = jnp.minimum(ints[HIGH + expert - 2], first + count)
    return low - first, jnp.maximum(high, low) - first


def each_span(expert, ints, first, rows, work):
    if expert < 2:
        work(slice(0, rows))
    else:
        low, high = tiles_of(expert, ints, first, rows // TILE)

        def one(index, _):
            work(pl.ds(pl.multiple_of(index * TILE, TILE), TILE))
            return 0

        lax.fori_loop(low, high, one, 0)


def join(pieces, held):
    count = len(pieces) // 2
    for core in range(2):
        mine = pieces[core * count : core * count + count]
        by_x, by_y = split_pieces(mine)
        nx, ny = len(by_x), len(by_y)
        rows = by_x[0].shape[3]
        nz = by_x[0].shape[1]

        def at(x, y, z):
            return pl.ds(((x * ny + y) * nz + z) * rows, rows)

        for x in range(nx):
            for y in range(ny):
                for z in range(nz):
                    held[core][at(x, y, z), :] = by_x[x][y, z, 0]
                    held[2 + core][at(x, y, z), :] = by_y[y][x, z, 0]


def split_pieces(pieces):
    nx = pieces[-1].shape[0]
    return pieces[:nx], pieces[nx:]


def forward_kernel(experts, own, aliased, number, gives, ints, x_ref, *refs):
    arrays = sorted({e // 3 for e in experts})
    weights = {a: refs[number * k : number * (k + 1)] for k, a in enumerate(arrays)}
    refs = refs[number * len(arrays) :]
    refs, held = refs[:-4], refs[-4:]
    wi_a, wi_b, wo_a, wo_b = held
    bi_ref, vec_ref, cols_in, mix_in = refs[:4]
    cols_ref, mix_ref, *norm_refs = refs[4 + aliased :]
    if gives:
        *norm_refs, give_ref = norm_refs
    norm_refs = dict(zip(arrays, norm_refs))
    rows = x_ref.shape[0]
    half = ints[ROLE] if own else 1 - ints[ROLE]
    step = pl.program_id(0)

    @pl.when(step == 0)
    def _():
        cols_ref[...] = cols_in[...]
        mix_ref[...] = mix_in[...]

    def work(expert, span):
        x = x_ref[span, :]
        pre_a = nn(x, wi_a[...]) + bi_ref[expert : expert + 1, :HALF]
        act_a = gelu_parts(pre_a)[0].astype(bf16)
        pre_b = nn(x, wi_b[...]) + bi_ref[expert : expert + 1, HALF:]
        act_b = gelu_parts(pre_b)[0].astype(bf16)
        out = nt(act_a, wo_a[...]) + nt(act_b, wo_b[...]) + vec_ref[expert : expert + 1, :]
        centre = jnp.mean(out, axis=1, keepdims=True)
        centred = out - centre
        scale = lax.rsqrt(jnp.mean(centred * centred, axis=1, keepdims=True) + EPS)
        norm = centred * scale
        norm_refs[expert // 3][0, span, :] = norm.astype(bf16)
        cols = cols_ref[span, :]
        cols_ref[span, :] = with_column(cols, SCALE + expert, scale)
        gain = vec_ref[LOCAL + expert : LOCAL + expert + 1, :]
        shift = vec_ref[2 * LOCAL + expert : 2 * LOCAL + expert + 1, :]
        mix_ref[span, :] += cols[:, COEF + expert : COEF + expert + 1] * (norm * gain + shift)

    for place, expert in enumerate(experts):

        @pl.when(step == place)
        def _(expert=expert):
            join(weights[expert // 3], held)
            each_span(expert, ints, half * (rows // TILE), rows, functools.partial(work, expert))

    if gives:

        @pl.when(step == len(experts) - 1)
        def _():
            give_ref[...] = mix_ref[...].astype(bf16)


def backward_kernel(experts, halves, keeps_back, adds, number, ints, x_ref, *refs):
    gb_refs, refs = refs[: len(halves)], refs[len(halves) :]
    norm_ref, pieces, refs = refs[0], refs[1 : 1 + number], refs[1 + number :]
    bi_ref, vec_ref, cols_in = refs[:3]
    refs, held = refs[3:-4], refs[-4:]
    wi_a, wi_b, wo_a, wo_b = held
    join(pieces, held)
    back_in, refs = refs[0], refs[1:]
    if adds:
        dvec_in, dbi_in, keep_in, give_in = refs[:4]
        refs = refs[4:]
    cols_ref, back_ref, keep_ref, give_ref, dvec_ref, dbi_ref, in_a, in_b, out_a, out_b = refs
    rows = x_ref.shape[0]
    half_tiles = rows // TILE // len(halves)
    first = 0 if len(halves) == 2 else (ints[ROLE] if halves[0] == "own" else 1 - ints[ROLE]) * half_tiles
    step = pl.program_id(0)

    @pl.when(step == 0)
    def _():
        cols_ref[...] = cols_in[...]
        back_ref[...] = back_in[...] if keeps_back else jnp.zeros_like(back_ref)

    dvec_ref[...] = dvec_in[...] if adds else jnp.zeros_like(dvec_ref)
    dbi_ref[...] = dbi_in[...] if adds else jnp.zeros_like(dbi_ref)

    def work(expert, span):
        whole = isinstance(span, slice)

        def add(ref, target, which, values):
            if whole and adds:
                before = keep_in if target is keep_ref else give_in
                target[0, which] = (values + before[0, which].astype(f32)).astype(bf16)
            elif whole:
                target[0, which] = values.astype(bf16)
            else:
                ref[...] += values

        x = x_ref[span, :]
        norm = norm_ref[0, span, :].astype(f32)
        cols = cols_ref[span, :]
        if len(halves) == 1:
            grad_block = gb_refs[0][span, :].astype(f32)
        else:
            half = span.start // (half_tiles * TILE)
            inner = pl.ds(pl.multiple_of(span.start - half * (half_tiles * TILE), TILE), TILE)
            grad_block = jnp.where(
                half == ints[ROLE], gb_refs[0][inner, :].astype(f32), gb_refs[1][inner, :].astype(f32)
            )
        gain = vec_ref[LOCAL + expert : LOCAL + expert + 1, :]
        shift = vec_ref[2 * LOCAL + expert : 2 * LOCAL + expert + 1, :]
        scale = cols[:, SCALE + expert : SCALE + expert + 1]
        grad_exp = cols[:, COEF + expert : COEF + expert + 1] * grad_block
        scaled = grad_exp * norm
        dx = grad_exp * gain
        first_mean = jnp.mean(dx, axis=1, keepdims=True)
        second_mean = jnp.mean(dx * norm, axis=1, keepdims=True)
        grad_sum = scale * (dx - first_mean - norm * second_mean)
        grad_low = grad_sum.astype(bf16)
        pre_a = nn(x, wi_a[...]) + bi_ref[expert : expert + 1, :HALF]
        act_a, slope_a = gelu_parts(pre_a)
        low_a = (nn(grad_low, wo_a[...]) * slope_a).astype(bf16)
        pre_b = nn(x, wi_b[...]) + bi_ref[expert : expert + 1, HALF:]
        act_b, slope_b = gelu_parts(pre_b)
        low_b = (nn(grad_low, wo_b[...]) * slope_b).astype(bf16)
        add(out_a, keep_ref, 1, tn(grad_low, act_a.astype(bf16)))
        add(in_a, keep_ref, 0, tn(x, low_a))
        add(out_b, give_ref, 1, tn(grad_low, act_b.astype(bf16)))
        add(in_b, give_ref, 0, tn(x, low_b))
        back_ref[span, :] += nt(low_a, wi_a[...]) + nt(low_b, wi_b[...])
        dcoef = jnp.sum(grad_block * (norm * gain + shift), axis=1, keepdims=True)
        if expert < 2:
            cols_ref[span, :] = with_column(cols, DCOEF + expert, dcoef)
        else:
            mine = cols[:, DOMAIN : DOMAIN + 1] == ints[DOMAIN_OF + expert - 2].astype(f32)
            column = cols[:, DCOEF + 2 : DCOEF + 3] + jnp.where(mine, dcoef, 0.0)
            cols_ref[span, :] = with_column(cols, DCOEF + 2, column)
        dvec_ref[0, 0:1, :] += jnp.sum(grad_sum, axis=0, keepdims=True)
        dvec_ref[0, 1:2, :] += jnp.sum(scaled, axis=0, keepdims=True)
        dvec_ref[0, 2:3, :] += jnp.sum(grad_exp, axis=0, keepdims=True)
        dbi_ref[0, 0:1, :HALF] += jnp.sum(low_a.astype(f32), axis=0, keepdims=True)
        dbi_ref[0, 0:1, HALF:] += jnp.sum(low_b.astype(f32), axis=0, keepdims=True)

    for place, expert in enumerate(experts):

        @pl.when(step == place)
        def _(expert=expert):
            if expert >= 2:
                for ref in (in_a, in_b, out_a, out_b):
                    ref[...] = jnp.zeros_like(ref)
            each_span(expert, ints, first, rows, functools.partial(work, expert))
            if expert >= 2:
                keep_ref[0, 0] = in_a[...].astype(bf16)
                keep_ref[0, 1] = out_a[...].astype(bf16)
                give_ref[0, 0] = in_b[...].astype(bf16)
                give_ref[0, 1] = out_b[...].astype(bf16)


def tower_kernel(
    ints, mix_ref, other_ref, cols_ref, tw_ref, tv_ref, out_ref, gb_ref, low_ref, dw_ref, dv_ref, db_ref
):
    @pl.when(pl.program_id(0) == 0)
    def _():
        db_ref[...] = jnp.zeros_like(db_ref)
        dw_ref[...] = jnp.zeros_like(dw_ref)
        dv_ref[...] = jnp.zeros_like(dv_ref)

    bias = tv_ref[0:1, :]
    head = tv_ref[1:2, :]
    cols = cols_ref[...]
    block = (mix_ref[...] + other_ref[...].astype(f32)).astype(bf16)
    tower = slice(PACK - 128 - DOM * TW, PACK - 128)
    pre = nn(block, tw_ref[:, tower]) + bias
    act, slope = gelu_parts(pre)
    group = lax.broadcasted_iota(jnp.int32, pre.shape, 1) // TW
    mine = group == cols[:, DOMAIN : DOMAIN + 1].astype(jnp.int32)
    act = jnp.where(mine, act, 0.0)
    logit = jnp.sum(act * head, axis=1, keepdims=True) + cols[:, BIAS : BIAS + 1]
    predicted = 1.0 / (1.0 + jnp.exp(-logit))
    grad_logit = cols[:, WEIGHT : WEIGHT + 1] * (predicted - cols[:, LABEL : LABEL + 1])
    lane = lax.broadcasted_iota(jnp.int32, cols.shape, 1)
    out_ref[...] = jnp.transpose(jnp.where(lane == 0, predicted, jnp.where(lane == 1, grad_logit, 0.0)))[:8]
    by_domain = jnp.where(lane.astype(f32) == cols[:, DOMAIN : DOMAIN + 1], grad_logit, 0.0)
    db_ref[0:1, :] += jnp.sum(by_domain, axis=0, keepdims=True)
    dv_ref[1:2, :] += jnp.sum(grad_logit * act, axis=0, keepdims=True)
    grad_pre = jnp.where(mine, grad_logit * head * slope, 0.0)
    dv_ref[0:1, :] += jnp.sum(grad_pre, axis=0, keepdims=True)
    grad_low = grad_pre.astype(bf16)
    grad_block = nt(grad_low, tw_ref[:, tower])
    gb_ref[...] = grad_block
    low_ref[...] = grad_block.astype(bf16)
    dw_ref[...] += tn(block, grad_low)


def softmax_back(probability, grad_probs):
    return probability * (grad_probs - jnp.sum(probability * grad_probs, axis=0, keepdims=True))


def gate_kernel(ints, back_ref, cols_ref, prob_ref, x_ref, gates_ref, sum_ref, low_ref, gate_ref):
    index = pl.program_id(0)
    first = ints[ROLE] == 0

    @pl.when(index == 0)
    def _():
        gate_ref[...] = jnp.zeros_like(gate_ref)

    mine = jnp.transpose(cols_ref[...])[DCOEF : DCOEF + 3]
    none = jnp.zeros_like(mine)
    one, two = jnp.where(first, mine, none), jnp.where(first, none, mine)
    d_shared = jnp.concatenate([one[0:2], two[0:2]], axis=0)
    d_domain = jnp.concatenate([one[2:3], two[2:3]], axis=0)
    top, shared, domain = prob_ref[0:2, :], prob_ref[2:6, :], prob_ref[6:8, :]
    d_top = jnp.concatenate(
        [
            jnp.sum(d_shared * shared, axis=0, keepdims=True),
            jnp.sum(d_domain * domain, axis=0, keepdims=True),
        ],
        axis=0,
    )
    grads = (
        softmax_back(top, d_top),
        softmax_back(shared, d_shared * top[0:1]),
        softmax_back(domain, d_domain * top[1:2]),
    )
    rows = top.shape[1]
    place = index * rows + lax.broadcasted_iota(jnp.int32, (1, rows), 1)
    picks = [
        jnp.where((place >= ints[START + d]) & (place < ints[END + d]), 1.0, 0.0) for d in range(DOM)
    ]
    spread = jnp.concatenate(
        [picks[d] * grad for grad in grads for d in range(DOM)] + [jnp.zeros((96, rows), f32)],
        axis=0,
    )
    spread = jnp.transpose(spread).astype(bf16)
    gate_ref[...] += tn(x_ref[...], spread)
    added = back_ref[...] + nt(spread, gates_ref[...])
    sum_ref[...] = added
    low_ref[...] = added.astype(bf16)


def call_gate(ints, back, cols, probs, x, small):
    rows = x.shape[0]
    half = rows // 2

    def tile(width):
        return pl.BlockSpec((half, width), lambda i, *_: (i, 0))

    return pl.pallas_call(
        gate_kernel,
        grid_spec=pltpu.PrefetchScalarGridSpec(
            num_scalar_prefetch=1,
            grid=(2,),
            in_specs=[
                tile(D),
                tile(128),
                pl.BlockSpec((8, half), lambda i, *_: (0, i)),
                tile(D),
                GATES_SPEC,
            ],
            out_specs=(tile(D), tile(D), fixed((D, 128))),
        ),
        out_shape=(
            jax.ShapeDtypeStruct((rows, D), f32),
            jax.ShapeDtypeStruct((rows, D), bf16),
            jax.ShapeDtypeStruct((D, 128), f32),
        ),
        compiler_params=params(),
        cost_estimate=pl.CostEstimate(
            flops=4 * rows * D * 128, bytes_accessed=10_000_000, transcendentals=0
        ),
        name="gates",
    )(ints, back, cols, probs, x, small)


def hidden_lines(ints, lane_ref, tv_ref, line_refs):
    first_set, first_core = ints[ROLE] == 0, ints[CORE] == 0
    mine = [r[k, 0:1, :] for r in line_refs for k in range(r.shape[0])]
    mine = jnp.concatenate(mine, axis=0)
    mine = jnp.where(first_core, mine, pltpu.roll(mine, HALF, 1))
    mine = jnp.where(first_set, mine, 0.0), jnp.where(first_set, 0.0, mine)
    found = {j: mine[r][i : i + 1] for r, row in enumerate(SETS) for i, j in enumerate(row)}
    mine = jnp.concatenate([found[j] for j in range(2 * LOCAL)], axis=0).astype(bf16)

    def lanes(values, row):
        lane = lax.broadcasted_iota(jnp.int32, (H, D), 0)
        chosen = jnp.where(lane == lane_ref[row : row + 1, :], 1.0, 0.0).astype(bf16)
        return nn(values, chosen)

    tower = tv_ref[...].astype(bf16)
    rows = [lanes(mine, 0), lanes(mine, 1)]
    head = lane_ref[6:7, :] == 1
    for d in range(DOM):
        both = lanes(tower, 2 + d)
        rows.append(jnp.where(head, both[1:2], both[0:1]))
    return rows


def finish_kernel(
    ints, gb_ref, gb_in_ref, sum_ref, in_ref, ev_ref, proj_ref, tower_ref, gate_ref, *refs
):
    lane_ref, tv_ref, *vec_refs, ge_ref, small_ref, proj_sum, bias_sum = refs
    vec_refs, line_refs = vec_refs[: len(vec_refs) // 2], vec_refs[len(vec_refs) // 2 :]
    index = pl.program_id(0)
    last = pl.num_programs(0) - 1
    first = ints[ROLE] == 0
    at_home = jnp.where(ints[CORE] == ints[ROLE], 1.0, 0.0)
    mine_half = index == ints[ROLE]

    @pl.when(index == 0)
    def _():
        for ref in (proj_sum, bias_sum):
            ref[...] = jnp.zeros_like(ref)

    grad_mixed = jnp.where(mine_half, gb_ref[...], gb_in_ref[...].astype(f32))
    grad_mixed = at_home * (grad_mixed + sum_ref[...] + in_ref[...].astype(f32))
    bias_sum[0:1, :] += jnp.sum(grad_mixed, axis=0, keepdims=True)
    low = grad_mixed.astype(bf16)
    proj_sum[...] += tn(low, ev_ref[...])
    ge_ref[...] = nn(low, proj_ref[...]).astype(bf16)

    @pl.when(index == last)
    def _():
        e_in = proj_sum.shape[1]
        vectors = jnp.concatenate(
            [r[k, 0:3, :] for r in vec_refs for k in range(r.shape[0])], axis=0
        )
        rows = jnp.concatenate(
            [
                jnp.zeros((32, D), f32),
                jnp.where(first, vectors, 0.0),
                jnp.where(first, 0.0, vectors),
                bias_sum[0:1, :],
                *hidden_lines(ints, lane_ref, tv_ref, line_refs),
                jnp.zeros((31, D), f32),
            ],
            axis=0,
        )
        small_ref[:, :e_in] = proj_sum[...].astype(bf16)
        small_ref[:, e_in : e_in + DOM * TW] = tower_ref[...].astype(bf16)
        small_ref[:, e_in + DOM * TW :] = (gate_ref[...] + jnp.transpose(rows)).astype(bf16)


def call_finish(ints, gb, gb_in, added, arrived, events, small, tower, gate, lanes, tower_vec, sums):
    rows, e_in = events.shape
    half = rows // 2

    def tile(width):
        return pl.BlockSpec((half, width), lambda i, *_: (i, 0))

    halves = (gb, gb_in)
    wholes = (tower, gate, lanes, tower_vec)
    vecs = [v for v, _ in sums] + [b for _, b in sums]
    return pl.pallas_call(
        finish_kernel,
        grid_spec=pltpu.PrefetchScalarGridSpec(
            num_scalar_prefetch=1,
            grid=(2,),
            in_specs=[fixed(a.shape) for a in halves]
            + [tile(D), tile(D), tile(e_in), proj_spec(e_in)]
            + [fixed(a.shape) for a in (*wholes, *vecs)],
            out_specs=(tile(e_in), fixed((D, PACK))),
            scratch_shapes=[pltpu.VMEM((D, e_in), f32), pltpu.VMEM((8, D), f32)],
        ),
        out_shape=(jax.ShapeDtypeStruct((rows, e_in), bf16), jax.ShapeDtypeStruct((D, PACK), bf16)),
        compiler_params=params(),
        cost_estimate=pl.CostEstimate(flops=4 * rows * D * e_in, bytes_accessed=14_000_000, transcendentals=0),
        name="finish",
    )(ints, *halves, added, arrived, events, small, *wholes, *vecs)


VECTOR_ROW = {j: 32 + 18 * r + 3 * i for r, row in enumerate(SETS) for i, j in enumerate(row)}


def small_kernel(*refs):
    parts, vec_refs = refs[:-12], refs[-3:]
    proj_ref, tower_ref, top_ref, shared_ref, domain_ref, bias_ref, hidden_ref, tb_ref, to_ref = refs[-12:-3]
    added = functools.reduce(jnp.add, [p[...].astype(f32) for p in parts])
    width, e_in = proj_ref.shape
    proj_ref[...] = added[:, :e_in]
    for d in range(DOM):
        tower_ref[d] = added[:, e_in + d * TW : e_in + (d + 1) * TW]
    rows = jnp.concatenate([added[:, e_in + DOM * TW :], jnp.zeros((128 - width, 128), f32)], axis=0)
    rows = jnp.transpose(rows)[:, :width]
    for ref, low, size in ((top_ref, 0, 2), (shared_ref, 2 * DOM, S), (domain_ref, (2 + S) * DOM, K)):
        for d in range(DOM):
            ref[d] = rows[low + d * size : low + (d + 1) * size]
    bias_ref[...] = rows[68:69]
    hidden_ref[:, :width] = rows[69:81]
    hidden_ref[:, width:] = rows[81:93]
    tb_ref[...] = rows[93:97, : width // 2]
    to_ref[...] = rows[93:97, width // 2 :]
    for which, ref in enumerate(vec_refs):
        for j in range(2 * LOCAL):
            ref[j : j + 1, :] = rows[VECTOR_ROW[j] + which : VECTOR_ROW[j] + which + 1]


def call_small(parts):
    width = parts[0].shape[0]
    e_in = PACK - DOM * TW - 128
    shapes = [(width, e_in), (DOM, width, TW), (DOM, 2, width), (DOM, S, width), (DOM, K, width), (1, width)]
    shapes += [(2 * LOCAL, 2 * width), (DOM, width // 2), (DOM, width // 2)]
    shapes += [(2 * LOCAL, width)] * 3
    return pl.pallas_call(
        small_kernel,
        grid=(1,),
        in_specs=[fixed(p.shape) for p in parts],
        out_specs=tuple(fixed(shape) for shape in shapes),
        out_shape=tuple(jax.ShapeDtypeStruct(shape, f32) for shape in shapes),
        compiler_params=params(),
        name="small",
    )(*parts)


def place_kernel(ints, *refs):
    *parts, in_ref, out_ref = refs
    half = len(parts) // 2
    first = ints[ROLE] == 0
    for chunk, (own, other) in enumerate(zip(parts[:half], parts[half:])):
        for place, expert in enumerate(CHUNKS[chunk]):
            for which, ref in enumerate((in_ref, out_ref)):
                a, b = own[which, place].astype(f32), other[which, place].astype(f32)
                ref[SETS[0][expert]] = jnp.where(first, a, b)
                ref[SETS[1][expert]] = jnp.where(first, b, a)


def call_place(ints, own, other):
    rows, width = own[0].shape[2:]
    shape = (2 * LOCAL, rows, width)
    return pl.pallas_call(
        place_kernel,
        grid_spec=pltpu.PrefetchScalarGridSpec(
            num_scalar_prefetch=1,
            grid=(1,),
            in_specs=[fixed(a.shape) for a in (*own, *other)],
            out_specs=(fixed(shape), fixed(shape)),
        ),
        out_shape=(jax.ShapeDtypeStruct(shape, f32),) * 2,
        compiler_params=params(),
        name="place",
    )(ints, *own, *other)


def params():
    return pltpu.CompilerParams(vmem_limit_bytes=VMEM_LIMIT)


def fixed(shape):
    return pl.BlockSpec(shape, lambda i, *_: (0,) * len(shape))


def pack_kernel(proj_ref, tower_ref, gate_ref, rest_ref, out_ref):
    width, e_in = proj_ref.shape
    out_ref[:, :e_in] = proj_ref[...]
    for d in range(DOM):
        out_ref[:, e_in + d * TW : e_in + (d + 1) * TW] = tower_ref[d]
    gates, rest = gate_ref[...].astype(f32), rest_ref[...].astype(f32)
    rows = []
    for low, size in ((0, 2), (2, S), (2 + S, K)):
        rows += [gates[d, low : low + size] for d in range(DOM)]
    rows += [rest[:12, k * width : (k + 1) * width] for k in range(3)] + [rest[16:17, :width]]
    rows += [rest[:12, k * width : (k + 1) * width] for k in (3, 4)] + [rest[12:16, :width]]
    rows = jnp.concatenate(rows + [jnp.zeros((31, width), f32)], axis=0)
    rows = jnp.concatenate([rows, jnp.zeros((128, 128 - width), f32)], axis=1)
    out_ref[:, e_in + DOM * TW :] = jnp.transpose(rows)[:width].astype(bf16)


def call_pack(*arrays):
    width = arrays[0].shape[0]
    return pl.pallas_call(
        pack_kernel,
        grid=(1,),
        in_specs=[fixed(a.shape) for a in arrays],
        out_specs=fixed((width, PACK)),
        out_shape=jax.ShapeDtypeStruct((width, PACK), bf16),
        compiler_params=params(),
        name="pack",
    )(*arrays)


PICKED = [
    [32 + e for e in row] + [44 + e for e in row] + [56 + e for e in row] + [68] + [127] * 5
    + [69 + e for e in row] + [81 + e for e in row] + [93 + d for d in range(DOM)]
    for row in SETS
]


def unpack_kernel(ints, small_ref, choose_ref, lane_ref, vec_ref, bi_ref, tower_ref):
    vec = nt(choose_ref[0], small_ref[...])
    vec_ref[...] = vec

    def lanes(values, row):
        lane = lax.broadcasted_iota(jnp.int32, (H, D), 0)
        chosen = jnp.where(lane == lane_ref[row : row + 1, :], 1.0, 0.0).astype(bf16)
        return nt(values.astype(bf16), chosen)

    bias = lanes(jnp.concatenate([vec[24:30], jnp.zeros((2, D), f32)], axis=0), 0)
    bias += lanes(jnp.concatenate([vec[30:36], jnp.zeros((2, D), f32)], axis=0), 1)
    bi_ref[...] = jnp.where(ints[1] == 0, bias, pltpu.roll(bias, HALF, 1))
    head = lane_ref[6:7, :] == 1
    tower = jnp.zeros((8, H), f32)
    for d in range(DOM):
        row = vec[36 + d : 37 + d]
        rows = [jnp.where(head, 0.0, row), jnp.where(head, row, 0.0), jnp.zeros((6, D), f32)]
        tower += lanes(jnp.concatenate(rows, axis=0), 2 + d)
    tower_ref[...] = tower


def call_unpack(ints, small, lanes):
    choose = np.zeros((2, 40, 128), np.float32)
    for r in range(2):
        for row, column in enumerate(PICKED[r]):
            choose[r, row, column] = 1.0
    shapes = [(40, D), (8, H), (8, DOM * TW)]
    return pl.pallas_call(
        unpack_kernel,
        grid_spec=pltpu.PrefetchScalarGridSpec(
            num_scalar_prefetch=1,
            grid=(1,),
            in_specs=[
                pl.BlockSpec((D, 128), lambda i, ints: (0, PACK // 128 - 1)),
                pl.BlockSpec((1, 40, 128), lambda i, ints: (ints[0], 0, 0)),
                fixed(lanes.shape),
            ],
            out_specs=tuple(fixed(shape) for shape in shapes),
        ),
        out_shape=tuple(jax.ShapeDtypeStruct(shape, f32) for shape in shapes),
        compiler_params=params(),
        name="unpack",
    )(ints, small, jnp.asarray(choose, bf16), lanes)


def choose_kernel(own_ids, other_ids, in_own, out_own, in_other, out_other, *refs):
    own_refs, other_refs, all_ref = refs[:2], refs[2:4], refs[4]
    step = pl.program_id(0)
    for part in range(2):

        @pl.when(step // 3 == part)
        def _(part=part):
            own_refs[part][0], own_refs[part][1] = in_own[...], out_own[...]
            other_refs[part][0], other_refs[part][1] = in_other[...], out_other[...]

    all_ref[0], all_ref[1] = in_other[...], out_other[...]


def call_choose(own_ids, other_ids, w_in, w_out_t):
    tail = w_in.shape[1:]
    block = (1,) + tail

    def shape(count):
        return jax.ShapeDtypeStruct((2, count) + tail, bf16)

    own = pl.BlockSpec(block, lambda i, a, b: (a[i], 0, 0))
    other = pl.BlockSpec(block, lambda i, a, b: (b[i], 0, 0))
    low = pl.BlockSpec((2,) + block, lambda i, a, b: (0, jnp.minimum(i, 2), 0, 0))
    high = pl.BlockSpec((2,) + block, lambda i, a, b: (0, jnp.maximum(i - 3, 0), 0, 0))
    every = pl.BlockSpec((2,) + block, lambda i, a, b: (0, i, 0, 0))
    return pl.pallas_call(
        choose_kernel,
        grid_spec=pltpu.PrefetchScalarGridSpec(
            num_scalar_prefetch=2,
            grid=(LOCAL,),
            in_specs=[own, own, other, other],
            out_specs=(low, high, low, high, every),
        ),
        out_shape=(shape(3), shape(3), shape(3), shape(3), shape(6)),
        compiler_params=params(),
        cost_estimate=pl.CostEstimate(flops=0, bytes_accessed=3_000_000, transcendentals=0),
        name="choose",
    )(own_ids, other_ids, w_in, w_out_t, w_in, w_out_t)


def proj_spec(e_in):
    return pl.BlockSpec((D, e_in), lambda *_: (0, 0))


GATES_SPEC = pl.BlockSpec((D, 128), lambda *_: (0, PACK // 128 - 1))


def call_prepare(ints, floats, table, embeds, embeds_in, small, vec):
    rows = embeds.shape[0]
    tiles = rows // TILE
    e_in = embeds.shape[1]

    def tile(width):
        return pl.BlockSpec((TILE, width), lambda i, *_: (i, 0))

    return pl.pallas_call(
        prepare_kernel,
        grid_spec=pltpu.PrefetchScalarGridSpec(
            num_scalar_prefetch=2,
            grid=(tiles,),
            in_specs=[fixed(table.shape)]
            + [pl.BlockSpec(memory_space=pl.ANY)] * 2
            + [proj_spec(e_in), GATES_SPEC, fixed(vec.shape)],
            scratch_shapes=[pltpu.VMEM(embeds.shape, bf16), pltpu.SemaphoreType.DMA((1,))],
            out_specs=(
                tile(e_in),
                tile(D),
                tile(D),
                tile(128),
                pl.BlockSpec((8, TILE), lambda i, *_: (0, i)),
            ),
        ),
        out_shape=(
            pltpu.HBM((rows, e_in), bf16),
            pltpu.HBM((rows, D), bf16),
            jax.ShapeDtypeStruct((rows, D), f32),
            jax.ShapeDtypeStruct((rows, 128), f32),
            jax.ShapeDtypeStruct((8, rows), f32),
        ),
        compiler_params=params(),
        cost_estimate=pl.CostEstimate(
            flops=2 * rows * e_in * (rows + D), bytes_accessed=12_000_000, transcendentals=rows * 8
        ),
        name="prepare",
    )(ints, floats, table, embeds, embeds_in, small, small, vec)


def half_spec(own, shape):
    rest = (0,) * (len(shape) - 1)
    return pl.BlockSpec(shape, lambda i, ints: ((ints[ROLE] if own else 1 - ints[ROLE]),) + rest)


def piece_spec(array, place):
    a, b, _, rows, width = array.shape
    return pl.BlockSpec((a, b, 1, rows, width), lambda i, *_: (0, 0, place(i), 0, 0))


MATRICES = [pltpu.VMEM((D, HALF), bf16)] * 4


def call_forward(experts, own, ints, x, weights, bi, vec, cols, mix, norms, gives=False):
    rows = x.shape[0]
    half = rows // 2
    arrays = sorted({e // 3 for e in experts})
    first = {a: min(k for k, e in enumerate(experts) if e // 3 == a) for a in arrays}
    number = {a: sum(1 for e in experts if e // 3 == a) for a in arrays}

    def place(a):
        return lambda i: jnp.clip(i - first[a], 0, number[a] - 1)

    weight_specs = [piece_spec(w, place(a)) for a in arrays for w in weights[a]]
    norm_specs = [
        pl.BlockSpec(
            (1, half, D),
            lambda i, ints, a=a: (place(a)(i), ints[ROLE] if own else 1 - ints[ROLE], 0),
        )
        for a in arrays
    ]
    kept = [norms[a] for a in arrays if a in norms]
    inputs = [x] + [w for a in arrays for w in weights[a]] + [bi, vec, cols, mix] + kept
    at = len(inputs) - len(kept)
    aliases = {at - 1: 0, at: 1}
    aliases.update({at + 1 + k: 2 + k for k in range(len(kept))})
    shared = sum(1 for e in experts if e < 2)
    out = pl.pallas_call(
        functools.partial(
            forward_kernel, experts, own, len(kept), len(weights[arrays[0]]), gives
        ),
        grid_spec=pltpu.PrefetchScalarGridSpec(
            num_scalar_prefetch=1,
            grid=(len(experts),),
            in_specs=[half_spec(own, (half, D))]
            + weight_specs
            + [fixed(bi.shape), fixed(vec.shape), half_spec(own, (half, 128)), half_spec(own, (half, D))]
            + [pl.BlockSpec(memory_space=pl.ANY)] * len(kept),
            out_specs=(half_spec(own, (half, 128)), half_spec(own, (half, D)), *norm_specs)
            + ((fixed((half, D)),) if gives else ()),
            scratch_shapes=MATRICES,
        ),
        out_shape=(
            jax.ShapeDtypeStruct((rows, 128), f32),
            jax.ShapeDtypeStruct((rows, D), f32),
            *[jax.ShapeDtypeStruct((3, rows, D), bf16)] * len(arrays),
        )
        + ((jax.ShapeDtypeStruct((half, D), bf16),) if gives else ()),
        input_output_aliases=aliases,
        compiler_params=params(),
        cost_estimate=pl.CostEstimate(
            flops=4 * (shared + 1) * half * D * H, bytes_accessed=12_000_000, transcendentals=0
        ),
        name="experts_forward",
    )(ints, *inputs)
    found = out[0], out[1], {**norms, **dict(zip(arrays, out[2:]))}
    return found + (out[-1],) if gives else found


def call_backward(experts, halves, ints, x, gbs, norms, weights, bi, vec, cols, back, sums=None):
    rows, count = x.shape[0], len(experts)
    part = rows // 2 * len(halves)
    array, low = experts[0] // 3, experts[0] % 3
    split = any(e // 3 != array for e in experts)

    def span(width):
        if len(halves) == 2:
            return fixed((rows, width))
        return half_spec(halves[0] == "own", (part, width))

    def norm_index(i, ints):
        if len(halves) == 2:
            return (low + i, 0, 0)
        return (low + i, ints[ROLE] if halves[0] == "own" else 1 - ints[ROLE], 0)

    assert not split
    pairs = pl.BlockSpec((1, 2, D, HALF), lambda i, *_: (i, 0, 0, 0))
    vec_spec = pl.BlockSpec((1, 8, D), lambda i, *_: (i, 0, 0))
    bi_spec = pl.BlockSpec((1, 8, H), lambda i, *_: (i, 0, 0))
    mode, back_array = back if back is not None else ("fresh", jnp.zeros((8, 128), f32))
    inputs = [x, *gbs, norms[array], *weights[array], bi, vec, cols, back_array]
    in_specs = (
        [span(D)]
        + [fixed(g.shape) for g in gbs]
        + [pl.BlockSpec((1, part, D), norm_index)]
        + [piece_spec(w, lambda i: low + i) for w in weights[array]]
        + [fixed(bi.shape), fixed(vec.shape), span(128)]
        + [span(D) if mode == "add" else pl.BlockSpec(memory_space=pl.ANY)]
    )
    aliases = {len(inputs) - 1: 0}
    if back is not None:
        aliases[len(inputs)] = 1
    if sums is not None:
        inputs += list(sums)
        in_specs += [vec_spec, bi_spec, pairs, pairs]
    return pl.pallas_call(
        functools.partial(
            backward_kernel, experts, halves, mode == "add", sums is not None, len(weights[array])
        ),
        grid_spec=pltpu.PrefetchScalarGridSpec(
            num_scalar_prefetch=1,
            grid=(count,),
            in_specs=in_specs,
            out_specs=(span(128), span(D), pairs, pairs, vec_spec, bi_spec),
            scratch_shapes=[pltpu.VMEM((D, HALF), f32)] * 4 + MATRICES,
        ),
        out_shape=(
            jax.ShapeDtypeStruct((rows, 128), f32),
            jax.ShapeDtypeStruct((rows, D), f32),
            jax.ShapeDtypeStruct((count, 2, D, HALF), bf16),
            jax.ShapeDtypeStruct((count, 2, D, HALF), bf16),
            jax.ShapeDtypeStruct((count, 8, D), f32),
            jax.ShapeDtypeStruct((count, 8, H), f32),
        ),
        input_output_aliases=aliases,
        compiler_params=params(),
        cost_estimate=pl.CostEstimate(
            flops=10 * count * (rows // 2) * D * H, bytes_accessed=20_000_000, transcendentals=0
        ),
        name="experts_backward",
    )(ints, *inputs)


def call_tower(ints, mix, other, cols, small, tower_vec):
    rows = other.shape[0]
    tiles = 2
    size = rows // tiles

    def kept(width):
        return pl.BlockSpec((size, width), lambda i, ints: (ints[ROLE] * tiles + i, 0))

    def tile(width):
        return pl.BlockSpec((size, width), lambda i, *_: (i, 0))

    return pl.pallas_call(
        tower_kernel,
        grid_spec=pltpu.PrefetchScalarGridSpec(
            num_scalar_prefetch=1,
            grid=(tiles,),
            in_specs=[kept(D), tile(D), kept(128), fixed(small.shape), fixed(tower_vec.shape)],
            out_specs=(
                pl.BlockSpec((8, size), lambda i, *_: (0, i)),
                tile(D),
                tile(D),
                fixed((D, DOM * TW)),
                fixed((8, DOM * TW)),
                fixed((8, 128)),
            ),
        ),
        out_shape=(
            jax.ShapeDtypeStruct((8, rows), f32),
            pltpu.HBM((rows, D), f32),
            jax.ShapeDtypeStruct((rows, D), bf16),
            jax.ShapeDtypeStruct((D, DOM * TW), f32),
            jax.ShapeDtypeStruct((8, DOM * TW), f32),
            jax.ShapeDtypeStruct((8, 128), f32),
        ),
        compiler_params=params(),
        cost_estimate=pl.CostEstimate(
            flops=6 * rows * D * DOM * TW, bytes_accessed=10_000_000, transcendentals=rows * DOM * TW
        ),
        name="towers",
    )(ints, mix, other, cols, small, tower_vec)


def per_device(
    box,
    embeds,
    domain,
    frozen,
    labels,
    proj_w,
    proj_b,
    w_in,
    in_bias,
    w_out,
    out_bias,
    ln_gain,
    ln_shift,
    gate_top,
    gate_shared,
    gate_domain,
    tower_w,
    tower_b,
    tower_out,
    tower_out_b,
):
    core = lax.axis_index("tensor")
    role = box.role(lax.axis_index("dp"))
    at_home = core == role
    places = box.count
    rows = embeds.shape[0]
    half_rows = rows // 2
    width = proj_w.shape[1]
    e_in = proj_w.shape[0]
    nz, ny, nx = box.dims[1:]
    sets = jnp.array(SETS, jnp.int32)
    set_own, set_other = sets[role], sets[1 - role]

    def half(values, which, axis=0):
        return lax.dynamic_slice_in_dim(values, which * half_rows, half_rows, axis)

    w_out_t = jnp.swapaxes(w_out, 1, 2)
    first, second, first_other, second_other, others = call_choose(set_own, set_other, w_in, w_out_t)

    def wide(values):
        return jnp.pad(values, ((0, 0), (0, 5 * width - values.shape[1])))

    arrays = (
        proj_w.T,
        tower_w,
        jnp.concatenate([jnp.swapaxes(g, 1, 2) for g in (gate_top, gate_shared, gate_domain)], axis=1),
        jnp.concatenate(
            [
                jnp.concatenate([out_bias, ln_gain, ln_shift, in_bias], axis=1),
                wide(jnp.concatenate([tower_b, tower_out], axis=1)),
                wide(proj_b[None]),
            ]
        ),
    )

    flips = box.send(others, flip=1)
    first_z = box.line(first, first_other)
    pack = call_pack(*step(arrays, first)[0])
    pack = in_order(role, pack, box.send(pack, flip=1), 0)
    pack = jnp.concatenate([pack] + box.pieces(pack, "z"))
    flips, first, first_z, second, second_other = step(flips, first, first_z, second, second_other)

    def along_z(shard, flip, found):
        found = box.in_line(shard, flip, found, role, 2)
        return jnp.stack([b[0] for b in found]), jnp.stack([b[1] for b in found])

    first_i, first_o = along_z(first, flips[:, :3], first_z)
    first_iy, first_ox = box.pieces(first_i, "y"), box.pieces(first_o, "x")
    second_z = box.line(second, second_other)
    pack = jnp.concatenate([pack] + box.pieces(pack, "y"))
    pack = jnp.concatenate([pack] + box.pieces(pack, "x")).reshape(places, 1, width, PACK)
    domain, labels = step((domain, labels), first)[0]
    event_rows = jnp.concatenate(
        [domain.astype(f32).T, labels.astype(f32)[None], jnp.zeros((6, rows), f32)]
    )
    event_rows = jnp.where(at_home, event_rows, box.to_partner(event_rows, True))
    ids = event_rows[0]
    onehot = (ids[None, :] == jnp.arange(DOM, dtype=f32)[:, None]).astype(f32)
    rank = jnp.cumsum(onehot, axis=1)
    counts = rank[:, -1]
    ends = jnp.cumsum(counts)
    starts = ends - counts
    position = jnp.sum(onehot * (rank + starts[:, None]), axis=0) - 1.0
    embeds_in = box.to_partner(step(embeds, second_z[0])[0], True)
    first_i, first_o, first_iy, first_ox, second, second_z, flips, starts, ends, position = step(
        first_i, first_o, first_iy, first_ox, second, second_z, flips, starts, ends, position
    )

    small = in_order(core, pack, swap_cores(pack), 1).reshape(D, PACK)
    first_i = jnp.stack([first_i] + first_iy)
    first_o = jnp.stack([first_o] + first_ox)
    first_ix, first_oy = box.pieces(first_i, "x"), box.pieces(first_o, "y")
    second, flips, second_z, _ = step(second, flips, second_z, (first_i, first_o))
    second_i, second_o = along_z(second, flips[:, 3:], second_z)
    second_iy, second_ox = box.pieces(second_i, "y"), box.pieces(second_o, "x")

    at = lax.broadcasted_iota(jnp.int32, (8, D), 1)
    row = lax.broadcasted_iota(jnp.int32, (8, D), 0)
    unit, narrow = at % width, width // 2
    device = 2 * box.ahead(at // (2 * width)) + (at // width) % 2
    hidden = device * (2 * width) + jnp.where(row == 1, width, 0) + unit
    lanes = (row - 2) * TW + device * narrow + unit % narrow
    lanes = jnp.where(row < 2, hidden, jnp.where(row < 2 + DOM, lanes, unit // narrow))
    vec, bi, tower_vec = call_unpack(jnp.stack([role, core]), small, lanes)

    table = jnp.concatenate([position[None], event_rows[1:]])
    start_i, end_i = starts.astype(jnp.int32), ends.astype(jnp.int32)
    empty = end_i == start_i
    low = jnp.where(empty, 0, start_i // TILE)
    high = jnp.where(empty, 0, (end_i + TILE - 1) // TILE)
    domains = jnp.arange(DOM, dtype=jnp.int32)
    ints = jnp.concatenate(
        [
            jnp.where(role == 0, low[::-1], low),
            jnp.where(role == 0, high[::-1], high),
            role[None],
            jnp.where(role == 0, DOM - 1 - domains, domains),
            start_i,
            end_i,
            core[None],
            jnp.zeros((2,), jnp.int32),
        ]
    )
    loss_weight = 1.0 - (1.0 - FROZEN_SHARE) * frozen.astype(f32)
    floats = jnp.concatenate([loss_weight, tower_out_b.astype(f32)])
    events, x, mix, cols, probs = call_prepare(ints, floats, table, embeds, embeds_in, small, vec)
    (
        first_i, first_o, first_ix, first_oy, second_i, second_o, second_iy, second_ox,
        ints, events, x, mix, cols, probs, vec, bi, small, tower_vec, lanes,
    ) = step(
        first_i, first_o, first_ix, first_oy, second_i, second_o, second_iy, second_ox,
        ints, events, x, mix, cols, probs, vec, bi, small, tower_vec, lanes,
    )

    def pieces(i, ix, o, oy):
        own = [i] + ix + [o] + oy
        return own + [swap_cores(w) for w in own]

    second_i = jnp.stack([second_i] + second_iy)
    second_o = jnp.stack([second_o] + second_ox)
    second_ix, second_oy = box.pieces(second_i, "x"), box.pieces(second_o, "y")
    weights = {0: pieces(first_i, first_ix, first_o, first_oy)}
    cols, mix, norms = call_forward((0, 1, 2), False, ints, x, weights, bi, vec, cols, mix, {})
    second_ix, second_oy, cols, mix = step(second_ix, second_oy, cols, mix)
    weights[1] = pieces(second_i, second_ix, second_o, second_oy)
    cols, mix, norms, give_mix = call_forward(
        (3, 4), False, ints, x, weights, bi, vec, cols, mix, norms, True
    )
    give_mix, mix = step(give_mix, mix)
    other_mix = box.send(give_mix, flip=1)
    cols, mix, norms = call_forward(
        tuple(range(LOCAL)), True, ints, x, weights, bi, vec, cols, mix, norms
    )
    row_out, grad_block, grad_low, d_tower, d_tower_vec, d_logit_bias = call_tower(
        ints, mix, other_mix, cols, small, tower_vec
    )

    box_shape = (nx, ny, nz, 2, 2 * width, HALF)

    def both_cores(keeps, gives):
        def one(which):
            added = total(keeps[0][:, which], [a[:, which] for a in keeps[1:] + gives])
            return added.astype(bf16).reshape((-1,) + box_shape)

        return one(0), one(1)

    class Scatter:
        def __init__(self, *parts):
            i, o = [jnp.concatenate(p) for p in zip(*parts)]
            i, o = [i[:, k] for k in range(nx)], [o[:, :, k] for k in range(ny)]
            self.state = (i[0], o[0], box.hand_out(i, "x"), box.hand_out(o, "y"))

        def second(self):
            i, o, i_in, o_in = self.state
            i, o = total(i, i_in).astype(bf16), total(o, o_in).astype(bf16)
            i, o = [i[:, k] for k in range(ny)], [o[:, k] for k in range(nx)]
            self.state = (i[0], o[0], box.hand_out(i, "y"), box.hand_out(o, "x"))

        def third(self):
            i, o, i_in, o_in = self.state
            both = jnp.stack([total(i, i_in).astype(bf16), total(o, o_in).astype(bf16)])
            both = [both[:, :, k] for k in range(nz)]
            self.state = (both[0], box.hand_out(both, "z"))

        def fourth(self):
            both = total(*self.state)
            mine = lax.dynamic_index_in_dim(both, role, 2, keepdims=False)
            other = lax.dynamic_index_in_dim(both, 1 - role, 2, keepdims=False).astype(bf16)
            self.state = (mine, box.send(other, flip=1))

    def sync(scatters, *values):
        states, values = step([c.state for c in scatters], values)
        for c, state in zip(scatters, states):
            c.state = state
        return values

    common = (ints, x)
    shared = (norms, weights, bi, vec)
    grad_in = box.send(grad_low, flip=1)
    cols, back, keep_a, give_a, *sums = call_backward(
        (0, 1), ("own",), *common, [grad_low], *shared, cols, None
    )
    logit_in = swap_cores(d_logit_bias)
    grad_in, cols, back, keep_a, give_a, sums, logit_in = step(
        grad_in, cols, back, keep_a, give_a, sums, logit_in
    )
    d_logit_bias = d_logit_bias + logit_in
    cols, back, keep_b, give_b, *sums_0 = call_backward(
        (0, 1), ("other",), *common, [grad_in], *shared, cols, ("fresh", back), sums + [keep_a, give_a]
    )
    logit_in = box.pieces(d_logit_bias, "y")
    cols, back, keep_b, give_b, logit_in = step(cols, back, keep_b, give_b, logit_in)
    d_logit_bias = box.same_sum(d_logit_bias, logit_in, "y")
    give_b = swap_cores(give_b)
    grads = [grad_low, grad_in]
    cols, back, keep_c, give_c, *sums_1 = call_backward(
        (2,), ("own", "other"), *common, grads, *shared, cols, ("add", back)
    )
    logit_in = box.pieces(d_logit_bias, "x")
    cols, back, keep_b, give_b, keep_c, give_c, row_out, logit_in = step(
        cols, back, keep_b, give_b, keep_c, give_c, row_out, logit_in
    )
    d_logit_bias = box.same_sum(d_logit_bias, logit_in, "x")
    give_c = swap_cores(give_c)
    ab = both_cores([keep_b], [give_b])
    give_c, keep_c, ab, cols = step(give_c, keep_c, ab, cols)
    c0 = Scatter(ab, both_cores([keep_c], [give_c]))
    cols, back, keep_d, give_d, *sums_2 = call_backward(
        (3, 4, 5), ("own", "other"), *common, grads, *shared, cols, ("add", back)
    )
    rows_in = box.to_partner(row_out, False)
    logit_in = box.pieces(d_logit_bias, "flip")
    cols, back, keep_d, give_d, rows_in, logit_in = sync(
        [c0], cols, back, keep_d, give_d, rows_in, logit_in
    )
    d_logit_bias = box.same_sum(d_logit_bias, logit_in, "flip")
    c0.second()
    give_d = swap_cores(give_d)
    g_sum, g_low, d_gate = call_gate(ints, back, cols, probs, x, small)
    cd = both_cores([keep_d], [give_d])
    logit_in = box.pieces(d_logit_bias, "z")
    g_sum, g_low, d_gate, cd, logit_in = sync([c0], g_sum, g_low, d_gate, cd, logit_in)
    d_logit_bias = box.same_sum(d_logit_bias, logit_in, "z")
    c1 = Scatter(cd)
    back_in = box.to_partner(g_low, False)
    (back_in,) = sync([c0, c1], back_in)
    c0.third()
    c1.second()
    back_in, _ = step(back_in, c1.state[:2])
    grad_events, d_small = call_finish(
        ints, grad_block, grad_in, g_sum, back_in, events, small, d_tower, d_gate, lanes, d_tower_vec,
        [sums_0, sums_1, sums_2],
    )
    grad_events, d_small = sync([c0, c1], grad_events, d_small)
    c1.third()
    c0.fourth()
    d_small, _ = step(d_small, c1.state[0])
    d_small = d_small.reshape(places, 2, width, PACK)
    d_other = swap_cores(lax.dynamic_index_in_dim(d_small, 1 - core, 1, keepdims=False))
    d_mine = total(lax.dynamic_index_in_dim(d_small, core, 1, keepdims=False), [d_other])
    d_mine = d_mine.astype(bf16).reshape(nx * ny, nz, 2, width, PACK)
    d_parts = [d_mine[k] for k in range(nx * ny)]
    d_in = box.hand_out_plane(d_parts)
    order = position[None, :] == jnp.arange(rows, dtype=f32)[:, None]
    grad_embeds = lax.dot_general(
        order.astype(bf16), grad_events, (((0,), (0,)), ((), ())), preferred_element_type=f32
    ).astype(bf16)
    predicted = in_order(role, row_out, rows_in, 1)
    predictions = jnp.sum(jnp.where(order, predicted[0][:, None], 0.0), axis=0)
    predictions = jnp.broadcast_to(predictions[None], (8, rows))
    d_mine, d_in, grad_embeds, predictions = sync(
        [c0, c1], d_parts[0], d_in, grad_embeds, predictions
    )
    c1.fourth()
    d_mine, _ = step(d_mine, c1.state[0])
    d_mine = total(d_mine, d_in).astype(bf16)
    same = [lax.dynamic_index_in_dim(d_mine[k], role, 0, keepdims=False) for k in range(nz)]
    flip = [lax.dynamic_index_in_dim(d_mine[k], 1 - role, 0, keepdims=False) for k in range(nz)]
    d_in = box.hand_out(same, "z") + box.hand_out_flip(flip)
    grad_embeds = jnp.where(at_home, grad_embeds, swap_cores(grad_embeds))
    predictions = jnp.where(at_home, predictions, swap_cores(predictions))[0]
    d_in, grad_embeds, predictions = sync([c1], d_in, grad_embeds, predictions)
    (
        proj_grad, tower_grad, top, shared_gate, domain_gate, proj_b_grad, in_bias_grad, tower_b_grad,
        tower_out_grad, *vectors,
    ) = call_small([same[0]] + d_in)
    grad_w_in, grad_w_out = call_place(
        ints, [c0.state[0], c1.state[0]], [c0.state[1], c1.state[1]]
    )
    return (
        predictions,
        grad_embeds,
        proj_grad.T,
        proj_b_grad[0],
        grad_w_in,
        in_bias_grad,
        jnp.swapaxes(grad_w_out, 1, 2),
        *vectors,
        jnp.swapaxes(top, 1, 2),
        jnp.swapaxes(shared_gate, 1, 2),
        jnp.swapaxes(domain_gate, 1, 2),
        tower_grad,
        tower_b_grad,
        tower_out_grad,
        d_logit_bias[0, :DOM],
    )


def solution(mesh):
    both = ("dp", "tensor")
    in_specs = (
        P("dp", None),
        P("dp", None),
        P(),
        P("dp"),
        P(None, both),
        P(both),
        P(None, "dp", "tensor"),
        P(None, both),
        P(None, "tensor", "dp"),
        P(None, both),
        P(None, both),
        P(None, both),
        P(None, both, None),
        P(None, both, None),
        P(None, both, None),
        P(None, both, None),
        P(None, both),
        P(None, both),
        P(),
    )
    out_specs = (
        P("dp"),
        P("dp", None),
        P(None, both),
        P(both),
        P(None, "dp", "tensor"),
        P(None, both),
        P(None, "tensor", "dp"),
        P(None, both),
        P(None, both),
        P(None, both),
        P(None, both, None),
        P(None, both, None),
        P(None, both, None),
        P(None, both, None),
        P(None, both),
        P(None, both),
        P(),
    )
    return jax.shard_map(
        functools.partial(per_device, Box(mesh.shape["dp"])),
        mesh=mesh,
        in_specs=in_specs,
        out_specs=out_specs,
        check_vma=False,
    )
```

```python
import functools
import math

import jax
import jax.numpy as jnp
import numpy as np
from jax import lax
from jax.experimental import pallas as pl
from jax.experimental.pallas import tpu as pltpu
from jax.sharding import PartitionSpec as P

D = 512
H = 1024
HALF = H // 2
TW = 256
S = 4
DOM = 4
K = 2
EPS = 1e-05
FROZEN_SHARE = 0.25
TILE = 256
LOCAL = 6
CHUNKS = ((0, 1, 2), (3, 4, 5))
VMEM_LIMIT = 48 * 1024 * 1024
PACK = 1792
SETS = (
    tuple(range(2)) + tuple(S + K * d for d in reversed(range(DOM))),
    tuple(range(2, 4)) + tuple(S + K * d + 1 for d in range(DOM)),
)
COEF, SCALE, DCOEF, DOMAIN, LABEL, WEIGHT, BIAS = 0, 6, 12, 18, 19, 20, 21
LOW, HIGH, ROLE, DOMAIN_OF, START, END, CORE = 0, 4, 8, 9, 13, 17, 21

bf16 = jnp.bfloat16
f32 = jnp.float32


def dims_of(count):
    if count % 4 == 0:
        rest = count // 4
        root = math.isqrt(rest)
        if root * root == rest:
            return (4, root, root)
    return (count, 1, 1)


class Box:
    def __init__(self, count):
        first, second, third = dims_of(count)
        self.count = count
        self.dims = (2, first // 2, second, third)
        self.strides = (second * third, 2 * second * third, third, 1)

    def role(self, chip):
        return (chip // self.strides[0]) % 2

    def partner(self, chip):
        return chip + (1 - 2 * self.role(chip)) * self.strides[0]

    def send(self, values, flip=0, z=0, y=0, x=0):
        pairs = []
        for chip in range(self.count):
            to = chip
            for step, size, stride in zip((flip, z, y, x), self.dims, self.strides):
                place = (chip // stride) % size
                to += ((place + step) % size - place) * stride
            pairs.append((chip, to))
        return lax.ppermute(values, "dp", pairs)

    def to_partner(self, values, home):
        pairs = []
        for chip in range(self.count):
            for core in range(2):
                if (core == self.role(chip)) == home:
                    pairs.append((2 * chip + core, 2 * self.partner(chip) + core))
        return lax.ppermute(values, ("dp", "tensor"), pairs)

    def pieces(self, values, dim):
        size = self.dims[("flip", "z", "y", "x").index(dim)]
        return [self.send(values, **{dim: -k}) for k in range(1, size)]

    def hand_out(self, parts, dim):
        return [self.send(part, **{dim: k}) for k, part in enumerate(parts) if k]

    def line(self, same, other):
        steps = range(1, self.dims[1])
        return [self.send(same, z=-z) for z in steps], [self.send(other, flip=1, z=-z) for z in steps]

    def in_line(self, own, flip, found, role, axis):
        same, other = found
        return [in_order(role, s, o, axis) for s, o in zip([own] + same, [flip] + other)]

    def hand_out_flip(self, parts):
        return [self.send(part, flip=1, z=k) for k, part in enumerate(parts)]

    def plane(self):
        _, _, ny, nx = self.dims
        return [(x, y) for x in range(nx) for y in range(ny)][1:]

    def gather_plane(self, values):
        return [values] + [self.send(values, y=-y, x=-x) for x, y in self.plane()]

    def hand_out_plane(self, parts):
        return [self.send(part, y=y, x=x) for part, (x, y) in zip(parts[1:], self.plane())]

    def same_sum(self, values, found, dim):
        number = ("flip", "z", "y", "x").index(dim)
        size, stride = self.dims[number], self.strides[number]
        found = jnp.stack([values] + found)
        if size > 2:
            mine = (lax.axis_index("dp") // stride) % size
            found = jnp.take(found, (jnp.arange(size) - mine) % size, axis=0)
        return functools.reduce(jnp.add, [found[k] for k in range(size)])

    def ahead(self, place):
        me = lax.axis_index("dp")
        chip, weight = 0, 1
        for dim, (size, stride) in enumerate(zip(self.dims, self.strides)):
            mine = (me // stride) % size if dim else 0
            chip = chip + ((mine + (place // weight) % size) % size) * stride
            weight *= size
        return chip


def swap_cores(values):
    return lax.ppermute(values, "tensor", [(0, 1), (1, 0)])


def in_order(which, own, other, axis):
    return jnp.where(
        which == 0,
        jnp.concatenate([own, other], axis),
        jnp.concatenate([other, own], axis),
    )


def step(*values):
    return lax.optimization_barrier(values)


def total(first, arrived):
    return functools.reduce(jnp.add, [a.astype(f32) for a in arrived], first.astype(f32))


def gelu_parts(v):
    inner = math.sqrt(2.0 / math.pi)
    square = v * v
    th = jnp.tanh(v * (inner + inner * 0.044715 * square))
    half = 0.5 * (1.0 + th)
    act = v * half
    slope = half + 0.5 * v * (1.0 - th * th) * (inner + 3.0 * inner * 0.044715 * square)
    return act, slope


def nt(a, b):
    return lax.dot_general(a, b, (((1,), (1,)), ((), ())), preferred_element_type=f32)


def tn(a, b):
    return lax.dot_general(a, b, (((0,), (0,)), ((), ())), preferred_element_type=f32)


def nn(a, b):
    return jnp.dot(a, b, preferred_element_type=f32)


def softmax_rows(v):
    e = jnp.exp(v - jnp.max(v, axis=0, keepdims=True))
    return e / jnp.sum(e, axis=0, keepdims=True)


def prepare_kernel(
    ints, floats, rows_ref, own_ref, in_ref, proj_ref, gates_ref, vec_ref, ev_ref, x_ref, mix_ref, cols_ref, prob_ref, embeds_ref, arrived
):
    tiles_of_half = pl.num_programs(0) // 2
    index = pl.program_id(0)
    role = ints[ROLE]
    count = rows_ref.shape[1]
    at_home = ints[CORE] == role

    @pl.when((index == 0) & at_home)
    def _():
        copy = pltpu.make_async_copy(own_ref, embeds_ref, arrived.at[0])
        copy.start()
        copy.wait()

    @pl.when((index == 0) & jnp.logical_not(at_home))
    def _():
        copy = pltpu.make_async_copy(in_ref, embeds_ref, arrived.at[0])
        copy.start()
        copy.wait()

    slot = index * TILE + lax.broadcasted_iota(jnp.int32, (TILE, count), 0)
    here = rows_ref[0:1, :].astype(jnp.int32) == slot
    order = jnp.where(here, 1.0, 0.0).astype(bf16)
    label = jnp.sum(jnp.where(here, rows_ref[1:2, :], 0.0), axis=1, keepdims=True)
    events = nn(order, embeds_ref[...]).astype(bf16)
    ev_ref[...] = events
    mixed = nt(events, proj_ref[...]) + vec_ref[3 * LOCAL : 3 * LOCAL + 1, :]
    low = mixed.astype(bf16)
    x_ref[...] = low
    mix_ref[...] = mixed * jnp.where(index // tiles_of_half == role, 1.0, 0.0)
    logits = jnp.transpose(nn(low, gates_ref[...]))
    place = index * TILE + lax.broadcasted_iota(jnp.int32, (1, TILE), 1)
    picks = [
        jnp.where((place >= ints[START + d]) & (place < ints[END + d]), 1.0, 0.0) for d in range(DOM)
    ]

    def pick(low_row, size):
        return softmax_rows(
            functools.reduce(
                jnp.add,
                [picks[d] * logits[low_row + d * size : low_row + (d + 1) * size] for d in range(DOM)],
            )
        )

    top, shared, domain = pick(0, 2), pick(2 * DOM, S), pick((2 + S) * DOM, K)
    prob_ref[...] = jnp.concatenate([top, shared, domain], axis=0)
    first = role == 0
    own_shared = top[0:1] * jnp.where(first, shared[:2], shared[2:])
    own_domain = top[1:2] * jnp.where(first, domain[0:1], domain[1:2])
    coef = [own_domain * jnp.where(first, picks[DOM - 1 - d], picks[d]) for d in range(DOM)]
    table = [
        own_shared,
        *coef,
        jnp.zeros((DOMAIN - SCALE, TILE), f32),
        sum(float(d) * picks[d] for d in range(DOM)),
        jnp.zeros((1, TILE), f32),
        sum(floats[d] * picks[d] for d in range(DOM)),
        sum(floats[DOM + d] * picks[d] for d in range(DOM)),
        jnp.zeros((128 - BIAS - 1, TILE), f32),
    ]
    cols_ref[...] = with_column(jnp.transpose(jnp.concatenate(table, axis=0)), LABEL, label)


def with_column(table, column, values):
    lane = lax.broadcasted_iota(jnp.int32, table.shape, 1)
    return jnp.where(lane == column, values, table)


def tiles_of(expert, ints, first, count):
    low = jnp.maximum(ints[LOW + expert - 2], first)
    high = jnp.minimum(ints[HIGH + expert - 2], first + count)
    return low - first, jnp.maximum(high, low) - first


def each_span(expert, ints, first, rows, work):
    if expert < 2:
        work(slice(0, rows))
    else:
        low, high = tiles_of(expert, ints, first, rows // TILE)

        def one(index, _):
            work(pl.ds(pl.multiple_of(index * TILE, TILE), TILE))
            return 0

        lax.fori_loop(low, high, one, 0)


def join(pieces, held):
    count = len(pieces) // 2
    for core in range(2):
        mine = pieces[core * count : core * count + count]
        by_x, by_y = split_pieces(mine)
        nx, ny = len(by_x), len(by_y)
        rows = by_x[0].shape[3]
        nz = by_x[0].shape[1]

        def at(x, y, z):
            return pl.ds(((x * ny + y) * nz + z) * rows, rows)

        for x in range(nx):
            for y in range(ny):
                for z in range(nz):
                    held[core][at(x, y, z), :] = by_x[x][y, z, 0]
                    held[2 + core][at(x, y, z), :] = by_y[y][x, z, 0]


def split_pieces(pieces):
    nx = pieces[-1].shape[0]
    return pieces[:nx], pieces[nx:]


def forward_kernel(experts, own, aliased, number, gives, ints, x_ref, *refs):
    arrays = sorted({e // 3 for e in experts})
    weights = {a: refs[number * k : number * (k + 1)] for k, a in enumerate(arrays)}
    refs = refs[number * len(arrays) :]
    refs, held = refs[:-4], refs[-4:]
    wi_a, wi_b, wo_a, wo_b = held
    bi_ref, vec_ref, cols_in, mix_in = refs[:4]
    cols_ref, mix_ref, *norm_refs = refs[4 + aliased :]
    if gives:
        *norm_refs, give_ref = norm_refs
    norm_refs = dict(zip(arrays, norm_refs))
    rows = x_ref.shape[0]
    half = ints[ROLE] if own else 1 - ints[ROLE]
    step = pl.program_id(0)

    @pl.when(step == 0)
    def _():
        cols_ref[...] = cols_in[...]
        mix_ref[...] = mix_in[...]

    def work(expert, span):
        x = x_ref[span, :]
        pre_a = nn(x, wi_a[...]) + bi_ref[expert : expert + 1, :HALF]
        act_a = gelu_parts(pre_a)[0].astype(bf16)
        pre_b = nn(x, wi_b[...]) + bi_ref[expert : expert + 1, HALF:]
        act_b = gelu_parts(pre_b)[0].astype(bf16)
        out = nt(act_a, wo_a[...]) + nt(act_b, wo_b[...]) + vec_ref[expert : expert + 1, :]
        centre = jnp.mean(out, axis=1, keepdims=True)
        centred = out - centre
        scale = lax.rsqrt(jnp.mean(centred * centred, axis=1, keepdims=True) + EPS)
        norm = centred * scale
        norm_refs[expert // 3][0, span, :] = norm.astype(bf16)
        cols = cols_ref[span, :]
        cols_ref[span, :] = with_column(cols, SCALE + expert, scale)
        gain = vec_ref[LOCAL + expert : LOCAL + expert + 1, :]
        shift = vec_ref[2 * LOCAL + expert : 2 * LOCAL + expert + 1, :]
        mix_ref[span, :] += cols[:, COEF + expert : COEF + expert + 1] * (norm * gain + shift)

    for place, expert in enumerate(experts):

        @pl.when(step == place)
        def _(expert=expert):
            join(weights[expert // 3], held)
            each_span(expert, ints, half * (rows // TILE), rows, functools.partial(work, expert))

    if gives:

        @pl.when(step == len(experts) - 1)
        def _():
            give_ref[...] = mix_ref[...].astype(bf16)


def backward_kernel(experts, halves, keeps_back, adds, number, ints, x_ref, *refs):
    gb_refs, refs = refs[: len(halves)], refs[len(halves) :]
    norm_ref, pieces, refs = refs[0], refs[1 : 1 + number], refs[1 + number :]
    bi_ref, vec_ref, cols_in = refs[:3]
    refs, held = refs[3:-4], refs[-4:]
    wi_a, wi_b, wo_a, wo_b = held
    join(pieces, held)
    back_in, refs = refs[0], refs[1:]
    if adds:
        dvec_in, dbi_in, keep_in, give_in = refs[:4]
        refs = refs[4:]
    cols_ref, back_ref, keep_ref, give_ref, dvec_ref, dbi_ref, in_a, in_b, out_a, out_b = refs
    rows = x_ref.shape[0]
    half_tiles = rows // TILE // len(halves)
    first = 0 if len(halves) == 2 else (ints[ROLE] if halves[0] == "own" else 1 - ints[ROLE]) * half_tiles
    step = pl.program_id(0)

    @pl.when(step == 0)
    def _():
        cols_ref[...] = cols_in[...]
        back_ref[...] = back_in[...] if keeps_back else jnp.zeros_like(back_ref)

    dvec_ref[...] = dvec_in[...] if adds else jnp.zeros_like(dvec_ref)
    dbi_ref[...] = dbi_in[...] if adds else jnp.zeros_like(dbi_ref)

    def work(expert, span):
        whole = isinstance(span, slice)

        def add(ref, target, which, values):
            if whole and adds:
                before = keep_in if target is keep_ref else give_in
                target[0, which] = (values + before[0, which].astype(f32)).astype(bf16)
            elif whole:
                target[0, which] = values.astype(bf16)
            else:
                ref[...] += values

        x = x_ref[span, :]
        norm = norm_ref[0, span, :].astype(f32)
        cols = cols_ref[span, :]
        if len(halves) == 1:
            grad_block = gb_refs[0][span, :].astype(f32)
        else:
            half = span.start // (half_tiles * TILE)
            inner = pl.ds(pl.multiple_of(span.start - half * (half_tiles * TILE), TILE), TILE)
            grad_block = jnp.where(
                half == ints[ROLE], gb_refs[0][inner, :].astype(f32), gb_refs[1][inner, :].astype(f32)
            )
        gain = vec_ref[LOCAL + expert : LOCAL + expert + 1, :]
        shift = vec_ref[2 * LOCAL + expert : 2 * LOCAL + expert + 1, :]
        scale = cols[:, SCALE + expert : SCALE + expert + 1]
        grad_exp = cols[:, COEF + expert : COEF + expert + 1] * grad_block
        scaled = grad_exp * norm
        dx = grad_exp * gain
        first_mean = jnp.mean(dx, axis=1, keepdims=True)
        second_mean = jnp.mean(dx * norm, axis=1, keepdims=True)
        grad_sum = scale * (dx - first_mean - norm * second_mean)
        grad_low = grad_sum.astype(bf16)
        pre_a = nn(x, wi_a[...]) + bi_ref[expert : expert + 1, :HALF]
        act_a, slope_a = gelu_parts(pre_a)
        low_a = (nn(grad_low, wo_a[...]) * slope_a).astype(bf16)
        pre_b = nn(x, wi_b[...]) + bi_ref[expert : expert + 1, HALF:]
        act_b, slope_b = gelu_parts(pre_b)
        low_b = (nn(grad_low, wo_b[...]) * slope_b).astype(bf16)
        add(out_a, keep_ref, 1, tn(grad_low, act_a.astype(bf16)))
        add(in_a, keep_ref, 0, tn(x, low_a))
        add(out_b, give_ref, 1, tn(grad_low, act_b.astype(bf16)))
        add(in_b, give_ref, 0, tn(x, low_b))
        back_ref[span, :] += nt(low_a, wi_a[...]) + nt(low_b, wi_b[...])
        dcoef = jnp.sum(grad_block * (norm * gain + shift), axis=1, keepdims=True)
        if expert < 2:
            cols_ref[span, :] = with_column(cols, DCOEF + expert, dcoef)
        else:
            mine = cols[:, DOMAIN : DOMAIN + 1] == ints[DOMAIN_OF + expert - 2].astype(f32)
            column = cols[:, DCOEF + 2 : DCOEF + 3] + jnp.where(mine, dcoef, 0.0)
            cols_ref[span, :] = with_column(cols, DCOEF + 2, column)
        dvec_ref[0, 0:1, :] += jnp.sum(grad_sum, axis=0, keepdims=True)
        dvec_ref[0, 1:2, :] += jnp.sum(scaled, axis=0, keepdims=True)
        dvec_ref[0, 2:3, :] += jnp.sum(grad_exp, axis=0, keepdims=True)
        dbi_ref[0, 0:1, :HALF] += jnp.sum(low_a.astype(f32), axis=0, keepdims=True)
        dbi_ref[0, 0:1, HALF:] += jnp.sum(low_b.astype(f32), axis=0, keepdims=True)

    for place, expert in enumerate(experts):

        @pl.when(step == place)
        def _(expert=expert):
            if expert >= 2:
                for ref in (in_a, in_b, out_a, out_b):
                    ref[...] = jnp.zeros_like(ref)
            each_span(expert, ints, first, rows, functools.partial(work, expert))
            if expert >= 2:
                keep_ref[0, 0] = in_a[...].astype(bf16)
                keep_ref[0, 1] = out_a[...].astype(bf16)
                give_ref[0, 0] = in_b[...].astype(bf16)
                give_ref[0, 1] = out_b[...].astype(bf16)


def tower_kernel(
    ints, mix_ref, other_ref, cols_ref, tw_ref, tv_ref, out_ref, gb_ref, low_ref, dw_ref, dv_ref, db_ref
):
    @pl.when(pl.program_id(0) == 0)
    def _():
        db_ref[...] = jnp.zeros_like(db_ref)
        dw_ref[...] = jnp.zeros_like(dw_ref)
        dv_ref[...] = jnp.zeros_like(dv_ref)

    bias = tv_ref[0:1, :]
    head = tv_ref[1:2, :]
    cols = cols_ref[...]
    block = (mix_ref[...] + other_ref[...].astype(f32)).astype(bf16)
    tower = slice(PACK - 128 - DOM * TW, PACK - 128)
    pre = nn(block, tw_ref[:, tower]) + bias
    act, slope = gelu_parts(pre)
    group = lax.broadcasted_iota(jnp.int32, pre.shape, 1) // TW
    mine = group == cols[:, DOMAIN : DOMAIN + 1].astype(jnp.int32)
    act = jnp.where(mine, act, 0.0)
    logit = jnp.sum(act * head, axis=1, keepdims=True) + cols[:, BIAS : BIAS + 1]
    small = jnp.exp(-jnp.abs(logit))
    predicted = jnp.where(logit >= 0.0, 1.0, small) / (1.0 + small)
    grad_logit = cols[:, WEIGHT : WEIGHT + 1] * (predicted - cols[:, LABEL : LABEL + 1])
    lane = lax.broadcasted_iota(jnp.int32, cols.shape, 1)
    out_ref[...] = jnp.transpose(jnp.where(lane == 0, predicted, jnp.where(lane == 1, grad_logit, 0.0)))[:8]
    by_domain = jnp.where(lane.astype(f32) == cols[:, DOMAIN : DOMAIN + 1], grad_logit, 0.0)
    db_ref[0:1, :] += jnp.sum(by_domain, axis=0, keepdims=True)
    dv_ref[1:2, :] += jnp.sum(grad_logit * act, axis=0, keepdims=True)
    grad_pre = jnp.where(mine, grad_logit * head * slope, 0.0)
    dv_ref[0:1, :] += jnp.sum(grad_pre, axis=0, keepdims=True)
    grad_low = grad_pre.astype(bf16)
    grad_block = nt(grad_low, tw_ref[:, tower])
    gb_ref[...] = grad_block
    low_ref[...] = grad_block.astype(bf16)
    dw_ref[...] += tn(block, grad_low)


def softmax_back(probability, grad_probs):
    return probability * (grad_probs - jnp.sum(probability * grad_probs, axis=0, keepdims=True))


def gate_kernel(ints, back_ref, cols_ref, prob_ref, x_ref, gates_ref, sum_ref, low_ref, gate_ref):
    index = pl.program_id(0)
    first = ints[ROLE] == 0

    @pl.when(index == 0)
    def _():
        gate_ref[...] = jnp.zeros_like(gate_ref)

    mine = jnp.transpose(cols_ref[...])[DCOEF : DCOEF + 3]
    none = jnp.zeros_like(mine)
    one, two = jnp.where(first, mine, none), jnp.where(first, none, mine)
    d_shared = jnp.concatenate([one[0:2], two[0:2]], axis=0)
    d_domain = jnp.concatenate([one[2:3], two[2:3]], axis=0)
    top, shared, domain = prob_ref[0:2, :], prob_ref[2:6, :], prob_ref[6:8, :]
    d_top = jnp.concatenate(
        [
            jnp.sum(d_shared * shared, axis=0, keepdims=True),
            jnp.sum(d_domain * domain, axis=0, keepdims=True),
        ],
        axis=0,
    )
    grads = (
        softmax_back(top, d_top),
        softmax_back(shared, d_shared * top[0:1]),
        softmax_back(domain, d_domain * top[1:2]),
    )
    rows = top.shape[1]
    place = index * rows + lax.broadcasted_iota(jnp.int32, (1, rows), 1)
    picks = [
        jnp.where((place >= ints[START + d]) & (place < ints[END + d]), 1.0, 0.0) for d in range(DOM)
    ]
    spread = jnp.concatenate(
        [picks[d] * grad for grad in grads for d in range(DOM)] + [jnp.zeros((96, rows), f32)],
        axis=0,
    )
    spread = jnp.transpose(spread).astype(bf16)
    gate_ref[...] += tn(x_ref[...], spread)
    added = back_ref[...] + nt(spread, gates_ref[...])
    sum_ref[...] = added
    low_ref[...] = added.astype(bf16)


def call_gate(ints, back, cols, probs, x, small):
    rows = x.shape[0]
    half = rows // 2

    def tile(width):
        return pl.BlockSpec((half, width), lambda i, *_: (i, 0))

    return pl.pallas_call(
        gate_kernel,
        grid_spec=pltpu.PrefetchScalarGridSpec(
            num_scalar_prefetch=1,
            grid=(2,),
            in_specs=[
                tile(D),
                tile(128),
                pl.BlockSpec((8, half), lambda i, *_: (0, i)),
                tile(D),
                GATES_SPEC,
            ],
            out_specs=(tile(D), tile(D), fixed((D, 128))),
        ),
        out_shape=(
            jax.ShapeDtypeStruct((rows, D), f32),
            jax.ShapeDtypeStruct((rows, D), bf16),
            jax.ShapeDtypeStruct((D, 128), f32),
        ),
        compiler_params=params(),
        cost_estimate=pl.CostEstimate(
            flops=4 * rows * D * 128, bytes_accessed=10_000_000, transcendentals=0
        ),
        name="gates",
    )(ints, back, cols, probs, x, small)


def hidden_lines(ints, lane_ref, tv_ref, line_refs):
    first_set, first_core = ints[ROLE] == 0, ints[CORE] == 0
    mine = [r[k, 0:1, :] for r in line_refs for k in range(r.shape[0])]
    mine = jnp.concatenate(mine, axis=0)
    mine = jnp.where(first_core, mine, pltpu.roll(mine, HALF, 1))
    mine = jnp.where(first_set, mine, 0.0), jnp.where(first_set, 0.0, mine)
    found = {j: mine[r][i : i + 1] for r, row in enumerate(SETS) for i, j in enumerate(row)}
    mine = jnp.concatenate([found[j] for j in range(2 * LOCAL)], axis=0).astype(bf16)

    def lanes(values, row):
        lane = lax.broadcasted_iota(jnp.int32, (H, D), 0)
        chosen = jnp.where(lane == lane_ref[row : row + 1, :], 1.0, 0.0).astype(bf16)
        return nn(values, chosen)

    tower = tv_ref[...].astype(bf16)
    rows = [lanes(mine, 0), lanes(mine, 1)]
    head = lane_ref[6:7, :] == 1
    for d in range(DOM):
        both = lanes(tower, 2 + d)
        rows.append(jnp.where(head, both[1:2], both[0:1]))
    return rows


def finish_kernel(
    ints, gb_ref, gb_in_ref, sum_ref, in_ref, ev_ref, proj_ref, tower_ref, gate_ref, *refs
):
    lane_ref, tv_ref, *vec_refs, ge_ref, small_ref, proj_sum, bias_sum = refs
    vec_refs, line_refs = vec_refs[: len(vec_refs) // 2], vec_refs[len(vec_refs) // 2 :]
    index = pl.program_id(0)
    last = pl.num_programs(0) - 1
    first = ints[ROLE] == 0
    at_home = jnp.where(ints[CORE] == ints[ROLE], 1.0, 0.0)
    mine_half = index == ints[ROLE]

    @pl.when(index == 0)
    def _():
        for ref in (proj_sum, bias_sum):
            ref[...] = jnp.zeros_like(ref)

    grad_mixed = jnp.where(mine_half, gb_ref[...], gb_in_ref[...].astype(f32))
    grad_mixed = at_home * (grad_mixed + sum_ref[...] + in_ref[...].astype(f32))
    bias_sum[0:1, :] += jnp.sum(grad_mixed, axis=0, keepdims=True)
    low = grad_mixed.astype(bf16)
    proj_sum[...] += tn(low, ev_ref[...])
    ge_ref[...] = nn(low, proj_ref[...]).astype(bf16)

    @pl.when(index == last)
    def _():
        e_in = proj_sum.shape[1]
        vectors = jnp.concatenate(
            [r[k, 0:3, :] for r in vec_refs for k in range(r.shape[0])], axis=0
        )
        rows = jnp.concatenate(
            [
                jnp.zeros((32, D), f32),
                jnp.where(first, vectors, 0.0),
                jnp.where(first, 0.0, vectors),
                bias_sum[0:1, :],
                *hidden_lines(ints, lane_ref, tv_ref, line_refs),
                jnp.zeros((31, D), f32),
            ],
            axis=0,
        )
        small_ref[:, :e_in] = proj_sum[...].astype(bf16)
        small_ref[:, e_in : e_in + DOM * TW] = tower_ref[...].astype(bf16)
        small_ref[:, e_in + DOM * TW :] = (gate_ref[...] + jnp.transpose(rows)).astype(bf16)


def call_finish(ints, gb, gb_in, added, arrived, events, small, tower, gate, lanes, tower_vec, sums):
    rows, e_in = events.shape
    half = rows // 2

    def tile(width):
        return pl.BlockSpec((half, width), lambda i, *_: (i, 0))

    halves = (gb, gb_in)
    wholes = (tower, gate, lanes, tower_vec)
    vecs = [v for v, _ in sums] + [b for _, b in sums]
    return pl.pallas_call(
        finish_kernel,
        grid_spec=pltpu.PrefetchScalarGridSpec(
            num_scalar_prefetch=1,
            grid=(2,),
            in_specs=[fixed(a.shape) for a in halves]
            + [tile(D), tile(D), tile(e_in), proj_spec(e_in)]
            + [fixed(a.shape) for a in (*wholes, *vecs)],
            out_specs=(tile(e_in), fixed((D, PACK))),
            scratch_shapes=[pltpu.VMEM((D, e_in), f32), pltpu.VMEM((8, D), f32)],
        ),
        out_shape=(jax.ShapeDtypeStruct((rows, e_in), bf16), jax.ShapeDtypeStruct((D, PACK), bf16)),
        compiler_params=params(),
        cost_estimate=pl.CostEstimate(flops=4 * rows * D * e_in, bytes_accessed=14_000_000, transcendentals=0),
        name="finish",
    )(ints, *halves, added, arrived, events, small, *wholes, *vecs)


VECTOR_ROW = {j: 32 + 18 * r + 3 * i for r, row in enumerate(SETS) for i, j in enumerate(row)}


def small_kernel(*refs):
    parts, vec_refs = refs[:-12], refs[-3:]
    proj_ref, tower_ref, top_ref, shared_ref, domain_ref, bias_ref, hidden_ref, tb_ref, to_ref = refs[-12:-3]
    added = functools.reduce(jnp.add, [p[...].astype(f32) for p in parts])
    width, e_in = proj_ref.shape
    proj_ref[...] = added[:, :e_in]
    for d in range(DOM):
        tower_ref[d] = added[:, e_in + d * TW : e_in + (d + 1) * TW]
    rows = jnp.concatenate([added[:, e_in + DOM * TW :], jnp.zeros((128 - width, 128), f32)], axis=0)
    rows = jnp.transpose(rows)[:, :width]
    for ref, low, size in ((top_ref, 0, 2), (shared_ref, 2 * DOM, S), (domain_ref, (2 + S) * DOM, K)):
        for d in range(DOM):
            ref[d] = rows[low + d * size : low + (d + 1) * size]
    bias_ref[...] = rows[68:69]
    hidden_ref[:, :width] = rows[69:81]
    hidden_ref[:, width:] = rows[81:93]
    tb_ref[...] = rows[93:97, : width // 2]
    to_ref[...] = rows[93:97, width // 2 :]
    for which, ref in enumerate(vec_refs):
        for j in range(2 * LOCAL):
            ref[j : j + 1, :] = rows[VECTOR_ROW[j] + which : VECTOR_ROW[j] + which + 1]


def call_small(parts):
    width = parts[0].shape[0]
    e_in = PACK - DOM * TW - 128
    shapes = [(width, e_in), (DOM, width, TW), (DOM, 2, width), (DOM, S, width), (DOM, K, width), (1, width)]
    shapes += [(2 * LOCAL, 2 * width), (DOM, width // 2), (DOM, width // 2)]
    shapes += [(2 * LOCAL, width)] * 3
    return pl.pallas_call(
        small_kernel,
        grid=(1,),
        in_specs=[fixed(p.shape) for p in parts],
        out_specs=tuple(fixed(shape) for shape in shapes),
        out_shape=tuple(jax.ShapeDtypeStruct(shape, f32) for shape in shapes),
        compiler_params=params(),
        name="small",
    )(*parts)


def place_kernel(ints, *refs):
    *parts, in_ref, out_ref = refs
    half = len(parts) // 2
    first = ints[ROLE] == 0
    for chunk, (own, other) in enumerate(zip(parts[:half], parts[half:])):
        for place, expert in enumerate(CHUNKS[chunk]):
            for which, ref in enumerate((in_ref, out_ref)):
                a, b = own[which, place].astype(f32), other[which, place].astype(f32)
                ref[SETS[0][expert]] = jnp.where(first, a, b)
                ref[SETS[1][expert]] = jnp.where(first, b, a)


def call_place(ints, own, other):
    rows, width = own[0].shape[2:]
    shape = (2 * LOCAL, rows, width)
    return pl.pallas_call(
        place_kernel,
        grid_spec=pltpu.PrefetchScalarGridSpec(
            num_scalar_prefetch=1,
            grid=(1,),
            in_specs=[fixed(a.shape) for a in (*own, *other)],
            out_specs=(fixed(shape), fixed(shape)),
        ),
        out_shape=(jax.ShapeDtypeStruct(shape, f32),) * 2,
        compiler_params=params(),
        name="place",
    )(ints, *own, *other)


def params():
    return pltpu.CompilerParams(vmem_limit_bytes=VMEM_LIMIT)


def fixed(shape):
    return pl.BlockSpec(shape, lambda i, *_: (0,) * len(shape))


def pack_kernel(proj_ref, tower_ref, gate_ref, rest_ref, out_ref):
    width, e_in = proj_ref.shape
    out_ref[:, :e_in] = proj_ref[...]
    for d in range(DOM):
        out_ref[:, e_in + d * TW : e_in + (d + 1) * TW] = tower_ref[d]
    gates, rest = gate_ref[...].astype(f32), rest_ref[...].astype(f32)
    rows = []
    for low, size in ((0, 2), (2, S), (2 + S, K)):
        rows += [gates[d, low : low + size] for d in range(DOM)]
    rows += [rest[:12, k * width : (k + 1) * width] for k in range(3)] + [rest[16:17, :width]]
    rows += [rest[:12, k * width : (k + 1) * width] for k in (3, 4)] + [rest[12:16, :width]]
    rows = jnp.concatenate(rows + [jnp.zeros((31, width), f32)], axis=0)
    rows = jnp.concatenate([rows, jnp.zeros((128, 128 - width), f32)], axis=1)
    out_ref[:, e_in + DOM * TW :] = jnp.transpose(rows)[:width].astype(bf16)


def call_pack(*arrays):
    width = arrays[0].shape[0]
    return pl.pallas_call(
        pack_kernel,
        grid=(1,),
        in_specs=[fixed(a.shape) for a in arrays],
        out_specs=fixed((width, PACK)),
        out_shape=jax.ShapeDtypeStruct((width, PACK), bf16),
        compiler_params=params(),
        name="pack",
    )(*arrays)


PICKED = [
    [32 + e for e in row] + [44 + e for e in row] + [56 + e for e in row] + [68] + [127] * 5
    + [69 + e for e in row] + [81 + e for e in row] + [93 + d for d in range(DOM)]
    for row in SETS
]


def unpack_kernel(ints, small_ref, choose_ref, lane_ref, vec_ref, bi_ref, tower_ref):
    vec = nt(choose_ref[0], small_ref[...])
    vec_ref[...] = vec

    def lanes(values, row):
        lane = lax.broadcasted_iota(jnp.int32, (H, D), 0)
        chosen = jnp.where(lane == lane_ref[row : row + 1, :], 1.0, 0.0).astype(bf16)
        return nt(values.astype(bf16), chosen)

    bias = lanes(jnp.concatenate([vec[24:30], jnp.zeros((2, D), f32)], axis=0), 0)
    bias += lanes(jnp.concatenate([vec[30:36], jnp.zeros((2, D), f32)], axis=0), 1)
    bi_ref[...] = jnp.where(ints[1] == 0, bias, pltpu.roll(bias, HALF, 1))
    head = lane_ref[6:7, :] == 1
    tower = jnp.zeros((8, H), f32)
    for d in range(DOM):
        row = vec[36 + d : 37 + d]
        rows = [jnp.where(head, 0.0, row), jnp.where(head, row, 0.0), jnp.zeros((6, D), f32)]
        tower += lanes(jnp.concatenate(rows, axis=0), 2 + d)
    tower_ref[...] = tower


def call_unpack(ints, small, lanes):
    choose = np.zeros((2, 40, 128), np.float32)
    for r in range(2):
        for row, column in enumerate(PICKED[r]):
            choose[r, row, column] = 1.0
    shapes = [(40, D), (8, H), (8, DOM * TW)]
    return pl.pallas_call(
        unpack_kernel,
        grid_spec=pltpu.PrefetchScalarGridSpec(
            num_scalar_prefetch=1,
            grid=(1,),
            in_specs=[
                pl.BlockSpec((D, 128), lambda i, ints: (0, PACK // 128 - 1)),
                pl.BlockSpec((1, 40, 128), lambda i, ints: (ints[0], 0, 0)),
                fixed(lanes.shape),
            ],
            out_specs=tuple(fixed(shape) for shape in shapes),
        ),
        out_shape=tuple(jax.ShapeDtypeStruct(shape, f32) for shape in shapes),
        compiler_params=params(),
        name="unpack",
    )(ints, small, jnp.asarray(choose, bf16), lanes)


def choose_kernel(own_ids, other_ids, in_own, out_own, in_other, out_other, *refs):
    own_refs, other_refs, all_ref = refs[:2], refs[2:4], refs[4]
    step = pl.program_id(0)
    for part in range(2):

        @pl.when(step // 3 == part)
        def _(part=part):
            own_refs[part][0], own_refs[part][1] = in_own[...], out_own[...]
            other_refs[part][0], other_refs[part][1] = in_other[...], out_other[...]

    all_ref[0], all_ref[1] = in_other[...], out_other[...]


def call_choose(own_ids, other_ids, w_in, w_out_t):
    tail = w_in.shape[1:]
    block = (1,) + tail

    def shape(count):
        return jax.ShapeDtypeStruct((2, count) + tail, bf16)

    own = pl.BlockSpec(block, lambda i, a, b: (a[i], 0, 0))
    other = pl.BlockSpec(block, lambda i, a, b: (b[i], 0, 0))
    low = pl.BlockSpec((2,) + block, lambda i, a, b: (0, jnp.minimum(i, 2), 0, 0))
    high = pl.BlockSpec((2,) + block, lambda i, a, b: (0, jnp.maximum(i - 3, 0), 0, 0))
    every = pl.BlockSpec((2,) + block, lambda i, a, b: (0, i, 0, 0))
    return pl.pallas_call(
        choose_kernel,
        grid_spec=pltpu.PrefetchScalarGridSpec(
            num_scalar_prefetch=2,
            grid=(LOCAL,),
            in_specs=[own, own, other, other],
            out_specs=(low, high, low, high, every),
        ),
        out_shape=(shape(3), shape(3), shape(3), shape(3), shape(6)),
        compiler_params=params(),
        cost_estimate=pl.CostEstimate(flops=0, bytes_accessed=3_000_000, transcendentals=0),
        name="choose",
    )(own_ids, other_ids, w_in, w_out_t, w_in, w_out_t)


def proj_spec(e_in):
    return pl.BlockSpec((D, e_in), lambda *_: (0, 0))


GATES_SPEC = pl.BlockSpec((D, 128), lambda *_: (0, PACK // 128 - 1))


def call_prepare(ints, floats, table, embeds, embeds_in, small, vec):
    rows = embeds.shape[0]
    tiles = rows // TILE
    e_in = embeds.shape[1]

    def tile(width):
        return pl.BlockSpec((TILE, width), lambda i, *_: (i, 0))

    return pl.pallas_call(
        prepare_kernel,
        grid_spec=pltpu.PrefetchScalarGridSpec(
            num_scalar_prefetch=2,
            grid=(tiles,),
            in_specs=[fixed(table.shape)]
            + [pl.BlockSpec(memory_space=pl.ANY)] * 2
            + [proj_spec(e_in), GATES_SPEC, fixed(vec.shape)],
            scratch_shapes=[pltpu.VMEM(embeds.shape, bf16), pltpu.SemaphoreType.DMA((1,))],
            out_specs=(
                tile(e_in),
                tile(D),
                tile(D),
                tile(128),
                pl.BlockSpec((8, TILE), lambda i, *_: (0, i)),
            ),
        ),
        out_shape=(
            pltpu.HBM((rows, e_in), bf16),
            pltpu.HBM((rows, D), bf16),
            jax.ShapeDtypeStruct((rows, D), f32),
            jax.ShapeDtypeStruct((rows, 128), f32),
            jax.ShapeDtypeStruct((8, rows), f32),
        ),
        compiler_params=params(),
        cost_estimate=pl.CostEstimate(
            flops=2 * rows * e_in * (rows + D), bytes_accessed=12_000_000, transcendentals=rows * 8
        ),
        name="prepare",
    )(ints, floats, table, embeds, embeds_in, small, small, vec)


def half_spec(own, shape):
    rest = (0,) * (len(shape) - 1)
    return pl.BlockSpec(shape, lambda i, ints: ((ints[ROLE] if own else 1 - ints[ROLE]),) + rest)


def piece_spec(array, place):
    a, b, _, rows, width = array.shape
    return pl.BlockSpec((a, b, 1, rows, width), lambda i, *_: (0, 0, place(i), 0, 0))


MATRICES = [pltpu.VMEM((D, HALF), bf16)] * 4


def call_forward(experts, own, ints, x, weights, bi, vec, cols, mix, norms, gives=False):
    rows = x.shape[0]
    half = rows // 2
    arrays = sorted({e // 3 for e in experts})
    first = {a: min(k for k, e in enumerate(experts) if e // 3 == a) for a in arrays}
    number = {a: sum(1 for e in experts if e // 3 == a) for a in arrays}

    def place(a):
        return lambda i: jnp.clip(i - first[a], 0, number[a] - 1)

    weight_specs = [piece_spec(w, place(a)) for a in arrays for w in weights[a]]
    norm_specs = [
        pl.BlockSpec(
            (1, half, D),
            lambda i, ints, a=a: (place(a)(i), ints[ROLE] if own else 1 - ints[ROLE], 0),
        )
        for a in arrays
    ]
    kept = [norms[a] for a in arrays if a in norms]
    inputs = [x] + [w for a in arrays for w in weights[a]] + [bi, vec, cols, mix] + kept
    at = len(inputs) - len(kept)
    aliases = {at - 1: 0, at: 1}
    aliases.update({at + 1 + k: 2 + k for k in range(len(kept))})
    shared = sum(1 for e in experts if e < 2)
    out = pl.pallas_call(
        functools.partial(
            forward_kernel, experts, own, len(kept), len(weights[arrays[0]]), gives
        ),
        grid_spec=pltpu.PrefetchScalarGridSpec(
            num_scalar_prefetch=1,
            grid=(len(experts),),
            in_specs=[half_spec(own, (half, D))]
            + weight_specs
            + [fixed(bi.shape), fixed(vec.shape), half_spec(own, (half, 128)), half_spec(own, (half, D))]
            + [pl.BlockSpec(memory_space=pl.ANY)] * len(kept),
            out_specs=(half_spec(own, (half, 128)), half_spec(own, (half, D)), *norm_specs)
            + ((fixed((half, D)),) if gives else ()),
            scratch_shapes=MATRICES,
        ),
        out_shape=(
            jax.ShapeDtypeStruct((rows, 128), f32),
            jax.ShapeDtypeStruct((rows, D), f32),
            *[jax.ShapeDtypeStruct((3, rows, D), bf16)] * len(arrays),
        )
        + ((jax.ShapeDtypeStruct((half, D), bf16),) if gives else ()),
        input_output_aliases=aliases,
        compiler_params=params(),
        cost_estimate=pl.CostEstimate(
            flops=4 * (shared + 1) * half * D * H, bytes_accessed=12_000_000, transcendentals=0
        ),
        name="experts_forward",
    )(ints, *inputs)
    found = out[0], out[1], {**norms, **dict(zip(arrays, out[2:]))}
    return found + (out[-1],) if gives else found


def call_backward(experts, halves, ints, x, gbs, norms, weights, bi, vec, cols, back, sums=None):
    rows, count = x.shape[0], len(experts)
    part = rows // 2 * len(halves)
    array, low = experts[0] // 3, experts[0] % 3
    split = any(e // 3 != array for e in experts)

    def span(width):
        if len(halves) == 2:
            return fixed((rows, width))
        return half_spec(halves[0] == "own", (part, width))

    def norm_index(i, ints):
        if len(halves) == 2:
            return (low + i, 0, 0)
        return (low + i, ints[ROLE] if halves[0] == "own" else 1 - ints[ROLE], 0)

    assert not split
    pairs = pl.BlockSpec((1, 2, D, HALF), lambda i, *_: (i, 0, 0, 0))
    vec_spec = pl.BlockSpec((1, 8, D), lambda i, *_: (i, 0, 0))
    bi_spec = pl.BlockSpec((1, 8, H), lambda i, *_: (i, 0, 0))
    mode, back_array = back if back is not None else ("fresh", jnp.zeros((8, 128), f32))
    inputs = [x, *gbs, norms[array], *weights[array], bi, vec, cols, back_array]
    in_specs = (
        [span(D)]
        + [fixed(g.shape) for g in gbs]
        + [pl.BlockSpec((1, part, D), norm_index)]
        + [piece_spec(w, lambda i: low + i) for w in weights[array]]
        + [fixed(bi.shape), fixed(vec.shape), span(128)]
        + [span(D) if mode == "add" else pl.BlockSpec(memory_space=pl.ANY)]
    )
    aliases = {len(inputs) - 1: 0}
    if back is not None:
        aliases[len(inputs)] = 1
    if sums is not None:
        inputs += list(sums)
        in_specs += [vec_spec, bi_spec, pairs, pairs]
    return pl.pallas_call(
        functools.partial(
            backward_kernel, experts, halves, mode == "add", sums is not None, len(weights[array])
        ),
        grid_spec=pltpu.PrefetchScalarGridSpec(
            num_scalar_prefetch=1,
            grid=(count,),
            in_specs=in_specs,
            out_specs=(span(128), span(D), pairs, pairs, vec_spec, bi_spec),
            scratch_shapes=[pltpu.VMEM((D, HALF), f32)] * 4 + MATRICES,
        ),
        out_shape=(
            jax.ShapeDtypeStruct((rows, 128), f32),
            jax.ShapeDtypeStruct((rows, D), f32),
            jax.ShapeDtypeStruct((count, 2, D, HALF), bf16),
            jax.ShapeDtypeStruct((count, 2, D, HALF), bf16),
            jax.ShapeDtypeStruct((count, 8, D), f32),
            jax.ShapeDtypeStruct((count, 8, H), f32),
        ),
        input_output_aliases=aliases,
        compiler_params=params(),
        cost_estimate=pl.CostEstimate(
            flops=10 * count * (rows // 2) * D * H, bytes_accessed=20_000_000, transcendentals=0
        ),
        name="experts_backward",
    )(ints, *inputs)


def call_tower(ints, mix, other, cols, small, tower_vec):
    rows = other.shape[0]
    tiles = 2
    size = rows // tiles

    def kept(width):
        return pl.BlockSpec((size, width), lambda i, ints: (ints[ROLE] * tiles + i, 0))

    def tile(width):
        return pl.BlockSpec((size, width), lambda i, *_: (i, 0))

    return pl.pallas_call(
        tower_kernel,
        grid_spec=pltpu.PrefetchScalarGridSpec(
            num_scalar_prefetch=1,
            grid=(tiles,),
            in_specs=[kept(D), tile(D), kept(128), fixed(small.shape), fixed(tower_vec.shape)],
            out_specs=(
                pl.BlockSpec((8, size), lambda i, *_: (0, i)),
                tile(D),
                tile(D),
                fixed((D, DOM * TW)),
                fixed((8, DOM * TW)),
                fixed((8, 128)),
            ),
        ),
        out_shape=(
            jax.ShapeDtypeStruct((8, rows), f32),
            pltpu.HBM((rows, D), f32),
            jax.ShapeDtypeStruct((rows, D), bf16),
            jax.ShapeDtypeStruct((D, DOM * TW), f32),
            jax.ShapeDtypeStruct((8, DOM * TW), f32),
            jax.ShapeDtypeStruct((8, 128), f32),
        ),
        compiler_params=params(),
        cost_estimate=pl.CostEstimate(
            flops=6 * rows * D * DOM * TW, bytes_accessed=10_000_000, transcendentals=rows * DOM * TW
        ),
        name="towers",
    )(ints, mix, other, cols, small, tower_vec)


def per_device(
    box,
    embeds,
    domain,
    frozen,
    labels,
    proj_w,
    proj_b,
    w_in,
    in_bias,
    w_out,
    out_bias,
    ln_gain,
    ln_shift,
    gate_top,
    gate_shared,
    gate_domain,
    tower_w,
    tower_b,
    tower_out,
    tower_out_b,
):
    core = lax.axis_index("tensor")
    role = box.role(lax.axis_index("dp"))
    at_home = core == role
    places = box.count
    rows = embeds.shape[0]
    half_rows = rows // 2
    width = proj_w.shape[1]
    e_in = proj_w.shape[0]
    nz, ny, nx = box.dims[1:]
    sets = jnp.array(SETS, jnp.int32)
    set_own, set_other = sets[role], sets[1 - role]

    def half(values, which, axis=0):
        return lax.dynamic_slice_in_dim(values, which * half_rows, half_rows, axis)

    w_out_t = jnp.swapaxes(w_out, 1, 2)
    first, second, first_other, second_other, others = call_choose(set_own, set_other, w_in, w_out_t)

    def wide(values):
        return jnp.pad(values, ((0, 0), (0, 5 * width - values.shape[1])))

    arrays = (
        proj_w.T,
        tower_w,
        jnp.concatenate([jnp.swapaxes(g, 1, 2) for g in (gate_top, gate_shared, gate_domain)], axis=1),
        jnp.concatenate(
            [
                jnp.concatenate([out_bias, ln_gain, ln_shift, in_bias], axis=1),
                wide(jnp.concatenate([tower_b, tower_out], axis=1)),
                wide(proj_b[None]),
            ]
        ),
    )

    flips = box.send(others, flip=1)
    first_z = box.line(first, first_other)
    pack = call_pack(*step(arrays, first)[0])
    pack = in_order(role, pack, box.send(pack, flip=1), 0)
    pack = jnp.concatenate([pack] + box.pieces(pack, "z"))
    flips, first, first_z, second, second_other = step(flips, first, first_z, second, second_other)

    def along_z(shard, flip, found):
        found = box.in_line(shard, flip, found, role, 2)
        return jnp.stack([b[0] for b in found]), jnp.stack([b[1] for b in found])

    first_i, first_o = along_z(first, flips[:, :3], first_z)
    first_iy, first_ox = box.pieces(first_i, "y"), box.pieces(first_o, "x")
    second_z = box.line(second, second_other)
    pack = jnp.concatenate([pack] + box.pieces(pack, "y"))
    pack = jnp.concatenate([pack] + box.pieces(pack, "x")).reshape(places, 1, width, PACK)
    domain, labels = step((domain, labels), first)[0]
    event_rows = jnp.concatenate(
        [domain.astype(f32).T, labels.astype(f32)[None], jnp.zeros((6, rows), f32)]
    )
    event_rows = jnp.where(at_home, event_rows, box.to_partner(event_rows, True))
    ids = event_rows[0]
    onehot = (ids[None, :] == jnp.arange(DOM, dtype=f32)[:, None]).astype(f32)
    rank = jnp.cumsum(onehot, axis=1)
    counts = rank[:, -1]
    ends = jnp.cumsum(counts)
    starts = ends - counts
    position = jnp.sum(onehot * (rank + starts[:, None]), axis=0) - 1.0
    embeds_in = box.to_partner(step(embeds, second_z[0])[0], True)
    first_i, first_o, first_iy, first_ox, second, second_z, flips, starts, ends, position = step(
        first_i, first_o, first_iy, first_ox, second, second_z, flips, starts, ends, position
    )

    small = in_order(core, pack, swap_cores(pack), 1).reshape(D, PACK)
    first_i = jnp.stack([first_i] + first_iy)
    first_o = jnp.stack([first_o] + first_ox)
    first_ix, first_oy = box.pieces(first_i, "x"), box.pieces(first_o, "y")
    second, flips, second_z, _ = step(second, flips, second_z, (first_i, first_o))
    second_i, second_o = along_z(second, flips[:, 3:], second_z)
    second_iy, second_ox = box.pieces(second_i, "y"), box.pieces(second_o, "x")

    at = lax.broadcasted_iota(jnp.int32, (8, D), 1)
    row = lax.broadcasted_iota(jnp.int32, (8, D), 0)
    unit, narrow = at % width, width // 2
    device = 2 * box.ahead(at // (2 * width)) + (at // width) % 2
    hidden = device * (2 * width) + jnp.where(row == 1, width, 0) + unit
    lanes = (row - 2) * TW + device * narrow + unit % narrow
    lanes = jnp.where(row < 2, hidden, jnp.where(row < 2 + DOM, lanes, unit // narrow))
    vec, bi, tower_vec = call_unpack(jnp.stack([role, core]), small, lanes)

    table = jnp.concatenate([position[None], event_rows[1:]])
    start_i, end_i = starts.astype(jnp.int32), ends.astype(jnp.int32)
    empty = end_i == start_i
    low = jnp.where(empty, 0, start_i // TILE)
    high = jnp.where(empty, 0, (end_i + TILE - 1) // TILE)
    domains = jnp.arange(DOM, dtype=jnp.int32)
    ints = jnp.concatenate(
        [
            jnp.where(role == 0, low[::-1], low),
            jnp.where(role == 0, high[::-1], high),
            role[None],
            jnp.where(role == 0, DOM - 1 - domains, domains),
            start_i,
            end_i,
            core[None],
            jnp.zeros((2,), jnp.int32),
        ]
    )
    loss_weight = 1.0 - (1.0 - FROZEN_SHARE) * frozen.astype(f32)
    floats = jnp.concatenate([loss_weight, tower_out_b.astype(f32)])
    events, x, mix, cols, probs = call_prepare(ints, floats, table, embeds, embeds_in, small, vec)
    (
        first_i, first_o, first_ix, first_oy, second_i, second_o, second_iy, second_ox,
        ints, events, x, mix, cols, probs, vec, bi, small, tower_vec, lanes,
    ) = step(
        first_i, first_o, first_ix, first_oy, second_i, second_o, second_iy, second_ox,
        ints, events, x, mix, cols, probs, vec, bi, small, tower_vec, lanes,
    )

    def pieces(i, ix, o, oy):
        own = [i] + ix + [o] + oy
        return own + [swap_cores(w) for w in own]

    second_i = jnp.stack([second_i] + second_iy)
    second_o = jnp.stack([second_o] + second_ox)
    second_ix, second_oy = box.pieces(second_i, "x"), box.pieces(second_o, "y")
    weights = {0: pieces(first_i, first_ix, first_o, first_oy)}
    cols, mix, norms = call_forward((0, 1, 2), False, ints, x, weights, bi, vec, cols, mix, {})
    second_ix, second_oy, cols, mix = step(second_ix, second_oy, cols, mix)
    weights[1] = pieces(second_i, second_ix, second_o, second_oy)
    cols, mix, norms, give_mix = call_forward(
        (3, 4), False, ints, x, weights, bi, vec, cols, mix, norms, True
    )
    give_mix, mix = step(give_mix, mix)
    other_mix = box.send(give_mix, flip=1)
    cols, mix, norms = call_forward(
        tuple(range(LOCAL)), True, ints, x, weights, bi, vec, cols, mix, norms
    )
    row_out, grad_block, grad_low, d_tower, d_tower_vec, d_logit_bias = call_tower(
        ints, mix, other_mix, cols, small, tower_vec
    )

    box_shape = (nx, ny, nz, 2, 2 * width, HALF)

    def both_cores(keeps, gives):
        def one(which):
            added = total(keeps[0][:, which], [a[:, which] for a in keeps[1:] + gives])
            return added.astype(bf16).reshape((-1,) + box_shape)

        return one(0), one(1)

    class Scatter:
        def __init__(self, *parts):
            i, o = [jnp.concatenate(p) for p in zip(*parts)]
            i, o = [i[:, k] for k in range(nx)], [o[:, :, k] for k in range(ny)]
            self.state = (i[0], o[0], box.hand_out(i, "x"), box.hand_out(o, "y"))

        def second(self):
            i, o, i_in, o_in = self.state
            i, o = total(i, i_in).astype(bf16), total(o, o_in).astype(bf16)
            i, o = [i[:, k] for k in range(ny)], [o[:, k] for k in range(nx)]
            self.state = (i[0], o[0], box.hand_out(i, "y"), box.hand_out(o, "x"))

        def third(self):
            i, o, i_in, o_in = self.state
            both = jnp.stack([total(i, i_in).astype(bf16), total(o, o_in).astype(bf16)])
            both = [both[:, :, k] for k in range(nz)]
            self.state = (both[0], box.hand_out(both, "z"))

        def fourth(self):
            both = total(*self.state)
            mine = lax.dynamic_index_in_dim(both, role, 2, keepdims=False)
            other = lax.dynamic_index_in_dim(both, 1 - role, 2, keepdims=False).astype(bf16)
            self.state = (mine, box.send(other, flip=1))

    def sync(scatters, *values):
        states, values = step([c.state for c in scatters], values)
        for c, state in zip(scatters, states):
            c.state = state
        return values

    common = (ints, x)
    shared = (norms, weights, bi, vec)
    grad_in = box.send(grad_low, flip=1)
    cols, back, keep_a, give_a, *sums = call_backward(
        (0, 1), ("own",), *common, [grad_low], *shared, cols, None
    )
    logit_in = swap_cores(d_logit_bias)
    grad_in, cols, back, keep_a, give_a, sums, logit_in = step(
        grad_in, cols, back, keep_a, give_a, sums, logit_in
    )
    d_logit_bias = d_logit_bias + logit_in
    cols, back, keep_b, give_b, *sums_0 = call_backward(
        (0, 1), ("other",), *common, [grad_in], *shared, cols, ("fresh", back), sums + [keep_a, give_a]
    )
    logit_in = box.pieces(d_logit_bias, "y")
    cols, back, keep_b, give_b, logit_in = step(cols, back, keep_b, give_b, logit_in)
    d_logit_bias = box.same_sum(d_logit_bias, logit_in, "y")
    give_b = swap_cores(give_b)
    grads = [grad_low, grad_in]
    cols, back, keep_c, give_c, *sums_1 = call_backward(
        (2,), ("own", "other"), *common, grads, *shared, cols, ("add", back)
    )
    logit_in = box.pieces(d_logit_bias, "x")
    cols, back, keep_b, give_b, keep_c, give_c, row_out, logit_in = step(
        cols, back, keep_b, give_b, keep_c, give_c, row_out, logit_in
    )
    d_logit_bias = box.same_sum(d_logit_bias, logit_in, "x")
    give_c = swap_cores(give_c)
    ab = both_cores([keep_b], [give_b])
    give_c, keep_c, ab, cols = step(give_c, keep_c, ab, cols)
    c0 = Scatter(ab, both_cores([keep_c], [give_c]))
    cols, back, keep_d, give_d, *sums_2 = call_backward(
        (3, 4, 5), ("own", "other"), *common, grads, *shared, cols, ("add", back)
    )
    rows_in = box.to_partner(row_out, False)
    logit_in = box.pieces(d_logit_bias, "flip")
    cols, back, keep_d, give_d, rows_in, logit_in = sync(
        [c0], cols, back, keep_d, give_d, rows_in, logit_in
    )
    d_logit_bias = box.same_sum(d_logit_bias, logit_in, "flip")
    c0.second()
    give_d = swap_cores(give_d)
    g_sum, g_low, d_gate = call_gate(ints, back, cols, probs, x, small)
    cd = both_cores([keep_d], [give_d])
    logit_in = box.pieces(d_logit_bias, "z")
    g_sum, g_low, d_gate, cd, logit_in = sync([c0], g_sum, g_low, d_gate, cd, logit_in)
    d_logit_bias = box.same_sum(d_logit_bias, logit_in, "z")
    c1 = Scatter(cd)
    back_in = box.to_partner(g_low, False)
    (back_in,) = sync([c0, c1], back_in)
    c0.third()
    c1.second()
    back_in, _ = step(back_in, c1.state[:2])
    grad_events, d_small = call_finish(
        ints, grad_block, grad_in, g_sum, back_in, events, small, d_tower, d_gate, lanes, d_tower_vec,
        [sums_0, sums_1, sums_2],
    )
    grad_events, d_small = sync([c0, c1], grad_events, d_small)
    c1.third()
    c0.fourth()
    d_small, _ = step(d_small, c1.state[0])
    d_small = d_small.reshape(places, 2, width, PACK)
    d_other = swap_cores(lax.dynamic_index_in_dim(d_small, 1 - core, 1, keepdims=False))
    d_mine = total(lax.dynamic_index_in_dim(d_small, core, 1, keepdims=False), [d_other])
    d_mine = d_mine.astype(bf16).reshape(nx * ny, nz, 2, width, PACK)
    d_parts = [d_mine[k] for k in range(nx * ny)]
    d_in = box.hand_out_plane(d_parts)
    order = position[None, :] == jnp.arange(rows, dtype=f32)[:, None]
    grad_embeds = lax.dot_general(
        order.astype(bf16), grad_events, (((0,), (0,)), ((), ())), preferred_element_type=f32
    ).astype(bf16)
    predicted = in_order(role, row_out, rows_in, 1)
    predictions = jnp.sum(jnp.where(order, predicted[0][:, None], 0.0), axis=0)
    predictions = jnp.broadcast_to(predictions[None], (8, rows))
    d_mine, d_in, grad_embeds, predictions = sync(
        [c0, c1], d_parts[0], d_in, grad_embeds, predictions
    )
    c1.fourth()
    d_mine, _ = step(d_mine, c1.state[0])
    d_mine = total(d_mine, d_in).astype(bf16)
    same = [lax.dynamic_index_in_dim(d_mine[k], role, 0, keepdims=False) for k in range(nz)]
    flip = [lax.dynamic_index_in_dim(d_mine[k], 1 - role, 0, keepdims=False) for k in range(nz)]
    d_in = box.hand_out(same, "z") + box.hand_out_flip(flip)
    grad_embeds = jnp.where(at_home, grad_embeds, swap_cores(grad_embeds))
    predictions = jnp.where(at_home, predictions, swap_cores(predictions))[0]
    d_in, grad_embeds, predictions = sync([c1], d_in, grad_embeds, predictions)
    (
        proj_grad, tower_grad, top, shared_gate, domain_gate, proj_b_grad, in_bias_grad, tower_b_grad,
        tower_out_grad, *vectors,
    ) = call_small([same[0]] + d_in)
    grad_w_in, grad_w_out = call_place(
        ints, [c0.state[0], c1.state[0]], [c0.state[1], c1.state[1]]
    )
    return (
        predictions,
        grad_embeds,
        proj_grad.T,
        proj_b_grad[0],
        grad_w_in,
        in_bias_grad,
        jnp.swapaxes(grad_w_out, 1, 2),
        *vectors,
        jnp.swapaxes(top, 1, 2),
        jnp.swapaxes(shared_gate, 1, 2),
        jnp.swapaxes(domain_gate, 1, 2),
        tower_grad,
        tower_b_grad,
        tower_out_grad,
        d_logit_bias[0, :DOM],
    )


def solution(mesh):
    both = ("dp", "tensor")
    in_specs = (
        P("dp", None),
        P("dp", None),
        P(),
        P("dp"),
        P(None, both),
        P(both),
        P(None, "dp", "tensor"),
        P(None, both),
        P(None, "tensor", "dp"),
        P(None, both),
        P(None, both),
        P(None, both),
        P(None, both, None),
        P(None, both, None),
        P(None, both, None),
        P(None, both, None),
        P(None, both),
        P(None, both),
        P(),
    )
    out_specs = (
        P("dp"),
        P("dp", None),
        P(None, both),
        P(both),
        P(None, "dp", "tensor"),
        P(None, both),
        P(None, "tensor", "dp"),
        P(None, both),
        P(None, both),
        P(None, both),
        P(None, both, None),
        P(None, both, None),
        P(None, both, None),
        P(None, both, None),
        P(None, both),
        P(None, both),
        P(),
    )
    return jax.shard_map(
        functools.partial(per_device, Box(mesh.shape["dp"])),
        mesh=mesh,
        in_specs=in_specs,
        out_specs=out_specs,
        check_vma=False,
    )
```

```python
import functools
import math

import jax
import jax.numpy as jnp
import numpy as np
from jax import lax
from jax.experimental import pallas as pl
from jax.experimental.pallas import tpu as pltpu
from jax.sharding import PartitionSpec as P

D = 512
H = 1024
HALF = H // 2
TW = 256
S = 4
DOM = 4
K = 2
EPS = 1e-05
FROZEN_SHARE = 0.25
TILE = 256
LOCAL = 6
CHUNKS = ((0, 1, 2), (3, 4, 5))
VMEM_LIMIT = 48 * 1024 * 1024
PACK = 1792
SETS = (
    tuple(range(2)) + tuple(S + K * d for d in reversed(range(DOM))),
    tuple(range(2, 4)) + tuple(S + K * d + 1 for d in range(DOM)),
)
COEF, SCALE, DCOEF, DOMAIN, LABEL, WEIGHT, BIAS = 0, 6, 12, 18, 19, 20, 21
LOW, HIGH, ROLE, DOMAIN_OF, START, END, CORE = 0, 4, 8, 9, 13, 17, 21

bf16 = jnp.bfloat16
f32 = jnp.float32


def dims_of(count):
    if count % 4 == 0:
        rest = count // 4
        root = math.isqrt(rest)
        if root * root == rest:
            return (4, root, root)
    return (count, 1, 1)


class Box:
    def __init__(self, count):
        first, second, third = dims_of(count)
        self.count = count
        self.dims = (2, first // 2, second, third)
        self.strides = (second * third, 2 * second * third, third, 1)

    def role(self, chip):
        return (chip // self.strides[0]) % 2

    def partner(self, chip):
        return chip + (1 - 2 * self.role(chip)) * self.strides[0]

    def send(self, values, flip=0, z=0, y=0, x=0):
        pairs = []
        for chip in range(self.count):
            to = chip
            for step, size, stride in zip((flip, z, y, x), self.dims, self.strides):
                place = (chip // stride) % size
                to += ((place + step) % size - place) * stride
            pairs.append((chip, to))
        return lax.ppermute(values, "dp", pairs)

    def to_partner(self, values, home):
        pairs = []
        for chip in range(self.count):
            for core in range(2):
                if (core == self.role(chip)) == home:
                    pairs.append((2 * chip + core, 2 * self.partner(chip) + core))
        return lax.ppermute(values, ("dp", "tensor"), pairs)

    def pieces(self, values, dim):
        size = self.dims[("flip", "z", "y", "x").index(dim)]
        return [self.send(values, **{dim: -k}) for k in range(1, size)]

    def hand_out(self, parts, dim):
        return [self.send(part, **{dim: k}) for k, part in enumerate(parts) if k]

    def line(self, same, other):
        steps = range(1, self.dims[1])
        return [self.send(same, z=-z) for z in steps], [self.send(other, flip=1, z=-z) for z in steps]

    def in_line(self, own, flip, found, role, axis):
        same, other = found
        return [in_order(role, s, o, axis) for s, o in zip([own] + same, [flip] + other)]

    def hand_out_flip(self, parts):
        return [self.send(part, flip=1, z=k) for k, part in enumerate(parts)]

    def plane(self):
        _, _, ny, nx = self.dims
        return [(x, y) for x in range(nx) for y in range(ny)][1:]

    def gather_plane(self, values):
        return [values] + [self.send(values, y=-y, x=-x) for x, y in self.plane()]

    def hand_out_plane(self, parts):
        return [self.send(part, y=y, x=x) for part, (x, y) in zip(parts[1:], self.plane())]

    def same_sum(self, values, found, dim):
        number = ("flip", "z", "y", "x").index(dim)
        size, stride = self.dims[number], self.strides[number]
        found = jnp.stack([values] + found)
        if size > 2:
            mine = (lax.axis_index("dp") // stride) % size
            found = jnp.take(found, (jnp.arange(size) - mine) % size, axis=0)
        return functools.reduce(jnp.add, [found[k] for k in range(size)])

    def ahead(self, place):
        me = lax.axis_index("dp")
        chip, weight = 0, 1
        for dim, (size, stride) in enumerate(zip(self.dims, self.strides)):
            mine = (me // stride) % size if dim else 0
            chip = chip + ((mine + (place // weight) % size) % size) * stride
            weight *= size
        return chip


def swap_cores(values):
    return lax.ppermute(values, "tensor", [(0, 1), (1, 0)])


def in_order(which, own, other, axis):
    return jnp.where(
        which == 0,
        jnp.concatenate([own, other], axis),
        jnp.concatenate([other, own], axis),
    )


def step(*values):
    return lax.optimization_barrier(values)


def total(first, arrived):
    return functools.reduce(jnp.add, [a.astype(f32) for a in arrived], first.astype(f32))


def gelu_parts(v):
    inner = math.sqrt(2.0 / math.pi)
    square = v * v
    th = jnp.tanh(v * (inner + inner * 0.044715 * square))
    half = 0.5 * (1.0 + th)
    act = v * half
    slope = half + 0.5 * v * (1.0 - th * th) * (inner + 3.0 * inner * 0.044715 * square)
    return act, slope


def nt(a, b):
    return lax.dot_general(a, b, (((1,), (1,)), ((), ())), preferred_element_type=f32)


def tn(a, b):
    return lax.dot_general(a, b, (((0,), (0,)), ((), ())), preferred_element_type=f32)


def nn(a, b):
    return jnp.dot(a, b, preferred_element_type=f32)


def softmax_rows(v):
    e = jnp.exp(v - jnp.max(v, axis=0, keepdims=True))
    return e / jnp.sum(e, axis=0, keepdims=True)


def prepare_kernel(
    ints, floats, rows_ref, own_ref, in_ref, proj_ref, gates_ref, vec_ref, ev_ref, x_ref, mix_ref, cols_ref, prob_ref, embeds_ref, arrived
):
    tiles_of_half = pl.num_programs(0) // 2
    index = pl.program_id(0)
    role = ints[ROLE]
    count = rows_ref.shape[1]
    at_home = ints[CORE] == role

    @pl.when((index == 0) & at_home)
    def _():
        copy = pltpu.make_async_copy(own_ref, embeds_ref, arrived.at[0])
        copy.start()
        copy.wait()

    @pl.when((index == 0) & jnp.logical_not(at_home))
    def _():
        copy = pltpu.make_async_copy(in_ref, embeds_ref, arrived.at[0])
        copy.start()
        copy.wait()

    slot = index * TILE + lax.broadcasted_iota(jnp.int32, (TILE, count), 0)
    here = rows_ref[0:1, :].astype(jnp.int32) == slot
    order = jnp.where(here, 1.0, 0.0).astype(bf16)
    label = jnp.sum(jnp.where(here, rows_ref[1:2, :], 0.0), axis=1, keepdims=True)
    events = nn(order, embeds_ref[...]).astype(bf16)
    ev_ref[...] = events
    mixed = nt(events, proj_ref[...]) + vec_ref[3 * LOCAL : 3 * LOCAL + 1, :]
    low = mixed.astype(bf16)
    x_ref[...] = low
    mix_ref[...] = mixed * jnp.where(index // tiles_of_half == role, 1.0, 0.0)
    logits = jnp.transpose(nn(low, gates_ref[...]))
    place = index * TILE + lax.broadcasted_iota(jnp.int32, (1, TILE), 1)
    picks = [
        jnp.where((place >= ints[START + d]) & (place < ints[END + d]), 1.0, 0.0) for d in range(DOM)
    ]

    def pick(low_row, size):
        return softmax_rows(
            functools.reduce(
                jnp.add,
                [picks[d] * logits[low_row + d * size : low_row + (d + 1) * size] for d in range(DOM)],
            )
        )

    top, shared, domain = pick(0, 2), pick(2 * DOM, S), pick((2 + S) * DOM, K)
    prob_ref[...] = jnp.concatenate([top, shared, domain], axis=0)
    first = role == 0
    own_shared = top[0:1] * jnp.where(first, shared[:2], shared[2:])
    own_domain = top[1:2] * jnp.where(first, domain[0:1], domain[1:2])
    coef = [own_domain * jnp.where(first, picks[DOM - 1 - d], picks[d]) for d in range(DOM)]
    table = [
        own_shared,
        *coef,
        jnp.zeros((DOMAIN - SCALE, TILE), f32),
        sum(float(d) * picks[d] for d in range(DOM)),
        jnp.zeros((1, TILE), f32),
        sum(floats[d] * picks[d] for d in range(DOM)),
        sum(floats[DOM + d] * picks[d] for d in range(DOM)),
        jnp.zeros((128 - BIAS - 1, TILE), f32),
    ]
    cols_ref[...] = with_column(jnp.transpose(jnp.concatenate(table, axis=0)), LABEL, label)


def with_column(table, column, values):
    lane = lax.broadcasted_iota(jnp.int32, table.shape, 1)
    return jnp.where(lane == column, values, table)


def tiles_of(expert, ints, first, count):
    low = jnp.maximum(ints[LOW + expert - 2], first)
    high = jnp.minimum(ints[HIGH + expert - 2], first + count)
    return low - first, jnp.maximum(high, low) - first


def each_span(expert, ints, first, rows, work):
    if expert < 2:
        work(slice(0, rows))
    else:
        low, high = tiles_of(expert, ints, first, rows // TILE)

        def one(index, _):
            work(pl.ds(pl.multiple_of(index * TILE, TILE), TILE))
            return 0

        lax.fori_loop(low, high, one, 0)


def join(pieces, held):
    count = len(pieces) // 2
    for core in range(2):
        mine = pieces[core * count : core * count + count]
        by_x, by_y = split_pieces(mine)
        nx, ny = len(by_x), len(by_y)
        rows = by_x[0].shape[3]
        nz = by_x[0].shape[1]

        def at(x, y, z):
            return pl.ds(((x * ny + y) * nz + z) * rows, rows)

        for x in range(nx):
            for y in range(ny):
                for z in range(nz):
                    held[core][at(x, y, z), :] = by_x[x][y, z, 0]
                    held[2 + core][at(x, y, z), :] = by_y[y][x, z, 0]


def split_pieces(pieces):
    nx = pieces[-1].shape[0]
    return pieces[:nx], pieces[nx:]


def forward_kernel(experts, own, aliased, number, gives, ints, x_ref, *refs):
    arrays = sorted({e // 3 for e in experts})
    weights = {a: refs[number * k : number * (k + 1)] for k, a in enumerate(arrays)}
    refs = refs[number * len(arrays) :]
    refs, held = refs[:-4], refs[-4:]
    wi_a, wi_b, wo_a, wo_b = held
    bi_ref, vec_ref, cols_in, mix_in = refs[:4]
    cols_ref, mix_ref, *norm_refs = refs[4 + aliased :]
    if gives:
        *norm_refs, give_ref = norm_refs
    norm_refs = dict(zip(arrays, norm_refs))
    rows = x_ref.shape[0]
    half = ints[ROLE] if own else 1 - ints[ROLE]
    step = pl.program_id(0)

    @pl.when(step == 0)
    def _():
        cols_ref[...] = cols_in[...]
        mix_ref[...] = mix_in[...]

    def work(expert, span):
        x = x_ref[span, :]
        pre_a = nn(x, wi_a[...]) + bi_ref[expert : expert + 1, :HALF]
        act_a = gelu_parts(pre_a)[0].astype(bf16)
        pre_b = nn(x, wi_b[...]) + bi_ref[expert : expert + 1, HALF:]
        act_b = gelu_parts(pre_b)[0].astype(bf16)
        out = nt(act_a, wo_a[...]) + nt(act_b, wo_b[...]) + vec_ref[expert : expert + 1, :]
        centre = jnp.mean(out, axis=1, keepdims=True)
        centred = out - centre
        scale = lax.rsqrt(jnp.mean(centred * centred, axis=1, keepdims=True) + EPS)
        norm = centred * scale
        norm_refs[expert // 3][0, span, :] = norm.astype(bf16)
        cols = cols_ref[span, :]
        cols_ref[span, :] = with_column(cols, SCALE + expert, scale)
        gain = vec_ref[LOCAL + expert : LOCAL + expert + 1, :]
        shift = vec_ref[2 * LOCAL + expert : 2 * LOCAL + expert + 1, :]
        mix_ref[span, :] += cols[:, COEF + expert : COEF + expert + 1] * (norm * gain + shift)

    for place, expert in enumerate(experts):

        @pl.when(step == place)
        def _(expert=expert):
            join(weights[expert // 3], held)
            each_span(expert, ints, half * (rows // TILE), rows, functools.partial(work, expert))

    if gives:

        @pl.when(step == len(experts) - 1)
        def _():
            give_ref[...] = mix_ref[...].astype(bf16)


def backward_kernel(experts, halves, keeps_back, adds, number, ints, x_ref, *refs):
    gb_refs, refs = refs[: len(halves)], refs[len(halves) :]
    norm_ref, pieces, refs = refs[0], refs[1 : 1 + number], refs[1 + number :]
    bi_ref, vec_ref, cols_in = refs[:3]
    refs, held = refs[3:-4], refs[-4:]
    wi_a, wi_b, wo_a, wo_b = held
    join(pieces, held)
    back_in, refs = refs[0], refs[1:]
    if adds:
        dvec_in, dbi_in, keep_in, give_in = refs[:4]
        refs = refs[4:]
    cols_ref, back_ref, keep_ref, give_ref, dvec_ref, dbi_ref, in_a, in_b, out_a, out_b = refs
    rows = x_ref.shape[0]
    half_tiles = rows // TILE // len(halves)
    first = 0 if len(halves) == 2 else (ints[ROLE] if halves[0] == "own" else 1 - ints[ROLE]) * half_tiles
    step = pl.program_id(0)

    @pl.when(step == 0)
    def _():
        cols_ref[...] = cols_in[...]
        back_ref[...] = back_in[...] if keeps_back else jnp.zeros_like(back_ref)

    dvec_ref[...] = dvec_in[...] if adds else jnp.zeros_like(dvec_ref)
    dbi_ref[...] = dbi_in[...] if adds else jnp.zeros_like(dbi_ref)

    def work(expert, span):
        whole = isinstance(span, slice)

        def add(ref, target, which, values):
            if whole and adds:
                before = keep_in if target is keep_ref else give_in
                target[0, which] = (values + before[0, which].astype(f32)).astype(bf16)
            elif whole:
                target[0, which] = values.astype(bf16)
            else:
                ref[...] += values

        x = x_ref[span, :]
        norm = norm_ref[0, span, :].astype(f32)
        cols = cols_ref[span, :]
        if len(halves) == 1:
            grad_block = gb_refs[0][span, :].astype(f32)
        else:
            half = span.start // (half_tiles * TILE)
            inner = pl.ds(pl.multiple_of(span.start - half * (half_tiles * TILE), TILE), TILE)
            grad_block = jnp.where(
                half == ints[ROLE], gb_refs[0][inner, :].astype(f32), gb_refs[1][inner, :].astype(f32)
            )
        gain = vec_ref[LOCAL + expert : LOCAL + expert + 1, :]
        shift = vec_ref[2 * LOCAL + expert : 2 * LOCAL + expert + 1, :]
        scale = cols[:, SCALE + expert : SCALE + expert + 1]
        grad_exp = cols[:, COEF + expert : COEF + expert + 1] * grad_block
        scaled = grad_exp * norm
        dx = grad_exp * gain
        first_mean = jnp.mean(dx, axis=1, keepdims=True)
        second_mean = jnp.mean(dx * norm, axis=1, keepdims=True)
        grad_sum = scale * (dx - first_mean - norm * second_mean)
        grad_low = grad_sum.astype(bf16)
        pre_a = nn(x, wi_a[...]) + bi_ref[expert : expert + 1, :HALF]
        act_a, slope_a = gelu_parts(pre_a)
        low_a = (nn(grad_low, wo_a[...]) * slope_a).astype(bf16)
        pre_b = nn(x, wi_b[...]) + bi_ref[expert : expert + 1, HALF:]
        act_b, slope_b = gelu_parts(pre_b)
        low_b = (nn(grad_low, wo_b[...]) * slope_b).astype(bf16)
        add(out_a, keep_ref, 1, tn(grad_low, act_a.astype(bf16)))
        add(in_a, keep_ref, 0, tn(x, low_a))
        add(out_b, give_ref, 1, tn(grad_low, act_b.astype(bf16)))
        add(in_b, give_ref, 0, tn(x, low_b))
        back_ref[span, :] += nt(low_a, wi_a[...]) + nt(low_b, wi_b[...])
        dcoef = jnp.sum(grad_block * (norm * gain + shift), axis=1, keepdims=True)
        if expert < 2:
            cols_ref[span, :] = with_column(cols, DCOEF + expert, dcoef)
        else:
            mine = cols[:, DOMAIN : DOMAIN + 1] == ints[DOMAIN_OF + expert - 2].astype(f32)
            column = cols[:, DCOEF + 2 : DCOEF + 3] + jnp.where(mine, dcoef, 0.0)
            cols_ref[span, :] = with_column(cols, DCOEF + 2, column)
        dvec_ref[0, 0:1, :] += jnp.sum(grad_sum, axis=0, keepdims=True)
        dvec_ref[0, 1:2, :] += jnp.sum(scaled, axis=0, keepdims=True)
        dvec_ref[0, 2:3, :] += jnp.sum(grad_exp, axis=0, keepdims=True)
        dbi_ref[0, 0:1, :HALF] += jnp.sum(low_a.astype(f32), axis=0, keepdims=True)
        dbi_ref[0, 0:1, HALF:] += jnp.sum(low_b.astype(f32), axis=0, keepdims=True)

    for place, expert in enumerate(experts):

        @pl.when(step == place)
        def _(expert=expert):
            if expert >= 2:
                for ref in (in_a, in_b, out_a, out_b):
                    ref[...] = jnp.zeros_like(ref)
            each_span(expert, ints, first, rows, functools.partial(work, expert))
            if expert >= 2:
                keep_ref[0, 0] = in_a[...].astype(bf16)
                keep_ref[0, 1] = out_a[...].astype(bf16)
                give_ref[0, 0] = in_b[...].astype(bf16)
                give_ref[0, 1] = out_b[...].astype(bf16)


def tower_kernel(
    ints, mix_ref, other_ref, cols_ref, tw_ref, tv_ref, out_ref, gb_ref, low_ref, dw_ref, dv_ref, db_ref
):
    @pl.when(pl.program_id(0) == 0)
    def _():
        db_ref[...] = jnp.zeros_like(db_ref)
        dw_ref[...] = jnp.zeros_like(dw_ref)
        dv_ref[...] = jnp.zeros_like(dv_ref)

    bias = tv_ref[0:1, :]
    head = tv_ref[1:2, :]
    cols = cols_ref[...]
    block = (mix_ref[...] + other_ref[...].astype(f32)).astype(bf16)
    tower = slice(PACK - 128 - DOM * TW, PACK - 128)
    pre = nn(block, tw_ref[:, tower]) + bias
    act, slope = gelu_parts(pre)
    group = lax.broadcasted_iota(jnp.int32, pre.shape, 1) // TW
    mine = group == cols[:, DOMAIN : DOMAIN + 1].astype(jnp.int32)
    act = jnp.where(mine, act, 0.0)
    logit = jnp.sum(act * head, axis=1, keepdims=True) + cols[:, BIAS : BIAS + 1]
    small = jnp.exp(-jnp.abs(logit))
    predicted = jnp.where(logit >= 0.0, 1.0, small) / (1.0 + small)
    grad_logit = cols[:, WEIGHT : WEIGHT + 1] * (predicted - cols[:, LABEL : LABEL + 1])
    lane = lax.broadcasted_iota(jnp.int32, cols.shape, 1)
    out_ref[...] = jnp.transpose(jnp.where(lane == 0, predicted, jnp.where(lane == 1, grad_logit, 0.0)))[:8]
    by_domain = jnp.where(lane.astype(f32) == cols[:, DOMAIN : DOMAIN + 1], grad_logit, 0.0)
    db_ref[0:1, :] += jnp.sum(by_domain, axis=0, keepdims=True)
    dv_ref[1:2, :] += jnp.sum(grad_logit * act, axis=0, keepdims=True)
    grad_pre = jnp.where(mine, grad_logit * head * slope, 0.0)
    dv_ref[0:1, :] += jnp.sum(grad_pre, axis=0, keepdims=True)
    grad_low = grad_pre.astype(bf16)
    grad_block = nt(grad_low, tw_ref[:, tower])
    gb_ref[...] = grad_block
    low_ref[...] = grad_block.astype(bf16)
    dw_ref[...] += tn(block, grad_low)


def softmax_back(probability, grad_probs):
    return probability * (grad_probs - jnp.sum(probability * grad_probs, axis=0, keepdims=True))


def gate_kernel(ints, back_ref, cols_ref, prob_ref, x_ref, gates_ref, sum_ref, low_ref, gate_ref):
    index = pl.program_id(0)
    first = ints[ROLE] == 0

    @pl.when(index == 0)
    def _():
        gate_ref[...] = jnp.zeros_like(gate_ref)

    mine = jnp.transpose(cols_ref[...])[DCOEF : DCOEF + 3]
    none = jnp.zeros_like(mine)
    one, two = jnp.where(first, mine, none), jnp.where(first, none, mine)
    d_shared = jnp.concatenate([one[0:2], two[0:2]], axis=0)
    d_domain = jnp.concatenate([one[2:3], two[2:3]], axis=0)
    top, shared, domain = prob_ref[0:2, :], prob_ref[2:6, :], prob_ref[6:8, :]
    d_top = jnp.concatenate(
        [
            jnp.sum(d_shared * shared, axis=0, keepdims=True),
            jnp.sum(d_domain * domain, axis=0, keepdims=True),
        ],
        axis=0,
    )
    grads = (
        softmax_back(top, d_top),
        softmax_back(shared, d_shared * top[0:1]),
        softmax_back(domain, d_domain * top[1:2]),
    )
    rows = top.shape[1]
    place = index * rows + lax.broadcasted_iota(jnp.int32, (1, rows), 1)
    picks = [
        jnp.where((place >= ints[START + d]) & (place < ints[END + d]), 1.0, 0.0) for d in range(DOM)
    ]
    spread = jnp.concatenate(
        [picks[d] * grad for grad in grads for d in range(DOM)] + [jnp.zeros((96, rows), f32)],
        axis=0,
    )
    spread = jnp.transpose(spread).astype(bf16)
    gate_ref[...] += tn(x_ref[...], spread)
    added = back_ref[...] + nt(spread, gates_ref[...])
    sum_ref[...] = added
    low_ref[...] = added.astype(bf16)


def call_gate(ints, back, cols, probs, x, small):
    rows = x.shape[0]
    half = rows // 2

    def tile(width):
        return pl.BlockSpec((half, width), lambda i, *_: (i, 0))

    return pl.pallas_call(
        gate_kernel,
        grid_spec=pltpu.PrefetchScalarGridSpec(
            num_scalar_prefetch=1,
            grid=(2,),
            in_specs=[
                tile(D),
                tile(128),
                pl.BlockSpec((8, half), lambda i, *_: (0, i)),
                tile(D),
                GATES_SPEC,
            ],
            out_specs=(tile(D), tile(D), fixed((D, 128))),
        ),
        out_shape=(
            jax.ShapeDtypeStruct((rows, D), f32),
            jax.ShapeDtypeStruct((rows, D), bf16),
            jax.ShapeDtypeStruct((D, 128), f32),
        ),
        compiler_params=params(),
        cost_estimate=cost(5),
        name="gates",
    )(ints, back, cols, probs, x, small)


def hidden_lines(ints, lane_ref, tv_ref, line_refs):
    first_set, first_core = ints[ROLE] == 0, ints[CORE] == 0
    mine = [r[k, 0:1, :] for r in line_refs for k in range(r.shape[0])]
    mine = jnp.concatenate(mine, axis=0)
    mine = jnp.where(first_core, mine, pltpu.roll(mine, HALF, 1))
    mine = jnp.where(first_set, mine, 0.0), jnp.where(first_set, 0.0, mine)
    found = {j: mine[r][i : i + 1] for r, row in enumerate(SETS) for i, j in enumerate(row)}
    mine = jnp.concatenate([found[j] for j in range(2 * LOCAL)], axis=0).astype(bf16)

    def lanes(values, row):
        lane = lax.broadcasted_iota(jnp.int32, (H, D), 0)
        chosen = jnp.where(lane == lane_ref[row : row + 1, :], 1.0, 0.0).astype(bf16)
        return nn(values, chosen)

    tower = tv_ref[...].astype(bf16)
    rows = [lanes(mine, 0), lanes(mine, 1)]
    head = lane_ref[6:7, :] == 1
    for d in range(DOM):
        both = lanes(tower, 2 + d)
        rows.append(jnp.where(head, both[1:2], both[0:1]))
    return rows


def finish_kernel(
    ints, gb_ref, gb_in_ref, sum_ref, in_ref, ev_ref, proj_ref, tower_ref, gate_ref, *refs
):
    lane_ref, tv_ref, *vec_refs, ge_ref, small_ref, proj_sum, bias_sum = refs
    vec_refs, line_refs = vec_refs[: len(vec_refs) // 2], vec_refs[len(vec_refs) // 2 :]
    index = pl.program_id(0)
    last = pl.num_programs(0) - 1
    first = ints[ROLE] == 0
    at_home = jnp.where(ints[CORE] == ints[ROLE], 1.0, 0.0)
    mine_half = index == ints[ROLE]

    @pl.when(index == 0)
    def _():
        for ref in (proj_sum, bias_sum):
            ref[...] = jnp.zeros_like(ref)

    grad_mixed = jnp.where(mine_half, gb_ref[...], gb_in_ref[...].astype(f32))
    grad_mixed = at_home * (grad_mixed + sum_ref[...] + in_ref[...].astype(f32))
    bias_sum[0:1, :] += jnp.sum(grad_mixed, axis=0, keepdims=True)
    low = grad_mixed.astype(bf16)
    proj_sum[...] += tn(low, ev_ref[...])
    ge_ref[...] = nn(low, proj_ref[...]).astype(bf16)

    @pl.when(index == last)
    def _():
        e_in = proj_sum.shape[1]
        vectors = jnp.concatenate(
            [r[k, 0:3, :] for r in vec_refs for k in range(r.shape[0])], axis=0
        )
        rows = jnp.concatenate(
            [
                jnp.zeros((32, D), f32),
                jnp.where(first, vectors, 0.0),
                jnp.where(first, 0.0, vectors),
                bias_sum[0:1, :],
                *hidden_lines(ints, lane_ref, tv_ref, line_refs),
                jnp.zeros((31, D), f32),
            ],
            axis=0,
        )
        small_ref[:, :e_in] = proj_sum[...].astype(bf16)
        small_ref[:, e_in : e_in + DOM * TW] = tower_ref[...].astype(bf16)
        small_ref[:, e_in + DOM * TW :] = (gate_ref[...] + jnp.transpose(rows)).astype(bf16)


def call_finish(ints, gb, gb_in, added, arrived, events, small, tower, gate, lanes, tower_vec, sums):
    rows, e_in = events.shape
    half = rows // 2

    def tile(width):
        return pl.BlockSpec((half, width), lambda i, *_: (i, 0))

    halves = (gb, gb_in)
    wholes = (tower, gate, lanes, tower_vec)
    vecs = [v for v, _ in sums] + [b for _, b in sums]
    return pl.pallas_call(
        finish_kernel,
        grid_spec=pltpu.PrefetchScalarGridSpec(
            num_scalar_prefetch=1,
            grid=(2,),
            in_specs=[fixed(a.shape) for a in halves]
            + [tile(D), tile(D), tile(e_in), proj_spec(e_in)]
            + [fixed(a.shape) for a in (*wholes, *vecs)],
            out_specs=(tile(e_in), fixed((D, PACK))),
            scratch_shapes=[pltpu.VMEM((D, e_in), f32), pltpu.VMEM((8, D), f32)],
        ),
        out_shape=(jax.ShapeDtypeStruct((rows, e_in), bf16), jax.ShapeDtypeStruct((D, PACK), bf16)),
        compiler_params=params(),
        cost_estimate=cost(10),
        name="finish",
    )(ints, *halves, added, arrived, events, small, *wholes, *vecs)


VECTOR_ROW = {j: 32 + 18 * r + 3 * i for r, row in enumerate(SETS) for i, j in enumerate(row)}


def small_kernel(*refs):
    parts, vec_refs = refs[:-12], refs[-3:]
    proj_ref, tower_ref, top_ref, shared_ref, domain_ref, bias_ref, hidden_ref, tb_ref, to_ref = refs[-12:-3]
    added = functools.reduce(jnp.add, [p[...].astype(f32) for p in parts])
    width, e_in = proj_ref.shape
    proj_ref[...] = added[:, :e_in]
    for d in range(DOM):
        tower_ref[d] = added[:, e_in + d * TW : e_in + (d + 1) * TW]
    rows = jnp.concatenate([added[:, e_in + DOM * TW :], jnp.zeros((128 - width, 128), f32)], axis=0)
    rows = jnp.transpose(rows)[:, :width]
    for ref, low, size in ((top_ref, 0, 2), (shared_ref, 2 * DOM, S), (domain_ref, (2 + S) * DOM, K)):
        for d in range(DOM):
            ref[d] = rows[low + d * size : low + (d + 1) * size]
    bias_ref[...] = rows[68:69]
    hidden_ref[:, :width] = rows[69:81]
    hidden_ref[:, width:] = rows[81:93]
    tb_ref[...] = rows[93:97, : width // 2]
    to_ref[...] = rows[93:97, width // 2 :]
    for which, ref in enumerate(vec_refs):
        for j in range(2 * LOCAL):
            ref[j : j + 1, :] = rows[VECTOR_ROW[j] + which : VECTOR_ROW[j] + which + 1]


def call_small(parts):
    width = parts[0].shape[0]
    e_in = PACK - DOM * TW - 128
    shapes = [(width, e_in), (DOM, width, TW), (DOM, 2, width), (DOM, S, width), (DOM, K, width), (1, width)]
    shapes += [(2 * LOCAL, 2 * width), (DOM, width // 2), (DOM, width // 2)]
    shapes += [(2 * LOCAL, width)] * 3
    return pl.pallas_call(
        small_kernel,
        grid=(1,),
        in_specs=[fixed(p.shape) for p in parts],
        out_specs=tuple(fixed(shape) for shape in shapes),
        out_shape=tuple(jax.ShapeDtypeStruct(shape, f32) for shape in shapes),
        compiler_params=params(),
        name="small",
    )(*parts)


def place_kernel(ints, *refs):
    *parts, in_ref, out_ref = refs
    half = len(parts) // 2
    first = ints[ROLE] == 0
    for chunk, (own, other) in enumerate(zip(parts[:half], parts[half:])):
        for place, expert in enumerate(CHUNKS[chunk]):
            for which, ref in enumerate((in_ref, out_ref)):
                a, b = own[which, place].astype(f32), other[which, place].astype(f32)
                ref[SETS[0][expert]] = jnp.where(first, a, b)
                ref[SETS[1][expert]] = jnp.where(first, b, a)


def call_place(ints, own, other):
    rows, width = own[0].shape[2:]
    shape = (2 * LOCAL, rows, width)
    return pl.pallas_call(
        place_kernel,
        grid_spec=pltpu.PrefetchScalarGridSpec(
            num_scalar_prefetch=1,
            grid=(1,),
            in_specs=[fixed(a.shape) for a in (*own, *other)],
            out_specs=(fixed(shape), fixed(shape)),
        ),
        out_shape=(jax.ShapeDtypeStruct(shape, f32),) * 2,
        compiler_params=params(),
        name="place",
    )(ints, *own, *other)


def cost(microseconds):
    return pl.CostEstimate(flops=int(microseconds * 1.15e9), bytes_accessed=0, transcendentals=0)


def params():
    return pltpu.CompilerParams(vmem_limit_bytes=VMEM_LIMIT)


def fixed(shape):
    return pl.BlockSpec(shape, lambda i, *_: (0,) * len(shape))


def pack_kernel(proj_ref, tower_ref, gate_ref, rest_ref, out_ref):
    width, e_in = proj_ref.shape
    out_ref[:, :e_in] = proj_ref[...]
    for d in range(DOM):
        out_ref[:, e_in + d * TW : e_in + (d + 1) * TW] = tower_ref[d]
    gates, rest = gate_ref[...].astype(f32), rest_ref[...].astype(f32)
    rows = []
    for low, size in ((0, 2), (2, S), (2 + S, K)):
        rows += [gates[d, low : low + size] for d in range(DOM)]
    rows += [rest[:12, k * width : (k + 1) * width] for k in range(3)] + [rest[16:17, :width]]
    rows += [rest[:12, k * width : (k + 1) * width] for k in (3, 4)] + [rest[12:16, :width]]
    rows = jnp.concatenate(rows + [jnp.zeros((31, width), f32)], axis=0)
    rows = jnp.concatenate([rows, jnp.zeros((128, 128 - width), f32)], axis=1)
    out_ref[:, e_in + DOM * TW :] = jnp.transpose(rows)[:width].astype(bf16)


def call_pack(*arrays):
    width = arrays[0].shape[0]
    return pl.pallas_call(
        pack_kernel,
        grid=(1,),
        in_specs=[fixed(a.shape) for a in arrays],
        out_specs=fixed((width, PACK)),
        out_shape=jax.ShapeDtypeStruct((width, PACK), bf16),
        compiler_params=params(),
        name="pack",
    )(*arrays)


PICKED = [
    [32 + e for e in row] + [44 + e for e in row] + [56 + e for e in row] + [68] + [127] * 5
    + [69 + e for e in row] + [81 + e for e in row] + [93 + d for d in range(DOM)]
    for row in SETS
]


def unpack_kernel(ints, small_ref, choose_ref, lane_ref, vec_ref, bi_ref, tower_ref):
    vec = nt(choose_ref[0], small_ref[...])
    vec_ref[...] = vec

    def lanes(values, row):
        lane = lax.broadcasted_iota(jnp.int32, (H, D), 0)
        chosen = jnp.where(lane == lane_ref[row : row + 1, :], 1.0, 0.0).astype(bf16)
        return nt(values.astype(bf16), chosen)

    bias = lanes(jnp.concatenate([vec[24:30], jnp.zeros((2, D), f32)], axis=0), 0)
    bias += lanes(jnp.concatenate([vec[30:36], jnp.zeros((2, D), f32)], axis=0), 1)
    bi_ref[...] = jnp.where(ints[1] == 0, bias, pltpu.roll(bias, HALF, 1))
    head = lane_ref[6:7, :] == 1
    tower = jnp.zeros((8, H), f32)
    for d in range(DOM):
        row = vec[36 + d : 37 + d]
        rows = [jnp.where(head, 0.0, row), jnp.where(head, row, 0.0), jnp.zeros((6, D), f32)]
        tower += lanes(jnp.concatenate(rows, axis=0), 2 + d)
    tower_ref[...] = tower


def call_unpack(ints, small, lanes):
    choose = np.zeros((2, 40, 128), np.float32)
    for r in range(2):
        for row, column in enumerate(PICKED[r]):
            choose[r, row, column] = 1.0
    shapes = [(40, D), (8, H), (8, DOM * TW)]
    return pl.pallas_call(
        unpack_kernel,
        grid_spec=pltpu.PrefetchScalarGridSpec(
            num_scalar_prefetch=1,
            grid=(1,),
            in_specs=[
                pl.BlockSpec((D, 128), lambda i, ints: (0, PACK // 128 - 1)),
                pl.BlockSpec((1, 40, 128), lambda i, ints: (ints[0], 0, 0)),
                fixed(lanes.shape),
            ],
            out_specs=tuple(fixed(shape) for shape in shapes),
        ),
        out_shape=tuple(jax.ShapeDtypeStruct(shape, f32) for shape in shapes),
        compiler_params=params(),
        name="unpack",
    )(ints, small, jnp.asarray(choose, bf16), lanes)


def choose_kernel(own_ids, other_ids, in_own, out_own, in_other, out_other, *refs):
    own_refs, other_refs, all_ref = refs[:2], refs[2:4], refs[4]
    step = pl.program_id(0)
    for part in range(2):

        @pl.when(step // 3 == part)
        def _(part=part):
            own_refs[part][0], own_refs[part][1] = in_own[...], out_own[...]
            other_refs[part][0], other_refs[part][1] = in_other[...], out_other[...]

    all_ref[0], all_ref[1] = in_other[...], out_other[...]


def call_choose(own_ids, other_ids, w_in, w_out_t):
    tail = w_in.shape[1:]
    block = (1,) + tail

    def shape(count):
        return jax.ShapeDtypeStruct((2, count) + tail, bf16)

    own = pl.BlockSpec(block, lambda i, a, b: (a[i], 0, 0))
    other = pl.BlockSpec(block, lambda i, a, b: (b[i], 0, 0))
    low = pl.BlockSpec((2,) + block, lambda i, a, b: (0, jnp.minimum(i, 2), 0, 0))
    high = pl.BlockSpec((2,) + block, lambda i, a, b: (0, jnp.maximum(i - 3, 0), 0, 0))
    every = pl.BlockSpec((2,) + block, lambda i, a, b: (0, i, 0, 0))
    return pl.pallas_call(
        choose_kernel,
        grid_spec=pltpu.PrefetchScalarGridSpec(
            num_scalar_prefetch=2,
            grid=(LOCAL,),
            in_specs=[own, own, other, other],
            out_specs=(low, high, low, high, every),
        ),
        out_shape=(shape(3), shape(3), shape(3), shape(3), shape(6)),
        compiler_params=params(),
        cost_estimate=cost(1),
        name="choose",
    )(own_ids, other_ids, w_in, w_out_t, w_in, w_out_t)


def proj_spec(e_in):
    return pl.BlockSpec((D, e_in), lambda *_: (0, 0))


GATES_SPEC = pl.BlockSpec((D, 128), lambda *_: (0, PACK // 128 - 1))


def call_prepare(ints, floats, table, embeds, embeds_in, small, vec):
    rows = embeds.shape[0]
    tiles = rows // TILE
    e_in = embeds.shape[1]

    def tile(width):
        return pl.BlockSpec((TILE, width), lambda i, *_: (i, 0))

    return pl.pallas_call(
        prepare_kernel,
        grid_spec=pltpu.PrefetchScalarGridSpec(
            num_scalar_prefetch=2,
            grid=(tiles,),
            in_specs=[fixed(table.shape)]
            + [pl.BlockSpec(memory_space=pl.ANY)] * 2
            + [proj_spec(e_in), GATES_SPEC, fixed(vec.shape)],
            scratch_shapes=[pltpu.VMEM(embeds.shape, bf16), pltpu.SemaphoreType.DMA((1,))],
            out_specs=(
                tile(e_in),
                tile(D),
                tile(D),
                tile(128),
                pl.BlockSpec((8, TILE), lambda i, *_: (0, i)),
            ),
        ),
        out_shape=(
            pltpu.HBM((rows, e_in), bf16),
            pltpu.HBM((rows, D), bf16),
            jax.ShapeDtypeStruct((rows, D), f32),
            jax.ShapeDtypeStruct((rows, 128), f32),
            jax.ShapeDtypeStruct((8, rows), f32),
        ),
        compiler_params=params(),
        cost_estimate=cost(11),
        name="prepare",
    )(ints, floats, table, embeds, embeds_in, small, small, vec)


def half_spec(own, shape):
    rest = (0,) * (len(shape) - 1)
    return pl.BlockSpec(shape, lambda i, ints: ((ints[ROLE] if own else 1 - ints[ROLE]),) + rest)


def piece_spec(array, place):
    a, b, _, rows, width = array.shape
    return pl.BlockSpec((a, b, 1, rows, width), lambda i, *_: (0, 0, place(i), 0, 0))


MATRICES = [pltpu.VMEM((D, HALF), bf16)] * 4


def call_forward(experts, own, ints, x, weights, bi, vec, cols, mix, norms, gives=False):
    rows = x.shape[0]
    half = rows // 2
    arrays = sorted({e // 3 for e in experts})
    first = {a: min(k for k, e in enumerate(experts) if e // 3 == a) for a in arrays}
    number = {a: sum(1 for e in experts if e // 3 == a) for a in arrays}

    def place(a):
        return lambda i: jnp.clip(i - first[a], 0, number[a] - 1)

    weight_specs = [piece_spec(w, place(a)) for a in arrays for w in weights[a]]
    norm_specs = [
        pl.BlockSpec(
            (1, half, D),
            lambda i, ints, a=a: (place(a)(i), ints[ROLE] if own else 1 - ints[ROLE], 0),
        )
        for a in arrays
    ]
    kept = [norms[a] for a in arrays if a in norms]
    inputs = [x] + [w for a in arrays for w in weights[a]] + [bi, vec, cols, mix] + kept
    at = len(inputs) - len(kept)
    aliases = {at - 1: 0, at: 1}
    aliases.update({at + 1 + k: 2 + k for k in range(len(kept))})
    shared = sum(1 for e in experts if e < 2)
    out = pl.pallas_call(
        functools.partial(
            forward_kernel, experts, own, len(kept), len(weights[arrays[0]]), gives
        ),
        grid_spec=pltpu.PrefetchScalarGridSpec(
            num_scalar_prefetch=1,
            grid=(len(experts),),
            in_specs=[half_spec(own, (half, D))]
            + weight_specs
            + [fixed(bi.shape), fixed(vec.shape), half_spec(own, (half, 128)), half_spec(own, (half, D))]
            + [pl.BlockSpec(memory_space=pl.ANY)] * len(kept),
            out_specs=(half_spec(own, (half, 128)), half_spec(own, (half, D)), *norm_specs)
            + ((fixed((half, D)),) if gives else ()),
            scratch_shapes=MATRICES,
        ),
        out_shape=(
            jax.ShapeDtypeStruct((rows, 128), f32),
            jax.ShapeDtypeStruct((rows, D), f32),
            *[jax.ShapeDtypeStruct((3, rows, D), bf16)] * len(arrays),
        )
        + ((jax.ShapeDtypeStruct((half, D), bf16),) if gives else ()),
        input_output_aliases=aliases,
        compiler_params=params(),
        cost_estimate=cost(5 * len(experts) - 5 * (len(experts) > 3)),
        name="experts_forward",
    )(ints, *inputs)
    found = out[0], out[1], {**norms, **dict(zip(arrays, out[2:]))}
    return found + (out[-1],) if gives else found


def call_backward(experts, halves, ints, x, gbs, norms, weights, bi, vec, cols, back, sums=None):
    rows, count = x.shape[0], len(experts)
    part = rows // 2 * len(halves)
    array, low = experts[0] // 3, experts[0] % 3
    split = any(e // 3 != array for e in experts)

    def span(width):
        if len(halves) == 2:
            return fixed((rows, width))
        return half_spec(halves[0] == "own", (part, width))

    def norm_index(i, ints):
        if len(halves) == 2:
            return (low + i, 0, 0)
        return (low + i, ints[ROLE] if halves[0] == "own" else 1 - ints[ROLE], 0)

    assert not split
    pairs = pl.BlockSpec((1, 2, D, HALF), lambda i, *_: (i, 0, 0, 0))
    vec_spec = pl.BlockSpec((1, 8, D), lambda i, *_: (i, 0, 0))
    bi_spec = pl.BlockSpec((1, 8, H), lambda i, *_: (i, 0, 0))
    mode, back_array = back if back is not None else ("fresh", jnp.zeros((8, 128), f32))
    inputs = [x, *gbs, norms[array], *weights[array], bi, vec, cols, back_array]
    in_specs = (
        [span(D)]
        + [fixed(g.shape) for g in gbs]
        + [pl.BlockSpec((1, part, D), norm_index)]
        + [piece_spec(w, lambda i: low + i) for w in weights[array]]
        + [fixed(bi.shape), fixed(vec.shape), span(128)]
        + [span(D) if mode == "add" else pl.BlockSpec(memory_space=pl.ANY)]
    )
    aliases = {len(inputs) - 1: 0}
    if back is not None:
        aliases[len(inputs)] = 1
    if sums is not None:
        inputs += list(sums)
        in_specs += [vec_spec, bi_spec, pairs, pairs]
    return pl.pallas_call(
        functools.partial(
            backward_kernel, experts, halves, mode == "add", sums is not None, len(weights[array])
        ),
        grid_spec=pltpu.PrefetchScalarGridSpec(
            num_scalar_prefetch=1,
            grid=(count,),
            in_specs=in_specs,
            out_specs=(span(128), span(D), pairs, pairs, vec_spec, bi_spec),
            scratch_shapes=[pltpu.VMEM((D, HALF), f32)] * 4 + MATRICES,
        ),
        out_shape=(
            jax.ShapeDtypeStruct((rows, 128), f32),
            jax.ShapeDtypeStruct((rows, D), f32),
            jax.ShapeDtypeStruct((count, 2, D, HALF), bf16),
            jax.ShapeDtypeStruct((count, 2, D, HALF), bf16),
            jax.ShapeDtypeStruct((count, 8, D), f32),
            jax.ShapeDtypeStruct((count, 8, H), f32),
        ),
        input_output_aliases=aliases,
        compiler_params=params(),
        cost_estimate=cost(8 * count),
        name="experts_backward",
    )(ints, *inputs)


def call_tower(ints, mix, other, cols, small, tower_vec):
    rows = other.shape[0]
    tiles = 2
    size = rows // tiles

    def kept(width):
        return pl.BlockSpec((size, width), lambda i, ints: (ints[ROLE] * tiles + i, 0))

    def tile(width):
        return pl.BlockSpec((size, width), lambda i, *_: (i, 0))

    return pl.pallas_call(
        tower_kernel,
        grid_spec=pltpu.PrefetchScalarGridSpec(
            num_scalar_prefetch=1,
            grid=(tiles,),
            in_specs=[kept(D), tile(D), kept(128), fixed(small.shape), fixed(tower_vec.shape)],
            out_specs=(
                pl.BlockSpec((8, size), lambda i, *_: (0, i)),
                tile(D),
                tile(D),
                fixed((D, DOM * TW)),
                fixed((8, DOM * TW)),
                fixed((8, 128)),
            ),
        ),
        out_shape=(
            jax.ShapeDtypeStruct((8, rows), f32),
            pltpu.HBM((rows, D), f32),
            jax.ShapeDtypeStruct((rows, D), bf16),
            jax.ShapeDtypeStruct((D, DOM * TW), f32),
            jax.ShapeDtypeStruct((8, DOM * TW), f32),
            jax.ShapeDtypeStruct((8, 128), f32),
        ),
        compiler_params=params(),
        cost_estimate=cost(8.5),
        name="towers",
    )(ints, mix, other, cols, small, tower_vec)


def per_device(
    box,
    embeds,
    domain,
    frozen,
    labels,
    proj_w,
    proj_b,
    w_in,
    in_bias,
    w_out,
    out_bias,
    ln_gain,
    ln_shift,
    gate_top,
    gate_shared,
    gate_domain,
    tower_w,
    tower_b,
    tower_out,
    tower_out_b,
):
    core = lax.axis_index("tensor")
    role = box.role(lax.axis_index("dp"))
    at_home = core == role
    places = box.count
    rows = embeds.shape[0]
    half_rows = rows // 2
    width = proj_w.shape[1]
    e_in = proj_w.shape[0]
    nz, ny, nx = box.dims[1:]
    sets = jnp.array(SETS, jnp.int32)
    set_own, set_other = sets[role], sets[1 - role]

    def half(values, which, axis=0):
        return lax.dynamic_slice_in_dim(values, which * half_rows, half_rows, axis)

    w_out_t = jnp.swapaxes(w_out, 1, 2)
    first, second, first_other, second_other, others = call_choose(set_own, set_other, w_in, w_out_t)

    def wide(values):
        return jnp.pad(values, ((0, 0), (0, 5 * width - values.shape[1])))

    arrays = (
        proj_w.T,
        tower_w,
        jnp.concatenate([jnp.swapaxes(g, 1, 2) for g in (gate_top, gate_shared, gate_domain)], axis=1),
        jnp.concatenate(
            [
                jnp.concatenate([out_bias, ln_gain, ln_shift, in_bias], axis=1),
                wide(jnp.concatenate([tower_b, tower_out], axis=1)),
                wide(proj_b[None]),
            ]
        ),
    )

    flips = box.send(others, flip=1)
    first_z = box.line(first, first_other)
    pack = call_pack(*step(arrays, first)[0])
    pack = in_order(role, pack, box.send(pack, flip=1), 0)
    pack = jnp.concatenate([pack] + box.pieces(pack, "z"))
    flips, first, first_z, second, second_other = step(flips, first, first_z, second, second_other)

    def along_z(shard, flip, found):
        found = box.in_line(shard, flip, found, role, 2)
        return jnp.stack([b[0] for b in found]), jnp.stack([b[1] for b in found])

    first_i, first_o = along_z(first, flips[:, :3], first_z)
    first_iy, first_ox = box.pieces(first_i, "y"), box.pieces(first_o, "x")
    second_z = box.line(second, second_other)
    pack = jnp.concatenate([pack] + box.pieces(pack, "y"))
    pack = jnp.concatenate([pack] + box.pieces(pack, "x")).reshape(places, 1, width, PACK)
    domain, labels = step((domain, labels), first)[0]
    event_rows = jnp.concatenate(
        [domain.astype(f32).T, labels.astype(f32)[None], jnp.zeros((6, rows), f32)]
    )
    event_rows = jnp.where(at_home, event_rows, box.to_partner(event_rows, True))
    ids = event_rows[0]
    onehot = (ids[None, :] == jnp.arange(DOM, dtype=f32)[:, None]).astype(f32)
    rank = jnp.cumsum(onehot, axis=1)
    counts = rank[:, -1]
    ends = jnp.cumsum(counts)
    starts = ends - counts
    position = jnp.sum(onehot * (rank + starts[:, None]), axis=0) - 1.0
    embeds_in = box.to_partner(step(embeds, second_z[0])[0], True)
    first_i, first_o, first_iy, first_ox, second, second_z, flips, starts, ends, position = step(
        first_i, first_o, first_iy, first_ox, second, second_z, flips, starts, ends, position
    )

    small = in_order(core, pack, swap_cores(pack), 1).reshape(D, PACK)
    first_i = jnp.stack([first_i] + first_iy)
    first_o = jnp.stack([first_o] + first_ox)
    first_ix, first_oy = box.pieces(first_i, "x"), box.pieces(first_o, "y")
    second, flips, second_z, _ = step(second, flips, second_z, (first_i, first_o))
    second_i, second_o = along_z(second, flips[:, 3:], second_z)
    second_iy, second_ox = box.pieces(second_i, "y"), box.pieces(second_o, "x")

    at = lax.broadcasted_iota(jnp.int32, (8, D), 1)
    row = lax.broadcasted_iota(jnp.int32, (8, D), 0)
    unit, narrow = at % width, width // 2
    device = 2 * box.ahead(at // (2 * width)) + (at // width) % 2
    hidden = device * (2 * width) + jnp.where(row == 1, width, 0) + unit
    lanes = (row - 2) * TW + device * narrow + unit % narrow
    lanes = jnp.where(row < 2, hidden, jnp.where(row < 2 + DOM, lanes, unit // narrow))
    vec, bi, tower_vec = call_unpack(jnp.stack([role, core]), small, lanes)

    table = jnp.concatenate([position[None], event_rows[1:]])
    start_i, end_i = starts.astype(jnp.int32), ends.astype(jnp.int32)
    empty = end_i == start_i
    low = jnp.where(empty, 0, start_i // TILE)
    high = jnp.where(empty, 0, (end_i + TILE - 1) // TILE)
    domains = jnp.arange(DOM, dtype=jnp.int32)
    ints = jnp.concatenate(
        [
            jnp.where(role == 0, low[::-1], low),
            jnp.where(role == 0, high[::-1], high),
            role[None],
            jnp.where(role == 0, DOM - 1 - domains, domains),
            start_i,
            end_i,
            core[None],
            jnp.zeros((2,), jnp.int32),
        ]
    )
    loss_weight = 1.0 - (1.0 - FROZEN_SHARE) * frozen.astype(f32)
    floats = jnp.concatenate([loss_weight, tower_out_b.astype(f32)])
    events, x, mix, cols, probs = call_prepare(ints, floats, table, embeds, embeds_in, small, vec)
    (
        first_i, first_o, first_ix, first_oy, second_i, second_o, second_iy, second_ox,
        ints, events, x, mix, cols, probs, vec, bi, small, tower_vec, lanes,
    ) = step(
        first_i, first_o, first_ix, first_oy, second_i, second_o, second_iy, second_ox,
        ints, events, x, mix, cols, probs, vec, bi, small, tower_vec, lanes,
    )

    def pieces(i, ix, o, oy):
        own = [i] + ix + [o] + oy
        return own + [swap_cores(w) for w in own]

    second_i = jnp.stack([second_i] + second_iy)
    second_o = jnp.stack([second_o] + second_ox)
    second_ix, second_oy = box.pieces(second_i, "x"), box.pieces(second_o, "y")
    weights = {0: pieces(first_i, first_ix, first_o, first_oy)}
    cols, mix, norms = call_forward((0, 1, 2), False, ints, x, weights, bi, vec, cols, mix, {})
    second_ix, second_oy, cols, mix = step(second_ix, second_oy, cols, mix)
    weights[1] = pieces(second_i, second_ix, second_o, second_oy)
    cols, mix, norms, give_mix = call_forward(
        (3, 4), False, ints, x, weights, bi, vec, cols, mix, norms, True
    )
    give_mix, mix = step(give_mix, mix)
    other_mix = box.send(give_mix, flip=1)
    cols, mix, norms = call_forward(
        tuple(range(LOCAL)), True, ints, x, weights, bi, vec, cols, mix, norms
    )
    row_out, grad_block, grad_low, d_tower, d_tower_vec, d_logit_bias = call_tower(
        ints, mix, other_mix, cols, small, tower_vec
    )

    box_shape = (nx, ny, nz, 2, 2 * width, HALF)

    def both_cores(keeps, gives):
        def one(which):
            added = total(keeps[0][:, which], [a[:, which] for a in keeps[1:] + gives])
            return added.astype(bf16).reshape((-1,) + box_shape)

        return one(0), one(1)

    class Scatter:
        def __init__(self, *parts):
            i, o = [jnp.concatenate(p) for p in zip(*parts)]
            i, o = [i[:, k] for k in range(nx)], [o[:, :, k] for k in range(ny)]
            self.state = (i[0], o[0], box.hand_out(i, "x"), box.hand_out(o, "y"))

        def second(self):
            i, o, i_in, o_in = self.state
            i, o = total(i, i_in).astype(bf16), total(o, o_in).astype(bf16)
            i, o = [i[:, k] for k in range(ny)], [o[:, k] for k in range(nx)]
            self.state = (i[0], o[0], box.hand_out(i, "y"), box.hand_out(o, "x"))

        def third(self):
            i, o, i_in, o_in = self.state
            both = jnp.stack([total(i, i_in).astype(bf16), total(o, o_in).astype(bf16)])
            both = [both[:, :, k] for k in range(nz)]
            self.state = (both[0], box.hand_out(both, "z"))

        def fourth(self):
            both = total(*self.state)
            mine = lax.dynamic_index_in_dim(both, role, 2, keepdims=False)
            other = lax.dynamic_index_in_dim(both, 1 - role, 2, keepdims=False).astype(bf16)
            self.state = (mine, box.send(other, flip=1))

    def sync(scatters, *values):
        states, values = step([c.state for c in scatters], values)
        for c, state in zip(scatters, states):
            c.state = state
        return values

    common = (ints, x)
    shared = (norms, weights, bi, vec)
    grad_in = box.send(grad_low, flip=1)
    cols, back, keep_a, give_a, *sums = call_backward(
        (0, 1), ("own",), *common, [grad_low], *shared, cols, None
    )
    logit_in = swap_cores(d_logit_bias)
    grad_in, cols, back, keep_a, give_a, sums, logit_in = step(
        grad_in, cols, back, keep_a, give_a, sums, logit_in
    )
    d_logit_bias = d_logit_bias + logit_in
    cols, back, keep_b, give_b, *sums_0 = call_backward(
        (0, 1), ("other",), *common, [grad_in], *shared, cols, ("fresh", back), sums + [keep_a, give_a]
    )
    logit_in = box.pieces(d_logit_bias, "y")
    cols, back, keep_b, give_b, logit_in = step(cols, back, keep_b, give_b, logit_in)
    d_logit_bias = box.same_sum(d_logit_bias, logit_in, "y")
    give_b = swap_cores(give_b)
    grads = [grad_low, grad_in]
    cols, back, keep_c, give_c, *sums_1 = call_backward(
        (2,), ("own", "other"), *common, grads, *shared, cols, ("add", back)
    )
    logit_in = box.pieces(d_logit_bias, "x")
    cols, back, keep_b, give_b, keep_c, give_c, row_out, logit_in = step(
        cols, back, keep_b, give_b, keep_c, give_c, row_out, logit_in
    )
    d_logit_bias = box.same_sum(d_logit_bias, logit_in, "x")
    give_c = swap_cores(give_c)
    ab = both_cores([keep_b], [give_b])
    give_c, keep_c, ab, cols = step(give_c, keep_c, ab, cols)
    c0 = Scatter(ab, both_cores([keep_c], [give_c]))
    cols, back, keep_d, give_d, *sums_2 = call_backward(
        (3, 4, 5), ("own", "other"), *common, grads, *shared, cols, ("add", back)
    )
    rows_in = box.to_partner(row_out, False)
    logit_in = box.pieces(d_logit_bias, "flip")
    cols, back, keep_d, give_d, rows_in, logit_in = sync(
        [c0], cols, back, keep_d, give_d, rows_in, logit_in
    )
    d_logit_bias = box.same_sum(d_logit_bias, logit_in, "flip")
    c0.second()
    give_d = swap_cores(give_d)
    g_sum, g_low, d_gate = call_gate(ints, back, cols, probs, x, small)
    cd = both_cores([keep_d], [give_d])
    logit_in = box.pieces(d_logit_bias, "z")
    g_sum, g_low, d_gate, cd, logit_in = sync([c0], g_sum, g_low, d_gate, cd, logit_in)
    d_logit_bias = box.same_sum(d_logit_bias, logit_in, "z")
    c1 = Scatter(cd)
    back_in = box.to_partner(g_low, False)
    (back_in,) = sync([c0, c1], back_in)
    c0.third()
    c1.second()
    back_in, _ = step(back_in, c1.state[:2])
    grad_events, d_small = call_finish(
        ints, grad_block, grad_in, g_sum, back_in, events, small, d_tower, d_gate, lanes, d_tower_vec,
        [sums_0, sums_1, sums_2],
    )
    grad_events, d_small = sync([c0, c1], grad_events, d_small)
    c1.third()
    c0.fourth()
    d_small, _ = step(d_small, c1.state[0])
    d_small = d_small.reshape(places, 2, width, PACK)
    d_other = swap_cores(lax.dynamic_index_in_dim(d_small, 1 - core, 1, keepdims=False))
    d_mine = total(lax.dynamic_index_in_dim(d_small, core, 1, keepdims=False), [d_other])
    d_mine = d_mine.astype(bf16).reshape(nx * ny, nz, 2, width, PACK)
    d_parts = [d_mine[k] for k in range(nx * ny)]
    d_in = box.hand_out_plane(d_parts)
    order = position[None, :] == jnp.arange(rows, dtype=f32)[:, None]
    grad_embeds = lax.dot_general(
        order.astype(bf16), grad_events, (((0,), (0,)), ((), ())), preferred_element_type=f32
    ).astype(bf16)
    predicted = in_order(role, row_out, rows_in, 1)
    predictions = jnp.sum(jnp.where(order, predicted[0][:, None], 0.0), axis=0)
    predictions = jnp.broadcast_to(predictions[None], (8, rows))
    d_mine, d_in, grad_embeds, predictions = sync(
        [c0, c1], d_parts[0], d_in, grad_embeds, predictions
    )
    c1.fourth()
    d_mine, _ = step(d_mine, c1.state[0])
    d_mine = total(d_mine, d_in).astype(bf16)
    same = [lax.dynamic_index_in_dim(d_mine[k], role, 0, keepdims=False) for k in range(nz)]
    flip = [lax.dynamic_index_in_dim(d_mine[k], 1 - role, 0, keepdims=False) for k in range(nz)]
    d_in = box.hand_out(same, "z") + box.hand_out_flip(flip)
    grad_embeds = jnp.where(at_home, grad_embeds, swap_cores(grad_embeds))
    predictions = jnp.where(at_home, predictions, swap_cores(predictions))[0]
    d_in, grad_embeds, predictions = sync([c1], d_in, grad_embeds, predictions)
    (
        proj_grad, tower_grad, top, shared_gate, domain_gate, proj_b_grad, in_bias_grad, tower_b_grad,
        tower_out_grad, *vectors,
    ) = call_small([same[0]] + d_in)
    grad_w_in, grad_w_out = call_place(
        ints, [c0.state[0], c1.state[0]], [c0.state[1], c1.state[1]]
    )
    return (
        predictions,
        grad_embeds,
        proj_grad.T,
        proj_b_grad[0],
        grad_w_in,
        in_bias_grad,
        jnp.swapaxes(grad_w_out, 1, 2),
        *vectors,
        jnp.swapaxes(top, 1, 2),
        jnp.swapaxes(shared_gate, 1, 2),
        jnp.swapaxes(domain_gate, 1, 2),
        tower_grad,
        tower_b_grad,
        tower_out_grad,
        d_logit_bias[0, :DOM],
    )


def solution(mesh):
    both = ("dp", "tensor")
    in_specs = (
        P("dp", None),
        P("dp", None),
        P(),
        P("dp"),
        P(None, both),
        P(both),
        P(None, "dp", "tensor"),
        P(None, both),
        P(None, "tensor", "dp"),
        P(None, both),
        P(None, both),
        P(None, both),
        P(None, both, None),
        P(None, both, None),
        P(None, both, None),
        P(None, both, None),
        P(None, both),
        P(None, both),
        P(),
    )
    out_specs = (
        P("dp"),
        P("dp", None),
        P(None, both),
        P(both),
        P(None, "dp", "tensor"),
        P(None, both),
        P(None, "tensor", "dp"),
        P(None, both),
        P(None, both),
        P(None, both),
        P(None, both, None),
        P(None, both, None),
        P(None, both, None),
        P(None, both, None),
        P(None, both),
        P(None, both),
        P(),
    )
    return jax.shard_map(
        functools.partial(per_device, Box(mesh.shape["dp"])),
        mesh=mesh,
        in_specs=in_specs,
        out_specs=out_specs,
        check_vma=False,
    )
```
